32 devices in a mesh: dp: 16 (over z, y, x), tensor: 2 (over core).
Axes of the slice: x: 2, y: 2, z: 4, core: 2. Of those that a mesh axis runs over, the one named last changes fastest.
Arguments:
- latents: float32 [256, 256, 16], P('dp'), may hold values from -6 to 6
- gauss_noise: float32 [256, 256, 16], P('dp'), may hold values from -6 to 6
- time_steps: float32 [256], P('dp'), may hold values from 0.05 to 0.95
- labels: int32 [256], replicated, may hold values from 0 to 999
- targets: float32 [256, 256, 16], P('dp'), may hold values from -12 to 12, as said below
- w_col: float32 [2, 384, 2688], P(None, 'dp', 'tensor'), may hold values from -0.3125 to 0.3125
- w_row: float32 [2, 1920, 384], P(None, 'tensor', 'dp'), may hold values from -0.3125 to 0.3125
- w_cond: float32 [384, 5376], P('dp'), may hold values from -0.3125 to 0.3125
- w_time: float32 [640, 384], P('dp'), may hold values from -0.375 to 0.375
- w_io: float32 [2, 384, 16], P(None, 'dp'), may hold values from -0.75 to 0.75
- class_table: float32 [1000, 384], P(None, 'dp'), may hold values from -0.3125 to 0.3125
- b_col: float32 [2, 2688], P(None, 'tensor'), may hold values from -1.75 to 1.75
- b_rep: float32 [8080], replicated, may hold values from -1.75 to 1.75
- mom_col: float32 [2, 384, 2688], P(None, 'dp', 'tensor'), may hold values from -0.01953125 to 0.01953125
- mom_row: float32 [2, 1920, 384], P(None, 'tensor', 'dp'), may hold values from -0.01953125 to 0.01953125
- mom_cond: float32 [384, 5376], P('dp'), may hold values from -0.01953125 to 0.01953125
- mom_time: float32 [640, 384], P('dp'), may hold values from -0.01953125 to 0.01953125
- mom_io: float32 [2, 384, 16], P(None, 'dp'), may hold values from -0.0625 to 0.0625
- mom_table: float32 [1000, 384], P(None, 'dp'), may hold values from -0.0012207031 to 0.0012207031
- mom_bcol: float32 [2, 2688], P(None, 'tensor'), may hold values from -0.0625 to 0.0625
- mom_brep: float32 [8080], replicated, may hold values from -0.0625 to 0.0625
- err_col: float32 [32, 384, 2688], P('dp', None, 'tensor'), may hold values from -6144 to 6144
- err_row: float32 [32, 1920, 384], P('dp', 'tensor'), may hold values from -6144 to 6144
- err_io: float32 [32, 384, 16], P('dp'), may hold values from -65536 to 65536
- fac_col: float32 [2, 2688, 8], P(None, 'tensor'), may hold values from -6 to 6
- fac_row: float32 [2, 768, 8], P(None, 'tensor'), may hold values from -6 to 6
- fac_io: float32 [2, 16, 8], replicated, may hold values from -6 to 6
Outputs:
- loss_sum: float32 [], replicated
- clip_norm: float32 [], replicated
- next_w_col: float32 [2, 384, 2688], P(None, 'dp', 'tensor')
- next_w_row: float32 [2, 1920, 384], P(None, 'tensor', 'dp')
- next_w_cond: float32 [384, 5376], P('dp')
- next_w_time: float32 [640, 384], P('dp')
- next_w_io: float32 [2, 384, 16], P(None, 'dp')
- next_table: float32 [1000, 384], P(None, 'dp')
- next_b_col: float32 [2, 2688], P(None, 'tensor')
- next_b_rep: float32 [8080], replicated
- next_mom_col: float32 [2, 384, 2688], P(None, 'dp', 'tensor')
- next_mom_row: float32 [2, 1920, 384], P(None, 'tensor', 'dp')
- next_mom_cond: float32 [384, 5376], P('dp')
- next_mom_time: float32 [640, 384], P('dp')
- next_mom_io: float32 [2, 384, 16], P(None, 'dp')
- next_mom_table: float32 [1000, 384], P(None, 'dp')
- next_mom_bcol: float32 [2, 2688], P(None, 'tensor')
- next_mom_brep: float32 [8080], replicated
- next_err_col: float32 [32, 384, 2688], P('dp', None, 'tensor')
- next_err_row: float32 [32, 1920, 384], P('dp', 'tensor')
- next_err_io: float32 [32, 384, 16], P('dp')
- next_fac_col: float32 [2, 2688, 8], P(None, 'tensor')
- next_fac_row: float32 [2, 768, 8], P(None, 'tensor')
- next_fac_io: float32 [2, 16, 8], replicated
The draws below stay inside these ranges and needn't reach their ends.
Inputs may be any that keep to these rules, and one draw needn't show every extreme that they name: `targets`: rows of velocity grow in size along the latents.
All inputs are finite; a program needn't handle non-finite values.
Results may differ from the reference program's by a relative error of at most 0.00045.
The reference program's roundings to bfloat16 on the way count: a program that leaves them out, or rounds other values in their place, can miss the bound.
Values may be sent and summed in bfloat16 or wider, within the bound.
No kernel may reach another device: no remote copies, remote signals or barrier semaphores. Data moves between devices by JAX's collectives and lax.ppermute only.
A program may use at most 320 MiB of HBM per device.

```python
import jax
import jax.numpy as jnp
from jax import lax

D = 384
HEADS = 6
HD = 64
MLP = 1536
CLASSES = 1000
FREQ = 256
PV = 16
GRID = 16
L = 2
MB = 2
R = 8
LAT_DEV = 8
TOK = 256
LATENTS = 256
NBR = 8080
N_DP = 16
N_TENSOR = 2


def draw_targets(key, part):
    key = jax.random.fold_in(key, 11)
    ramp = jnp.arange(LATENTS, dtype=jnp.float32) / (LATENTS - 1)
    values = jax.random.truncated_normal(key, -4.0, 4.0, (LATENTS, TOK, PV), jnp.float32)
    scale = 1.0 + 2.0 * ramp
    return values * scale[:, None, None]


def set_ends(drawn, rng, smallest, largest):
    longest = drawn.shape.index(max(drawn.shape))
    spots = []
    for shift in (0, 1):
        where = [jax.random.randint(jax.random.fold_in(rng, axis), (), 0, length) for axis, length in enumerate(drawn.shape)]
        where[longest] = (where[longest] + shift) % drawn.shape[longest]
        spots.append(tuple(where))
    return drawn.at[spots[0]].set(smallest).at[spots[1]].set(largest)


def shard_levels(stream_key, dims, cuts, low, high):
    level, own = 1.0, jax.random.fold_in(stream_key, 6)
    for axis_at, shards_of in cuts:
        heights = jnp.exp(jax.random.uniform(jax.random.fold_in(own, axis_at), (shards_of,), jnp.float32, low / len(cuts), high / len(cuts)))
        level = level * jnp.repeat(heights, dims[axis_at] // shards_of).reshape([-1 if axis == axis_at else 1 for axis in range(len(dims))])
    return level


def gaussian(rng, shape, spread, most, cuts=(), kind=jnp.bfloat16):
    values = jax.random.normal(rng, shape, jnp.float32) * spread
    if len(cuts) > 0:
        values = shard_levels(rng, shape, cuts, -0.22, 0.18) * values
    return jnp.clip(values, min=-most, max=most).astype(kind)


def setup_inputs(seed: int = 0) -> dict:
    seeds = jax.random.split(jax.random.key(seed), 28)
    return {
        "latents": gaussian(seeds[0], (LATENTS, TOK, PV), 1.0, 6.0, ((0, 16),), jnp.float32),
        "gauss_noise": gaussian(seeds[1], (LATENTS, TOK, PV), 1.0, 6.0, ((0, 16),), jnp.float32),
        "time_steps": jnp.clip(0.05 + 0.9 * jax.random.uniform(seeds[2], (LATENTS,), jnp.float32) ** shard_levels(seeds[2], (LATENTS,), ((0, 16),), -0.2, 0.2), 0.05, 0.95),
        "labels": set_ends(jax.random.randint(seeds[3], (LATENTS,), 0, CLASSES), jax.random.fold_in(seeds[3], 1), 0, CLASSES - 1).astype(jnp.int32),
        "targets": draw_targets(jax.random.fold_in(seeds[27], 71), 0),
        "w_col": gaussian(seeds[5], (L, D, 3 * D + MLP), D ** -0.5, 0.3125, ((1, 16), (2, 2)), jnp.float32),
        "w_row": gaussian(seeds[6], (L, D + MLP, D), D ** -0.5, 0.3125, ((1, 2), (2, 16)), jnp.float32),
        "w_cond": gaussian(seeds[7], (D, (6 * L + 2) * D), D ** -0.5, 0.3125, ((0, 16),), jnp.float32),
        "w_time": gaussian(seeds[8], (FREQ + D, D), FREQ ** -0.5, 0.375, ((0, 16),), jnp.float32),
        "w_io": gaussian(seeds[9], (2, D, PV), (4 * PV) ** -0.5, 0.75, ((1, 16),), jnp.float32),
        "class_table": gaussian(seeds[10], (CLASSES, D), 0.05, 0.3125, ((1, 16),), jnp.float32),
        "b_col": gaussian(seeds[11], (L, 3 * D + MLP), 0.3, 1.75, ((1, 2),), jnp.float32),
        "b_rep": gaussian(seeds[12], (NBR,), 0.3, 1.75, (), jnp.float32),
        "mom_col": gaussian(seeds[13], (L, D, 3 * D + MLP), (9.0 / (43 * D * D) ** 0.5), 0.01953125, ((1, 16), (2, 2)), jnp.float32),
        "mom_row": gaussian(seeds[14], (L, D + MLP, D), (9.0 / (43 * D * D) ** 0.5), 0.01953125, ((1, 2), (2, 16)), jnp.float32),
        "mom_cond": gaussian(seeds[15], (D, (6 * L + 2) * D), (9.0 / (43 * D * D) ** 0.5), 0.01953125, ((0, 16),), jnp.float32),
        "mom_time": gaussian(seeds[16], (FREQ + D, D), (9.0 / (43 * D * D) ** 0.5), 0.01953125, ((0, 16),), jnp.float32),
        "mom_io": gaussian(seeds[17], (2, D, PV), (30.0 / (43 * D * D) ** 0.5), 0.0625, ((1, 16),), jnp.float32),
        "mom_table": gaussian(seeds[18], (CLASSES, D), (0.5 / (43 * D * D) ** 0.5), 0.0012207031, ((1, 16),), jnp.float32),
        "mom_bcol": gaussian(seeds[19], (L, 3 * D + MLP), (30.0 / (43 * D * D) ** 0.5), 0.0625, ((1, 2),), jnp.float32),
        "mom_brep": gaussian(seeds[20], (NBR,), (30.0 / (43 * D * D) ** 0.5), 0.0625, (), jnp.float32),
        "err_col": gaussian(seeds[21], (N_DP * L, D, 3 * D + MLP), (TOK * (LAT_DEV * MB) ** 0.5), 6144.0, ((0, 16), (2, 2)), jnp.float32),
        "err_row": gaussian(seeds[22], (N_DP * L, D + MLP, D), (TOK * (LAT_DEV * MB) ** 0.5), 6144.0, ((0, 16), (1, 2)), jnp.float32),
        "err_io": gaussian(seeds[23], (N_DP * 2, D, PV), (10 * TOK * (LAT_DEV * MB) ** 0.5), 65536.0, ((0, 16),), jnp.float32),
        "fac_col": gaussian(seeds[24], (L, 3 * D + MLP, R), 1.0, 6.0, ((1, 2),), jnp.float32),
        "fac_row": gaussian(seeds[25], (L, N_TENSOR * D, R), 1.0, 6.0, ((1, 2),), jnp.float32),
        "fac_io": gaussian(seeds[26], (2, PV, R), 1.0, 6.0, (), jnp.float32),
    }


highest = lax.Precision.HIGHEST
norm_eps = 1e-06
ortho_eps = 1e-06
clip_limit = 1.0
momentum_decay = 0.9
learn_rate = 4.0

@jax.custom_vjp
def low(v):
    return lax.optimization_barrier(v.astype(jnp.bfloat16)).astype(jnp.float32)

@jax.custom_vjp
def low_back(v):
    return v

def low_keep(v):
    return (low(v), None)

def low_pass(kept, grad):
    return (grad,)

def back_keep(v):
    return (v, None)

def back_low(kept, grad):
    return (low(grad),)
low.defvjp(low_keep, low_pass)
low_back.defvjp(back_keep, back_low)

def product(left, right):
    return jnp.matmul(left, right, precision=highest)

def position_table():
    quarter = D // 4
    omega = 1.0 / 10000.0 ** (jnp.arange(quarter, dtype=jnp.float32) / quarter)
    index = jnp.arange(TOK, dtype=jnp.int32)
    across = (index % GRID).astype(jnp.float32)[:, None] * omega[None, :]
    down = (index // GRID).astype(jnp.float32)[:, None] * omega[None, :]
    return jnp.concatenate([jnp.sin(across), jnp.cos(across), jnp.sin(down), jnp.cos(down)], 1)

def frequency_features(steps):
    half = FREQ // 2
    rates = jnp.exp(-jnp.log(10000.0) * jnp.arange(half, dtype=jnp.float32) / half)
    angles = steps[:, None] * rates[None, :]
    return jnp.concatenate([jnp.cos(angles), jnp.sin(angles)], 1)

def normalize(values):
    centered = values - lax.optimization_barrier(jnp.mean(values, -1, keepdims=True))
    return centered * lax.rsqrt(lax.optimization_barrier(jnp.mean(centered * centered, -1, keepdims=True)) + norm_eps)

def modulate(values, shift, scale):
    return normalize(values) * (1.0 + scale[:, None, :]) + shift[:, None, :]

def bias_offsets():
    start_cond = 2 * L * D
    start_first = start_cond + (6 * L + 2) * D
    return (L * D, start_cond, start_first, start_first + D, start_first + 2 * D, start_first + 3 * D)

def forward(params, inputs):
    w_col, w_row, w_cond, w_time, w_io, class_table, b_col, b_rep = params
    latents, gauss_noise, time_steps, labels, targets = inputs
    col_width = (3 * D + MLP) // N_TENSOR
    qkv_width = 3 * D // N_TENSOR
    row_width = (D + MLP) // N_TENSOR
    attn_rows = D // N_TENSOR
    start_fc2, start_cond, start_first, start_second, start_patch, start_head = bias_offsets()
    count = latents.shape[0]
    steps_col = time_steps[:, None, None]
    mixed_in = low((1.0 - steps_col) * latents + steps_col * gauss_noise)
    first = low_back(product(low(frequency_features(time_steps)), low(w_time[:FREQ])) + b_rep[start_first:start_second])
    second = low_back(product(low(jax.nn.silu(first)), low(w_time[FREQ:])) + b_rep[start_second:start_patch])
    cond = second + low(class_table)[labels]
    mods = low_back(product(low(jax.nn.silu(cond)), low(w_cond)) + b_rep[start_cond:start_first])
    embedded = jnp.einsum('ntp,dp->ntd', mixed_in, low(w_io[0]), precision=highest)
    hidden = low_back(embedded + b_rep[start_patch:start_head]) + position_table()[None]
    for layer in range(L):
        col_blocks = low(w_col[layer]).reshape(D, N_TENSOR, col_width)
        w_qkv = col_blocks[:, :, :qkv_width].reshape(D, 3 * D)
        w_fc1 = col_blocks[:, :, qkv_width:].reshape(D, MLP)
        bias_blocks = b_col[layer].reshape(N_TENSOR, col_width)
        row_blocks = low(w_row[layer]).reshape(N_TENSOR, row_width, D)
        w_proj = row_blocks[:, :attn_rows].reshape(D, D)
        w_fc2 = row_blocks[:, attn_rows:].reshape(MLP, D)
        parts = [mods[:, (6 * layer + j) * D:(6 * layer + j + 1) * D] for j in range(6)]
        input_a = low(modulate(hidden, parts[0], parts[1]))
        qkv = low(low_back(product(input_a, w_qkv) + bias_blocks[:, :qkv_width].reshape(3 * D)))
        qkv = qkv.reshape(count, TOK, HEADS, 3, HD)
        scores = jnp.einsum('nqhd,nkhd->nhqk', qkv[:, :, :, 0], qkv[:, :, :, 1], precision=highest)
        scores = low_back(scores * HD ** (-0.5))
        probs = low(jax.nn.softmax(scores, -1))
        attended = jnp.einsum('nhqk,nkhd->nqhd', probs, qkv[:, :, :, 2], precision=highest).reshape(count, TOK, D)
        attended = low(low_back(attended))
        branch_a = low_back(product(attended, w_proj) + b_rep[layer * D:(layer + 1) * D])
        hidden = hidden + parts[2][:, None, :] * branch_a
        input_m = low(modulate(hidden, parts[3], parts[4]))
        pre_act = low_back(product(input_m, w_fc1) + bias_blocks[:, qkv_width:].reshape(MLP))
        acted = low(jax.nn.gelu(pre_act, approximate=True))
        branch_m = low_back(product(acted, w_fc2) + b_rep[start_fc2 + layer * D:start_fc2 + (layer + 1) * D])
        hidden = hidden + parts[5][:, None, :] * branch_m
    base = 6 * L * D
    input_f = low(modulate(hidden, mods[:, base:base + D], mods[:, base + D:base + 2 * D]))
    predicted = jnp.einsum('ntd,dp->ntp', input_f, low(w_io[1]), precision=highest)
    predicted = low_back(predicted + b_rep[start_head:start_head + PV])
    miss = predicted - targets
    return jnp.sum(miss * miss)

def orthonormal(basis):
    columns = []
    for index in range(basis.shape[-1]):
        column = basis[..., index]
        for earlier in columns:
            column = column - lax.optimization_barrier(jnp.sum(earlier * column, -1, keepdims=True)) * earlier
        column = column * lax.rsqrt(lax.optimization_barrier(jnp.sum(column * column, -1, keepdims=True)) + ortho_eps)
        columns.append(column)
    return jnp.stack(columns, -1)

def compress(matrices, factor):
    total = lax.optimization_barrier(jnp.sum(matrices, 0))
    basis = orthonormal(jnp.einsum('...nm,...mr->...nr', total, factor, precision=highest))
    fresh = jnp.einsum('...nm,...nr->...mr', total, basis, precision=highest)
    approx = jnp.einsum('...nr,...mr->...nm', basis, fresh, precision=highest)
    return (approx, fresh, matrices - approx[None])

def reference(latents, gauss_noise, time_steps, labels, targets, w_col, w_row, w_cond, w_time, w_io, class_table, b_col, b_rep, mom_col, mom_row, mom_cond, mom_time, mom_io, mom_table, mom_bcol, mom_brep, err_col, err_row, err_io, fac_col, fac_row, fac_io):
    per_device = LAT_DEV * MB
    params = (w_col, w_row, w_cond, w_time, w_io, class_table, b_col, b_rep)

    def split(values):
        return values.reshape((N_DP, per_device) + values.shape[1:])
    data = (split(latents), split(gauss_noise), split(time_steps), split(labels), split(targets))

    def device_grads(inputs):
        value, pull = jax.vjp(lambda weights: forward(weights, inputs), params)
        return (value, pull(jnp.ones_like(value))[0])
    losses, grads = lax.map(device_grads, data)
    col_width = (3 * D + MLP) // N_TENSOR
    row_width = (D + MLP) // N_TENSOR
    col_mats = (grads[0] + err_col.reshape(N_DP, L, D, 3 * D + MLP)).reshape(N_DP, L, D, N_TENSOR, col_width)
    col_mats = col_mats.transpose(0, 1, 3, 2, 4)
    col_approx, col_fresh, col_err = compress(col_mats, fac_col.reshape(L, N_TENSOR, col_width, R))
    row_mats = (grads[1] + err_row.reshape(N_DP, L, D + MLP, D)).reshape(N_DP, L, N_TENSOR, row_width, D)
    row_approx, row_fresh, row_err = compress(row_mats, fac_row.reshape(L, N_TENSOR, D, R))
    io_mats = grads[4] + err_io.reshape(N_DP, 2, D, PV)
    io_approx, io_fresh, io_err = compress(io_mats, fac_io)
    cond_grad = lax.optimization_barrier(jnp.sum(grads[2], 0))
    time_grad = lax.optimization_barrier(jnp.sum(grads[3], 0))
    table_grad = lax.optimization_barrier(jnp.sum(grads[5], 0))
    bcol_grad = lax.optimization_barrier(jnp.sum(grads[6], 0))
    brep_grad = lax.optimization_barrier(jnp.sum(grads[7], 0))
    col_grad = col_approx.transpose(0, 2, 1, 3).reshape(L, D, 3 * D + MLP)
    row_grad = row_approx.reshape(L, D + MLP, D)
    pieces = (col_grad, row_grad, cond_grad, time_grad, io_approx, table_grad, bcol_grad, brep_grad)
    square = jnp.zeros((), jnp.float32)
    for piece in pieces:
        square = square + jnp.sum(piece * piece)
    clip_norm = jnp.sqrt(square)
    scaling = jnp.minimum(1.0, clip_limit / clip_norm)
    olds = (w_col, w_row, w_cond, w_time, w_io, class_table, b_col, b_rep)
    moms = (mom_col, mom_row, mom_cond, mom_time, mom_io, mom_table, mom_bcol, mom_brep)
    next_moms = tuple((momentum_decay * m + scaling * g for m, g in zip(moms, pieces)))
    next_weights = tuple((w - learn_rate * m for w, m in zip(olds, next_moms)))
    next_err_col = col_err.transpose(0, 1, 3, 2, 4).reshape(N_DP * L, D, 3 * D + MLP)
    next_err_row = row_err.reshape(N_DP * L, D + MLP, D)
    next_err_io = io_err.reshape(N_DP * 2, D, PV)
    next_fac_col = col_fresh.reshape(L, 3 * D + MLP, R)
    next_fac_row = row_fresh.reshape(L, N_TENSOR * D, R)
    return (jnp.sum(losses), clip_norm, next_weights[0], next_weights[1], next_weights[2], next_weights[3], next_weights[4], next_weights[5], next_weights[6], next_weights[7], next_moms[0], next_moms[1], next_moms[2], next_moms[3], next_moms[4], next_moms[5], next_moms[6], next_moms[7], next_err_col, next_err_row, next_err_io, next_fac_col, next_fac_row, io_fresh)
```

```python
import jax
import jax.numpy as jnp
import numpy as np
from jax import lax
from jax.experimental import pallas as pl
from jax.experimental.pallas import tpu as pltpu
from jax.sharding import PartitionSpec as P

D = 384
HEADS = 6
HD = 64
MLP = 1536
CLASSES = 1000
FREQ = 256
PV = 16
GRID = 16
L = 2
TOK = 256
RANK = 8

norm_eps = 1e-06
ortho_eps = 1e-06
clip_limit = 1.0
momentum_decay = 0.9
learn_rate = 4.0

HALF = D // 2
HMLP = MLP // 2
QKV_S = 3 * HALF
COL_S = QKV_S + HMLP
ROW_S = HALF + HMLP
OFF_W2 = HMLP
OFF_Q = 2 * HMLP
GATH = 2 * HMLP + 4 * HALF

f32 = jnp.float32
bf16 = jnp.bfloat16
highest = lax.Precision.HIGHEST
NN = (((1,), (0,)), ((), ()))
NT = (((1,), (1,)), ((), ()))
TN = (((0,), (0,)), ((), ()))


def dot(left, right, dims=NN):
    return lax.dot_general(left, right, dims, preferred_element_type=f32)


def dot_full(left, right, dims=NN):
    return lax.dot_general(left, right, dims, precision=highest, preferred_element_type=f32)


def position_table():
    quarter = D // 4
    omega = 1.0 / 10000.0 ** (np.arange(quarter, dtype=np.float32) / quarter)
    index = np.arange(TOK)
    across = (index % GRID).astype(np.float32)[:, None] * omega[None, :].astype(np.float32)
    down = (index // GRID).astype(np.float32)[:, None] * omega[None, :].astype(np.float32)
    table = np.concatenate([np.sin(across), np.cos(across), np.sin(down), np.cos(down)], 1)
    return table.astype(np.float32)


def frequency_features(steps):
    half = FREQ // 2
    rates = jnp.exp(-jnp.log(10000.0) * jnp.arange(half, dtype=f32) / half)
    angles = steps[:, None] * rates[None, :]
    return jnp.concatenate([jnp.cos(angles), jnp.sin(angles)], 1)


def normalize(values):
    centered = values - jnp.mean(values, -1, keepdims=True)
    inv_std = lax.rsqrt(jnp.mean(centered * centered, -1, keepdims=True) + norm_eps)
    return centered * inv_std, inv_std


def norm_back(grad, normed, inv_std):
    mean_grad = jnp.mean(grad, -1, keepdims=True)
    mean_mixed = jnp.mean(grad * normed, -1, keepdims=True)
    return inv_std * (grad - mean_grad - normed * mean_mixed)


def token_sum(values):
    return jnp.sum(values, 0, keepdims=True)


def assemble(own, other, wqkv, wo):
    for part in range(3):
        start = OFF_Q + part * HALF
        wqkv[:, part * D : part * D + HALF] = own[:, start : start + HALF]
        wqkv[:, part * D + HALF : (part + 1) * D] = other[:, start : start + HALF]
    start = OFF_Q + 3 * HALF
    wo[:, :HALF] = own[:, start : start + HALF]
    wo[:, HALF:] = other[:, start : start + HALF]


def head_mask(which):
    lane = lax.broadcasted_iota(jnp.int32, (1, 2 * HD), 1)
    return (lane < HD) if which == 0 else (lane >= HD)


def keep(values, mask):
    return jnp.where(mask, values, jnp.zeros_like(values))


def layer_forward(x, mod, own, other, wqkv, wo, bqkv, bfc1, bproj, bfc2, put):
    normed, inv_a = normalize(x)
    input_a = (normed * (1.0 + mod(1)) + mod(0)).astype(bf16)
    qkv = (dot(input_a, wqkv[...]) + bqkv).astype(bf16)
    query = qkv[:, :D] * jnp.asarray(HD**-0.5, bf16)
    keyed = qkv[:, D : 2 * D]
    valued = qkv[:, 2 * D :]
    put("input_a", input_a)
    put("query", query)
    put("keyed", keyed)
    put("valued", valued)
    pieces = []
    for pair in range(HEADS // 2):
        span = slice(pair * 2 * HD, (pair + 1) * 2 * HD)
        q_pair, k_pair, v_pair = query[:, span], keyed[:, span], valued[:, span]
        total = None
        for which in range(2):
            mask = head_mask(which)
            scores = dot(keep(q_pair, mask), k_pair, NT)
            expo = jnp.exp(scores - jnp.max(scores, -1, keepdims=True))
            probs = expo * (1.0 / jnp.sum(expo, -1, keepdims=True))
            put("probs", probs, 2 * pair + which)
            mixed = dot(probs.astype(bf16), keep(v_pair, mask))
            total = mixed if total is None else total + mixed
        pieces.append(total.astype(bf16))
    mixed = jnp.concatenate(pieces, 1)
    put("mixed", mixed)
    branch_a = dot(mixed, wo[...], NT) + bproj
    put("branch_a", branch_a)
    middle = x + mod(2) * branch_a
    put("middle", middle)
    normed_m, inv_m = normalize(middle)
    input_m = (normed_m * (1.0 + mod(4)) + mod(3)).astype(bf16)
    put("input_m", input_m)
    branch_m = bfc2
    for side, weights in enumerate((own, other)):
        pre = dot(input_m, weights[:, :HMLP]) + bfc1[:, side * HMLP : (side + 1) * HMLP]
        squared = pre * pre
        coef = np.float32(np.sqrt(2.0 / np.pi))
        tanh = jnp.tanh(pre * (coef + np.float32(coef * 0.044715) * squared))
        half = 0.5 * (1.0 + tanh)
        acted = (pre * half).astype(bf16)
        slope = half + (0.5 * pre) * (1.0 - tanh * tanh) * (
            coef + np.float32(3.0 * 0.044715 * coef) * squared
        )
        put("acted", acted, side)
        put("slope", slope, side)
        branch_m = branch_m + dot(acted, weights[:, OFF_W2 : OFF_W2 + HMLP], NT)
    put("branch_m", branch_m)
    return middle + mod(5) * branch_m


def layer_backward(grad, x, mod, own, other, wqkv, wo, take, rows, stash, mods_out, bias):
    branch_m = take("branch_m")
    mods_out(5, token_sum(grad * branch_m))
    grad_branch_m = (grad * mod(5)).astype(bf16)
    bias("fc2", 0, grad_branch_m)
    stash["dym"][rows, :] = grad_branch_m
    middle = take("middle")
    normed_m, inv_m = normalize(middle)
    grad_input = None
    for side, weights in enumerate((own, other)):
        span = slice(side * HMLP, (side + 1) * HMLP)
        grad_acted = dot(grad_branch_m, weights[:, OFF_W2 : OFF_W2 + HMLP])
        grad_pre = (grad_acted * take("slope", side)).astype(bf16)
        stash["dg"][rows, span] = grad_pre
        bias("fc1", side * HMLP, grad_pre)
        part = dot(grad_pre, weights[:, :HMLP], NT)
        grad_input = part if grad_input is None else grad_input + part
    mods_out(3, token_sum(grad_input))
    mods_out(4, token_sum(grad_input * normed_m))
    grad_middle = grad + norm_back(grad_input * (1.0 + mod(4)), normed_m, inv_m)
    branch_a = take("branch_a")
    mods_out(2, token_sum(grad_middle * branch_a))
    grad_branch_a = (grad_middle * mod(2)).astype(bf16)
    bias("proj", 0, grad_branch_a)
    stash["dya"][rows, :] = grad_branch_a
    grad_mixed = dot(grad_branch_a, wo[...]).astype(bf16)
    query, keyed, valued = take("query"), take("keyed"), take("valued")
    grads_q, grads_k, grads_v = [], [], []
    for pair in range(HEADS // 2):
        span = slice(pair * 2 * HD, (pair + 1) * 2 * HD)
        q_pair, k_pair, v_pair = query[:, span], keyed[:, span], valued[:, span]
        g_pair = grad_mixed[:, span]
        grad_q = grad_k = grad_v = None
        for which in range(2):
            mask = head_mask(which)
            probs = take("probs", 2 * pair + which)
            g_head = keep(g_pair, mask)
            grad_probs = dot(g_head, v_pair, NT)
            row_dot = jnp.sum(grad_probs * probs, -1, keepdims=True)
            grad_scores = (probs * (grad_probs - row_dot)).astype(bf16)
            part_q = dot(grad_scores, keep(k_pair, mask))
            part_k = dot(grad_scores, keep(q_pair, mask), TN)
            part_v = dot(probs.astype(bf16), g_head, TN)
            grad_q = part_q if grad_q is None else grad_q + part_q
            grad_k = part_k if grad_k is None else grad_k + part_k
            grad_v = part_v if grad_v is None else grad_v + part_v
        grads_q.append((grad_q * HD**-0.5).astype(bf16))
        grads_k.append(grad_k.astype(bf16))
        grads_v.append(grad_v.astype(bf16))
    grad_qkv = jnp.concatenate(grads_q + grads_k + grads_v, 1)
    stash["dqkv"][rows, :] = grad_qkv
    bias("qkv", 0, grad_qkv)
    grad_input_a = dot(grad_qkv, wqkv[...], NT)
    normed, inv_a = normalize(x)
    mods_out(0, token_sum(grad_input_a))
    mods_out(1, token_sum(grad_input_a * normed))
    return grad_middle + norm_back(grad_input_a * (1.0 + mod(1)), normed, inv_a)


def weight_grads(input_a, input_m, mixed, acted, stash, col_own, col_other, row_own, row_other):
    for part in range(3):
        piece = dot(input_a[...], stash["dqkv"][:, part * D : (part + 1) * D], TN)
        for side, out in enumerate((col_own, col_other)):
            for head in range(HEADS // 2):
                start = side * HALF + head * HD
                place = (3 * head + part) * HD
                out[:, place : place + HD] = piece[:, start : start + HD]
    for side, out in enumerate((col_own, col_other)):
        out[:, QKV_S:] = dot(input_m[...], stash["dg"][:, side * HMLP : (side + 1) * HMLP], TN)
    piece = dot(mixed[...], stash["dya"][...], TN)
    for side, out in enumerate((row_own, row_other)):
        out[:HALF, :] = piece[side * HALF : (side + 1) * HALF, :]
        out[HALF:, :] = dot(acted[:, side * HMLP : (side + 1) * HMLP], stash["dym"][...], TN)


BIAS = {"qkv": 0, "fc1": 3 * D, "proj": 3 * D + MLP, "fc2": 4 * D + MLP}
BIAS_WIDTH = 5 * D + MLP


def forward_kernel(xt, mods, wpatch, posbias, own, other, bqkv, bfc1, bproj, bfc2,
                   x0, query, keyed, valued, probs, branch_a, middle, slope, branch_m, mixed, acted,
                   input_a, input_m, x2, wqkv, wo):
    @pl.when(pl.program_id(0) == 0)
    def _():
        assemble(own, other, wqkv, wo)

    named = dict(query=query, keyed=keyed, valued=valued, mixed=mixed, branch_a=branch_a,
                 middle=middle, branch_m=branch_m, input_a=input_a, input_m=input_m)

    def put(name, value, index=None):
        if name == "probs":
            probs[0, index] = value
        elif name == "acted":
            acted[0, :, index * HMLP : (index + 1) * HMLP] = value
        elif name == "slope":
            slope[0, :, index * HMLP : (index + 1) * HMLP] = value
        else:
            named[name][0] = value

    x = dot(xt[0], wpatch[...], NT) + posbias[...]
    x0[0] = x
    x2[0] = layer_forward(x, lambda j: mods[0, j : j + 1, :], own, other, wqkv, wo, bqkv[...],
                          bfc1[...], bproj[...], bfc2[...], put)


def middle_kernel(x2, mods, own, other, bqkv, bfc1, bproj, bfc2, whead, bhead, targets,
                  dx, dmods, col_own, col_other, row_own, row_other, dbias, dhead, dbhead, loss,
                  wqkv, wo, query, keyed, valued, probs, mixed, branch_a, middle, acted, slope,
                  branch_m, input_a, input_m, s_dqkv, s_dg, s_dya, s_dym):
    step = pl.program_id(0)

    @pl.when(step == 0)
    def _():
        assemble(own, other, wqkv, wo)
        dbias[...] = jnp.zeros_like(dbias)
        dhead[...] = jnp.zeros_like(dhead)
        dbhead[...] = jnp.zeros_like(dbhead)
        loss[...] = jnp.zeros_like(loss)

    rows = pl.ds(pl.multiple_of(step * TOK, TOK), TOK)
    stacked = dict(mixed=mixed, input_a=input_a, input_m=input_m)
    single = dict(query=query, keyed=keyed, valued=valued, branch_a=branch_a, middle=middle,
                  branch_m=branch_m)

    def put(name, value, index=None):
        if name == "probs":
            probs[index] = value
        elif name == "acted":
            acted[rows, index * HMLP : (index + 1) * HMLP] = value
        elif name == "slope":
            slope[:, index * HMLP : (index + 1) * HMLP] = value
        elif name in stacked:
            stacked[name][rows, :] = value
        else:
            single[name][...] = value

    def take(name, index=None):
        if name == "probs":
            return probs[index]
        if name == "slope":
            return slope[:, index * HMLP : (index + 1) * HMLP]
        return single[name][...]

    def mod(j):
        return mods[0, 6 + j : 7 + j, :]

    x = x2[0]
    x = layer_forward(x, mod, own, other, wqkv, wo, bqkv[...], bfc1[...], bproj[...], bfc2[...], put)
    normed, inv_std = normalize(x)
    input_f = (normed * (1.0 + mod(7)) + mod(6)).astype(bf16)
    miss = dot(input_f, whead[...]) + bhead[...] - targets[0]
    loss[...] += jnp.sum(miss * miss).reshape(1, 1)
    grad_pred = (2.0 * miss).astype(bf16)
    dhead[...] += dot(grad_pred, input_f, TN)
    dbhead[...] += token_sum(grad_pred.astype(f32))
    grad_input = dot(grad_pred, whead[...], NT)
    dmods[0, 6:7, :] = token_sum(grad_input)
    dmods[0, 7:8, :] = token_sum(grad_input * normed)
    grad = norm_back(grad_input * (1.0 + mod(7)), normed, inv_std)

    def mods_out(j, value):
        dmods[0, j : j + 1, :] = value

    def bias(name, start, value):
        at = BIAS[name] + start
        dbias[:, at : at + value.shape[1]] += token_sum(value.astype(f32))

    stash = dict(dqkv=s_dqkv, dg=s_dg, dya=s_dya, dym=s_dym)
    dx[0] = layer_backward(grad, x2[0], mod, own, other, wqkv, wo, take, rows, stash, mods_out, bias)

    @pl.when(step == pl.num_programs(0) - 1)
    def _():
        weight_grads(input_a, input_m, mixed, acted, stash, col_own, col_other, row_own, row_other)


def last_kernel(dx, x0, mods, own, other, xt, query, keyed, valued, probs, branch_a, middle,
                slope, branch_m, mixed, acted, input_a, input_m,
                dmods, col_own, col_other, row_own, row_other, dbias, dpatch, dbpatch,
                wqkv, wo, a_input_a, a_input_m, a_mixed, a_acted, s_dqkv, s_dg, s_dya, s_dym, sems):
    step = pl.program_id(0)
    pairs = ((input_a, a_input_a), (input_m, a_input_m), (mixed, a_mixed), (acted, a_acted))
    copies = [pltpu.make_async_copy(src, dst, sems.at[i]) for i, (src, dst) in enumerate(pairs)]

    @pl.when(step == 0)
    def _():
        assemble(own, other, wqkv, wo)
        dbias[...] = jnp.zeros_like(dbias)
        dpatch[...] = jnp.zeros_like(dpatch)
        dbpatch[...] = jnp.zeros_like(dbpatch)
        for copy in copies:
            copy.start()

    rows = pl.ds(pl.multiple_of(step * TOK, TOK), TOK)
    single = dict(query=query, keyed=keyed, valued=valued, branch_a=branch_a, middle=middle,
                  branch_m=branch_m)

    def take(name, index=None):
        if name == "probs":
            return probs[0, index]
        if name == "slope":
            return slope[0, :, index * HMLP : (index + 1) * HMLP]
        return single[name][0]

    def mods_out(j, value):
        dmods[0, j : j + 1, :] = value

    def bias(name, start, value):
        at = BIAS[name] + start
        dbias[:, at : at + value.shape[1]] += token_sum(value.astype(f32))

    stash = dict(dqkv=s_dqkv, dg=s_dg, dya=s_dya, dym=s_dym)
    grad = layer_backward(dx[0], x0[0], lambda j: mods[0, j : j + 1, :], own, other, wqkv, wo,
                          take, rows, stash, mods_out, bias)
    grad = grad.astype(bf16)
    dpatch[...] += dot(xt[0], grad, TN)
    dbpatch[...] += token_sum(grad.astype(f32))

    @pl.when(step == pl.num_programs(0) - 1)
    def _():
        for copy in copies:
            copy.wait()
        weight_grads(a_input_a, a_input_m, a_mixed, a_acted, stash,
                     col_own, col_other, row_own, row_other)


def per_latent(*shape):
    zeros = (0,) * len(shape)
    return pl.BlockSpec((1,) + shape, lambda n: (n,) + zeros)


def fixed(*shape):
    zeros = (0,) * len(shape)
    return pl.BlockSpec(shape, lambda n: zeros, pipeline_mode=pl.Buffered(1))


def params():
    return pltpu.CompilerParams(dimension_semantics=("arbitrary",), vmem_limit_bytes=62 * 2**20)


SAVED = [
    ("query", (TOK, D), bf16), ("keyed", (TOK, D), bf16), ("valued", (TOK, D), bf16),
    ("probs", (HEADS, TOK, TOK), f32), ("branch_a", (TOK, D), f32), ("middle", (TOK, D), f32),
    ("slope", (TOK, MLP), f32), ("branch_m", (TOK, D), f32), ("mixed", (TOK, D), bf16),
    ("acted", (TOK, MLP), bf16), ("input_a", (TOK, D), bf16), ("input_m", (TOK, D), bf16),
]
WEIGHT_SPECS = [fixed(D, GATH), fixed(D, GATH)]
BIAS_SPECS = [fixed(1, 3 * D), fixed(1, MLP), fixed(1, D), fixed(1, D)]
GRAD_SHAPES = [(D, COL_S), (D, COL_S), (ROW_S, D), (ROW_S, D)]
WEIGHT_SCRATCH = [pltpu.VMEM((D, 3 * D), bf16), pltpu.VMEM((D, D), bf16)]


def stash_scratch(count):
    rows = count * TOK
    return [pltpu.VMEM((rows, 3 * D), bf16), pltpu.VMEM((rows, MLP), bf16),
            pltpu.VMEM((rows, D), bf16), pltpu.VMEM((rows, D), bf16)]


def cost(flops, nbytes, count):
    return pl.CostEstimate(flops=int(flops * count), bytes_accessed=int(nbytes * count),
                           transcendentals=int(2e6 * count))


def run_forward(xt, mods, wpatch, posbias, own, other, biases):
    count = xt.shape[0]
    outs = [("x0", (TOK, D), f32)] + SAVED + [("x2", (TOK, D), f32)]
    return pl.pallas_call(
        forward_kernel,
        grid=(count,),
        in_specs=[per_latent(TOK, PV), per_latent(14, D), fixed(D, PV), fixed(TOK, D)]
        + WEIGHT_SPECS + BIAS_SPECS,
        out_specs=[per_latent(*shape) for _, shape, _ in outs],
        out_shape=[jax.ShapeDtypeStruct((count,) + shape, kind) for _, shape, kind in outs],
        scratch_shapes=WEIGHT_SCRATCH,
        compiler_params=params(),
        cost_estimate=cost(1.0e9, 6e6, count),
        name="forward_first",
    )(xt, mods, wpatch, posbias, own, other, *biases)


def run_middle(x2, mods, own, other, biases, whead, bhead, targets):
    count = x2.shape[0]
    rows = count * TOK
    outs = [((count, TOK, D), per_latent(TOK, D)), ((count, 8, D), per_latent(8, D))]
    outs += [(shape, fixed(*shape)) for shape in GRAD_SHAPES]
    outs += [((1, BIAS_WIDTH), fixed(1, BIAS_WIDTH)), ((PV, D), fixed(PV, D)),
             ((1, PV), fixed(1, PV)), ((1, 1), fixed(1, 1))]
    return pl.pallas_call(
        middle_kernel,
        grid=(count,),
        in_specs=[per_latent(TOK, D), per_latent(14, D)] + WEIGHT_SPECS + BIAS_SPECS
        + [fixed(D, PV), fixed(1, PV), per_latent(TOK, PV)],
        out_specs=[spec for _, spec in outs],
        out_shape=[jax.ShapeDtypeStruct(shape, f32) for shape, _ in outs],
        scratch_shapes=WEIGHT_SCRATCH
        + [pltpu.VMEM((TOK, D), bf16)] * 3
        + [pltpu.VMEM((HEADS, TOK, TOK), f32), pltpu.VMEM((rows, D), bf16),
           pltpu.VMEM((TOK, D), f32), pltpu.VMEM((TOK, D), f32), pltpu.VMEM((rows, MLP), bf16),
           pltpu.VMEM((TOK, MLP), f32), pltpu.VMEM((TOK, D), f32),
           pltpu.VMEM((rows, D), bf16), pltpu.VMEM((rows, D), bf16)]
        + stash_scratch(count),
        compiler_params=params(),
        cost_estimate=cost(3.2e9, 3e6, count),
        name="layer_second",
    )(x2, mods, own, other, *biases, whead, bhead, targets)


def run_last(dx, x0, mods, own, other, xt, saved):
    count = dx.shape[0]
    rows = count * TOK
    outs = [((count, 6, D), per_latent(6, D))]
    outs += [(shape, fixed(*shape)) for shape in GRAD_SHAPES]
    outs += [((1, BIAS_WIDTH), fixed(1, BIAS_WIDTH)), ((PV, D), fixed(PV, D)), ((1, D), fixed(1, D))]
    return pl.pallas_call(
        last_kernel,
        grid=(count,),
        in_specs=[per_latent(TOK, D), per_latent(TOK, D), per_latent(14, D)] + WEIGHT_SPECS
        + [per_latent(TOK, PV)] + [per_latent(*shape) for _, shape, _ in SAVED[:-4]]
        + [pl.BlockSpec(memory_space=pl.ANY)] * 4,
        out_specs=[spec for _, spec in outs],
        out_shape=[jax.ShapeDtypeStruct(shape, f32) for shape, _ in outs],
        scratch_shapes=WEIGHT_SCRATCH
        + [pltpu.VMEM((rows, D), bf16)] * 3 + [pltpu.VMEM((rows, MLP), bf16)]
        + stash_scratch(count) + [pltpu.SemaphoreType.DMA((4,))],
        compiler_params=params(),
        cost_estimate=cost(2.2e9, 8e6, count),
        name="backward_first",
    )(dx, x0, mods, own, other, xt, *saved[:-4], *[v.reshape(rows, -1) for v in saved[-4:]])


def project_kernel(err_col, own_col, got_col, err_row, own_row, got_row, fac_col, fac_row,
                   mat_col, mat_row, left_col, left_row):
    matrix = err_col[0] + (own_col[...] + got_col[...])
    mat_col[...] = matrix
    left_col[...] = dot_full(fac_col[...], matrix, NT)
    matrix = err_row[0] + (own_row[...] + got_row[...])
    mat_row[...] = matrix
    left_row[...] = dot_full(fac_row[...], matrix, NT)


def run_project(layer, err_col, own_col, got_col, err_row, own_row, got_row, fac_col, fac_row):
    whole = [fixed(D, COL_S), fixed(D, COL_S)]
    tall = [fixed(ROW_S, D), fixed(ROW_S, D)]
    shapes = [(D, COL_S), (ROW_S, D), (RANK, D), (RANK, ROW_S)]
    return pl.pallas_call(
        project_kernel,
        grid=(1,),
        in_specs=[pl.BlockSpec((1, D, COL_S), lambda n: (layer, 0, 0))] + whole
        + [pl.BlockSpec((1, ROW_S, D), lambda n: (layer, 0, 0))] + tall
        + [fixed(RANK, COL_S), fixed(RANK, D)],
        out_specs=[fixed(*shape) for shape in shapes],
        out_shape=[jax.ShapeDtypeStruct(shape, f32) for shape in shapes],
        compiler_params=params(),
        name="left_factors",
    )(err_col, own_col, got_col, err_row, own_row, got_row, fac_col, fac_row)


def ortho_kernel(basis, out):
    columns = []
    for index in range(RANK):
        column = basis[index]
        for earlier in columns:
            column = column - jnp.sum(earlier * column, -1, keepdims=True) * earlier
        column = column * lax.rsqrt(jnp.sum(column * column, -1, keepdims=True) + ortho_eps)
        out[index] = column
        columns.append(column)


def run_ortho(basis):
    return pl.pallas_call(
        ortho_kernel,
        out_shape=jax.ShapeDtypeStruct(basis.shape, f32),
        name="orthonormal",
    )(basis)


def right_kernel(mat_col0, mat_row0, mat_col1, mat_row1, left_col, left_row, right_col, right_row):
    for layer, (col, row) in enumerate(((mat_col0, mat_row0), (mat_col1, mat_row1))):
        right_col[layer] = dot_full(left_col[layer], col[...])
        right_row[layer] = dot_full(left_row[layer], row[...])


def run_right(mats, left_col, left_row):
    return pl.pallas_call(
        right_kernel,
        out_shape=[jax.ShapeDtypeStruct((L, RANK, COL_S), f32),
                   jax.ShapeDtypeStruct((L, RANK, D), f32)],
        compiler_params=pltpu.CompilerParams(vmem_limit_bytes=62 * 2**20),
        name="right_factors",
    )(*mats, left_col, left_row)


def error_kernel(mat_col0, mat_row0, mat_col1, mat_row1, left_col, left_row, right_col, right_row,
                 err_col, err_row):
    for layer, (col, row) in enumerate(((mat_col0, mat_row0), (mat_col1, mat_row1))):
        err_col[layer] = col[...] - dot_full(left_col[layer], right_col[layer], TN)
        err_row[layer] = row[...] - dot_full(left_row[layer], right_row[layer], TN)


def run_error(mats, left_col, left_row, right_col, right_row):
    return pl.pallas_call(
        error_kernel,
        out_shape=[jax.ShapeDtypeStruct((L, D, COL_S), f32),
                   jax.ShapeDtypeStruct((L, ROW_S, D), f32)],
        compiler_params=pltpu.CompilerParams(vmem_limit_bytes=62 * 2**20),
        name="next_errors",
    )(*mats, left_col, left_row, right_col, right_row)


def swap(values):
    return lax.ppermute(values, "tensor", [(0, 1), (1, 0)])


def spread(values, axes):
    count = lax.axis_size(axes)
    sent = jnp.broadcast_to(values[None], (count,) + values.shape)
    return lax.all_to_all(sent, axes, 0, 0, tiled=True)


def flat_sum(parts):
    count = lax.axis_size("dp")
    sizes = [int(np.prod(part.shape)) for part in parts]
    total = sum(sizes)
    unit = count * 128
    padded = -(-total // unit) * unit
    flat = jnp.concatenate([part.reshape(-1) for part in parts] + [jnp.zeros((padded - total,), f32)])
    got = lax.all_to_all(flat.reshape(count, padded // unit, 128), "dp", 0, 0, tiled=True)
    share = jnp.sum(got, 0)
    flat = spread(share, "dp").reshape(-1)
    outs, at = [], 0
    for part, size in zip(parts, sizes):
        outs.append(flat[at : at + size].reshape(part.shape))
        at += size
    return outs


def squares(values):
    return jnp.sum(values * values)


def on_device(
    latents, gauss_noise, time_steps, labels, targets,
    w_col, w_row, w_cond, w_time, w_io, class_table, b_col, b_rep,
    mom_col, mom_row, mom_cond, mom_time, mom_io, mom_table, mom_bcol, mom_brep,
    err_col, err_row, err_io, fac_col, fac_row, fac_io,
):
    both = ("dp", "tensor")
    n_dp = lax.axis_size("dp")
    index_dp = lax.axis_index("dp")
    index_t = lax.axis_index("tensor")
    n_all = labels.shape[0]
    count = latents.shape[0] // 2
    rows = w_col.shape[1]
    start_fc2 = L * D
    start_cond = 2 * L * D
    n_mods = (6 * L + 2) * D
    start_first = start_cond + n_mods
    start_second = start_first + D
    start_patch = start_first + 2 * D
    start_head = start_first + 3 * D

    heads = HEADS // 2
    qkv_sh = w_col[:, :, :QKV_S].reshape(L, rows, heads, 3, HD).transpose(0, 1, 3, 2, 4)
    row_sh = w_row.transpose(0, 2, 1)
    shard = jnp.concatenate(
        [w_col[:, :, QKV_S:], row_sh[:, :, HALF:], qkv_sh.reshape(L, rows, QKV_S), row_sh[:, :, :HALF]],
        2,
    ).astype(bf16)
    own = [lax.all_gather(shard[layer], "dp", axis=0, tiled=True) for layer in range(L)]
    other = [swap(own[layer]) for layer in range(L)]
    bcol_other = swap(b_col)

    steps_all = spread(time_steps, "dp").reshape(n_all)
    classes = jnp.arange(CLASSES, dtype=jnp.int32)
    onehot = labels[:, None] == classes[None, :]
    looked = dot(onehot.astype(bf16), class_table.astype(bf16)).astype(bf16)
    looked = spread(looked, "dp").transpose(1, 0, 2).reshape(n_all, D)
    full_time = spread(w_time.astype(bf16), "dp").reshape(FREQ + D, D)
    full_io = spread(w_io.astype(bf16), "dp").transpose(1, 0, 2, 3).reshape(2, D, PV)
    half_cols = n_mods // 2
    block = half_cols // n_dp
    cond_half = lax.dynamic_slice_in_dim(w_cond, index_t * half_cols, half_cols, 1).astype(bf16)
    cond_cols = lax.all_to_all(
        cond_half.reshape(rows, n_dp, block).transpose(1, 0, 2), "dp", 0, 0, tiled=True
    ).reshape(D, block)
    features = frequency_features(steps_all).astype(bf16)
    first = dot(features, full_time[:FREQ]) + b_rep[start_first:start_second]
    first_act, first_pull = jax.vjp(jax.nn.silu, first)
    first_act = first_act.astype(bf16)
    second = dot(first_act, full_time[FREQ:]) + b_rep[start_second:start_patch]
    cond = second + looked.astype(f32)
    cond_act, cond_pull = jax.vjp(jax.nn.silu, cond)
    cond_act = cond_act.astype(bf16)
    mods_cols = dot(cond_act, cond_cols)
    mods = lax.all_to_all(mods_cols.reshape(2 * n_dp, count, block), both, 0, 0, tiled=True)
    mods = mods.reshape(n_dp, 2, count, block).transpose(2, 1, 0, 3).reshape(count, n_mods)
    mods = (mods + b_rep[start_cond:start_first]).reshape(count, 6 * L + 2, D)
    full_cond = lax.all_gather(w_cond.astype(bf16), "dp", axis=0, tiled=True)

    begin = index_t * count
    steps_own = lax.dynamic_slice_in_dim(time_steps, begin, count, 0)[:, None, None]
    xt = (
        (1.0 - steps_own) * lax.dynamic_slice_in_dim(latents, begin, count, 0)
        + steps_own * lax.dynamic_slice_in_dim(gauss_noise, begin, count, 0)
    ).astype(bf16)
    targets_own = lax.dynamic_slice_in_dim(targets, begin, count, 0)
    posbias = jnp.asarray(position_table()) + b_rep[start_patch:start_head]

    def layer_biases(layer):
        pair = []
        for values in (b_col[layer], bcol_other[layer]):
            pair.append(values[:QKV_S].reshape(heads, 3, HD).transpose(1, 0, 2).reshape(3, HALF))
        bqkv = jnp.concatenate(pair, 1).reshape(1, 3 * D)
        bfc1 = jnp.concatenate([b_col[layer, QKV_S:], bcol_other[layer, QKV_S:]])[None]
        bproj = b_rep[layer * D : (layer + 1) * D][None]
        bfc2 = b_rep[start_fc2 + layer * D : start_fc2 + (layer + 1) * D][None]
        return [bqkv, bfc1, bproj, bfc2]

    x0, *saved, x2 = run_forward(xt, mods, full_io[0], posbias, own[0], other[0], layer_biases(0))
    dx, dmods1, col_own1, col_oth1, row_own1, row_oth1, dbias1, dhead, dbhead, loss = run_middle(
        x2, mods, own[1], other[1], layer_biases(1), full_io[1],
        b_rep[start_head : start_head + PV][None], targets_own,
    )
    dmods0, col_own0, col_oth0, row_own0, row_oth0, dbias0, dpatch, dbpatch = run_last(
        dx, x0, mods, own[0], other[0], xt, saved
    )

    dmods = jnp.concatenate([dmods0, dmods1], 1).reshape(count, n_mods).astype(bf16)
    grad_cond_act = dot(dmods, full_cond, NT)
    mine = (index_dp * 2 + index_t) * count
    cond_own = lax.dynamic_slice_in_dim(cond, mine, count, 0)
    grad_cond = jax.vjp(jax.nn.silu, cond_own)[1](grad_cond_act)[0]
    grad_cond = spread(grad_cond, both).reshape(n_all, D)
    dmods_cols = lax.all_to_all(
        dmods.reshape(count, 2, n_dp, block).transpose(2, 1, 0, 3).reshape(2 * n_dp, count, block),
        both, 0, 0, tiled=True,
    ).reshape(n_all, block)
    cond_grad = dot(cond_act, dmods_cols, TN)
    cond_bias = jnp.sum(dmods_cols.astype(f32), 0)
    cond_part = lax.all_to_all(cond_grad.reshape(n_dp, rows, block), "dp", 0, 0, tiled=True)
    cond_part = cond_part.transpose(1, 0, 2).reshape(rows, half_cols)

    def both_halves(mine_half, axis):
        theirs = swap(mine_half)
        return jnp.where(
            index_t == 0,
            jnp.concatenate([mine_half, theirs], axis),
            jnp.concatenate([theirs, mine_half], axis),
        )

    cond_share = both_halves(cond_part, 1)
    table_share = dot_full(
        onehot.astype(f32), lax.dynamic_slice_in_dim(grad_cond, index_dp * rows, rows, 1), TN
    )
    grad_second = grad_cond.astype(bf16)
    grad_first = first_pull(dot(grad_second, full_time[FREQ:], NT))[0].astype(bf16)
    time_grad = jnp.concatenate([dot(features, grad_first, TN), dot(first_act, grad_second, TN)], 0)
    first_bias = jnp.sum(grad_first.astype(f32), 0)
    second_bias = jnp.sum(grad_second.astype(f32), 0)

    def side_bias(dbias, side):
        qkv = dbias[0, : 3 * D].reshape(3, 2, heads, HD)[:, side].transpose(1, 0, 2).reshape(QKV_S)
        return jnp.concatenate([qkv, dbias[0, 3 * D + side * HMLP : 3 * D + (side + 1) * HMLP]])

    small = jnp.concatenate(
        [dbias0[0, BIAS["proj"] :][:D], dbias1[0, BIAS["proj"] :][:D],
         dbias0[0, BIAS["fc2"] :], dbias1[0, BIAS["fc2"] :], dbpatch[0], dbhead[0], loss[0]]
    )
    io_t = jnp.stack([dpatch, dhead], 0)
    small_got, io_got, bias_got, col_got1, row_got1, col_got0, row_got0 = (
        swap(small), swap(io_t), swap(jnp.stack([side_bias(dbias0, 1), side_bias(dbias1, 1)])),
        swap(col_oth1), swap(row_oth1), swap(col_oth0), swap(row_oth0),
    )
    small = small + small_got
    bcol_part = jnp.stack([side_bias(dbias0, 0), side_bias(dbias1, 0)]) + bias_got
    fac_col_t = fac_col.transpose(0, 2, 1)
    fac_row_t = fac_row.transpose(0, 2, 1)
    fac_io_t = fac_io.transpose(0, 2, 1)
    mat_col1, mat_row1, left_col1, left_row1 = run_project(
        1, err_col, col_own1, col_got1, err_row, row_own1, row_got1, fac_col_t[1], fac_row_t[1]
    )
    mat_col0, mat_row0, left_col0, left_row0 = run_project(
        0, err_col, col_own0, col_got0, err_row, row_own0, row_got0, fac_col_t[0], fac_row_t[0]
    )
    mats = (mat_col0, mat_row0, mat_col1, mat_row1)
    mat_io = (io_t + io_got) + err_io.transpose(0, 2, 1)
    left_io = jnp.einsum("lrp,lpd->lrd", fac_io_t, mat_io, precision=highest)
    left_col, left_row, left_io, bcol_grad, small = flat_sum(
        [jnp.stack([left_col0, left_col1]), jnp.stack([left_row0, left_row1]), left_io, bcol_part, small]
    )
    pad = ((0, 0), (0, 0), (0, ROW_S - D))
    basis = jnp.concatenate([jnp.pad(left_col, pad), left_row, jnp.pad(left_io, pad)], 0)
    basis = run_ortho(basis.transpose(1, 0, 2)).transpose(1, 0, 2)
    left_col, left_row, left_io = basis[:2, :, :D], basis[2:4], basis[4:, :, :D]
    right_col, right_row = run_right(mats, left_col, left_row)
    right_io = jnp.einsum("lrd,lpd->lrp", left_io, mat_io, precision=highest)
    part_squares = jnp.stack([squares(cond_grad), squares(table_share)])
    right_col, right_row, right_io, part_squares = flat_sum(
        [right_col, right_row, right_io, part_squares]
    )
    next_err_col, next_err_row = run_error(mats, left_col, left_row, right_col, right_row)
    approx_io = jnp.einsum("lrd,lrp->ldp", left_io, right_io, precision=highest)
    next_err_io = mat_io.transpose(0, 2, 1) - approx_io

    def gram_squares(left, right):
        gram_left = jnp.einsum("lrn,lsn->lrs", left, left, precision=highest)
        gram_right = jnp.einsum("lrn,lsn->lrs", right, right, precision=highest)
        return jnp.sum(gram_left * gram_right)

    cond_bias = spread(cond_bias, both).reshape(n_dp, 2, block).transpose(1, 0, 2).reshape(n_mods)
    loss_total = small[5 * D + PV]
    brep_grad = jnp.concatenate(
        [small[: 4 * D], cond_bias, first_bias, second_bias, small[4 * D : 5 * D + PV]]
    )
    split_part = (
        gram_squares(left_col, right_col) + gram_squares(left_row, right_row)
        + squares(bcol_grad) + part_squares[0]
    )
    whole_part = squares(approx_io) + squares(brep_grad) + squares(time_grad) + part_squares[1]
    clip_norm = jnp.sqrt(split_part + swap(split_part) + whole_part)
    scaling = jnp.minimum(1.0, clip_limit / clip_norm)

    def advance(weight, momentum, gradient):
        moved = momentum_decay * momentum + scaling * gradient
        return (weight - learn_rate * moved, moved)

    at = index_dp * rows
    grad_col = jnp.einsum(
        "lrn,lrm->lnm", lax.dynamic_slice_in_dim(left_col, at, rows, 2), right_col, precision=highest
    )
    grad_row = jnp.einsum(
        "lrn,lrm->lnm", left_row, lax.dynamic_slice_in_dim(right_row, at, rows, 2), precision=highest
    )
    next_w_col, next_mom_col = advance(w_col, mom_col, grad_col)
    next_w_row, next_mom_row = advance(w_row, mom_row, grad_row)
    next_w_cond, next_mom_cond = advance(w_cond, mom_cond, cond_share)
    time_rows = w_time.shape[0]
    next_w_time, next_mom_time = advance(
        w_time, mom_time, lax.dynamic_slice_in_dim(time_grad, index_dp * time_rows, time_rows, 0)
    )
    next_w_io, next_mom_io = advance(
        w_io, mom_io, lax.dynamic_slice_in_dim(approx_io, at, rows, 1)
    )
    next_table, next_mom_table = advance(class_table, mom_table, table_share)
    next_b_col, next_mom_bcol = advance(b_col, mom_bcol, bcol_grad)
    next_b_rep, next_mom_brep = advance(b_rep, mom_brep, brep_grad)
    return (
        loss_total, clip_norm,
        next_w_col, next_w_row, next_w_cond, next_w_time, next_w_io, next_table, next_b_col, next_b_rep,
        next_mom_col, next_mom_row, next_mom_cond, next_mom_time, next_mom_io, next_mom_table,
        next_mom_bcol, next_mom_brep,
        next_err_col, next_err_row, next_err_io,
        right_col.transpose(0, 2, 1), right_row.transpose(0, 2, 1), right_io.transpose(0, 2, 1),
    )


def solution(mesh):
    weights = (
        P(None, "dp", "tensor"), P(None, "tensor", "dp"), P("dp", None), P("dp", None),
        P(None, "dp", None), P(None, "dp"), P(None, "tensor"), P(),
    )
    errors = (P("dp", None, "tensor"), P("dp", "tensor", None), P("dp", None, None))
    factors = (P(None, "tensor", None), P(None, "tensor", None), P())
    rows = P("dp", None, None)
    return jax.shard_map(
        on_device,
        mesh=mesh,
        in_specs=(rows, rows, P("dp"), P(), rows) + weights + weights + errors + factors,
        out_specs=(P(), P()) + weights + weights + errors + factors,
        check_vma=False,
    )
```

```python
import jax
import jax.numpy as jnp
import numpy as np
from jax import lax
from jax.experimental import pallas as pl
from jax.experimental.pallas import tpu as pltpu
from jax.sharding import PartitionSpec as P

D = 384
HEADS = 6
HD = 64
MLP = 1536
NBR = 8080
CLASSES = 1000
FREQ = 256
PV = 16
GRID = 16
L = 2
TOK = 256
RANK = 8

norm_eps = 1e-06
ortho_eps = 1e-06
clip_limit = 1.0
momentum_decay = 0.9
learn_rate = 4.0

HALF = D // 2
HMLP = MLP // 2
QKV_S = 3 * HALF
COL_S = QKV_S + HMLP
ROW_S = HALF + HMLP
OFF_W2 = HMLP
OFF_Q = 2 * HMLP
GATH = 2 * HMLP + 4 * HALF

f32 = jnp.float32
bf16 = jnp.bfloat16
highest = lax.Precision.HIGHEST
NN = (((1,), (0,)), ((), ()))
NT = (((1,), (1,)), ((), ()))
TN = (((0,), (0,)), ((), ()))


def dot(left, right, dims=NN):
    return lax.dot_general(left, right, dims, preferred_element_type=f32)


def dot_full(left, right, dims=NN):
    return lax.dot_general(left, right, dims, precision=highest, preferred_element_type=f32)


def position_table():
    quarter = D // 4
    omega = 1.0 / 10000.0 ** (np.arange(quarter, dtype=np.float32) / quarter)
    index = np.arange(TOK)
    across = (index % GRID).astype(np.float32)[:, None] * omega[None, :].astype(np.float32)
    down = (index // GRID).astype(np.float32)[:, None] * omega[None, :].astype(np.float32)
    table = np.concatenate([np.sin(across), np.cos(across), np.sin(down), np.cos(down)], 1)
    return table.astype(np.float32)


def frequency_features(steps):
    half = FREQ // 2
    rates = jnp.exp(-jnp.log(10000.0) * jnp.arange(half, dtype=f32) / half)
    angles = steps[:, None] * rates[None, :]
    return jnp.concatenate([jnp.cos(angles), jnp.sin(angles)], 1)


def normalize(values):
    centered = values - jnp.mean(values, -1, keepdims=True)
    inv_std = lax.rsqrt(jnp.mean(centered * centered, -1, keepdims=True) + norm_eps)
    return centered * inv_std, inv_std


def norm_back(grad, normed, inv_std):
    mean_grad = jnp.mean(grad, -1, keepdims=True)
    mean_mixed = jnp.mean(grad * normed, -1, keepdims=True)
    return inv_std * (grad - mean_grad - normed * mean_mixed)


def token_sum(values):
    return jnp.sum(values, 0, keepdims=True)


START_FC2 = L * D
START_COND = 2 * L * D
N_MODS = (6 * L + 2) * D
START_FIRST = START_COND + N_MODS
START_SECOND = START_FIRST + D
START_PATCH = START_FIRST + 2 * D
START_HEAD = START_FIRST + 3 * D


def assemble(layer, own, other, bcol_own, bcol_other, wqkv, wo, bqkv, bfc1):
    for side, (weights, bias) in enumerate(((own, bcol_own), (other, bcol_other))):
        for head in range(HEADS // 2):
            for part in range(3):
                at = (3 * head + part) * HD
                to = part * D + side * HALF + head * HD
                wqkv[:, to : to + HD] = weights[:, OFF_Q + at : OFF_Q + at + HD]
                bqkv[:, to : to + HD] = bias[layer : layer + 1, at : at + HD]
        wo[:, side * HALF : (side + 1) * HALF] = weights[:, OFF_Q + QKV_S :]
        bfc1[:, side * HMLP : (side + 1) * HMLP] = bias[layer : layer + 1, QKV_S:]


def vector(b_rep, at):
    return b_rep[:, at : at + D]


def head_mask(which):
    lane = lax.broadcasted_iota(jnp.int32, (1, 2 * HD), 1)
    return (lane < HD) if which == 0 else (lane >= HD)


def keep(values, mask):
    return jnp.where(mask, values, jnp.zeros_like(values))


def layer_forward(x, mod, own, other, wqkv, wo, bqkv, bfc1, bproj, bfc2, put):
    normed, inv_a = normalize(x)
    input_a = (normed * (1.0 + mod(1)) + mod(0)).astype(bf16)
    qkv = (dot(input_a, wqkv[...]) + bqkv).astype(bf16)
    query = qkv[:, :D] * jnp.asarray(HD**-0.5, bf16)
    keyed = qkv[:, D : 2 * D]
    valued = qkv[:, 2 * D :]
    put("input_a", input_a)
    put("query", query)
    put("keyed", keyed)
    put("valued", valued)
    pieces = []
    for pair in range(HEADS // 2):
        span = slice(pair * 2 * HD, (pair + 1) * 2 * HD)
        q_pair, k_pair, v_pair = query[:, span], keyed[:, span], valued[:, span]
        total = None
        for which in range(2):
            mask = head_mask(which)
            scores = dot(keep(q_pair, mask), k_pair, NT)
            expo = jnp.exp(scores - jnp.max(scores, -1, keepdims=True))
            probs = expo * (1.0 / jnp.sum(expo, -1, keepdims=True))
            put("probs", probs, 2 * pair + which)
            mixed = dot(probs.astype(bf16), keep(v_pair, mask))
            total = mixed if total is None else total + mixed
        pieces.append(total.astype(bf16))
    mixed = jnp.concatenate(pieces, 1)
    put("mixed", mixed)
    branch_a = dot(mixed, wo[...], NT) + bproj
    put("branch_a", branch_a)
    middle = x + mod(2) * branch_a
    put("middle", middle)
    normed_m, inv_m = normalize(middle)
    input_m = (normed_m * (1.0 + mod(4)) + mod(3)).astype(bf16)
    put("input_m", input_m)
    branch_m = bfc2
    for side, weights in enumerate((own, other)):
        pre = dot(input_m, weights[:, :HMLP]) + bfc1[:, side * HMLP : (side + 1) * HMLP]
        squared = pre * pre
        coef = np.float32(np.sqrt(2.0 / np.pi))
        tanh = jnp.tanh(pre * (coef + np.float32(coef * 0.044715) * squared))
        half = 0.5 * (1.0 + tanh)
        acted = (pre * half).astype(bf16)
        slope = half + (0.5 * pre) * (1.0 - tanh * tanh) * (
            coef + np.float32(3.0 * 0.044715 * coef) * squared
        )
        put("acted", acted, side)
        put("slope", slope, side)
        branch_m = branch_m + dot(acted, weights[:, OFF_W2 : OFF_W2 + HMLP], NT)
    put("branch_m", branch_m)
    return middle + mod(5) * branch_m


def layer_backward(grad, x, mod, own, other, wqkv, wo, take, rows, stash, mods_out, bias):
    branch_m = take("branch_m")
    mods_out(5, token_sum(grad * branch_m))
    grad_branch_m = (grad * mod(5)).astype(bf16)
    bias("fc2", 0, grad_branch_m)
    stash["dym"][rows, :] = grad_branch_m
    middle = take("middle")
    normed_m, inv_m = normalize(middle)
    grad_input = None
    for side, weights in enumerate((own, other)):
        span = slice(side * HMLP, (side + 1) * HMLP)
        grad_acted = dot(grad_branch_m, weights[:, OFF_W2 : OFF_W2 + HMLP])
        grad_pre = (grad_acted * take("slope", side)).astype(bf16)
        stash["dg"][rows, span] = grad_pre
        bias("fc1", side * HMLP, grad_pre)
        part = dot(grad_pre, weights[:, :HMLP], NT)
        grad_input = part if grad_input is None else grad_input + part
    mods_out(3, token_sum(grad_input))
    mods_out(4, token_sum(grad_input * normed_m))
    grad_middle = grad + norm_back(grad_input * (1.0 + mod(4)), normed_m, inv_m)
    branch_a = take("branch_a")
    mods_out(2, token_sum(grad_middle * branch_a))
    grad_branch_a = (grad_middle * mod(2)).astype(bf16)
    bias("proj", 0, grad_branch_a)
    stash["dya"][rows, :] = grad_branch_a
    grad_mixed = dot(grad_branch_a, wo[...]).astype(bf16)
    query, keyed, valued = take("query"), take("keyed"), take("valued")
    grads_q, grads_k, grads_v = [], [], []
    for pair in range(HEADS // 2):
        span = slice(pair * 2 * HD, (pair + 1) * 2 * HD)
        q_pair, k_pair, v_pair = query[:, span], keyed[:, span], valued[:, span]
        g_pair = grad_mixed[:, span]
        grad_q = grad_k = grad_v = None
        for which in range(2):
            mask = head_mask(which)
            probs = take("probs", 2 * pair + which)
            g_head = keep(g_pair, mask)
            grad_probs = dot(g_head, v_pair, NT)
            row_dot = jnp.sum(grad_probs * probs, -1, keepdims=True)
            grad_scores = (probs * (grad_probs - row_dot)).astype(bf16)
            part_q = dot(grad_scores, keep(k_pair, mask))
            part_k = dot(grad_scores, keep(q_pair, mask), TN)
            part_v = dot(probs.astype(bf16), g_head, TN)
            grad_q = part_q if grad_q is None else grad_q + part_q
            grad_k = part_k if grad_k is None else grad_k + part_k
            grad_v = part_v if grad_v is None else grad_v + part_v
        grads_q.append((grad_q * HD**-0.5).astype(bf16))
        grads_k.append(grad_k.astype(bf16))
        grads_v.append(grad_v.astype(bf16))
    grad_qkv = jnp.concatenate(grads_q + grads_k + grads_v, 1)
    stash["dqkv"][rows, :] = grad_qkv
    bias("qkv", 0, grad_qkv)
    grad_input_a = dot(grad_qkv, wqkv[...], NT)
    normed, inv_a = normalize(x)
    mods_out(0, token_sum(grad_input_a))
    mods_out(1, token_sum(grad_input_a * normed))
    return grad_middle + norm_back(grad_input_a * (1.0 + mod(1)), normed, inv_a)


def weight_grads(input_a, input_m, mixed, acted, stash, cols, rows_out):
    for part in range(3):
        piece = dot(stash["dqkv"][:, part * D : (part + 1) * D], input_a[...], TN)
        for side, out in enumerate(cols):
            for head in range(HEADS // 2):
                start = side * HALF + head * HD
                place = (3 * head + part) * HD
                out[place : place + HD, :] = piece[start : start + HD, :]
    for side, out in enumerate(cols):
        out[QKV_S:, :] = dot(stash["dg"][:, side * HMLP : (side + 1) * HMLP], input_m[...], TN)
    piece = dot(mixed[...], stash["dya"][...], TN)
    for side, out in enumerate(rows_out):
        out[:HALF, :] = piece[side * HALF : (side + 1) * HALF, :]
        out[HALF:, :] = dot(acted[:, side * HMLP : (side + 1) * HMLP], stash["dym"][...], TN)


BIAS = {"qkv": 0, "fc1": 3 * D, "proj": 3 * D + MLP, "fc2": 4 * D + MLP}
BIAS_WIDTH = 5 * D + MLP

PAY_PATCH, PAY_HEAD, PAY_PROJ, PAY_FC2, PAY_BPATCH, PAY_BHEAD, PAY_COND, PAY_BCOL = 0, 16, 32, 34, 36, 37, 38, 52
PAY_ROWS = 64
SMALL_ROWS = PAY_BCOL + 8 - PAY_PROJ


def forward_kernel(xt, mods, wpatch, pos, own, other, bcol_own, bcol_other, b_rep,
                   x0, query, keyed, valued, probs, branch_a, middle, slope, branch_m, mixed, acted,
                   input_a, input_m, x2, wqkv, wo, bqkv, bfc1):
    @pl.when(pl.program_id(0) == 0)
    def _():
        assemble(0, own, other, bcol_own, bcol_other, wqkv, wo, bqkv, bfc1)

    named = dict(query=query, keyed=keyed, valued=valued, mixed=mixed, branch_a=branch_a,
                 middle=middle, branch_m=branch_m, input_a=input_a, input_m=input_m)

    def put(name, value, index=None):
        if name == "probs":
            probs[0, index] = value
        elif name == "acted":
            acted[0, :, index * HMLP : (index + 1) * HMLP] = value
        elif name == "slope":
            slope[0, :, index * HMLP : (index + 1) * HMLP] = value
        else:
            named[name][0] = value

    x = dot(xt[0], wpatch[0], TN) + vector(b_rep, START_PATCH) + pos[...]
    x0[0] = x
    x2[0] = layer_forward(x, lambda j: mods[0, j : j + 1, :], own, other, wqkv, wo, bqkv[...],
                          bfc1[...], vector(b_rep, 0), vector(b_rep, START_FC2), put)


def diagonal(count):
    down = lax.broadcasted_iota(jnp.int32, (count, count), 0)
    across = lax.broadcasted_iota(jnp.int32, (count, count), 1)
    return down == across


def write_bcol(dbias, side, out, layer):
    pieces = []
    for head in range(HEADS // 2):
        for part in range(3):
            start = part * D + side * HALF + head * HD
            pieces.append(dbias[:, start : start + HD])
    start = 3 * D + side * HMLP
    pieces.append(dbias[:, start : start + HMLP])
    pieces.append(jnp.zeros((1, 4 * D - COL_S), f32))
    line = jnp.concatenate(pieces, 1)
    for row in range(4):
        at = PAY_BCOL + 4 * layer + row
        out[at : at + 1, :] = line[:, row * D : (row + 1) * D]


def middle_kernel(x2, mods, own, other, bcol_own, bcol_other, b_rep, whead, targets,
                  dx, dmods, col_own, col_other, row_own, row_other, dbias, dhead, dbhead, loss,
                  wqkv, wo, bqkv, bfc1, query, keyed, valued, probs, mixed, branch_a, middle, acted,
                  slope, branch_m, input_a, input_m, s_dqkv, s_dg, s_dya, s_dym):
    step = pl.program_id(0)

    @pl.when(step == 0)
    def _():
        assemble(1, own, other, bcol_own, bcol_other, wqkv, wo, bqkv, bfc1)
        dbias[...] = jnp.zeros_like(dbias)
        dhead[...] = jnp.zeros_like(dhead)
        dbhead[...] = jnp.zeros_like(dbhead)
        loss[...] = jnp.zeros_like(loss)

    rows = pl.ds(pl.multiple_of(step * TOK, TOK), TOK)
    stacked = dict(mixed=mixed, input_a=input_a, input_m=input_m)
    single = dict(query=query, keyed=keyed, valued=valued, branch_a=branch_a, middle=middle,
                  branch_m=branch_m)

    def put(name, value, index=None):
        if name == "probs":
            probs[index] = value
        elif name == "acted":
            acted[rows, index * HMLP : (index + 1) * HMLP] = value
        elif name == "slope":
            slope[:, index * HMLP : (index + 1) * HMLP] = value
        elif name in stacked:
            stacked[name][rows, :] = value
        else:
            single[name][...] = value

    def take(name, index=None):
        if name == "probs":
            return probs[index]
        if name == "slope":
            return slope[:, index * HMLP : (index + 1) * HMLP]
        return single[name][...]

    def mod(j):
        return mods[0, 6 + j : 7 + j, :]

    x = layer_forward(x2[0], mod, own, other, wqkv, wo, bqkv[...], bfc1[...], vector(b_rep, D),
                      vector(b_rep, START_FC2 + D), put)
    normed, inv_std = normalize(x)
    input_f = (normed * (1.0 + mod(7)) + mod(6)).astype(bf16)
    bhead = jnp.sum(
        jnp.where(diagonal(PV), b_rep[:, START_HEAD : START_HEAD + PV], 0.0), 1, keepdims=True
    )
    miss = dot(whead[0], input_f, NT) + bhead - targets[0]
    loss[...] += jnp.sum(miss * miss, 0, keepdims=True)
    grad_pred = (2.0 * miss).astype(bf16)
    dhead[...] += dot(grad_pred, input_f)
    dbhead[...] += jnp.sum(grad_pred.astype(f32), 1, keepdims=True)
    grad_input = dot(grad_pred, whead[0], TN)
    dmods[0, 6:7, :] = token_sum(grad_input)
    dmods[0, 7:8, :] = token_sum(grad_input * normed)
    grad = norm_back(grad_input * (1.0 + mod(7)), normed, inv_std)

    def mods_out(j, value):
        dmods[0, j : j + 1, :] = value

    def bias(name, start, value):
        at = BIAS[name] + start
        dbias[:, at : at + value.shape[1]] += token_sum(value.astype(f32))

    stash = dict(dqkv=s_dqkv, dg=s_dg, dya=s_dya, dym=s_dym)
    dx[0] = layer_backward(grad, x2[0], mod, own, other, wqkv, wo, take, rows, stash, mods_out, bias)

    @pl.when(step == pl.num_programs(0) - 1)
    def _():
        weight_grads(input_a, input_m, mixed, acted, stash, (col_own, col_other), (row_own, row_other))


def last_kernel(dx, x0, mods, own, other, bcol_own, bcol_other, b_rep, xt,
                dbias1, dhead, dbhead, loss, dmods1,
                query, keyed, valued, probs, branch_a, middle, slope, branch_m, mixed, acted, input_a, input_m,
                dmods, col_own, col_other, row_own, row_other, pay_own, pay_other,
                wqkv, wo, bqkv, bfc1, a_input_a, a_input_m, a_mixed, a_acted, s_dqkv, s_dg, s_dya, s_dym,
                dbias, sems):
    step = pl.program_id(0)
    pairs = ((input_a, a_input_a), (input_m, a_input_m), (mixed, a_mixed), (acted, a_acted))
    copies = [pltpu.make_async_copy(src, dst, sems.at[i]) for i, (src, dst) in enumerate(pairs)]

    @pl.when(step == 0)
    def _():
        assemble(0, own, other, bcol_own, bcol_other, wqkv, wo, bqkv, bfc1)
        dbias[...] = jnp.zeros_like(dbias)
        pay_own[...] = jnp.zeros_like(pay_own)
        for copy in copies:
            copy.start()

    rows = pl.ds(pl.multiple_of(step * TOK, TOK), TOK)
    single = dict(query=query, keyed=keyed, valued=valued, branch_a=branch_a, middle=middle,
                  branch_m=branch_m)

    def take(name, index=None):
        if name == "probs":
            return probs[0, index]
        if name == "slope":
            return slope[0, :, index * HMLP : (index + 1) * HMLP]
        return single[name][0]

    def mods_out(j, value):
        dmods[0, j : j + 1, :] = value

    def bias(name, start, value):
        at = BIAS[name] + start
        dbias[:, at : at + value.shape[1]] += token_sum(value.astype(f32))

    stash = dict(dqkv=s_dqkv, dg=s_dg, dya=s_dya, dym=s_dym)
    grad = layer_backward(dx[0], x0[0], lambda j: mods[0, j : j + 1, :], own, other, wqkv, wo,
                          take, rows, stash, mods_out, bias)
    grad = grad.astype(bf16)
    pay_own[PAY_PATCH : PAY_PATCH + PV, :] += dot(xt[0], grad)
    pay_own[PAY_BPATCH : PAY_BPATCH + 1, :] += token_sum(grad.astype(f32))
    dmods[0, 6 : 6 + 8, :] = dmods1[0]
    rounded = dmods[0].astype(bf16).astype(f32)
    dmods[0] = rounded
    pay_own[PAY_COND : PAY_COND + 14, :] += rounded

    @pl.when(step == pl.num_programs(0) - 1)
    def _():
        for copy in copies:
            copy.wait()
        weight_grads(a_input_a, a_input_m, a_mixed, a_acted, stash,
                     (col_own, col_other), (row_own, row_other))
        pay_own[PAY_HEAD : PAY_HEAD + PV, :] = dhead[...]
        for layer, values in enumerate((dbias, dbias1)):
            pay_own[PAY_PROJ + layer : PAY_PROJ + layer + 1, :] = values[:, BIAS["proj"] : BIAS["proj"] + D]
            pay_own[PAY_FC2 + layer : PAY_FC2 + layer + 1, :] = values[:, BIAS["fc2"] : BIAS["fc2"] + D]
        head_line = jnp.sum(jnp.where(diagonal(PV), dbhead[...], 0.0), 0, keepdims=True)
        pay_own[PAY_BHEAD : PAY_BHEAD + 1, :] = jnp.concatenate(
            [head_line, jnp.sum(loss[...], 1, keepdims=True), jnp.zeros((1, D - PV - 1), f32)], 1
        )
        pay_other[...] = pay_own[...]
        for side, out in enumerate((pay_own, pay_other)):
            for layer, values in enumerate((dbias, dbias1)):
                write_bcol(values, side, out, layer)
        for out in (pay_own, pay_other):
            out[PAY_BCOL + 8 :, :] = jnp.zeros((PAY_ROWS - PAY_BCOL - 8, D), f32)


def per_latent(*shape):
    zeros = (0,) * len(shape)
    return pl.BlockSpec((1,) + shape, lambda n: (n,) + zeros)


def fixed(*shape):
    zeros = (0,) * len(shape)
    return pl.BlockSpec(shape, lambda n: zeros, pipeline_mode=pl.Buffered(1))


def params():
    return pltpu.CompilerParams(dimension_semantics=("arbitrary",), vmem_limit_bytes=62 * 2**20)


SAVED = [
    ("query", (TOK, D), bf16), ("keyed", (TOK, D), bf16), ("valued", (TOK, D), bf16),
    ("probs", (HEADS, TOK, TOK), f32), ("branch_a", (TOK, D), f32), ("middle", (TOK, D), f32),
    ("slope", (TOK, MLP), f32), ("branch_m", (TOK, D), f32), ("mixed", (TOK, D), bf16),
    ("acted", (TOK, MLP), bf16), ("input_a", (TOK, D), bf16), ("input_m", (TOK, D), bf16),
]
GRAD_SHAPES = [(COL_S, D), (COL_S, D), (ROW_S, D), (ROW_S, D)]
WEIGHT_SCRATCH = [pltpu.VMEM((D, 3 * D), bf16), pltpu.VMEM((D, D), bf16),
                  pltpu.VMEM((1, 3 * D), f32), pltpu.VMEM((1, MLP), f32)]


def weight_specs(layer):
    half = pl.BlockSpec((D, GATH), lambda n: (0, layer), pipeline_mode=pl.Buffered(1))
    return [half, half, fixed(L, COL_S), fixed(L, COL_S), fixed(1, NBR)]


def stash_scratch(count):
    rows = count * TOK
    return [pltpu.VMEM((rows, 3 * D), bf16), pltpu.VMEM((rows, MLP), bf16),
            pltpu.VMEM((rows, D), bf16), pltpu.VMEM((rows, D), bf16)]


def cost(flops, nbytes, count):
    return pl.CostEstimate(flops=int(flops * count), bytes_accessed=int(nbytes * count),
                           transcendentals=int(2e6 * count))


def run_forward(xt, mods, full_io, pos, weights):
    count = xt.shape[0]
    outs = [("x0", (TOK, D), f32)] + SAVED + [("x2", (TOK, D), f32)]
    return pl.pallas_call(
        forward_kernel,
        grid=(count,),
        in_specs=[per_latent(PV, TOK), per_latent(14, D),
                  pl.BlockSpec((1, PV, D), lambda n: (0, 0, 0)), fixed(TOK, D)] + weight_specs(0),
        out_specs=[per_latent(*shape) for _, shape, _ in outs],
        out_shape=[jax.ShapeDtypeStruct((count,) + shape, kind) for _, shape, kind in outs],
        scratch_shapes=WEIGHT_SCRATCH,
        compiler_params=params(),
        cost_estimate=cost(1.0e9, 6e6, count),
        name="forward_first",
    )(xt, mods, full_io, pos, *weights)


def run_middle(x2, mods, weights, full_io, targets):
    count = x2.shape[0]
    rows = count * TOK
    outs = [((count, TOK, D), per_latent(TOK, D)), ((count, 8, D), per_latent(8, D))]
    outs += [(shape, fixed(*shape)) for shape in GRAD_SHAPES]
    outs += [(shape, fixed(*shape)) for shape in ((1, BIAS_WIDTH), (PV, D), (PV, 1), (1, TOK))]
    return pl.pallas_call(
        middle_kernel,
        grid=(count,),
        in_specs=[per_latent(TOK, D), per_latent(14, D)] + weight_specs(1)
        + [pl.BlockSpec((1, PV, D), lambda n: (1, 0, 0)), per_latent(PV, TOK)],
        out_specs=[spec for _, spec in outs],
        out_shape=[jax.ShapeDtypeStruct(shape, f32) for shape, _ in outs],
        scratch_shapes=WEIGHT_SCRATCH
        + [pltpu.VMEM((TOK, D), bf16)] * 3
        + [pltpu.VMEM((HEADS, TOK, TOK), f32), pltpu.VMEM((rows, D), bf16),
           pltpu.VMEM((TOK, D), f32), pltpu.VMEM((TOK, D), f32), pltpu.VMEM((rows, MLP), bf16),
           pltpu.VMEM((TOK, MLP), f32), pltpu.VMEM((TOK, D), f32),
           pltpu.VMEM((rows, D), bf16), pltpu.VMEM((rows, D), bf16)]
        + stash_scratch(count),
        compiler_params=params(),
        cost_estimate=cost(3.2e9, 3e6, count),
        name="layer_second",
    )(x2, mods, *weights, full_io, targets)


def run_last(dx, x0, mods, weights, xt, smalls, dmods1, saved):
    count = dx.shape[0]
    rows = count * TOK
    outs = [((count, 14, D), per_latent(14, D))]
    outs += [(shape, fixed(*shape)) for shape in GRAD_SHAPES]
    outs += [(shape, fixed(*shape)) for shape in ((PAY_ROWS, D), (PAY_ROWS, D))]
    return pl.pallas_call(
        last_kernel,
        grid=(count,),
        in_specs=[per_latent(TOK, D), per_latent(TOK, D), per_latent(14, D)] + weight_specs(0)
        + [per_latent(PV, TOK)]
        + [fixed(*shape) for shape in ((1, BIAS_WIDTH), (PV, D), (PV, 1), (1, TOK))] + [per_latent(8, D)]
        + [per_latent(*shape) for _, shape, _ in SAVED[:-4]] + [pl.BlockSpec(memory_space=pl.ANY)] * 4,
        out_specs=[spec for _, spec in outs],
        out_shape=[jax.ShapeDtypeStruct(shape, f32) for shape, _ in outs],
        scratch_shapes=WEIGHT_SCRATCH
        + [pltpu.VMEM((rows, D), bf16)] * 3 + [pltpu.VMEM((rows, MLP), bf16)]
        + stash_scratch(count) + [pltpu.VMEM((1, BIAS_WIDTH), f32), pltpu.SemaphoreType.DMA((4,))],
        compiler_params=params(),
        cost_estimate=cost(2.2e9, 8e6, count),
        name="backward_first",
    )(dx, x0, mods, *weights, xt, *smalls, dmods1, *saved[:-4], *[v.reshape(rows, -1) for v in saved[-4:]])


PACK = 128
WIDE = 3 * D


def split3(values):
    high = values.astype(bf16)
    rest = values - high.astype(f32)
    mid = rest.astype(bf16)
    low = (rest - mid.astype(f32)).astype(bf16)
    return high, mid, low


def narrow_dot(small, big, dims):
    parts = split3(small)
    high, mid, low = split3(big)
    first = dot(jnp.concatenate(parts, 0), high, dims)
    second = dot(jnp.concatenate(parts[:2], 0), mid, dims)
    third = dot(parts[0], low, dims)
    r = small.shape[0]
    return first[:r] + ((first[r : 2 * r] + second[:r]) + (first[2 * r :] + second[r:] + third))


def outer(left, right):
    l1, l2, l3 = split3(left)
    r1, r2, r3 = split3(right)
    return dot(
        jnp.concatenate([l1, l1, l2, l2, l1, l3], 0), jnp.concatenate([r1, r2, r1, r2, r3, r1], 0), TN
    )


PROJECT_STEPS = 2
WIDE_BLOCK = COL_S // PROJECT_STEPS
TALL_BLOCK = ROW_S // PROJECT_STEPS


def project_step(err_col, own_col, got_col, err_row, own_row, got_row, fac_col, fac_row,
                 mat_col, mat_row, left_col, left_row):
    step = pl.program_id(0)
    matrix = err_col[0] + (own_col[...] + got_col[...])
    mat_col[...] = matrix
    part = narrow_dot(fac_col[0], matrix, NN)
    matrix = err_row[0] + (own_row[...] + got_row[...])
    mat_row[...] = matrix
    side = narrow_dot(fac_row[0], matrix, NT)

    @pl.when(step == 0)
    def _():
        left_col[...] = part
        left_row[...] = jnp.zeros_like(left_row)
        left_row[:, :TALL_BLOCK] = side

    @pl.when(step == 1)
    def _():
        left_col[...] += part
        left_row[:, TALL_BLOCK:ROW_S] = side


def project_second_kernel(block, err_col, own_col, got_col, err_row, own_row, got_row, fac_col, fac_row,
                          dmods, full_cond, cond_own,
                          mat_col, mat_row, left_col, left_row, grad_cond, cols_sent):
    project_step(err_col, own_col, got_col, err_row, own_row, got_row, fac_col, fac_row,
                 mat_col, mat_row, left_col, left_row)

    @pl.when(pl.program_id(0) == 0)
    def _():
        n_dp, count = cols_sent.shape[0], cols_sent.shape[1]
        line = jnp.concatenate([dmods[:, j, :] for j in range(14)], 1)
        grad_act = dot(line.astype(bf16), full_cond[...], NT)
        cond = cond_own[...]
        gate = 1.0 / (1.0 + jnp.exp(-cond))
        grad_cond[...] = grad_act * (gate * (1.0 + cond * (1.0 - gate)))
        for j in range(n_dp):
            cols_sent[j] = jnp.concatenate(
                [line[:, j * block : (j + 1) * block], jnp.zeros((count, D - block), f32)], 1
            )


def packed_slots():
    return ["row0", "row1", "col0", "col1", "io0", "io1", "row0", "row1", "row0", "row1"]


def project_first_kernel(err_col, own_col, got_col, err_row, own_row, got_row, fac_col, fac_row,
                         left_col1, left_row1, grad_cond, cols_sent, pay_own, pay_got, err_io, fac_io,
                         mat_col, mat_row, mat_io, sent, left_col, left_row):
    project_step(err_col, own_col, got_col, err_row, own_row, got_row, fac_col, fac_row,
                 mat_col, mat_row, left_col, left_row)

    @pl.when(pl.program_id(0) == PROJECT_STEPS - 1)
    def _():
        n_dp, count = cols_sent.shape[0], cols_sent.shape[1]
        share = PACK // n_dp
        pay = pay_own[...] + pay_got[...]
        left_io = []
        for index in range(2):
            matrix = pay[index * PV : (index + 1) * PV] + err_io[index]
            mat_io[index] = matrix
            left_io.append(dot_full(fac_io[index], matrix))
        sent[:, :count, :] = jnp.broadcast_to(grad_cond[...][None], (n_dp, count, D))
        sent[:, count : 2 * count, :] = cols_sent[...]
        sent[:, 2 * count :, :] = jnp.zeros((n_dp, share, D), f32)
        tall = (left_row, left_row1)
        for column in range(RANK):
            pick = slice(column, column + 1)
            lines = [tall[i % 2][pick, (i // 2) * D : (i // 2 + 1) * D] for i in (0, 1)]
            lines += [left_col[pick, :], left_col1[pick, :], left_io[0][pick], left_io[1][pick]]
            lines += [tall[i % 2][pick, (i // 2) * D : (i // 2 + 1) * D] for i in (2, 3, 4, 5)]
            for extra in range(6):
                at = column * 6 + extra
                if at < SMALL_ROWS:
                    lines.append(pay[PAY_PROJ + at : PAY_PROJ + at + 1])
            for slot, line in enumerate(lines):
                at = column * 16 + slot
                place = 2 * count + at % share
                sent[at // share, place : place + 1, :] = line


def project_specs(layer):
    col_block = pl.BlockSpec((WIDE_BLOCK, D), lambda n: (n, 0))
    row_block = pl.BlockSpec((TALL_BLOCK, D), lambda n: (n, 0))
    ins = [pl.BlockSpec((1, WIDE_BLOCK, D), lambda n: (layer, n, 0)), col_block, col_block,
           pl.BlockSpec((1, TALL_BLOCK, D), lambda n: (layer, n, 0)), row_block, row_block,
           pl.BlockSpec((1, RANK, WIDE_BLOCK), lambda n: (n, 0, 0)),
           pl.BlockSpec((1, RANK, D), lambda n: (layer, 0, 0))]
    return ins, [col_block, row_block]


def steps_of(fac_col):
    return fac_col.reshape(RANK, PROJECT_STEPS, WIDE_BLOCK).transpose(1, 0, 2)


def run_project_second(err_col, grads, err_row, fac_col, fac_row, dmods, full_cond, cond_own, n_dp):
    own_col, got_col, own_row, got_row = grads
    count = dmods.shape[0]
    ins, outs = project_specs(1)
    extra = [(RANK, D), (RANK, WIDE), (count, D), (n_dp, count, D)]
    return pl.pallas_call(
        lambda *refs: project_second_kernel(N_MODS // n_dp, *refs),
        grid=(PROJECT_STEPS,),
        in_specs=ins + [fixed(count, 14, D), fixed(D, N_MODS), fixed(count, D)],
        out_specs=outs + [fixed(*shape) for shape in extra],
        out_shape=[jax.ShapeDtypeStruct(shape, f32) for shape in [(COL_S, D), (ROW_S, D)] + extra],
        compiler_params=params(),
        name="left_second",
    )(err_col, own_col, got_col, err_row, own_row, got_row, steps_of(fac_col[1]), fac_row,
      dmods, full_cond, cond_own)


def run_project_first(err_col, grads, err_row, fac_col, fac_row, left_col1, left_row1, grad_cond, cols_sent,
                      pay_own, pay_got, err_io, fac_io):
    own_col, got_col, own_row, got_row = grads
    n_dp, count = cols_sent.shape[:2]
    ins, outs = project_specs(0)
    extra = [(2, PV, D), (n_dp, 2 * count + PACK // n_dp, D)]
    return pl.pallas_call(
        project_first_kernel,
        grid=(PROJECT_STEPS,),
        in_specs=ins + [fixed(RANK, D), fixed(RANK, WIDE), fixed(count, D), fixed(n_dp, count, D),
                        fixed(PAY_ROWS, D), fixed(PAY_ROWS, D), fixed(2, PV, D), fixed(2, RANK, PV)],
        out_specs=outs + [fixed(*shape) for shape in extra],
        out_shape=[jax.ShapeDtypeStruct(shape, f32) for shape in [(COL_S, D), (ROW_S, D)] + extra],
        scratch_shapes=[pltpu.VMEM((RANK, D), f32), pltpu.VMEM((RANK, WIDE), f32)],
        compiler_params=params(),
        name="left_first",
    )(err_col, own_col, got_col, err_row, own_row, got_row, steps_of(fac_col[0]), fac_row,
      left_col1, left_row1, grad_cond, cols_sent, pay_own, pay_got, err_io, fac_io)


TIME_ROWS = FREQ + D + 8


def modulation_kernel(block, core, got, act_half, features, first, first_act, full_time, labels,
                      cond_mine, cond_their, time_part, table_part):
    n_dp = got.shape[0]
    count = (got.shape[1] - PACK // n_dp) // 2
    half = block // 2
    grad_cond = got[:, :count, :].reshape(n_dp * count, D)
    cols = got[:, count : 2 * count, :].reshape(n_dp * count, D)
    left, right = cols[:, :half].astype(bf16), cols[:, half:block].astype(bf16)
    is_first = core[0] == 0
    grad_left = dot(act_half[...], left, TN)
    grad_right = dot(act_half[...], right, TN)
    cond_mine[...] = jnp.where(is_first, grad_left, grad_right)
    cond_their[...] = jnp.where(is_first, grad_right, grad_left)
    grad_second = grad_cond.astype(bf16)
    gate = 1.0 / (1.0 + jnp.exp(-first[...]))
    slope = gate * (1.0 + first[...] * (1.0 - gate))
    grad_first = (dot(grad_second, full_time[FREQ:, :], NT) * slope).astype(bf16)
    time_part[:FREQ, :] = dot(features[...], grad_first, TN)
    time_part[FREQ : FREQ + D, :] = dot(first_act[...], grad_second, TN)
    time_part[FREQ + D :, :] = jnp.concatenate(
        [token_sum(grad_first.astype(f32)), token_sum(grad_second.astype(f32)), jnp.zeros((6, D), f32)], 0
    )
    onehot = (labels[...] == lax.broadcasted_iota(jnp.int32, (n_dp * count, CLASSES), 1)).astype(f32).astype(bf16)
    high, mid, low = split3(grad_cond)
    table_part[...] = dot(high, onehot, TN) + (dot(mid, onehot, TN) + dot(low, onehot, TN))


def run_modulation(core, got, act_half, features, first, first_act, full_time, labels):
    half = N_MODS // got.shape[0] // 2
    shapes = [(D, half), (D, half), (TIME_ROWS, D), (D, CLASSES)]
    vmem = pl.BlockSpec(memory_space=pltpu.VMEM)
    return pl.pallas_call(
        lambda *refs: modulation_kernel(2 * half, *refs),
        in_specs=[pl.BlockSpec(memory_space=pltpu.SMEM)] + [vmem] * 7,
        out_shape=[jax.ShapeDtypeStruct(shape, f32) for shape in shapes],
        compiler_params=pltpu.CompilerParams(vmem_limit_bytes=62 * 2**20),
        name="modulation_gradients",
    )(core, got, act_half, features, first, first_act, full_time, labels)


COL_ROWS = 4 * RANK
ROW_AT = L * COL_ROWS
IO_AT = ROW_AT + L * RANK
EXTRA_AT = IO_AT + 2 * RANK


def cond_top(rows):
    return -(-((rows + 1) // 2) // 8) * 8


def ortho(packed, left_col, left_row, left_io):
    columns = []
    blank = jnp.zeros((4, D), f32)
    for index in range(RANK):
        block = packed[index]
        column = jnp.concatenate(
            [block[0:6], jnp.concatenate([block[6:8], blank], 0), jnp.concatenate([block[8:10], blank], 0)], 1
        )
        for earlier in columns:
            column = column - jnp.sum(earlier * column, -1, keepdims=True) * earlier
        column = column * lax.rsqrt(jnp.sum(column * column, -1, keepdims=True) + ortho_eps)
        for layer in range(L):
            left_row[layer, index : index + 1, :] = column[layer : layer + 1]
            left_col[layer, index : index + 1, :] = column[2 + layer : 3 + layer, :D]
            left_io[layer, index : index + 1, :] = column[4 + layer : 5 + layer, :D]
        columns.append(column)


def total_squares(values):
    return jnp.sum(values * values, keepdims=True)


def right_kernel(packed, mat_col0, mat_row0, mat_col1, mat_row1, mat_io, cond_own, cond_got, table_own, table_got,
                 sent, left_col, left_row, left_io, table_share, flat):
    ortho(packed, left_col, left_row, left_io)
    for layer, (col, row) in enumerate(((mat_col0, mat_row0), (mat_col1, mat_row1))):
        right = narrow_dot(left_col[layer], col[...], NT)
        for piece in range(4):
            wide = min(D, COL_S - piece * D)
            at = layer * COL_ROWS + piece * RANK
            if wide < D:
                flat[at : at + RANK, :] = jnp.zeros((RANK, D), f32)
            flat[at : at + RANK, :wide] = right[:, piece * D : piece * D + wide]
        at = ROW_AT + layer * RANK
        flat[at : at + RANK, :] = narrow_dot(left_row[layer][:, :ROW_S], row[...], NN)
        at = IO_AT + layer * RANK
        flat[at : at + RANK, :] = jnp.zeros((RANK, D), f32)
        flat[at : at + RANK, :PV] = dot_full(left_io[layer], mat_io[layer], NT)
    cond_grad = cond_own[...] + cond_got[...]
    table = table_own[...] + table_got[...]
    table_share[...] = table
    flat[EXTRA_AT:, :] = jnp.zeros((PACK - EXTRA_AT, D), f32)
    flat[EXTRA_AT : EXTRA_AT + 1, :] = jnp.concatenate(
        [total_squares(cond_grad), total_squares(table), jnp.zeros((1, D - 2), f32)], 1
    )
    n_dp = sent.shape[0]
    share = PACK // n_dp
    rows, half = D // n_dp, cond_grad.shape[1]
    top = cond_top(rows)
    sent[:, :share, :] = flat[...].reshape(n_dp, share, D)
    for j in range(n_dp):
        piece = cond_grad[j * rows : (j + 1) * rows]
        sent[j, share : share + min(top, rows), :half] = piece[:top]
        if rows > top:
            sent[j, share : share + rows - top, half : 2 * half] = piece[top:]


def run_right(n_dp, packed, mats, mat_io, cond_own, cond_got, table_own, table_got):
    shapes = [(n_dp, PACK // n_dp + cond_top(D // n_dp), D), (L, RANK, D), (L, RANK, WIDE), (2, RANK, D),
              table_own.shape]
    return pl.pallas_call(
        right_kernel,
        out_shape=[jax.ShapeDtypeStruct(shape, f32) for shape in shapes],
        scratch_shapes=[pltpu.VMEM((PACK, D), f32)],
        compiler_params=pltpu.CompilerParams(vmem_limit_bytes=62 * 2**20),
        name="right_factors",
    )(packed, *mats, mat_io, cond_own, cond_got, table_own, table_got)


def norm_kernel(packed, left_packed, left_col, left_row, left_io, time_own, time_got,
                right_col, right_row, right_io, parts, brep_grad, bcol_grad):
    for layer in range(L):
        for piece in range(4):
            wide = min(D, COL_S - piece * D)
            at = layer * COL_ROWS + piece * RANK
            right_col[layer, :, piece * D : piece * D + wide] = packed[at : at + RANK, :wide]
        at = ROW_AT + layer * RANK
        right_row[layer] = packed[at : at + RANK, :]
        at = IO_AT + layer * RANK
        right_io[layer] = packed[at : at + RANK, :PV]

    def small(at):
        row = at - PAY_PROJ
        return left_packed[row // 6, 10 + row % 6 : 11 + row % 6, :]

    time_bias = time_own[FREQ + D :, :] + time_got[FREQ + D :, :]
    lines = [small(PAY_PROJ + row) for row in range(4)] + [small(PAY_COND + row) for row in range(14)]
    lines += [time_bias[0:1], time_bias[1:2], small(PAY_BPATCH), small(PAY_BHEAD)[:, :PV]]
    whole = jnp.zeros((1, 1), f32)
    for row, line in enumerate(lines):
        brep_grad[:, row * D : row * D + line.shape[1]] = line
        whole = whole + total_squares(line)
    split = jnp.zeros((1, 1), f32)
    for layer in range(L):
        line = jnp.concatenate([small(PAY_BCOL + 4 * layer + row) for row in range(4)], 1)[:, :COL_S]
        bcol_grad[layer : layer + 1, :] = line
        split = split + total_squares(line)
    whole = whole + total_squares(time_own[: FREQ + D, :] + time_got[: FREQ + D, :])

    def gram(left, right):
        return jnp.sum(dot_full(left, left, NT) * dot_full(right, right, NT), keepdims=True)

    for layer in range(L):
        split = split + gram(left_col[layer], right_col[layer]) + gram(left_row[layer], right_row[layer])
        whole = whole + gram(left_io[layer], right_io[layer])
    sums = packed[EXTRA_AT : EXTRA_AT + 1, :]
    split = split + sums[:, 0:1]
    whole = whole + sums[:, 1:2]
    loss = small(PAY_BHEAD)[:, PV : PV + 1]
    parts[...] = jnp.concatenate([split, whole, loss, jnp.zeros((1, 125), f32)], 1)


def run_norm(packed, left_packed, lefts, time_own, time_got):
    shapes = [(L, RANK, COL_S), (L, RANK, D), (2, RANK, PV), (1, 128), (1, NBR), (L, COL_S)]
    return pl.pallas_call(
        norm_kernel,
        out_shape=[jax.ShapeDtypeStruct(shape, f32) for shape in shapes],
        compiler_params=pltpu.CompilerParams(vmem_limit_bytes=62 * 2**20),
        name="gradient_norm",
    )(packed, left_packed, *lefts, time_own, time_got)


def error_kernel(mat_col0, mat_row0, mat_col1, mat_row1, mat_io, left_col, left_row, left_io,
                 right_col, right_row, right_io, err_col, err_row, err_io):
    for layer, (col, row) in enumerate(((mat_col0, mat_row0), (mat_col1, mat_row1))):
        @pl.when(pl.program_id(0) == layer)
        def _():
            err_col[0] = col[...] - outer(right_col[layer], left_col[layer])
            err_row[0] = row[...] - outer(left_row[layer][:, :ROW_S], right_row[layer])
            err_io[layer] = mat_io[layer] - outer(right_io[layer], left_io[layer])


def run_error(mats, mat_io, lefts, rights):
    return pl.pallas_call(
        error_kernel,
        grid=(L,),
        in_specs=[fixed(*v.shape) for v in (*mats, mat_io, *lefts, *rights)],
        out_specs=[pl.BlockSpec((1, COL_S, D), lambda n: (n, 0, 0)),
                   pl.BlockSpec((1, ROW_S, D), lambda n: (n, 0, 0)), fixed(2, PV, D)],
        out_shape=[jax.ShapeDtypeStruct((L, COL_S, D), f32), jax.ShapeDtypeStruct((L, ROW_S, D), f32),
                   jax.ShapeDtypeStruct((2, PV, D), f32)],
        compiler_params=params(),
        name="next_errors",
    )(*mats, mat_io, *lefts, *rights)


def update_kernel(core, parts, parts_got, left_col, right_col, right_row, left_row, right_io, left_io,
                  cond_own, cond_got, time_grad, table_grad, bcol_grad, brep_grad,
                  w_col, w_row, w_cond, w_time, w_io, w_table, b_col, b_rep,
                  m_col, m_row, m_cond, m_time, m_io, m_table, m_bcol, m_brep,
                  scalars, n_col, n_row, n_cond, n_time, n_io, n_table, n_bcol, n_brep,
                  v_col, v_row, v_cond, v_time, v_io, v_table, v_bcol, v_brep):
    clip_norm = jnp.sqrt(parts[:, 0:1] + parts_got[:, 0:1] + parts[:, 1:2])
    scaling = jnp.minimum(1.0, clip_limit / clip_norm)
    scalars[...] = jnp.concatenate([parts[:, 2:3], clip_norm, jnp.zeros((1, 126), f32)], 1)

    def advance(weight, momentum, gradient):
        moved = momentum_decay * momentum + scaling * gradient
        return weight - learn_rate * moved, moved

    for layer in range(L):
        n_col[layer], v_col[layer] = advance(
            w_col[layer], m_col[layer], outer(left_col[layer], right_col[layer]))
        n_row[layer], v_row[layer] = advance(
            w_row[layer], m_row[layer], outer(right_row[layer], left_row[layer][:, :ROW_S]))
        n_io[layer], v_io[layer] = advance(
            w_io[layer], m_io[layer], outer(right_io[layer], left_io[layer]))
    n_dp = cond_own.shape[0]
    rows = w_cond.shape[0]
    half = N_MODS // n_dp // 2
    top = cond_top(rows)
    share = cond_own.shape[1] - top
    is_first = core[0] == 0
    pieces = []
    for j in range(n_dp):
        mine, theirs = cond_own[j, share:, :], cond_got[j]
        for pair in ((mine, theirs), (theirs, mine)):
            block = jnp.where(is_first, pair[0], pair[1])
            if rows > top:
                block = jnp.concatenate([block[:top, :half], block[: rows - top, half : 2 * half]], 0)
            else:
                block = block[:rows, :half]
            pieces.append(block)
    n_cond[...], v_cond[...] = advance(w_cond[...], m_cond[...], jnp.concatenate(pieces, 1))
    n_time[...], v_time[...] = advance(w_time[...], m_time[...], time_grad[...])
    n_table[...], v_table[...] = advance(w_table[...], m_table[...], table_grad[...])
    n_bcol[...], v_bcol[...] = advance(b_col[...], m_bcol[...], bcol_grad[...])
    n_brep[...], v_brep[...] = advance(b_rep[...], m_brep[...], brep_grad[...])


def run_update(core, grads, weights, momenta):
    vmem = pl.BlockSpec(memory_space=pltpu.VMEM)
    shapes = [(1, 128)] + [v.shape for v in weights] * 2
    return pl.pallas_call(
        update_kernel,
        in_specs=[pl.BlockSpec(memory_space=pltpu.SMEM)] + [vmem] * (len(grads) + 2 * len(weights)),
        out_shape=[jax.ShapeDtypeStruct(shape, f32) for shape in shapes],
        compiler_params=pltpu.CompilerParams(vmem_limit_bytes=62 * 2**20),
        name="weight_update",
    )(core, *grads, *weights, *momenta)


def swap(values):
    return lax.ppermute(values, "tensor", [(0, 1), (1, 0)])


def trade(chunks):
    return lax.all_to_all(chunks, "dp", 0, 0, tiled=True)


def spread(values):
    return trade(jnp.broadcast_to(values[None], (lax.axis_size("dp"),) + values.shape))


def exact_parts(values):
    high = lax.reduce_precision(values, 8, 7)
    mid = lax.reduce_precision(values - high, 8, 7)
    return [part.astype(bf16) for part in (high, mid, (values - high) - mid)]


def on_device(
    latents, gauss_noise, time_steps, labels, targets,
    w_col, w_row, w_cond, w_time, w_io, class_table, b_col, b_rep,
    mom_col, mom_row, mom_cond, mom_time, mom_io, mom_table, mom_bcol, mom_brep,
    err_col, err_row, err_io, fac_col, fac_row, fac_io,
):
    n_dp = lax.axis_size("dp")
    index_dp = lax.axis_index("dp")
    index_t = lax.axis_index("tensor")
    core = index_t.astype(jnp.int32).reshape(1)
    first_core = index_t == 0
    n_all = labels.shape[0]
    per_dp = latents.shape[0]
    count = per_dp // 2
    rows = w_col.shape[1]

    def flip(values):
        return values.transpose(0, 2, 1)

    def halves(mine, theirs, axis):
        pair = jnp.stack([mine, theirs], axis)
        return jnp.where(first_core, pair, jnp.flip(pair, axis))

    row_sh = flip(w_row)
    shard = jnp.concatenate(
        [piece[layer] for layer in range(L)
         for piece in (w_col[:, :, QKV_S:], row_sh[:, :, HALF:], w_col[:, :, :QKV_S], row_sh[:, :, :HALF])], 1
    ).astype(bf16)
    full = lax.all_gather(shard, ("dp", "tensor"))

    block = N_MODS // n_dp
    half_block = block // 2
    classes = jnp.arange(CLASSES, dtype=jnp.int32)
    onehot_t = classes[:, None] == labels[None, :]
    looked = dot(class_table.astype(bf16), onehot_t.astype(bf16), TN).astype(bf16)
    time_rows = w_time.shape[0]
    sizes = [rows * n_all, time_rows * D, 2 * PV * rows, 3 * per_dp]
    wide = -(-sum(sizes) // 256) * 128
    common = jnp.concatenate(
        [part.reshape(-1) for part in
         (looked, w_time.astype(bf16), flip(w_io).astype(bf16), *exact_parts(time_steps))]
    )
    common = jnp.pad(common, (0, 2 * wide - common.shape[0]))
    common = lax.dynamic_slice_in_dim(common.reshape(2, wide), index_t, 1, 0)
    cond_bf = w_cond.astype(bf16).reshape(rows, n_dp, 2, half_block)
    cond_mine = lax.dynamic_slice_in_dim(cond_bf, index_t, 1, 2)[:, :, 0].transpose(1, 0, 2)
    sent = jnp.concatenate(
        [jnp.broadcast_to(common, (n_dp, wide)), cond_mine.reshape(n_dp, rows * half_block)], 1
    )
    got = trade(sent)
    cond_cols = got[:, wide:].reshape(D, half_block)
    mine = got[:, :wide]
    common = halves(mine, swap(mine), 1).reshape(n_dp, 2 * wide)
    ends = np.cumsum([0] + sizes)
    looked = common[:, : ends[1]].reshape(D, n_all).T
    full_time = common[:, ends[1] : ends[2]].reshape(FREQ + D, D)
    full_io = flip(common[:, ends[2] : ends[3]].reshape(n_dp, 2 * PV, rows).transpose(1, 0, 2).reshape(2, PV, D).transpose(0, 2, 1))
    steps_all = jnp.sum(common[:, ends[3] : ends[4]].reshape(n_dp, 3, per_dp).astype(f32), 1).reshape(n_all)

    features = frequency_features(steps_all).astype(bf16)
    first = dot(features, full_time[:FREQ]) + b_rep[START_FIRST:START_SECOND]
    first_act = jax.nn.silu(first).astype(bf16)
    second = dot(first_act, full_time[FREQ:]) + b_rep[START_SECOND:START_PATCH]
    cond = second + looked.astype(f32)
    cond_act = jax.nn.silu(cond).astype(bf16)
    mods = dot(cond_act, cond_cols).reshape(n_dp * 2, count, half_block)
    mods = lax.all_to_all(mods, ("dp", "tensor"), 0, 0, tiled=True)
    mods = mods.transpose(1, 0, 2).reshape(count, N_MODS)
    mods = (mods + b_rep[START_COND:START_FIRST]).reshape(count, 14, D)
    full, mods = lax.optimization_barrier((full, mods))
    full = full.reshape(n_dp, 2, rows, L * GATH)

    def half_of(values):
        split = values.reshape((n_dp, 2, count) + values.shape[1:])
        return lax.dynamic_slice_in_dim(split, index_t, 1, 1).reshape((n_dp * count,) + values.shape[1:])

    halves_of = [half_of(v) for v in (cond_act, features, first, first_act)]
    labels_half = half_of(labels)[:, None]
    cond_own = lax.dynamic_slice_in_dim(cond, (index_dp * 2 + index_t) * count, count, 0)

    def mine_of(values):
        return lax.dynamic_slice_in_dim(values, index_t * count, count, 0)

    steps_own = mine_of(time_steps)[:, None, None]
    xt = (
        (1.0 - steps_own) * flip(mine_of(latents)) + steps_own * flip(mine_of(gauss_noise))
    ).astype(bf16)
    b_line = b_rep[None]
    own = lax.dynamic_slice_in_dim(full, index_t, 1, 1).reshape(D, L * GATH)
    other = lax.dynamic_slice_in_dim(full, 1 - index_t, 1, 1).reshape(D, L * GATH)
    weights = (own, other, b_col, swap(b_col), b_line)
    x0, *saved, x2 = run_forward(xt, mods, full_io, jnp.asarray(position_table()), weights)
    x2, late_cond = lax.optimization_barrier((x2, w_cond))
    full_cond = lax.all_gather(late_cond.astype(bf16), "dp", axis=0, tiled=True)
    dx, dmods1, col_own1, col_oth1, row_own1, row_oth1, *smalls = run_middle(
        x2, mods, weights, full_io, flip(mine_of(targets))
    )
    grads1 = (col_own1, swap(col_oth1), row_own1, swap(row_oth1))
    dmods, col_own0, col_oth0, row_own0, row_oth0, pay_own, pay_oth = run_last(
        dx, x0, mods, weights, xt, smalls, dmods1, saved
    )
    grads0 = (col_own0, swap(col_oth0), row_own0, swap(row_oth0))
    pay_got = swap(pay_oth)

    err_col_t, err_io_t = flip(err_col), flip(err_io)
    fac_col_t, fac_row_t, fac_io_t = flip(fac_col), flip(fac_row), flip(fac_io)
    mat_col1, mat_row1, left_col1, left_row1, grad_cond, cols_sent = run_project_second(
        err_col_t, grads1, err_row, fac_col_t, fac_row_t, dmods, full_cond, cond_own, n_dp
    )
    mat_col0, mat_row0, mat_io, sent = run_project_first(
        err_col_t, grads0, err_row, fac_col_t, fac_row_t, left_col1, left_row1, grad_cond, cols_sent,
        pay_own, pay_got, err_io_t, fac_io_t
    )
    mats = (mat_col0, mat_row0, mat_col1, mat_row1)
    got = trade(sent)
    left_packed = spread(jnp.sum(got[:, 2 * count :], 0)).reshape(RANK, 16, D)

    cond_mine, cond_their, time_own, table_part = run_modulation(core, got, *halves_of, full_time, labels_half)
    cond_got, time_got = swap(cond_their), swap(time_own)
    table_own = lax.dynamic_slice_in_dim(table_part, index_dp * rows, rows, 0)
    table_got = swap(table_own)

    sent, left_col, left_row, left_io, table_share = run_right(
        n_dp, left_packed, mats, mat_io, cond_mine, cond_got, table_own, table_got
    )
    share = PACK // n_dp
    got = trade(sent)
    packed = spread(jnp.sum(got[:, :share], 0)).reshape(PACK, D)
    cond_rows_got = swap(got[:, share:])
    lefts = (left_col, left_row, left_io)
    right_col, right_row, right_io, parts, brep_grad, bcol_grad = run_norm(
        packed, left_packed, lefts, time_own, time_got
    )
    parts_got = swap(parts)
    next_err_col, next_err_row, next_err_io = run_error(mats, mat_io, lefts, (right_col, right_row, right_io))

    def mine_cols(values):
        return lax.dynamic_slice_in_dim(values, index_dp * rows, rows, 2)

    time_at = index_dp * time_rows
    time_grad = (
        lax.dynamic_slice_in_dim(time_own, time_at, time_rows, 0)
        + lax.dynamic_slice_in_dim(time_got, time_at, time_rows, 0)
    )
    olds = (w_col, flip(w_row), w_cond, w_time, flip(w_io), class_table.T, b_col, b_line)
    momenta = (mom_col, flip(mom_row), mom_cond, mom_time, flip(mom_io), mom_table.T, mom_bcol, mom_brep[None])
    scalars, *new = run_update(
        core,
        (parts, parts_got, mine_cols(left_col), right_col, mine_cols(right_row), left_row, right_io,
         mine_cols(left_io), got, cond_rows_got, time_grad, table_share, bcol_grad, brep_grad),
        olds, momenta,
    )

    def outward(col, row, cond, time, io, table, bcol, brep):
        return (col, flip(row), cond, time, flip(io), table.T, bcol, brep[0])

    return (
        scalars[0, 0], scalars[0, 1], *outward(*new[:8]), *outward(*new[8:]),
        flip(next_err_col), next_err_row, flip(next_err_io), flip(right_col), flip(right_row), flip(right_io),
    )


def solution(mesh):
    weights = (
        P(None, "dp", "tensor"), P(None, "tensor", "dp"), P("dp", None), P("dp", None),
        P(None, "dp", None), P(None, "dp"), P(None, "tensor"), P(),
    )
    errors = (P("dp", None, "tensor"), P("dp", "tensor", None), P("dp", None, None))
    factors = (P(None, "tensor", None), P(None, "tensor", None), P())
    rows = P("dp", None, None)
    return jax.shard_map(
        on_device,
        mesh=mesh,
        in_specs=(rows, rows, P("dp"), P(), rows) + weights + weights + errors + factors,
        out_specs=(P(), P()) + weights + weights + errors + factors,
        check_vma=False,
    )
```

```python
import jax
import jax.numpy as jnp
import numpy as np
from jax import lax
from jax.experimental import pallas as pl
from jax.experimental.pallas import tpu as pltpu
from jax.sharding import PartitionSpec as P

D = 384
HEADS = 6
HD = 64
MLP = 1536
NBR = 8080
CLASSES = 1000
FREQ = 256
PV = 16
GRID = 16
L = 2
TOK = 256
RANK = 8
GROUP = 2
AHEAD, MLP_AHEAD, BACK_AHEAD = 2, 2, 3
LAG = 1

norm_eps = 1e-06
ortho_eps = 1e-06
clip_limit = 1.0
momentum_decay = 0.9
learn_rate = 4.0

HALF = D // 2
HMLP = MLP // 2
QKV_S = 3 * HALF
COL_S = QKV_S + HMLP
ROW_S = HALF + HMLP
OFF_W2 = HMLP
OFF_Q = 2 * HMLP
GATH = 2 * HMLP + 4 * HALF

f32 = jnp.float32
bf16 = jnp.bfloat16
highest = lax.Precision.HIGHEST
NN = (((1,), (0,)), ((), ()))
NT = (((1,), (1,)), ((), ()))
TN = (((0,), (0,)), ((), ()))


def dot(left, right, dims=NN):
    return lax.dot_general(left, right, dims, preferred_element_type=f32)


def dot_full(left, right, dims=NN):
    return lax.dot_general(left, right, dims, precision=highest, preferred_element_type=f32)


def position_table():
    quarter = D // 4
    omega = 1.0 / 10000.0 ** (np.arange(quarter, dtype=np.float32) / quarter)
    index = np.arange(TOK)
    across = (index % GRID).astype(np.float32)[:, None] * omega[None, :].astype(np.float32)
    down = (index // GRID).astype(np.float32)[:, None] * omega[None, :].astype(np.float32)
    table = np.concatenate([np.sin(across), np.cos(across), np.sin(down), np.cos(down)], 1)
    return table.astype(np.float32)


def frequency_features(steps):
    half = FREQ // 2
    rates = jnp.exp(-jnp.log(10000.0) * jnp.arange(half, dtype=f32) / half)
    angles = steps[:, None] * rates[None, :]
    return jnp.concatenate([jnp.cos(angles), jnp.sin(angles)], 1)


def normalize(values):
    centered = values - jnp.mean(values, -1, keepdims=True)
    inv_std = lax.rsqrt(jnp.mean(centered * centered, -1, keepdims=True) + norm_eps)
    return centered * inv_std, inv_std


def norm_back(grad, normed, inv_std):
    mean_grad = jnp.mean(grad, -1, keepdims=True)
    mean_mixed = jnp.mean(grad * normed, -1, keepdims=True)
    return inv_std * (grad - mean_grad - normed * mean_mixed)


def token_sum(values):
    return jnp.sum(values, 0, keepdims=True)


START_FC2 = L * D
START_COND = 2 * L * D
N_MODS = (6 * L + 2) * D
START_FIRST = START_COND + N_MODS
START_SECOND = START_FIRST + D
START_PATCH = START_FIRST + 2 * D
START_HEAD = START_FIRST + 3 * D


def assemble(layer, own, other, bcol_own, bcol_other, wqkv, wo, bqkv, bfc1):
    for side, (weights, bias) in enumerate(((own, bcol_own), (other, bcol_other))):
        for head in range(HEADS // 2):
            for part in range(3):
                at = (3 * head + part) * HD
                to = part * D + side * HALF + head * HD
                wqkv[:, to : to + HD] = weights[:, OFF_Q + at : OFF_Q + at + HD]
                bqkv[:, to : to + HD] = bias[layer : layer + 1, at : at + HD]
        wo[:, side * HALF : (side + 1) * HALF] = weights[:, OFF_Q + QKV_S :]
        bfc1[:, side * HMLP : (side + 1) * HMLP] = bias[layer : layer + 1, QKV_S:]


def vector(b_rep, at):
    return b_rep[:, at : at + D]


def head_mask(which):
    lane = lax.broadcasted_iota(jnp.int32, (1, 2 * HD), 1)
    return (lane < HD) if which == 0 else (lane >= HD)


def keep(values, mask):
    return jnp.where(mask, values, jnp.zeros_like(values))


def gelu_parts(pre):
    squared = pre * pre
    coef = np.float32(np.sqrt(2.0 / np.pi))
    tanh = jnp.tanh(pre * (coef + np.float32(coef * 0.044715) * squared))
    half = 0.5 * (1.0 + tanh)
    slope = half + (0.5 * pre) * (1.0 - tanh * tanh) * (
        coef + np.float32(3.0 * 0.044715 * coef) * squared
    )
    return (pre * half).astype(bf16), slope


def ahead_of(products, depth):
    waiting = [next(products) for _ in range(depth)]
    while waiting:
        ready = waiting.pop(0)
        following = next(products, None)
        if following is not None:
            waiting.append(following)
        yield ready


def run_steps(chains, lag):
    waits = [lag * i for i in range(len(chains))]
    live = dict(enumerate(chains))
    while live:
        for i in list(live):
            if waits[i] > 0:
                waits[i] -= 1
            elif next(live[i], 1) is not None:
                del live[i]


def pair_span(pair):
    return slice(pair * 2 * HD, (pair + 1) * 2 * HD)


def layer_forward(x, mod, own, other, wqkv, wo, bqkv, bfc1, bproj, bfc2, put, result):
    normed, _ = normalize(x)
    input_a = (normed * (1.0 + mod(1)) + mod(0)).astype(bf16)
    put("input_a", input_a)
    yield
    thirds = []
    for part in range(3):
        span = slice(part * D, (part + 1) * D)
        value = (dot(input_a, wqkv[:, span]) + bqkv[:, span]).astype(bf16)
        if part == 0:
            value = value * jnp.asarray(HD**-0.5, bf16)
        put(("query", "keyed", "valued")[part], value)
        thirds.append(value)
        yield
    query, keyed, valued = thirds
    scored = ahead_of(
        (dot(keep(query[:, pair_span(pair)], head_mask(which)), keyed[:, pair_span(pair)], NT)
         for pair in range(HEADS // 2) for which in range(2)), AHEAD
    )
    pieces = []
    for pair in range(HEADS // 2):
        total = None
        for which in range(2):
            scores = next(scored)
            yield
            expo = jnp.exp(scores - jnp.max(scores, -1, keepdims=True))
            probs = expo * (1.0 / jnp.sum(expo, -1, keepdims=True))
            put("probs", probs, 2 * pair + which)
            yield
            mixed = dot(probs.astype(bf16), keep(valued[:, pair_span(pair)], head_mask(which)))
            total = mixed if total is None else total + mixed
        pieces.append(total.astype(bf16))
    mixed = jnp.concatenate(pieces, 1)
    put("mixed", mixed)
    yield
    branch_a = dot(mixed, wo[...], NT) + bproj
    put("branch_a", branch_a)
    middle = x + mod(2) * branch_a
    put("middle", middle)
    yield
    normed_m, _ = normalize(middle)
    input_m = (normed_m * (1.0 + mod(4)) + mod(3)).astype(bf16)
    put("input_m", input_m)
    yield
    branch_m = bfc2
    for side, weights in enumerate((own, other)):
        pre = dot(input_m, weights[:, :HMLP]) + bfc1[:, side * HMLP : (side + 1) * HMLP]
        yield
        acted, slope = gelu_parts(pre)
        put("acted", acted, side)
        put("slope", slope, side)
        yield
        branch_m = branch_m + dot(acted, weights[:, OFF_W2 : OFF_W2 + HMLP], NT)
        yield
    put("branch_m", branch_m)
    result.append(middle + mod(5) * branch_m)


def layer_backward(grad, x, mod, own, other, wqkv, wo, take, rows, stash, mods_out, bias, result):
    branch_m = take("branch_m")
    mods_out(5, token_sum(grad * branch_m))
    grad_branch_m = (grad * mod(5)).astype(bf16)
    bias("fc2", 0, grad_branch_m)
    stash["dym"][rows, :] = grad_branch_m
    yield
    grad_input = None
    acting = ahead_of(
        (dot(grad_branch_m, weights[:, OFF_W2 : OFF_W2 + HMLP]) for weights in (own, other)), MLP_AHEAD
    )
    for side, weights in enumerate((own, other)):
        span = slice(side * HMLP, (side + 1) * HMLP)
        grad_acted = next(acting)
        yield
        grad_pre = (grad_acted * take("slope", side)).astype(bf16)
        stash["dg"][rows, span] = grad_pre
        bias("fc1", side * HMLP, grad_pre)
        yield
        part = dot(grad_pre, weights[:, :HMLP], NT)
        grad_input = part if grad_input is None else grad_input + part
        yield
    middle = take("middle")
    normed_m, inv_m = normalize(middle)
    mods_out(3, token_sum(grad_input))
    mods_out(4, token_sum(grad_input * normed_m))
    grad_middle = grad + norm_back(grad_input * (1.0 + mod(4)), normed_m, inv_m)
    yield
    branch_a = take("branch_a")
    mods_out(2, token_sum(grad_middle * branch_a))
    grad_branch_a = (grad_middle * mod(2)).astype(bf16)
    bias("proj", 0, grad_branch_a)
    stash["dya"][rows, :] = grad_branch_a
    yield
    grad_mixed = dot(grad_branch_a, wo[...]).astype(bf16)
    yield
    query, keyed, valued = take("query"), take("keyed"), take("valued")
    scored = ahead_of(
        (dot(keep(grad_mixed[:, pair_span(pair)], head_mask(which)), valued[:, pair_span(pair)], NT)
         for pair in range(HEADS // 2) for which in range(2)), BACK_AHEAD
    )
    grads_q, grads_k, grads_v = [], [], []
    for pair in range(HEADS // 2):
        q_pair, k_pair = query[:, pair_span(pair)], keyed[:, pair_span(pair)]
        grad_q = grad_k = grad_v = None
        for which in range(2):
            mask = head_mask(which)
            grad_probs = next(scored)
            yield
            probs = take("probs", 2 * pair + which)
            row_dot = jnp.sum(grad_probs * probs, -1, keepdims=True)
            grad_scores = (probs * (grad_probs - row_dot)).astype(bf16)
            yield
            part_q = dot(grad_scores, keep(k_pair, mask))
            part_k = dot(grad_scores, keep(q_pair, mask), TN)
            part_v = dot(probs.astype(bf16), keep(grad_mixed[:, pair_span(pair)], mask), TN)
            grad_q = part_q if grad_q is None else grad_q + part_q
            grad_k = part_k if grad_k is None else grad_k + part_k
            grad_v = part_v if grad_v is None else grad_v + part_v
        grads_q.append((grad_q * HD**-0.5).astype(bf16))
        grads_k.append(grad_k.astype(bf16))
        grads_v.append(grad_v.astype(bf16))
    yield
    grad_qkv = jnp.concatenate(grads_q + grads_k + grads_v, 1)
    stash["dqkv"][rows, :] = grad_qkv
    bias("qkv", 0, grad_qkv)
    yield
    grad_input_a = dot(grad_qkv, wqkv[...], NT)
    yield
    normed, inv_a = normalize(x)
    mods_out(0, token_sum(grad_input_a))
    mods_out(1, token_sum(grad_input_a * normed))
    result.append(grad_middle + norm_back(grad_input_a * (1.0 + mod(1)), normed, inv_a))


def weight_grads(input_a, input_m, mixed, acted, stash, cols, rows_out):
    for part in range(3):
        piece = dot(stash["dqkv"][:, part * D : (part + 1) * D], input_a[...], TN)
        for side, out in enumerate(cols):
            for head in range(HEADS // 2):
                start = side * HALF + head * HD
                place = (3 * head + part) * HD
                out[place : place + HD, :] = piece[start : start + HD, :]
    for side, out in enumerate(cols):
        out[QKV_S:, :] = dot(stash["dg"][:, side * HMLP : (side + 1) * HMLP], input_m[...], TN)
    piece = dot(mixed[...], stash["dya"][...], TN)
    for side, out in enumerate(rows_out):
        out[:HALF, :] = piece[side * HALF : (side + 1) * HALF, :]
        out[HALF:, :] = dot(acted[:, side * HMLP : (side + 1) * HMLP], stash["dym"][...], TN)


BIAS = {"qkv": 0, "fc1": 3 * D, "proj": 3 * D + MLP, "fc2": 4 * D + MLP}
BIAS_WIDTH = 5 * D + MLP

PAY_PATCH, PAY_HEAD, PAY_PROJ, PAY_FC2, PAY_BPATCH, PAY_BHEAD, PAY_COND, PAY_BCOL = 0, 16, 32, 34, 36, 37, 38, 52
PAY_ROWS = 64
SMALL_ROWS = PAY_BCOL + 8 - PAY_PROJ


def forward_kernel(xt, mods, wpatch, pos, own, other, bcol_own, bcol_other, b_rep,
                   x0, query, keyed, valued, probs, branch_a, middle, slope, branch_m, mixed, acted,
                   input_a, input_m, x2, wqkv, wo, bqkv, bfc1):
    @pl.when(pl.program_id(0) == 0)
    def _():
        assemble(0, own, other, bcol_own, bcol_other, wqkv, wo, bqkv, bfc1)

    named = dict(query=query, keyed=keyed, valued=valued, mixed=mixed, branch_a=branch_a,
                 middle=middle, branch_m=branch_m, input_a=input_a, input_m=input_m)

    def chain(i):
        def put(name, value, index=None):
            if name == "probs":
                probs[i, index] = value
            elif name == "acted":
                acted[i, :, index * HMLP : (index + 1) * HMLP] = value
            elif name == "slope":
                slope[i, :, index * HMLP : (index + 1) * HMLP] = value
            else:
                named[name][i] = value

        x = dot(xt[i], wpatch[0], TN) + vector(b_rep, START_PATCH) + pos[...]
        x0[i] = x
        result = []
        yield from layer_forward(x, lambda j: mods[i, j : j + 1, :], own, other, wqkv, wo, bqkv[...],
                                 bfc1[...], vector(b_rep, 0), vector(b_rep, START_FC2), put, result)
        x2[i] = result[0]

    run_steps([chain(i) for i in range(xt.shape[0])], LAG)


def diagonal(count):
    down = lax.broadcasted_iota(jnp.int32, (count, count), 0)
    across = lax.broadcasted_iota(jnp.int32, (count, count), 1)
    return down == across


def write_bcol(dbias, side, out, layer):
    pieces = []
    for head in range(HEADS // 2):
        for part in range(3):
            start = part * D + side * HALF + head * HD
            pieces.append(dbias[:, start : start + HD])
    start = 3 * D + side * HMLP
    pieces.append(dbias[:, start : start + HMLP])
    pieces.append(jnp.zeros((1, 4 * D - COL_S), f32))
    line = jnp.concatenate(pieces, 1)
    for row in range(4):
        at = PAY_BCOL + 4 * layer + row
        out[at : at + 1, :] = line[:, row * D : (row + 1) * D]


def middle_kernel(x2, mods, own, other, bcol_own, bcol_other, b_rep, whead, targets,
                  dx, dmods, col_own, col_other, row_own, row_other, dbias, dhead, dbhead, loss,
                  wqkv, wo, bqkv, bfc1, query, keyed, valued, probs, mixed, branch_a, middle, acted,
                  slope, branch_m, input_a, input_m, s_dqkv, s_dg, s_dya, s_dym):
    step = pl.program_id(0)

    @pl.when(step == 0)
    def _():
        assemble(1, own, other, bcol_own, bcol_other, wqkv, wo, bqkv, bfc1)
        dbias[...] = jnp.zeros_like(dbias)
        dhead[...] = jnp.zeros_like(dhead)
        dbhead[...] = jnp.zeros_like(dbhead)
        loss[...] = jnp.zeros_like(loss)

    stacked = dict(mixed=mixed, input_a=input_a, input_m=input_m)
    single = dict(query=query, keyed=keyed, valued=valued, branch_a=branch_a, middle=middle,
                  branch_m=branch_m)
    stash = dict(dqkv=s_dqkv, dg=s_dg, dya=s_dya, dym=s_dym)
    group = x2.shape[0]

    def chain(i):
        rows = pl.ds(pl.multiple_of((step * group + i) * TOK, TOK), TOK)

        def put(name, value, index=None):
            if name == "probs":
                probs[i, index] = value
            elif name == "acted":
                acted[rows, index * HMLP : (index + 1) * HMLP] = value
            elif name == "slope":
                slope[i, :, index * HMLP : (index + 1) * HMLP] = value
            elif name in stacked:
                stacked[name][rows, :] = value
            else:
                single[name][i] = value

        def take(name, index=None):
            if name == "probs":
                return probs[i, index]
            if name == "slope":
                return slope[i, :, index * HMLP : (index + 1) * HMLP]
            return single[name][i]

        def mod(j):
            return mods[i, 6 + j : 7 + j, :]

        def mods_out(j, value):
            dmods[i, j : j + 1, :] = value

        def bias(name, start, value):
            at = BIAS[name] + start
            dbias[:, at : at + value.shape[1]] += token_sum(value.astype(f32))

        result = []
        yield from layer_forward(x2[i], mod, own, other, wqkv, wo, bqkv[...], bfc1[...], vector(b_rep, D),
                                 vector(b_rep, START_FC2 + D), put, result)
        yield
        normed, inv_std = normalize(result[0])
        input_f = (normed * (1.0 + mod(7)) + mod(6)).astype(bf16)
        bhead = jnp.sum(
            jnp.where(diagonal(PV), b_rep[:, START_HEAD : START_HEAD + PV], 0.0), 1, keepdims=True
        )
        yield
        miss = dot(whead[0], input_f, NT) + bhead - targets[i]
        loss[...] += jnp.sum(miss * miss, 0, keepdims=True)
        grad_pred = (2.0 * miss).astype(bf16)
        yield
        dhead[...] += dot(grad_pred, input_f)
        dbhead[...] += jnp.sum(grad_pred.astype(f32), 1, keepdims=True)
        grad_input = dot(grad_pred, whead[0], TN)
        yield
        mods_out(6, token_sum(grad_input))
        mods_out(7, token_sum(grad_input * normed))
        grad = norm_back(grad_input * (1.0 + mod(7)), normed, inv_std)
        result = []
        yield from layer_backward(grad, x2[i], mod, own, other, wqkv, wo, take, rows, stash, mods_out, bias,
                                  result)
        dx[i] = result[0]

    run_steps([chain(i) for i in range(group)], LAG)

    @pl.when(step == pl.num_programs(0) - 1)
    def _():
        weight_grads(input_a, input_m, mixed, acted, stash, (col_own, col_other), (row_own, row_other))


def last_kernel(dx, x0, mods, own, other, bcol_own, bcol_other, b_rep, xt,
                dbias1, dhead, dbhead, loss, dmods1,
                query, keyed, valued, probs, branch_a, middle, slope, branch_m, mixed, acted, input_a, input_m,
                dmods, col_own, col_other, row_own, row_other, pay_own, pay_other,
                wqkv, wo, bqkv, bfc1, a_input_a, a_input_m, a_mixed, a_acted, s_dqkv, s_dg, s_dya, s_dym,
                dbias, sems):
    step = pl.program_id(0)
    pairs = ((input_a, a_input_a), (input_m, a_input_m), (mixed, a_mixed), (acted, a_acted))
    copies = [pltpu.make_async_copy(src, dst, sems.at[i]) for i, (src, dst) in enumerate(pairs)]

    @pl.when(step == 0)
    def _():
        assemble(0, own, other, bcol_own, bcol_other, wqkv, wo, bqkv, bfc1)
        dbias[...] = jnp.zeros_like(dbias)
        pay_own[...] = jnp.zeros_like(pay_own)
        for copy in copies:
            copy.start()

    rows = pl.ds(pl.multiple_of(step * TOK, TOK), TOK)
    single = dict(query=query, keyed=keyed, valued=valued, branch_a=branch_a, middle=middle,
                  branch_m=branch_m)

    def take(name, index=None):
        if name == "probs":
            return probs[0, index]
        if name == "slope":
            return slope[0, :, index * HMLP : (index + 1) * HMLP]
        return single[name][0]

    def mods_out(j, value):
        dmods[0, j : j + 1, :] = value

    def bias(name, start, value):
        at = BIAS[name] + start
        dbias[:, at : at + value.shape[1]] += token_sum(value.astype(f32))

    stash = dict(dqkv=s_dqkv, dg=s_dg, dya=s_dya, dym=s_dym)
    result = []
    run_steps([layer_backward(dx[0], x0[0], lambda j: mods[0, j : j + 1, :], own, other, wqkv, wo,
                              take, rows, stash, mods_out, bias, result)], 0)
    (grad,) = result
    grad = grad.astype(bf16)
    pay_own[PAY_PATCH : PAY_PATCH + PV, :] += dot(xt[0], grad)
    pay_own[PAY_BPATCH : PAY_BPATCH + 1, :] += token_sum(grad.astype(f32))
    dmods[0, 6 : 6 + 8, :] = dmods1[0]
    rounded = dmods[0].astype(bf16).astype(f32)
    dmods[0] = rounded
    pay_own[PAY_COND : PAY_COND + 14, :] += rounded

    @pl.when(step == pl.num_programs(0) - 1)
    def _():
        for copy in copies:
            copy.wait()
        weight_grads(a_input_a, a_input_m, a_mixed, a_acted, stash,
                     (col_own, col_other), (row_own, row_other))
        pay_own[PAY_HEAD : PAY_HEAD + PV, :] = dhead[...]
        for layer, values in enumerate((dbias, dbias1)):
            pay_own[PAY_PROJ + layer : PAY_PROJ + layer + 1, :] = values[:, BIAS["proj"] : BIAS["proj"] + D]
            pay_own[PAY_FC2 + layer : PAY_FC2 + layer + 1, :] = values[:, BIAS["fc2"] : BIAS["fc2"] + D]
        head_line = jnp.sum(jnp.where(diagonal(PV), dbhead[...], 0.0), 0, keepdims=True)
        pay_own[PAY_BHEAD : PAY_BHEAD + 1, :] = jnp.concatenate(
            [head_line, jnp.sum(loss[...], 1, keepdims=True), jnp.zeros((1, D - PV - 1), f32)], 1
        )
        pay_other[...] = pay_own[...]
        for side, out in enumerate((pay_own, pay_other)):
            for layer, values in enumerate((dbias, dbias1)):
                write_bcol(values, side, out, layer)
        for out in (pay_own, pay_other):
            out[PAY_BCOL + 8 :, :] = jnp.zeros((PAY_ROWS - PAY_BCOL - 8, D), f32)


def per_latent(*shape, group=1):
    zeros = (0,) * len(shape)
    return pl.BlockSpec((group,) + shape, lambda n: (n,) + zeros)


def fixed(*shape):
    zeros = (0,) * len(shape)
    return pl.BlockSpec(shape, lambda n: zeros, pipeline_mode=pl.Buffered(1))


def params():
    return pltpu.CompilerParams(dimension_semantics=("arbitrary",), vmem_limit_bytes=62 * 2**20)


SAVED = [
    ("query", (TOK, D), bf16), ("keyed", (TOK, D), bf16), ("valued", (TOK, D), bf16),
    ("probs", (HEADS, TOK, TOK), f32), ("branch_a", (TOK, D), f32), ("middle", (TOK, D), f32),
    ("slope", (TOK, MLP), f32), ("branch_m", (TOK, D), f32), ("mixed", (TOK, D), bf16),
    ("acted", (TOK, MLP), bf16), ("input_a", (TOK, D), bf16), ("input_m", (TOK, D), bf16),
]
GRAD_SHAPES = [(COL_S, D), (COL_S, D), (ROW_S, D), (ROW_S, D)]
WEIGHT_SCRATCH = [pltpu.VMEM((D, 3 * D), bf16), pltpu.VMEM((D, D), bf16),
                  pltpu.VMEM((1, 3 * D), f32), pltpu.VMEM((1, MLP), f32)]


def weight_specs(layer):
    half = pl.BlockSpec((D, GATH), lambda n: (0, layer), pipeline_mode=pl.Buffered(1))
    return [half, half, fixed(L, COL_S), fixed(L, COL_S), fixed(1, NBR)]


def stash_scratch(count):
    rows = count * TOK
    return [pltpu.VMEM((rows, 3 * D), bf16), pltpu.VMEM((rows, MLP), bf16),
            pltpu.VMEM((rows, D), bf16), pltpu.VMEM((rows, D), bf16)]


def cost(flops, nbytes, count):
    return pl.CostEstimate(flops=int(flops * count), bytes_accessed=int(nbytes * count),
                           transcendentals=int(2e6 * count))


def run_forward(xt, mods, full_io, pos, weights):
    count = xt.shape[0]
    outs = [("x0", (TOK, D), f32)] + SAVED + [("x2", (TOK, D), f32)]
    return pl.pallas_call(
        forward_kernel,
        grid=(count // GROUP,),
        in_specs=[per_latent(PV, TOK, group=GROUP), per_latent(14, D, group=GROUP),
                  pl.BlockSpec((1, PV, D), lambda n: (0, 0, 0)), fixed(TOK, D)] + weight_specs(0),
        out_specs=[per_latent(*shape, group=GROUP) for _, shape, _ in outs],
        out_shape=[jax.ShapeDtypeStruct((count,) + shape, kind) for _, shape, kind in outs],
        scratch_shapes=WEIGHT_SCRATCH,
        compiler_params=params(),
        cost_estimate=cost(1.0e9, 6e6, count),
        name="forward_first",
    )(xt, mods, full_io, pos, *weights)


def run_middle(x2, mods, weights, full_io, targets):
    count = x2.shape[0]
    rows = count * TOK
    outs = [((count, TOK, D), per_latent(TOK, D, group=GROUP)), ((count, 8, D), per_latent(8, D, group=GROUP))]
    outs += [(shape, fixed(*shape)) for shape in GRAD_SHAPES]
    outs += [(shape, fixed(*shape)) for shape in ((1, BIAS_WIDTH), (PV, D), (PV, 1), (1, TOK))]
    return pl.pallas_call(
        middle_kernel,
        grid=(count // GROUP,),
        in_specs=[per_latent(TOK, D, group=GROUP), per_latent(14, D, group=GROUP)] + weight_specs(1)
        + [pl.BlockSpec((1, PV, D), lambda n: (1, 0, 0)), per_latent(PV, TOK, group=GROUP)],
        out_specs=[spec for _, spec in outs],
        out_shape=[jax.ShapeDtypeStruct(shape, f32) for shape, _ in outs],
        scratch_shapes=WEIGHT_SCRATCH
        + [pltpu.VMEM((GROUP, TOK, D), bf16)] * 3
        + [pltpu.VMEM((GROUP, HEADS, TOK, TOK), f32), pltpu.VMEM((rows, D), bf16),
           pltpu.VMEM((GROUP, TOK, D), f32), pltpu.VMEM((GROUP, TOK, D), f32), pltpu.VMEM((rows, MLP), bf16),
           pltpu.VMEM((GROUP, TOK, MLP), f32), pltpu.VMEM((GROUP, TOK, D), f32),
           pltpu.VMEM((rows, D), bf16), pltpu.VMEM((rows, D), bf16)]
        + stash_scratch(count),
        compiler_params=params(),
        cost_estimate=cost(3.2e9, 3e6, count),
        name="layer_second",
    )(x2, mods, *weights, full_io, targets)


def run_last(dx, x0, mods, weights, xt, smalls, dmods1, saved):
    count = dx.shape[0]
    rows = count * TOK
    outs = [((count, 14, D), per_latent(14, D))]
    outs += [(shape, fixed(*shape)) for shape in GRAD_SHAPES]
    outs += [(shape, fixed(*shape)) for shape in ((PAY_ROWS, D), (PAY_ROWS, D))]
    return pl.pallas_call(
        last_kernel,
        grid=(count,),
        in_specs=[per_latent(TOK, D), per_latent(TOK, D), per_latent(14, D)] + weight_specs(0)
        + [per_latent(PV, TOK)]
        + [fixed(*shape) for shape in ((1, BIAS_WIDTH), (PV, D), (PV, 1), (1, TOK))] + [per_latent(8, D)]
        + [per_latent(*shape) for _, shape, _ in SAVED[:-4]] + [pl.BlockSpec(memory_space=pl.ANY)] * 4,
        out_specs=[spec for _, spec in outs],
        out_shape=[jax.ShapeDtypeStruct(shape, f32) for shape, _ in outs],
        scratch_shapes=WEIGHT_SCRATCH
        + [pltpu.VMEM((rows, D), bf16)] * 3 + [pltpu.VMEM((rows, MLP), bf16)]
        + stash_scratch(count) + [pltpu.VMEM((1, BIAS_WIDTH), f32), pltpu.SemaphoreType.DMA((4,))],
        compiler_params=params(),
        cost_estimate=cost(2.2e9, 8e6, count),
        name="backward_first",
    )(dx, x0, mods, *weights, xt, *smalls, dmods1, *saved[:-4], *[v.reshape(rows, -1) for v in saved[-4:]])


PACK = 128
WIDE = 3 * D


def split3(values):
    high = values.astype(bf16)
    rest = values - high.astype(f32)
    mid = rest.astype(bf16)
    low = (rest - mid.astype(f32)).astype(bf16)
    return high, mid, low


def narrow_dot(small, big, dims):
    parts = split3(small)
    high, mid, low = split3(big)
    first = dot(jnp.concatenate(parts, 0), high, dims)
    second = dot(jnp.concatenate(parts[:2], 0), mid, dims)
    third = dot(parts[0], low, dims)
    r = small.shape[0]
    return first[:r] + ((first[r : 2 * r] + second[:r]) + (first[2 * r :] + second[r:] + third))


def outer(left, right):
    l1, l2, l3 = split3(left)
    r1, r2, r3 = split3(right)
    return dot(
        jnp.concatenate([l1, l1, l2, l2, l1, l3], 0), jnp.concatenate([r1, r2, r1, r2, r3, r1], 0), TN
    )


PROJECT_STEPS = 2
WIDE_BLOCK = COL_S // PROJECT_STEPS
TALL_BLOCK = ROW_S // PROJECT_STEPS


def project_step(err_col, own_col, got_col, err_row, own_row, got_row, fac_col, fac_row,
                 mat_col, mat_row, left_col, left_row):
    step = pl.program_id(0)
    matrix = err_col[0] + (own_col[...] + got_col[...])
    mat_col[...] = matrix
    part = narrow_dot(fac_col[0], matrix, NN)
    matrix = err_row[0] + (own_row[...] + got_row[...])
    mat_row[...] = matrix
    side = narrow_dot(fac_row[0], matrix, NT)

    @pl.when(step == 0)
    def _():
        left_col[...] = part
        left_row[...] = jnp.zeros_like(left_row)
        left_row[:, :TALL_BLOCK] = side

    @pl.when(step == 1)
    def _():
        left_col[...] += part
        left_row[:, TALL_BLOCK:ROW_S] = side


def project_second_kernel(block, err_col, own_col, got_col, err_row, own_row, got_row, fac_col, fac_row,
                          dmods, full_cond, cond_own,
                          mat_col, mat_row, left_col, left_row, grad_cond, cols_sent):
    project_step(err_col, own_col, got_col, err_row, own_row, got_row, fac_col, fac_row,
                 mat_col, mat_row, left_col, left_row)

    @pl.when(pl.program_id(0) == 0)
    def _():
        n_dp, count = cols_sent.shape[0], cols_sent.shape[1]
        line = jnp.concatenate([dmods[:, j, :] for j in range(14)], 1)
        grad_act = dot(line.astype(bf16), full_cond[...], NT)
        cond = cond_own[...]
        gate = 1.0 / (1.0 + jnp.exp(-cond))
        grad_cond[...] = grad_act * (gate * (1.0 + cond * (1.0 - gate)))
        for j in range(n_dp):
            cols_sent[j] = jnp.concatenate(
                [line[:, j * block : (j + 1) * block], jnp.zeros((count, D - block), f32)], 1
            )


def packed_slots():
    return ["row0", "row1", "col0", "col1", "io0", "io1", "row0", "row1", "row0", "row1"]


def project_first_kernel(err_col, own_col, got_col, err_row, own_row, got_row, fac_col, fac_row,
                         left_col1, left_row1, grad_cond, cols_sent, pay_own, pay_got, err_io, fac_io,
                         mat_col, mat_row, mat_io, sent, left_col, left_row):
    project_step(err_col, own_col, got_col, err_row, own_row, got_row, fac_col, fac_row,
                 mat_col, mat_row, left_col, left_row)

    @pl.when(pl.program_id(0) == PROJECT_STEPS - 1)
    def _():
        n_dp, count = cols_sent.shape[0], cols_sent.shape[1]
        share = PACK // n_dp
        pay = pay_own[...] + pay_got[...]
        left_io = []
        for index in range(2):
            matrix = pay[index * PV : (index + 1) * PV] + err_io[index]
            mat_io[index] = matrix
            left_io.append(dot_full(fac_io[index], matrix))
        sent[:, :count, :] = jnp.broadcast_to(grad_cond[...][None], (n_dp, count, D))
        sent[:, count : 2 * count, :] = cols_sent[...]
        sent[:, 2 * count :, :] = jnp.zeros((n_dp, share, D), f32)
        tall = (left_row, left_row1)
        for column in range(RANK):
            pick = slice(column, column + 1)
            lines = [tall[i % 2][pick, (i // 2) * D : (i // 2 + 1) * D] for i in (0, 1)]
            lines += [left_col[pick, :], left_col1[pick, :], left_io[0][pick], left_io[1][pick]]
            lines += [tall[i % 2][pick, (i // 2) * D : (i // 2 + 1) * D] for i in (2, 3, 4, 5)]
            for extra in range(6):
                at = column * 6 + extra
                if at < SMALL_ROWS:
                    lines.append(pay[PAY_PROJ + at : PAY_PROJ + at + 1])
            for slot, line in enumerate(lines):
                at = column * 16 + slot
                place = 2 * count + at % share
                sent[at // share, place : place + 1, :] = line


def project_specs(layer):
    col_block = pl.BlockSpec((WIDE_BLOCK, D), lambda n: (n, 0))
    row_block = pl.BlockSpec((TALL_BLOCK, D), lambda n: (n, 0))
    ins = [pl.BlockSpec((1, WIDE_BLOCK, D), lambda n: (layer, n, 0)), col_block, col_block,
           pl.BlockSpec((1, TALL_BLOCK, D), lambda n: (layer, n, 0)), row_block, row_block,
           pl.BlockSpec((1, RANK, WIDE_BLOCK), lambda n: (n, 0, 0)),
           pl.BlockSpec((1, RANK, D), lambda n: (layer, 0, 0))]
    return ins, [col_block, row_block]


def steps_of(fac_col):
    return fac_col.reshape(RANK, PROJECT_STEPS, WIDE_BLOCK).transpose(1, 0, 2)


def run_project_second(err_col, grads, err_row, fac_col, fac_row, dmods, full_cond, cond_own, n_dp):
    own_col, got_col, own_row, got_row = grads
    count = dmods.shape[0]
    ins, outs = project_specs(1)
    extra = [(RANK, D), (RANK, WIDE), (count, D), (n_dp, count, D)]
    return pl.pallas_call(
        lambda *refs: project_second_kernel(N_MODS // n_dp, *refs),
        grid=(PROJECT_STEPS,),
        in_specs=ins + [fixed(count, 14, D), fixed(D, N_MODS), fixed(count, D)],
        out_specs=outs + [fixed(*shape) for shape in extra],
        out_shape=[jax.ShapeDtypeStruct(shape, f32) for shape in [(COL_S, D), (ROW_S, D)] + extra],
        compiler_params=params(),
        name="left_second",
    )(err_col, own_col, got_col, err_row, own_row, got_row, steps_of(fac_col[1]), fac_row,
      dmods, full_cond, cond_own)


def run_project_first(err_col, grads, err_row, fac_col, fac_row, left_col1, left_row1, grad_cond, cols_sent,
                      pay_own, pay_got, err_io, fac_io):
    own_col, got_col, own_row, got_row = grads
    n_dp, count = cols_sent.shape[:2]
    ins, outs = project_specs(0)
    extra = [(2, PV, D), (n_dp, 2 * count + PACK // n_dp, D)]
    return pl.pallas_call(
        project_first_kernel,
        grid=(PROJECT_STEPS,),
        in_specs=ins + [fixed(RANK, D), fixed(RANK, WIDE), fixed(count, D), fixed(n_dp, count, D),
                        fixed(PAY_ROWS, D), fixed(PAY_ROWS, D), fixed(2, PV, D), fixed(2, RANK, PV)],
        out_specs=outs + [fixed(*shape) for shape in extra],
        out_shape=[jax.ShapeDtypeStruct(shape, f32) for shape in [(COL_S, D), (ROW_S, D)] + extra],
        scratch_shapes=[pltpu.VMEM((RANK, D), f32), pltpu.VMEM((RANK, WIDE), f32)],
        compiler_params=params(),
        name="left_first",
    )(err_col, own_col, got_col, err_row, own_row, got_row, steps_of(fac_col[0]), fac_row,
      left_col1, left_row1, grad_cond, cols_sent, pay_own, pay_got, err_io, fac_io)


TIME_ROWS = FREQ + D + 8


def modulation_kernel(block, core, got, act_half, features, first, first_act, full_time, labels,
                      cond_mine, cond_their, time_part, table_part):
    n_dp = got.shape[0]
    count = (got.shape[1] - PACK // n_dp) // 2
    half = block // 2
    grad_cond = got[:, :count, :].reshape(n_dp * count, D)
    cols = got[:, count : 2 * count, :].reshape(n_dp * count, D)
    left, right = cols[:, :half].astype(bf16), cols[:, half:block].astype(bf16)
    is_first = core[0] == 0
    grad_left = dot(act_half[...], left, TN)
    grad_right = dot(act_half[...], right, TN)
    cond_mine[...] = jnp.where(is_first, grad_left, grad_right)
    cond_their[...] = jnp.where(is_first, grad_right, grad_left)
    grad_second = grad_cond.astype(bf16)
    gate = 1.0 / (1.0 + jnp.exp(-first[...]))
    slope = gate * (1.0 + first[...] * (1.0 - gate))
    grad_first = (dot(grad_second, full_time[FREQ:, :], NT) * slope).astype(bf16)
    time_part[:FREQ, :] = dot(features[...], grad_first, TN)
    time_part[FREQ : FREQ + D, :] = dot(first_act[...], grad_second, TN)
    time_part[FREQ + D :, :] = jnp.concatenate(
        [token_sum(grad_first.astype(f32)), token_sum(grad_second.astype(f32)), jnp.zeros((6, D), f32)], 0
    )
    onehot = (labels[...] == lax.broadcasted_iota(jnp.int32, (n_dp * count, CLASSES), 1)).astype(f32).astype(bf16)
    high, mid, low = split3(grad_cond)
    table_part[...] = dot(high, onehot, TN) + (dot(mid, onehot, TN) + dot(low, onehot, TN))


def run_modulation(core, got, act_half, features, first, first_act, full_time, labels):
    half = N_MODS // got.shape[0] // 2
    shapes = [(D, half), (D, half), (TIME_ROWS, D), (D, CLASSES)]
    vmem = pl.BlockSpec(memory_space=pltpu.VMEM)
    return pl.pallas_call(
        lambda *refs: modulation_kernel(2 * half, *refs),
        in_specs=[pl.BlockSpec(memory_space=pltpu.SMEM)] + [vmem] * 7,
        out_shape=[jax.ShapeDtypeStruct(shape, f32) for shape in shapes],
        compiler_params=pltpu.CompilerParams(vmem_limit_bytes=62 * 2**20),
        name="modulation_gradients",
    )(core, got, act_half, features, first, first_act, full_time, labels)


COL_ROWS = 4 * RANK
ROW_AT = L * COL_ROWS
IO_AT = ROW_AT + L * RANK
EXTRA_AT = IO_AT + 2 * RANK


def cond_top(rows):
    return -(-((rows + 1) // 2) // 8) * 8


def ortho(packed, left_col, left_row, left_io):
    columns = []
    blank = jnp.zeros((4, D), f32)
    for index in range(RANK):
        block = packed[index]
        column = jnp.concatenate(
            [block[0:6], jnp.concatenate([block[6:8], blank], 0), jnp.concatenate([block[8:10], blank], 0)], 1
        )
        for earlier in columns:
            column = column - jnp.sum(earlier * column, -1, keepdims=True) * earlier
        column = column * lax.rsqrt(jnp.sum(column * column, -1, keepdims=True) + ortho_eps)
        for layer in range(L):
            left_row[layer, index : index + 1, :] = column[layer : layer + 1]
            left_col[layer, index : index + 1, :] = column[2 + layer : 3 + layer, :D]
            left_io[layer, index : index + 1, :] = column[4 + layer : 5 + layer, :D]
        columns.append(column)


def total_squares(values):
    return jnp.sum(values * values, keepdims=True)


def right_kernel(packed, mat_col0, mat_row0, mat_col1, mat_row1, mat_io, cond_own, cond_got, table_own, table_got,
                 sent, left_col, left_row, left_io, table_share, flat):
    ortho(packed, left_col, left_row, left_io)
    for layer, (col, row) in enumerate(((mat_col0, mat_row0), (mat_col1, mat_row1))):
        right = narrow_dot(left_col[layer], col[...], NT)
        for piece in range(4):
            wide = min(D, COL_S - piece * D)
            at = layer * COL_ROWS + piece * RANK
            if wide < D:
                flat[at : at + RANK, :] = jnp.zeros((RANK, D), f32)
            flat[at : at + RANK, :wide] = right[:, piece * D : piece * D + wide]
        at = ROW_AT + layer * RANK
        flat[at : at + RANK, :] = narrow_dot(left_row[layer][:, :ROW_S], row[...], NN)
        at = IO_AT + layer * RANK
        flat[at : at + RANK, :] = jnp.zeros((RANK, D), f32)
        flat[at : at + RANK, :PV] = dot_full(left_io[layer], mat_io[layer], NT)
    cond_grad = cond_own[...] + cond_got[...]
    table = table_own[...] + table_got[...]
    table_share[...] = table
    flat[EXTRA_AT:, :] = jnp.zeros((PACK - EXTRA_AT, D), f32)
    flat[EXTRA_AT : EXTRA_AT + 1, :] = jnp.concatenate(
        [total_squares(cond_grad), total_squares(table), jnp.zeros((1, D - 2), f32)], 1
    )
    n_dp = sent.shape[0]
    share = PACK // n_dp
    rows, half = D // n_dp, cond_grad.shape[1]
    top = cond_top(rows)
    sent[:, :share, :] = flat[...].reshape(n_dp, share, D)
    for j in range(n_dp):
        piece = cond_grad[j * rows : (j + 1) * rows]
        sent[j, share : share + min(top, rows), :half] = piece[:top]
        if rows > top:
            sent[j, share : share + rows - top, half : 2 * half] = piece[top:]


def run_right(n_dp, packed, mats, mat_io, cond_own, cond_got, table_own, table_got):
    shapes = [(n_dp, PACK // n_dp + cond_top(D // n_dp), D), (L, RANK, D), (L, RANK, WIDE), (2, RANK, D),
              table_own.shape]
    return pl.pallas_call(
        right_kernel,
        out_shape=[jax.ShapeDtypeStruct(shape, f32) for shape in shapes],
        scratch_shapes=[pltpu.VMEM((PACK, D), f32)],
        compiler_params=pltpu.CompilerParams(vmem_limit_bytes=62 * 2**20),
        name="right_factors",
    )(packed, *mats, mat_io, cond_own, cond_got, table_own, table_got)


def norm_kernel(packed, left_packed, left_col, left_row, left_io, time_own, time_got,
                right_col, right_row, right_io, parts, brep_grad, bcol_grad):
    for layer in range(L):
        for piece in range(4):
            wide = min(D, COL_S - piece * D)
            at = layer * COL_ROWS + piece * RANK
            right_col[layer, :, piece * D : piece * D + wide] = packed[at : at + RANK, :wide]
        at = ROW_AT + layer * RANK
        right_row[layer] = packed[at : at + RANK, :]
        at = IO_AT + layer * RANK
        right_io[layer] = packed[at : at + RANK, :PV]

    def small(at):
        row = at - PAY_PROJ
        return left_packed[row // 6, 10 + row % 6 : 11 + row % 6, :]

    time_bias = time_own[FREQ + D :, :] + time_got[FREQ + D :, :]
    lines = [small(PAY_PROJ + row) for row in range(4)] + [small(PAY_COND + row) for row in range(14)]
    lines += [time_bias[0:1], time_bias[1:2], small(PAY_BPATCH), small(PAY_BHEAD)[:, :PV]]
    whole = jnp.zeros((1, 1), f32)
    for row, line in enumerate(lines):
        brep_grad[:, row * D : row * D + line.shape[1]] = line
        whole = whole + total_squares(line)
    split = jnp.zeros((1, 1), f32)
    for layer in range(L):
        line = jnp.concatenate([small(PAY_BCOL + 4 * layer + row) for row in range(4)], 1)[:, :COL_S]
        bcol_grad[layer : layer + 1, :] = line
        split = split + total_squares(line)
    whole = whole + total_squares(time_own[: FREQ + D, :] + time_got[: FREQ + D, :])

    def gram(left, right):
        return jnp.sum(dot_full(left, left, NT) * dot_full(right, right, NT), keepdims=True)

    for layer in range(L):
        split = split + gram(left_col[layer], right_col[layer]) + gram(left_row[layer], right_row[layer])
        whole = whole + gram(left_io[layer], right_io[layer])
    sums = packed[EXTRA_AT : EXTRA_AT + 1, :]
    split = split + sums[:, 0:1]
    whole = whole + sums[:, 1:2]
    loss = small(PAY_BHEAD)[:, PV : PV + 1]
    parts[...] = jnp.concatenate([split, whole, loss, jnp.zeros((1, 125), f32)], 1)


def run_norm(packed, left_packed, lefts, time_own, time_got):
    shapes = [(L, RANK, COL_S), (L, RANK, D), (2, RANK, PV), (1, 128), (1, NBR), (L, COL_S)]
    return pl.pallas_call(
        norm_kernel,
        out_shape=[jax.ShapeDtypeStruct(shape, f32) for shape in shapes],
        compiler_params=pltpu.CompilerParams(vmem_limit_bytes=62 * 2**20),
        name="gradient_norm",
    )(packed, left_packed, *lefts, time_own, time_got)


def error_kernel(mat_col0, mat_row0, mat_col1, mat_row1, mat_io, left_col, left_row, left_io,
                 right_col, right_row, right_io, err_col, err_row, err_io):
    for layer, (col, row) in enumerate(((mat_col0, mat_row0), (mat_col1, mat_row1))):
        @pl.when(pl.program_id(0) == layer)
        def _():
            err_col[0] = col[...] - outer(right_col[layer], left_col[layer])
            err_row[0] = row[...] - outer(left_row[layer][:, :ROW_S], right_row[layer])
            err_io[layer] = mat_io[layer] - outer(right_io[layer], left_io[layer])


def run_error(mats, mat_io, lefts, rights):
    return pl.pallas_call(
        error_kernel,
        grid=(L,),
        in_specs=[fixed(*v.shape) for v in (*mats, mat_io, *lefts, *rights)],
        out_specs=[pl.BlockSpec((1, COL_S, D), lambda n: (n, 0, 0)),
                   pl.BlockSpec((1, ROW_S, D), lambda n: (n, 0, 0)), fixed(2, PV, D)],
        out_shape=[jax.ShapeDtypeStruct((L, COL_S, D), f32), jax.ShapeDtypeStruct((L, ROW_S, D), f32),
                   jax.ShapeDtypeStruct((2, PV, D), f32)],
        compiler_params=params(),
        name="next_errors",
    )(*mats, mat_io, *lefts, *rights)


def update_kernel(core, parts, parts_got, left_col, right_col, right_row, left_row, right_io, left_io,
                  cond_own, cond_got, time_grad, table_grad, bcol_grad, brep_grad,
                  w_col, w_row, w_cond, w_time, w_io, w_table, b_col, b_rep,
                  m_col, m_row, m_cond, m_time, m_io, m_table, m_bcol, m_brep,
                  scalars, n_col, n_row, n_cond, n_time, n_io, n_table, n_bcol, n_brep,
                  v_col, v_row, v_cond, v_time, v_io, v_table, v_bcol, v_brep):
    clip_norm = jnp.sqrt(parts[:, 0:1] + parts_got[:, 0:1] + parts[:, 1:2])
    scaling = jnp.minimum(1.0, clip_limit / clip_norm)
    scalars[...] = jnp.concatenate([parts[:, 2:3], clip_norm, jnp.zeros((1, 126), f32)], 1)

    def advance(weight, momentum, gradient):
        moved = momentum_decay * momentum + scaling * gradient
        return weight - learn_rate * moved, moved

    for layer in range(L):
        n_col[layer], v_col[layer] = advance(
            w_col[layer], m_col[layer], outer(left_col[layer], right_col[layer]))
        n_row[layer], v_row[layer] = advance(
            w_row[layer], m_row[layer], outer(right_row[layer], left_row[layer][:, :ROW_S]))
        n_io[layer], v_io[layer] = advance(
            w_io[layer], m_io[layer], outer(right_io[layer], left_io[layer]))
    n_dp = cond_own.shape[0]
    rows = w_cond.shape[0]
    half = N_MODS // n_dp // 2
    top = cond_top(rows)
    share = cond_own.shape[1] - top
    is_first = core[0] == 0
    pieces = []
    for j in range(n_dp):
        mine, theirs = cond_own[j, share:, :], cond_got[j]
        for pair in ((mine, theirs), (theirs, mine)):
            block = jnp.where(is_first, pair[0], pair[1])
            if rows > top:
                block = jnp.concatenate([block[:top, :half], block[: rows - top, half : 2 * half]], 0)
            else:
                block = block[:rows, :half]
            pieces.append(block)
    n_cond[...], v_cond[...] = advance(w_cond[...], m_cond[...], jnp.concatenate(pieces, 1))
    n_time[...], v_time[...] = advance(w_time[...], m_time[...], time_grad[...])
    n_table[...], v_table[...] = advance(w_table[...], m_table[...], table_grad[...])
    n_bcol[...], v_bcol[...] = advance(b_col[...], m_bcol[...], bcol_grad[...])
    n_brep[...], v_brep[...] = advance(b_rep[...], m_brep[...], brep_grad[...])


def run_update(core, grads, weights, momenta):
    vmem = pl.BlockSpec(memory_space=pltpu.VMEM)
    shapes = [(1, 128)] + [v.shape for v in weights] * 2
    return pl.pallas_call(
        update_kernel,
        in_specs=[pl.BlockSpec(memory_space=pltpu.SMEM)] + [vmem] * (len(grads) + 2 * len(weights)),
        out_shape=[jax.ShapeDtypeStruct(shape, f32) for shape in shapes],
        compiler_params=pltpu.CompilerParams(vmem_limit_bytes=62 * 2**20),
        name="weight_update",
    )(core, *grads, *weights, *momenta)


def swap(values):
    return lax.ppermute(values, "tensor", [(0, 1), (1, 0)])


def trade(chunks):
    return lax.all_to_all(chunks, "dp", 0, 0, tiled=True)


def spread(values):
    return trade(jnp.broadcast_to(values[None], (lax.axis_size("dp"),) + values.shape))


def exact_parts(values):
    high = lax.reduce_precision(values, 8, 7)
    mid = lax.reduce_precision(values - high, 8, 7)
    return [part.astype(bf16) for part in (high, mid, (values - high) - mid)]


def on_device(
    latents, gauss_noise, time_steps, labels, targets,
    w_col, w_row, w_cond, w_time, w_io, class_table, b_col, b_rep,
    mom_col, mom_row, mom_cond, mom_time, mom_io, mom_table, mom_bcol, mom_brep,
    err_col, err_row, err_io, fac_col, fac_row, fac_io,
):
    n_dp = lax.axis_size("dp")
    index_dp = lax.axis_index("dp")
    index_t = lax.axis_index("tensor")
    core = index_t.astype(jnp.int32).reshape(1)
    first_core = index_t == 0
    n_all = labels.shape[0]
    per_dp = latents.shape[0]
    count = per_dp // 2
    rows = w_col.shape[1]

    def flip(values):
        return values.transpose(0, 2, 1)

    def halves(mine, theirs, axis):
        pair = jnp.stack([mine, theirs], axis)
        return jnp.where(first_core, pair, jnp.flip(pair, axis))

    row_sh = flip(w_row)
    shard = jnp.concatenate(
        [piece[layer] for layer in range(L)
         for piece in (w_col[:, :, QKV_S:], row_sh[:, :, HALF:], w_col[:, :, :QKV_S], row_sh[:, :, :HALF])], 1
    ).astype(bf16)
    full = lax.all_gather(shard, ("dp", "tensor"))

    block = N_MODS // n_dp
    half_block = block // 2
    classes = jnp.arange(CLASSES, dtype=jnp.int32)
    onehot_t = classes[:, None] == labels[None, :]
    looked = dot(class_table.astype(bf16), onehot_t.astype(bf16), TN).astype(bf16)
    time_rows = w_time.shape[0]
    sizes = [rows * n_all, time_rows * D, 2 * PV * rows, 3 * per_dp]
    wide = -(-sum(sizes) // 256) * 128
    common = jnp.concatenate(
        [part.reshape(-1) for part in
         (looked, w_time.astype(bf16), flip(w_io).astype(bf16), *exact_parts(time_steps))]
    )
    common = jnp.pad(common, (0, 2 * wide - common.shape[0]))
    common = lax.dynamic_slice_in_dim(common.reshape(2, wide), index_t, 1, 0)
    cond_bf = w_cond.astype(bf16).reshape(rows, n_dp, 2, half_block)
    cond_mine = lax.dynamic_slice_in_dim(cond_bf, index_t, 1, 2)[:, :, 0].transpose(1, 0, 2)
    sent = jnp.concatenate(
        [jnp.broadcast_to(common, (n_dp, wide)), cond_mine.reshape(n_dp, rows * half_block)], 1
    )
    got = trade(sent)
    cond_cols = got[:, wide:].reshape(D, half_block)
    mine = got[:, :wide]
    common = halves(mine, swap(mine), 1).reshape(n_dp, 2 * wide)
    ends = np.cumsum([0] + sizes)
    looked = common[:, : ends[1]].reshape(D, n_all).T
    full_time = common[:, ends[1] : ends[2]].reshape(FREQ + D, D)
    full_io = flip(common[:, ends[2] : ends[3]].reshape(n_dp, 2 * PV, rows).transpose(1, 0, 2).reshape(2, PV, D).transpose(0, 2, 1))
    steps_all = jnp.sum(common[:, ends[3] : ends[4]].reshape(n_dp, 3, per_dp).astype(f32), 1).reshape(n_all)

    features = frequency_features(steps_all).astype(bf16)
    first = dot(features, full_time[:FREQ]) + b_rep[START_FIRST:START_SECOND]
    first_act = jax.nn.silu(first).astype(bf16)
    second = dot(first_act, full_time[FREQ:]) + b_rep[START_SECOND:START_PATCH]
    cond = second + looked.astype(f32)
    cond_act = jax.nn.silu(cond).astype(bf16)
    mods = dot(cond_act, cond_cols).reshape(n_dp * 2, count, half_block)
    mods = lax.all_to_all(mods, ("dp", "tensor"), 0, 0, tiled=True)
    mods = mods.transpose(1, 0, 2).reshape(count, N_MODS)
    mods = (mods + b_rep[START_COND:START_FIRST]).reshape(count, 14, D)
    full, mods = lax.optimization_barrier((full, mods))
    full = full.reshape(n_dp, 2, rows, L * GATH)

    def half_of(values):
        split = values.reshape((n_dp, 2, count) + values.shape[1:])
        return lax.dynamic_slice_in_dim(split, index_t, 1, 1).reshape((n_dp * count,) + values.shape[1:])

    halves_of = [half_of(v) for v in (cond_act, features, first, first_act)]
    labels_half = half_of(labels)[:, None]
    cond_own = lax.dynamic_slice_in_dim(cond, (index_dp * 2 + index_t) * count, count, 0)

    def mine_of(values):
        return lax.dynamic_slice_in_dim(values, index_t * count, count, 0)

    steps_own = mine_of(time_steps)[:, None, None]
    xt = (
        (1.0 - steps_own) * flip(mine_of(latents)) + steps_own * flip(mine_of(gauss_noise))
    ).astype(bf16)
    b_line = b_rep[None]
    own = lax.dynamic_slice_in_dim(full, index_t, 1, 1).reshape(D, L * GATH)
    other = lax.dynamic_slice_in_dim(full, 1 - index_t, 1, 1).reshape(D, L * GATH)
    weights = (own, other, b_col, swap(b_col), b_line)
    x0, *saved, x2 = run_forward(xt, mods, full_io, jnp.asarray(position_table()), weights)
    x2, late_cond = lax.optimization_barrier((x2, w_cond))
    full_cond = lax.all_gather(late_cond.astype(bf16), "dp", axis=0, tiled=True)
    dx, dmods1, col_own1, col_oth1, row_own1, row_oth1, *smalls = run_middle(
        x2, mods, weights, full_io, flip(mine_of(targets))
    )
    grads1 = (col_own1, swap(col_oth1), row_own1, swap(row_oth1))
    dmods, col_own0, col_oth0, row_own0, row_oth0, pay_own, pay_oth = run_last(
        dx, x0, mods, weights, xt, smalls, dmods1, saved
    )
    grads0 = (col_own0, swap(col_oth0), row_own0, swap(row_oth0))
    pay_got = swap(pay_oth)

    err_col_t, err_io_t = flip(err_col), flip(err_io)
    fac_col_t, fac_row_t, fac_io_t = flip(fac_col), flip(fac_row), flip(fac_io)
    mat_col1, mat_row1, left_col1, left_row1, grad_cond, cols_sent = run_project_second(
        err_col_t, grads1, err_row, fac_col_t, fac_row_t, dmods, full_cond, cond_own, n_dp
    )
    mat_col0, mat_row0, mat_io, sent = run_project_first(
        err_col_t, grads0, err_row, fac_col_t, fac_row_t, left_col1, left_row1, grad_cond, cols_sent,
        pay_own, pay_got, err_io_t, fac_io_t
    )
    mats = (mat_col0, mat_row0, mat_col1, mat_row1)
    got = trade(sent)
    left_packed = spread(jnp.sum(got[:, 2 * count :], 0)).reshape(RANK, 16, D)

    cond_mine, cond_their, time_own, table_part = run_modulation(core, got, *halves_of, full_time, labels_half)
    cond_got, time_got = swap(cond_their), swap(time_own)
    table_own = lax.dynamic_slice_in_dim(table_part, index_dp * rows, rows, 0)
    table_got = swap(table_own)

    sent, left_col, left_row, left_io, table_share = run_right(
        n_dp, left_packed, mats, mat_io, cond_mine, cond_got, table_own, table_got
    )
    share = PACK // n_dp
    got = trade(sent)
    packed = spread(jnp.sum(got[:, :share], 0)).reshape(PACK, D)
    cond_rows_got = swap(got[:, share:])
    lefts = (left_col, left_row, left_io)
    right_col, right_row, right_io, parts, brep_grad, bcol_grad = run_norm(
        packed, left_packed, lefts, time_own, time_got
    )
    parts_got = swap(parts)
    next_err_col, next_err_row, next_err_io = run_error(mats, mat_io, lefts, (right_col, right_row, right_io))

    def mine_cols(values):
        return lax.dynamic_slice_in_dim(values, index_dp * rows, rows, 2)

    time_at = index_dp * time_rows
    time_grad = (
        lax.dynamic_slice_in_dim(time_own, time_at, time_rows, 0)
        + lax.dynamic_slice_in_dim(time_got, time_at, time_rows, 0)
    )
    olds = (w_col, flip(w_row), w_cond, w_time, flip(w_io), class_table.T, b_col, b_line)
    momenta = (mom_col, flip(mom_row), mom_cond, mom_time, flip(mom_io), mom_table.T, mom_bcol, mom_brep[None])
    scalars, *new = run_update(
        core,
        (parts, parts_got, mine_cols(left_col), right_col, mine_cols(right_row), left_row, right_io,
         mine_cols(left_io), got, cond_rows_got, time_grad, table_share, bcol_grad, brep_grad),
        olds, momenta,
    )

    def outward(col, row, cond, time, io, table, bcol, brep):
        return (col, flip(row), cond, time, flip(io), table.T, bcol, brep[0])

    return (
        scalars[0, 0], scalars[0, 1], *outward(*new[:8]), *outward(*new[8:]),
        flip(next_err_col), next_err_row, flip(next_err_io), flip(right_col), flip(right_row), flip(right_io),
    )


def solution(mesh):
    weights = (
        P(None, "dp", "tensor"), P(None, "tensor", "dp"), P("dp", None), P("dp", None),
        P(None, "dp", None), P(None, "dp"), P(None, "tensor"), P(),
    )
    errors = (P("dp", None, "tensor"), P("dp", "tensor", None), P("dp", None, None))
    factors = (P(None, "tensor", None), P(None, "tensor", None), P())
    rows = P("dp", None, None)
    return jax.shard_map(
        on_device,
        mesh=mesh,
        in_specs=(rows, rows, P("dp"), P(), rows) + weights + weights + errors + factors,
        out_specs=(P(), P()) + weights + weights + errors + factors,
        check_vma=False,
    )
```

```python
import jax
import jax.numpy as jnp
import numpy as np
from jax import lax
from jax.experimental import pallas as pl
from jax.experimental.pallas import tpu as pltpu
from jax.sharding import PartitionSpec as P

D = 384
HEADS = 6
HD = 64
MLP = 1536
NBR = 8080
CLASSES = 1000
FREQ = 256
PV = 16
GRID = 16
L = 2
TOK = 256
RANK = 8
GROUP = 2
AHEAD, MLP_AHEAD, BACK_AHEAD = 2, 2, 3
LAG = 1

norm_eps = 1e-06
ortho_eps = 1e-06
clip_limit = 1.0
momentum_decay = 0.9
learn_rate = 4.0

HALF = D // 2
HMLP = MLP // 2
QKV_S = 3 * HALF
COL_S = QKV_S + HMLP
ROW_S = HALF + HMLP
OFF_W2 = HMLP
OFF_Q = 2 * HMLP
GATH = 2 * HMLP + 4 * HALF

f32 = jnp.float32
bf16 = jnp.bfloat16
highest = lax.Precision.HIGHEST
NN = (((1,), (0,)), ((), ()))
NT = (((1,), (1,)), ((), ()))
TN = (((0,), (0,)), ((), ()))


def dot(left, right, dims=NN):
    return lax.dot_general(left, right, dims, preferred_element_type=f32)


def dot_full(left, right, dims=NN):
    return lax.dot_general(left, right, dims, precision=highest, preferred_element_type=f32)


def position_table():
    quarter = D // 4
    omega = 1.0 / 10000.0 ** (np.arange(quarter, dtype=np.float32) / quarter)
    index = np.arange(TOK)
    across = (index % GRID).astype(np.float32)[:, None] * omega[None, :].astype(np.float32)
    down = (index // GRID).astype(np.float32)[:, None] * omega[None, :].astype(np.float32)
    table = np.concatenate([np.sin(across), np.cos(across), np.sin(down), np.cos(down)], 1)
    return table.astype(np.float32)


def frequency_features(steps):
    half = FREQ // 2
    rates = jnp.exp(-jnp.log(10000.0) * jnp.arange(half, dtype=f32) / half)
    angles = steps[:, None] * rates[None, :]
    return jnp.concatenate([jnp.cos(angles), jnp.sin(angles)], 1)


def normalize(values):
    centered = values - jnp.mean(values, -1, keepdims=True)
    inv_std = lax.rsqrt(jnp.mean(centered * centered, -1, keepdims=True) + norm_eps)
    return centered * inv_std, inv_std


def norm_back(grad, normed, inv_std):
    mean_grad = jnp.mean(grad, -1, keepdims=True)
    mean_mixed = jnp.mean(grad * normed, -1, keepdims=True)
    return inv_std * (grad - mean_grad - normed * mean_mixed)


def token_sum(values):
    return jnp.sum(values, 0, keepdims=True)


START_FC2 = L * D
START_COND = 2 * L * D
N_MODS = (6 * L + 2) * D
START_FIRST = START_COND + N_MODS
START_SECOND = START_FIRST + D
START_PATCH = START_FIRST + 2 * D
START_HEAD = START_FIRST + 3 * D


def assemble(layer, own, other, bcol_own, bcol_other, wqkv, wo, bqkv, bfc1):
    for side, (weights, bias) in enumerate(((own, bcol_own), (other, bcol_other))):
        for head in range(HEADS // 2):
            for part in range(3):
                at = (3 * head + part) * HD
                to = part * D + side * HALF + head * HD
                wqkv[:, to : to + HD] = weights[:, OFF_Q + at : OFF_Q + at + HD]
                bqkv[:, to : to + HD] = bias[layer : layer + 1, at : at + HD]
        wo[:, side * HALF : (side + 1) * HALF] = weights[:, OFF_Q + QKV_S :]
        bfc1[:, side * HMLP : (side + 1) * HMLP] = bias[layer : layer + 1, QKV_S:]


def vector(b_rep, at):
    return b_rep[:, at : at + D]


def head_mask(which):
    lane = lax.broadcasted_iota(jnp.int32, (1, 2 * HD), 1)
    return (lane < HD) if which == 0 else (lane >= HD)


def keep(values, mask):
    return jnp.where(mask, values, jnp.zeros_like(values))


def gelu_parts(pre):
    squared = pre * pre
    coef = np.float32(np.sqrt(2.0 / np.pi))
    tanh = jnp.tanh(pre * (coef + np.float32(coef * 0.044715) * squared))
    half = 0.5 * (1.0 + tanh)
    slope = half + (0.5 * pre) * (1.0 - tanh * tanh) * (
        coef + np.float32(3.0 * 0.044715 * coef) * squared
    )
    return (pre * half).astype(bf16), slope


def ahead_of(products, depth):
    waiting = [next(products) for _ in range(depth)]
    while waiting:
        ready = waiting.pop(0)
        following = next(products, None)
        if following is not None:
            waiting.append(following)
        yield ready


def run_steps(chains, lag):
    waits = [lag * i for i in range(len(chains))]
    live = dict(enumerate(chains))
    while live:
        for i in list(live):
            if waits[i] > 0:
                waits[i] -= 1
            elif next(live[i], 1) is not None:
                del live[i]


def pair_span(pair):
    return slice(pair * 2 * HD, (pair + 1) * 2 * HD)


def layer_forward(x, mod, own, other, wqkv, wo, bqkv, bfc1, bproj, bfc2, put, result):
    normed, _ = normalize(x)
    input_a = (normed * (1.0 + mod(1)) + mod(0)).astype(bf16)
    put("input_a", input_a)
    yield
    thirds = []
    for part in range(3):
        span = slice(part * D, (part + 1) * D)
        value = (dot(input_a, wqkv[:, span]) + bqkv[:, span]).astype(bf16)
        if part == 0:
            value = value * jnp.asarray(HD**-0.5, bf16)
        put(("query", "keyed", "valued")[part], value)
        thirds.append(value)
        yield
    query, keyed, valued = thirds
    scored = ahead_of(
        (dot(keep(query[:, pair_span(pair)], head_mask(which)), keyed[:, pair_span(pair)], NT)
         for pair in range(HEADS // 2) for which in range(2)), AHEAD
    )
    pieces = []
    for pair in range(HEADS // 2):
        total = None
        for which in range(2):
            scores = next(scored)
            yield
            expo = jnp.exp(scores - jnp.max(scores, -1, keepdims=True))
            probs = expo * (1.0 / jnp.sum(expo, -1, keepdims=True))
            put("probs", probs, 2 * pair + which)
            yield
            mixed = dot(probs.astype(bf16), keep(valued[:, pair_span(pair)], head_mask(which)))
            total = mixed if total is None else total + mixed
        pieces.append(total.astype(bf16))
    mixed = jnp.concatenate(pieces, 1)
    put("mixed", mixed)
    yield
    branch_a = dot(mixed, wo[...], NT) + bproj
    put("branch_a", branch_a)
    middle = x + mod(2) * branch_a
    put("middle", middle)
    yield
    normed_m, _ = normalize(middle)
    input_m = (normed_m * (1.0 + mod(4)) + mod(3)).astype(bf16)
    put("input_m", input_m)
    yield
    branch_m = bfc2
    for side, weights in enumerate((own, other)):
        pre = dot(input_m, weights[:, :HMLP]) + bfc1[:, side * HMLP : (side + 1) * HMLP]
        yield
        acted, slope = gelu_parts(pre)
        put("acted", acted, side)
        put("slope", slope, side)
        yield
        branch_m = branch_m + dot(acted, weights[:, OFF_W2 : OFF_W2 + HMLP], NT)
        yield
    put("branch_m", branch_m)
    result.append(middle + mod(5) * branch_m)


def layer_backward(grad, x, mod, own, other, wqkv, wo, take, rows, stash, mods_out, bias, result, inputs=None):
    branch_m = take("branch_m")
    mods_out(5, token_sum(grad * branch_m))
    grad_branch_m = (grad * mod(5)).astype(bf16)
    bias("fc2", 0, grad_branch_m)
    stash["dym"][rows, :] = grad_branch_m
    yield
    grad_input = None
    acting = ahead_of(
        (dot(grad_branch_m, weights[:, OFF_W2 : OFF_W2 + HMLP]) for weights in (own, other)), MLP_AHEAD
    )
    for side, weights in enumerate((own, other)):
        span = slice(side * HMLP, (side + 1) * HMLP)
        grad_acted = next(acting)
        yield
        grad_pre = (grad_acted * take("slope", side)).astype(bf16)
        stash["dg"][rows, span] = grad_pre
        bias("fc1", side * HMLP, grad_pre)
        yield
        part = dot(grad_pre, weights[:, :HMLP], NT)
        grad_input = part if grad_input is None else grad_input + part
        yield
    middle = take("middle")
    normed_m, inv_m = normalize(middle)
    if inputs is not None:
        inputs[1][rows, :] = (normed_m * (1.0 + mod(4)) + mod(3)).astype(bf16)
    mods_out(3, token_sum(grad_input))
    mods_out(4, token_sum(grad_input * normed_m))
    grad_middle = grad + norm_back(grad_input * (1.0 + mod(4)), normed_m, inv_m)
    yield
    branch_a = take("branch_a")
    mods_out(2, token_sum(grad_middle * branch_a))
    grad_branch_a = (grad_middle * mod(2)).astype(bf16)
    bias("proj", 0, grad_branch_a)
    stash["dya"][rows, :] = grad_branch_a
    yield
    grad_mixed = dot(grad_branch_a, wo[...]).astype(bf16)
    yield
    query, keyed, valued = take("query"), take("keyed"), take("valued")
    scored = ahead_of(
        (dot(keep(grad_mixed[:, pair_span(pair)], head_mask(which)), valued[:, pair_span(pair)], NT)
         for pair in range(HEADS // 2) for which in range(2)), BACK_AHEAD
    )
    grads_q, grads_k, grads_v = [], [], []
    for pair in range(HEADS // 2):
        q_pair, k_pair = query[:, pair_span(pair)], keyed[:, pair_span(pair)]
        grad_q = grad_k = grad_v = None
        for which in range(2):
            mask = head_mask(which)
            grad_probs = next(scored)
            yield
            probs = take("probs", 2 * pair + which)
            row_dot = jnp.sum(grad_probs * probs, -1, keepdims=True)
            grad_scores = (probs * (grad_probs - row_dot)).astype(bf16)
            yield
            part_q = dot(grad_scores, keep(k_pair, mask))
            part_k = dot(grad_scores, keep(q_pair, mask), TN)
            part_v = dot(probs.astype(bf16), keep(grad_mixed[:, pair_span(pair)], mask), TN)
            grad_q = part_q if grad_q is None else grad_q + part_q
            grad_k = part_k if grad_k is None else grad_k + part_k
            grad_v = part_v if grad_v is None else grad_v + part_v
        grads_q.append((grad_q * HD**-0.5).astype(bf16))
        grads_k.append(grad_k.astype(bf16))
        grads_v.append(grad_v.astype(bf16))
    yield
    grad_qkv = jnp.concatenate(grads_q + grads_k + grads_v, 1)
    stash["dqkv"][rows, :] = grad_qkv
    bias("qkv", 0, grad_qkv)
    yield
    grad_input_a = dot(grad_qkv, wqkv[...], NT)
    yield
    normed, inv_a = normalize(x)
    if inputs is not None:
        inputs[0][rows, :] = (normed * (1.0 + mod(1)) + mod(0)).astype(bf16)
    mods_out(0, token_sum(grad_input_a))
    mods_out(1, token_sum(grad_input_a * normed))
    result.append(grad_middle + norm_back(grad_input_a * (1.0 + mod(1)), normed, inv_a))


def weight_grads(input_a, input_m, mixed, acted, stash, places, outs, sems, fills):
    def add(side, start, value):
        rows = slice(start, start + value.shape[0])
        places[side][rows, :] = value if side else places[side][rows, :] + value

    for copy in fills:
        copy.wait()
    copies = []

    def send(side, start, stop):
        rows = pl.ds(start, stop - start)
        copy = pltpu.make_async_copy(places[side].at[rows, :], outs[side].at[rows, :], sems.at[len(copies)])
        copy.start()
        copies.append(copy)

    for part in range(3):
        piece = dot(stash["dqkv"][:, part * D : (part + 1) * D], input_a[...], TN)
        for side in range(2):
            for head in range(HEADS // 2):
                start = side * HALF + head * HD
                place = (3 * head + part) * HD
                add(side, place, piece[start : start + HD, :])
    for side in (1, 0):
        send(side, 0, QKV_S)
    for side in (1, 0):
        add(side, QKV_S, dot(stash["dg"][:, side * HMLP : (side + 1) * HMLP], input_m[...], TN))
        send(side, QKV_S, COL_S)
    for side in (1, 0):
        add(side, COL_S + HALF, dot(acted[:, side * HMLP : (side + 1) * HMLP], stash["dym"][...], TN))
        send(side, COL_S + HALF, BOTH)
    piece = dot(mixed[...], stash["dya"][...], TN)
    for side in (1, 0):
        add(side, COL_S, piece[side * HALF : (side + 1) * HALF, :])
        send(side, COL_S, COL_S + HALF)
    for copy in copies:
        copy.wait()


def error_fills(layer, err_col, err_row, place, sems):
    return [pltpu.make_async_copy(err_col.at[layer], place.at[pl.ds(0, COL_S), :], sems.at[0]),
            pltpu.make_async_copy(err_row.at[layer], place.at[pl.ds(COL_S, ROW_S), :], sems.at[1])]


BIAS = {"qkv": 0, "fc1": 3 * D, "proj": 3 * D + MLP, "fc2": 4 * D + MLP}
BIAS_WIDTH = 5 * D + MLP

PAY_PATCH, PAY_HEAD, PAY_PROJ, PAY_FC2, PAY_BPATCH, PAY_BHEAD, PAY_COND, PAY_BCOL = 0, 16, 32, 34, 36, 37, 38, 52
PAY_ROWS = 64
SMALL_ROWS = PAY_BCOL + 8 - PAY_PROJ


def forward_kernel(xt, mods, wpatch, pos, own, other, bcol_own, bcol_other, b_rep,
                   query, keyed, valued, probs, branch_a, middle, slope, branch_m, mixed, acted,
                   x2, wqkv, wo, bqkv, bfc1):
    @pl.when(pl.program_id(0) == 0)
    def _():
        assemble(0, own, other, bcol_own, bcol_other, wqkv, wo, bqkv, bfc1)

    named = dict(query=query, keyed=keyed, valued=valued, mixed=mixed, branch_a=branch_a,
                 middle=middle, branch_m=branch_m)

    def chain(i):
        def put(name, value, index=None):
            if name in ("input_a", "input_m"):
                return
            if name == "probs":
                probs[i, index] = value
            elif name == "acted":
                acted[i, :, index * HMLP : (index + 1) * HMLP] = value
            elif name == "slope":
                slope[i, :, index * HMLP : (index + 1) * HMLP] = value
            else:
                named[name][i] = value

        x = dot(xt[i], wpatch[0], TN) + vector(b_rep, START_PATCH) + pos[...]
        result = []
        yield from layer_forward(x, lambda j: mods[i, j : j + 1, :], own, other, wqkv, wo, bqkv[...],
                                 bfc1[...], vector(b_rep, 0), vector(b_rep, START_FC2), put, result)
        x2[i] = result[0]

    run_steps([chain(i) for i in range(xt.shape[0])], LAG)


def diagonal(count):
    down = lax.broadcasted_iota(jnp.int32, (count, count), 0)
    across = lax.broadcasted_iota(jnp.int32, (count, count), 1)
    return down == across


def write_bcol(dbias, side, out, layer):
    pieces = []
    for head in range(HEADS // 2):
        for part in range(3):
            start = part * D + side * HALF + head * HD
            pieces.append(dbias[:, start : start + HD])
    start = 3 * D + side * HMLP
    pieces.append(dbias[:, start : start + HMLP])
    pieces.append(jnp.zeros((1, 4 * D - COL_S), f32))
    line = jnp.concatenate(pieces, 1)
    for row in range(4):
        at = PAY_BCOL + 4 * layer + row
        out[at : at + 1, :] = line[:, row * D : (row + 1) * D]


def middle_kernel(x2, mods, own, other, bcol_own, bcol_other, b_rep, whead, targets, err_col, err_row,
                  dx, dmods, grad_own, grad_other, dbias, dhead, dbhead, loss,
                  wqkv, wo, bqkv, bfc1, query, keyed, valued, probs, mixed, branch_a, middle, acted,
                  slope, branch_m, input_a, input_m, s_dqkv, s_dg, s_dya, s_dym, place_own, place_other,
                  out_sems, fill_sems):
    step = pl.program_id(0)
    fills = error_fills(1, err_col, err_row, place_own, fill_sems)

    @pl.when(step == 0)
    def _():
        for copy in fills:
            copy.start()
        assemble(1, own, other, bcol_own, bcol_other, wqkv, wo, bqkv, bfc1)
        dbias[...] = jnp.zeros_like(dbias)
        dhead[...] = jnp.zeros_like(dhead)
        dbhead[...] = jnp.zeros_like(dbhead)
        loss[...] = jnp.zeros_like(loss)

    stacked = dict(mixed=mixed, input_a=input_a, input_m=input_m)
    single = dict(query=query, keyed=keyed, valued=valued, branch_a=branch_a, middle=middle,
                  branch_m=branch_m)
    stash = dict(dqkv=s_dqkv, dg=s_dg, dya=s_dya, dym=s_dym)
    group = x2.shape[0]

    def chain(i):
        rows = pl.ds(pl.multiple_of((step * group + i) * TOK, TOK), TOK)

        def put(name, value, index=None):
            if name == "probs":
                probs[i, index] = value
            elif name == "acted":
                acted[rows, index * HMLP : (index + 1) * HMLP] = value
            elif name == "slope":
                slope[i, :, index * HMLP : (index + 1) * HMLP] = value
            elif name in stacked:
                stacked[name][rows, :] = value
            else:
                single[name][i] = value

        def take(name, index=None):
            if name == "probs":
                return probs[i, index]
            if name == "slope":
                return slope[i, :, index * HMLP : (index + 1) * HMLP]
            return single[name][i]

        def mod(j):
            return mods[i, 6 + j : 7 + j, :]

        def mods_out(j, value):
            dmods[i, j : j + 1, :] = value

        def bias(name, start, value):
            at = BIAS[name] + start
            dbias[:, at : at + value.shape[1]] += token_sum(value.astype(f32))

        result = []
        yield from layer_forward(x2[i], mod, own, other, wqkv, wo, bqkv[...], bfc1[...], vector(b_rep, D),
                                 vector(b_rep, START_FC2 + D), put, result)
        yield
        normed, inv_std = normalize(result[0])
        input_f = (normed * (1.0 + mod(7)) + mod(6)).astype(bf16)
        bhead = jnp.sum(
            jnp.where(diagonal(PV), b_rep[:, START_HEAD : START_HEAD + PV], 0.0), 1, keepdims=True
        )
        yield
        miss = dot(whead[0], input_f, NT) + bhead - targets[i]
        loss[...] += jnp.sum(miss * miss, 0, keepdims=True)
        grad_pred = (2.0 * miss).astype(bf16)
        yield
        dhead[...] += dot(grad_pred, input_f)
        dbhead[...] += jnp.sum(grad_pred.astype(f32), 1, keepdims=True)
        grad_input = dot(grad_pred, whead[0], TN)
        yield
        mods_out(6, token_sum(grad_input))
        mods_out(7, token_sum(grad_input * normed))
        grad = norm_back(grad_input * (1.0 + mod(7)), normed, inv_std)
        result = []
        yield from layer_backward(grad, x2[i], mod, own, other, wqkv, wo, take, rows, stash, mods_out, bias,
                                  result)
        dx[i] = result[0]

    run_steps([chain(i) for i in range(group)], LAG)

    @pl.when(step == pl.num_programs(0) - 1)
    def _():
        weight_grads(input_a, input_m, mixed, acted, stash, (place_own, place_other),
                     (grad_own, grad_other), out_sems, fills)


def last_kernel(dx, mods, own, other, bcol_own, bcol_other, b_rep, xt, wpatch, pos,
                dbias1, dhead, dbhead, loss, dmods1, err_col, err_row,
                query, keyed, valued, probs, branch_a, middle, slope, branch_m, mixed, acted,
                dmods, grad_own, grad_other, pay_own, pay_other,
                wqkv, wo, bqkv, bfc1, a_input_a, a_input_m, a_mixed, a_acted, s_dqkv, s_dg, s_dya, s_dym,
                dbias, sems, place_own, place_other, out_sems, fill_sems):
    step = pl.program_id(0)
    pairs = ((mixed, a_mixed), (acted, a_acted))
    copies = [pltpu.make_async_copy(src, dst, sems.at[i]) for i, (src, dst) in enumerate(pairs)]
    fills = error_fills(0, err_col, err_row, place_own, fill_sems)

    @pl.when(step == 0)
    def _():
        assemble(0, own, other, bcol_own, bcol_other, wqkv, wo, bqkv, bfc1)
        dbias[...] = jnp.zeros_like(dbias)
        pay_own[...] = jnp.zeros_like(pay_own)
        for copy in copies + fills:
            copy.start()

    rows = pl.ds(pl.multiple_of(step * TOK, TOK), TOK)
    single = dict(query=query, keyed=keyed, valued=valued, branch_a=branch_a, middle=middle,
                  branch_m=branch_m)

    def take(name, index=None):
        if name == "probs":
            return probs[0, index]
        if name == "slope":
            return slope[0, :, index * HMLP : (index + 1) * HMLP]
        return single[name][0]

    def mods_out(j, value):
        dmods[0, j : j + 1, :] = value

    def bias(name, start, value):
        at = BIAS[name] + start
        dbias[:, at : at + value.shape[1]] += token_sum(value.astype(f32))

    stash = dict(dqkv=s_dqkv, dg=s_dg, dya=s_dya, dym=s_dym)
    result = []
    x = dot(xt[0], wpatch[0], TN) + vector(b_rep, START_PATCH) + pos[...]
    run_steps([layer_backward(dx[0], x, lambda j: mods[0, j : j + 1, :], own, other, wqkv, wo,
                              take, rows, stash, mods_out, bias, result, (a_input_a, a_input_m))], 0)
    (grad,) = result
    grad = grad.astype(bf16)
    pay_own[PAY_PATCH : PAY_PATCH + PV, :] += dot(xt[0], grad)
    pay_own[PAY_BPATCH : PAY_BPATCH + 1, :] += token_sum(grad.astype(f32))
    dmods[0, 6 : 6 + 8, :] = dmods1[0]
    rounded = dmods[0].astype(bf16).astype(f32)
    dmods[0] = rounded
    pay_own[PAY_COND : PAY_COND + 14, :] += rounded

    @pl.when(step == pl.num_programs(0) - 1)
    def _():
        for copy in copies:
            copy.wait()
        weight_grads(a_input_a, a_input_m, a_mixed, a_acted, stash, (place_own, place_other),
                     (grad_own, grad_other), out_sems, fills)
        pay_own[PAY_HEAD : PAY_HEAD + PV, :] = dhead[...]
        for layer, values in enumerate((dbias, dbias1)):
            pay_own[PAY_PROJ + layer : PAY_PROJ + layer + 1, :] = values[:, BIAS["proj"] : BIAS["proj"] + D]
            pay_own[PAY_FC2 + layer : PAY_FC2 + layer + 1, :] = values[:, BIAS["fc2"] : BIAS["fc2"] + D]
        head_line = jnp.sum(jnp.where(diagonal(PV), dbhead[...], 0.0), 0, keepdims=True)
        pay_own[PAY_BHEAD : PAY_BHEAD + 1, :] = jnp.concatenate(
            [head_line, jnp.sum(loss[...], 1, keepdims=True), jnp.zeros((1, D - PV - 1), f32)], 1
        )
        pay_other[...] = pay_own[...]
        for side, out in enumerate((pay_own, pay_other)):
            for layer, values in enumerate((dbias, dbias1)):
                write_bcol(values, side, out, layer)
        for out in (pay_own, pay_other):
            out[PAY_BCOL + 8 :, :] = jnp.zeros((PAY_ROWS - PAY_BCOL - 8, D), f32)


def per_latent(*shape, group=1):
    zeros = (0,) * len(shape)
    return pl.BlockSpec((group,) + shape, lambda n: (n,) + zeros)


def fixed(*shape):
    zeros = (0,) * len(shape)
    return pl.BlockSpec(shape, lambda n: zeros, pipeline_mode=pl.Buffered(1))


def params():
    return pltpu.CompilerParams(dimension_semantics=("arbitrary",), vmem_limit_bytes=62 * 2**20)


SAVED = [
    ("query", (TOK, D), bf16), ("keyed", (TOK, D), bf16), ("valued", (TOK, D), bf16),
    ("probs", (HEADS, TOK, TOK), f32), ("branch_a", (TOK, D), f32), ("middle", (TOK, D), f32),
    ("slope", (TOK, MLP), f32), ("branch_m", (TOK, D), f32), ("mixed", (TOK, D), bf16),
    ("acted", (TOK, MLP), bf16),
]
BOTH = COL_S + ROW_S
GRAD_SHAPES = [(BOTH, D), (BOTH, D)]
WEIGHT_SCRATCH = [pltpu.VMEM((D, 3 * D), bf16), pltpu.VMEM((D, D), bf16),
                  pltpu.VMEM((1, 3 * D), f32), pltpu.VMEM((1, MLP), f32)]


def weight_specs(layer):
    half = pl.BlockSpec((D, GATH), lambda n: (0, layer), pipeline_mode=pl.Buffered(1))
    return [half, half, fixed(L, COL_S), fixed(L, COL_S), fixed(1, NBR)]


def stash_scratch(count):
    rows = count * TOK
    return [pltpu.VMEM((rows, 3 * D), bf16), pltpu.VMEM((rows, MLP), bf16),
            pltpu.VMEM((rows, D), bf16), pltpu.VMEM((rows, D), bf16)]


def place_scratch():
    return [pltpu.VMEM(shape, f32) for shape in GRAD_SHAPES] + [pltpu.SemaphoreType.DMA((8,)), pltpu.SemaphoreType.DMA((2,))]


def cost(flops, nbytes, count):
    return pl.CostEstimate(flops=int(flops * count), bytes_accessed=int(nbytes * count),
                           transcendentals=int(2e6 * count))


def run_forward(xt, mods, full_io, pos, weights):
    count = xt.shape[0]
    outs = SAVED + [("x2", (TOK, D), f32)]
    return pl.pallas_call(
        forward_kernel,
        grid=(count // GROUP,),
        in_specs=[per_latent(PV, TOK, group=GROUP), per_latent(14, D, group=GROUP),
                  pl.BlockSpec((1, PV, D), lambda n: (0, 0, 0)), fixed(TOK, D)] + weight_specs(0),
        out_specs=[per_latent(*shape, group=GROUP) for _, shape, _ in outs],
        out_shape=[jax.ShapeDtypeStruct((count,) + shape, kind) for _, shape, kind in outs],
        scratch_shapes=WEIGHT_SCRATCH,
        compiler_params=params(),
        cost_estimate=cost(1.0e9, 6e6, count),
        name="forward_first",
    )(xt, mods, full_io, pos, *weights)


def run_middle(x2, mods, weights, full_io, targets, err_col, err_row):
    count = x2.shape[0]
    rows = count * TOK
    outs = [((count, TOK, D), per_latent(TOK, D, group=GROUP)), ((count, 8, D), per_latent(8, D, group=GROUP))]
    outs += [(shape, pl.BlockSpec(memory_space=pl.ANY)) for shape in GRAD_SHAPES]
    outs += [(shape, fixed(*shape)) for shape in ((1, BIAS_WIDTH), (PV, D), (PV, 1), (1, TOK))]
    return pl.pallas_call(
        middle_kernel,
        grid=(count // GROUP,),
        in_specs=[per_latent(TOK, D, group=GROUP), per_latent(14, D, group=GROUP)] + weight_specs(1)
        + [pl.BlockSpec((1, PV, D), lambda n: (1, 0, 0)), per_latent(PV, TOK, group=GROUP)]
        + [pl.BlockSpec(memory_space=pl.ANY)] * 2,
        out_specs=[spec for _, spec in outs],
        out_shape=[jax.ShapeDtypeStruct(shape, f32) for shape, _ in outs],
        scratch_shapes=WEIGHT_SCRATCH
        + [pltpu.VMEM((GROUP, TOK, D), bf16)] * 3
        + [pltpu.VMEM((GROUP, HEADS, TOK, TOK), f32), pltpu.VMEM((rows, D), bf16),
           pltpu.VMEM((GROUP, TOK, D), f32), pltpu.VMEM((GROUP, TOK, D), f32), pltpu.VMEM((rows, MLP), bf16),
           pltpu.VMEM((GROUP, TOK, MLP), f32), pltpu.VMEM((GROUP, TOK, D), f32),
           pltpu.VMEM((rows, D), bf16), pltpu.VMEM((rows, D), bf16)]
        + stash_scratch(count) + place_scratch(),
        compiler_params=params(),
        cost_estimate=cost(3.2e9, 3e6, count),
        name="layer_second",
    )(x2, mods, *weights, full_io, targets, err_col, err_row)


def run_last(dx, mods, weights, xt, full_io, pos, smalls, dmods1, err_col, err_row, saved):
    count = dx.shape[0]
    rows = count * TOK
    outs = [((count, 14, D), per_latent(14, D))]
    outs += [(shape, pl.BlockSpec(memory_space=pl.ANY)) for shape in GRAD_SHAPES]
    outs += [(shape, fixed(*shape)) for shape in ((PAY_ROWS, D), (PAY_ROWS, D))]
    return pl.pallas_call(
        last_kernel,
        grid=(count,),
        in_specs=[per_latent(TOK, D), per_latent(14, D)] + weight_specs(0)
        + [per_latent(PV, TOK), pl.BlockSpec((1, PV, D), lambda n: (0, 0, 0)), fixed(TOK, D)]
        + [fixed(*shape) for shape in ((1, BIAS_WIDTH), (PV, D), (PV, 1), (1, TOK))] + [per_latent(8, D)]
        + [pl.BlockSpec(memory_space=pl.ANY)] * 2
        + [per_latent(*shape) for _, shape, _ in SAVED[:-2]] + [pl.BlockSpec(memory_space=pl.ANY)] * 2,
        out_specs=[spec for _, spec in outs],
        out_shape=[jax.ShapeDtypeStruct(shape, f32) for shape, _ in outs],
        scratch_shapes=WEIGHT_SCRATCH
        + [pltpu.VMEM((rows, D), bf16)] * 3 + [pltpu.VMEM((rows, MLP), bf16)]
        + stash_scratch(count) + [pltpu.VMEM((1, BIAS_WIDTH), f32), pltpu.SemaphoreType.DMA((2,))]
        + place_scratch(),
        compiler_params=params(),
        cost_estimate=cost(2.2e9, 8e6, count),
        name="backward_first",
    )(dx, mods, *weights, xt, full_io, pos, *smalls, dmods1, err_col, err_row,
      *saved[:-2], *[v.reshape(rows, -1) for v in saved[-2:]])


PACK = 128
WIDE = 3 * D


def split3(values):
    high = values.astype(bf16)
    rest = values - high.astype(f32)
    mid = rest.astype(bf16)
    low = (rest - mid.astype(f32)).astype(bf16)
    return high, mid, low


def narrow_dot(small, big, dims):
    parts = split3(small)
    high, mid, low = split3(big)
    first = dot(jnp.concatenate(parts, 0), high, dims)
    second = dot(jnp.concatenate(parts[:2], 0), mid, dims)
    third = dot(parts[0], low, dims)
    r = small.shape[0]
    return first[:r] + ((first[r : 2 * r] + second[:r]) + (first[2 * r :] + second[r:] + third))


def outer(left, right):
    l1, l2, l3 = split3(left)
    r1, r2, r3 = split3(right)
    return dot(
        jnp.concatenate([l1, l1, l2, l2, l1, l3], 0), jnp.concatenate([r1, r2, r1, r2, r3, r1], 0), TN
    )


CHUNKS = [(448 * k, 448) for k in range(3)] + [(COL_S + 480 * k, 480) for k in range(2)]


def layer_chunks(layer, err_col, err_row):
    for at, size in CHUNKS:
        ref, start = (err_col, at) if at < COL_S else (err_row, at - COL_S)
        yield ref.at[layer, pl.ds(start, size), :], pl.ds(at, size)


def project(layer, own, got, fac_col, fac_row, mat, left_col, left_row, v_own, v_got, sems, out_sems):
    loads, stores = [], []
    for k, (at, size) in enumerate(CHUNKS):
        rows = pl.ds(at, size)
        loads.append([pltpu.make_async_copy(src.at[rows, :], dst.at[rows, :], sems.at[2 * k + i])
                      for i, (src, dst) in enumerate(((own, v_own), (got, v_got)))])
        stores.append(pltpu.make_async_copy(v_own.at[rows, :], mat.at[rows, :], out_sems.at[k]))
        for copy in loads[-1]:
            copy.start()
    left_row[...] = jnp.zeros_like(left_row)
    total = None
    for (at, size), copies, store in zip(CHUNKS, loads, stores):
        for copy in copies:
            copy.wait()
        matrix = v_own[at : at + size, :] + v_got[at : at + size, :]
        v_own[at : at + size, :] = matrix
        store.start()
        if at < COL_S:
            part = narrow_dot(fac_col[layer][:, at : at + size], matrix, NN)
            total = part if total is None else total + part
        else:
            left_row[:, at - COL_S : at - COL_S + size] = narrow_dot(fac_row[layer], matrix, NT)
    left_col[...] = total
    for store in stores:
        store.wait()


ANY = pl.BlockSpec(memory_space=pl.ANY)
VMEM = pl.BlockSpec(memory_space=pltpu.VMEM)
SMEM = pl.BlockSpec(memory_space=pltpu.SMEM)
PROJECT_SCRATCH = [pltpu.VMEM((BOTH, D), f32)] * 2 + [
    pltpu.SemaphoreType.DMA((2 * len(CHUNKS),)), pltpu.SemaphoreType.DMA((len(CHUNKS),))]


def large():
    return pltpu.CompilerParams(vmem_limit_bytes=62 * 2**20)


def shapes_of(shapes):
    return [jax.ShapeDtypeStruct(shape, f32) for shape in shapes]


def run_project_second(own, got, fac_col, fac_row):
    return pl.pallas_call(
        lambda *refs: project(1, *refs),
        in_specs=[ANY] * 2 + [VMEM] * 2,
        out_specs=[ANY, VMEM, VMEM],
        out_shape=shapes_of([(BOTH, D), (RANK, D), (RANK, WIDE)]),
        scratch_shapes=PROJECT_SCRATCH,
        compiler_params=large(),
        cost_estimate=pl.CostEstimate(flops=int(1e9), bytes_accessed=int(1.5e7), transcendentals=0),
        name="left_second",
    )(own, got, fac_col, fac_row)


def exchange_kernel(block, place, dmods, full_cond, cond, sent):
    n_dp = sent.shape[0]
    count = dmods.shape[0]
    line = jnp.concatenate([dmods[:, j, :] for j in range(14)], 1)
    grad_act = dot(line.astype(bf16), full_cond[...], NT)
    cond_own = cond[pl.ds(pl.multiple_of(place[0] * count, count), count), :]
    gate = 1.0 / (1.0 + jnp.exp(-cond_own))
    grad_cond = grad_act * (gate * (1.0 + cond_own * (1.0 - gate)))
    sent[:, :count, :] = jnp.broadcast_to(grad_cond[None], (n_dp, count, D))
    for j in range(n_dp):
        sent[j, count:, :] = jnp.concatenate(
            [line[:, j * block : (j + 1) * block], jnp.zeros((count, D - block), f32)], 1
        )


def run_exchange(n_dp, place, dmods, full_cond, cond):
    return pl.pallas_call(
        lambda *refs: exchange_kernel(N_MODS // n_dp, *refs),
        in_specs=[SMEM, VMEM, VMEM, VMEM],
        out_shape=jax.ShapeDtypeStruct((n_dp, 2 * dmods.shape[0], D), f32),
        compiler_params=large(),
        name="modulation_rows",
    )(place, dmods, full_cond, cond)


def project_first_kernel(own, got, fac_col, fac_row,
                         left_col1, left_row1, pay_own, pay_got, err_io, fac_io,
                         mat, mat_io, sent, left_col, left_row, *scratch):
    project(0, own, got, fac_col, fac_row, mat, left_col, left_row, *scratch)
    share = sent.shape[1]
    pay = pay_own[...] + pay_got[...]
    left_io = []
    for index in range(2):
        matrix = pay[index * PV : (index + 1) * PV] + err_io[index]
        mat_io[index] = matrix
        left_io.append(dot_full(fac_io[index], matrix))
    sent[...] = jnp.zeros_like(sent)
    tall = (left_row, left_row1)
    for column in range(RANK):
        pick = slice(column, column + 1)
        lines = [tall[i % 2][pick, (i // 2) * D : (i // 2 + 1) * D] for i in (0, 1)]
        lines += [left_col[pick, :], left_col1[pick, :], left_io[0][pick], left_io[1][pick]]
        lines += [tall[i % 2][pick, (i // 2) * D : (i // 2 + 1) * D] for i in (2, 3, 4, 5)]
        for extra in range(6):
            at = column * 6 + extra
            if at < SMALL_ROWS:
                lines.append(pay[PAY_PROJ + at : PAY_PROJ + at + 1])
        for slot, line in enumerate(lines):
            at = column * 16 + slot
            sent[at // share, at % share : at % share + 1, :] = line


def run_project_first(n_dp, own, got, fac_col, fac_row, left_col1, left_row1,
                      pay_own, pay_got, err_io, fac_io):
    return pl.pallas_call(
        project_first_kernel,
        in_specs=[ANY] * 2 + [VMEM] * 8,
        out_specs=[ANY, VMEM, VMEM],
        out_shape=shapes_of([(BOTH, D), (2, PV, D), (n_dp, PACK // n_dp, D)]),
        scratch_shapes=[pltpu.VMEM((RANK, D), f32), pltpu.VMEM((RANK, WIDE), f32)] + PROJECT_SCRATCH,
        compiler_params=large(),
        cost_estimate=pl.CostEstimate(flops=int(1e9), bytes_accessed=int(1.5e7), transcendentals=0),
        name="left_first",
    )(own, got, fac_col, fac_row, left_col1, left_row1, pay_own, pay_got, err_io, fac_io)


TIME_ROWS = FREQ + D + 8


def modulation_kernel(block, core, got, act_half, features, first, first_act, full_time, labels,
                      cond_mine, cond_their, time_part, table_part):
    n_dp = got.shape[0]
    count = got.shape[1] // 2
    half = block // 2
    grad_cond = got[:, :count, :].reshape(n_dp * count, D)
    cols = got[:, count : 2 * count, :].reshape(n_dp * count, D)
    left, right = cols[:, :half].astype(bf16), cols[:, half:block].astype(bf16)
    is_first = core[0] == 0
    grad_left = dot(act_half[...], left, TN)
    grad_right = dot(act_half[...], right, TN)
    cond_mine[...] = jnp.where(is_first, grad_left, grad_right)
    cond_their[...] = jnp.where(is_first, grad_right, grad_left)
    grad_second = grad_cond.astype(bf16)
    gate = 1.0 / (1.0 + jnp.exp(-first[...]))
    slope = gate * (1.0 + first[...] * (1.0 - gate))
    grad_first = (dot(grad_second, full_time[FREQ:, :], NT) * slope).astype(bf16)
    time_part[:FREQ, :] = dot(features[...], grad_first, TN)
    time_part[FREQ : FREQ + D, :] = dot(first_act[...], grad_second, TN)
    time_part[FREQ + D :, :] = jnp.concatenate(
        [token_sum(grad_first.astype(f32)), token_sum(grad_second.astype(f32)), jnp.zeros((6, D), f32)], 0
    )
    onehot = (labels[...] == lax.broadcasted_iota(jnp.int32, (n_dp * count, CLASSES), 1)).astype(f32).astype(bf16)
    high, mid, low = split3(grad_cond)
    table_part[...] = dot(high, onehot, TN) + (dot(mid, onehot, TN) + dot(low, onehot, TN))


def run_modulation(core, got, act_half, features, first, first_act, full_time, labels):
    half = N_MODS // got.shape[0] // 2
    shapes = [(D, half), (D, half), (TIME_ROWS, D), (D, CLASSES)]
    vmem = pl.BlockSpec(memory_space=pltpu.VMEM)
    return pl.pallas_call(
        lambda *refs: modulation_kernel(2 * half, *refs),
        in_specs=[pl.BlockSpec(memory_space=pltpu.SMEM)] + [vmem] * 7,
        out_shape=[jax.ShapeDtypeStruct(shape, f32) for shape in shapes],
        compiler_params=pltpu.CompilerParams(vmem_limit_bytes=62 * 2**20),
        name="modulation_gradients",
    )(core, got, act_half, features, first, first_act, full_time, labels)


COL_ROWS = 4 * RANK
ROW_AT = L * COL_ROWS
IO_AT = ROW_AT + L * RANK
EXTRA_AT = IO_AT + 2 * RANK


def cond_top(rows):
    return -(-((rows + 1) // 2) // 8) * 8


def ortho(packed, left_col, left_row, left_io):
    columns = []
    blank = jnp.zeros((4, D), f32)
    for index in range(RANK):
        block = packed[index]
        column = jnp.concatenate(
            [block[0:6], jnp.concatenate([block[6:8], blank], 0), jnp.concatenate([block[8:10], blank], 0)], 1
        )
        for earlier in columns:
            column = column - jnp.sum(earlier * column, -1, keepdims=True) * earlier
        column = column * lax.rsqrt(jnp.sum(column * column, -1, keepdims=True) + ortho_eps)
        for layer in range(L):
            left_row[layer, index : index + 1, :] = column[layer : layer + 1]
            left_col[layer, index : index + 1, :] = column[2 + layer : 3 + layer, :D]
            left_io[layer, index : index + 1, :] = column[4 + layer : 5 + layer, :D]
        columns.append(column)


def total_squares(values):
    return jnp.sum(values * values, keepdims=True)


def rows_kernel(cond_own, cond_got, table_own, table_got, sent, table_share, sums):
    cond_grad = cond_own[...] + cond_got[...]
    table = table_own[...] + table_got[...]
    table_share[...] = table
    sums[...] = jnp.concatenate([total_squares(cond_grad), total_squares(table), jnp.zeros((1, D - 2), f32)], 1)
    n_dp = sent.shape[0]
    rows, half = D // n_dp, cond_grad.shape[1]
    top = cond_top(rows)
    for j in range(n_dp):
        piece = cond_grad[j * rows : (j + 1) * rows]
        sent[j, : min(top, rows), :half] = piece[:top]
        if rows > top:
            sent[j, : rows - top, half : 2 * half] = piece[top:]


def run_rows(n_dp, cond_own, cond_got, table_own, table_got):
    return pl.pallas_call(
        rows_kernel,
        out_shape=shapes_of([(n_dp, cond_top(D // n_dp), D), table_own.shape, (1, D)]),
        compiler_params=large(),
        name="modulation_sums",
    )(cond_own, cond_got, table_own, table_got)


def mat_loads(mats, places, sems):
    return [[pltpu.make_async_copy(mat.at[pl.ds(at, size), :], place.at[pl.ds(at, size), :],
                                   sems.at[layer * len(CHUNKS) + k]) for k, (at, size) in enumerate(CHUNKS)]
            for layer, (mat, place) in enumerate(zip(mats, places))]


def right_kernel(packed, mat0, mat1, mat_io, sums, sent, left_col, left_row, left_io, flat, v0, v1, sems):
    loads = mat_loads((mat0, mat1), (v0, v1), sems)
    for copies in loads:
        for copy in copies:
            copy.start()
    ortho(packed, left_col, left_row, left_io)
    for copies in loads:
        for copy in copies:
            copy.wait()
    for layer, mat in enumerate((v0, v1)):
        right = narrow_dot(left_col[layer], mat[:COL_S, :], NT)
        for piece in range(4):
            wide = min(D, COL_S - piece * D)
            at = layer * COL_ROWS + piece * RANK
            if wide < D:
                flat[at : at + RANK, :] = jnp.zeros((RANK, D), f32)
            flat[at : at + RANK, :wide] = right[:, piece * D : piece * D + wide]
        at = ROW_AT + layer * RANK
        flat[at : at + RANK, :] = narrow_dot(left_row[layer][:, :ROW_S], mat[COL_S:, :], NN)
        at = IO_AT + layer * RANK
        flat[at : at + RANK, :] = jnp.zeros((RANK, D), f32)
        flat[at : at + RANK, :PV] = dot_full(left_io[layer], mat_io[layer], NT)
    flat[EXTRA_AT:, :] = jnp.zeros((PACK - EXTRA_AT, D), f32)
    flat[EXTRA_AT : EXTRA_AT + 1, :] = sums[...]
    sent[...] = flat[...].reshape(sent.shape)


def run_right(n_dp, packed, mats, mat_io, sums):
    return pl.pallas_call(
        right_kernel,
        in_specs=[VMEM, ANY, ANY, VMEM, VMEM],
        out_shape=shapes_of([(n_dp, PACK // n_dp, D), (L, RANK, D), (L, RANK, WIDE), (2, RANK, D)]),
        scratch_shapes=[pltpu.VMEM((PACK, D), f32), pltpu.VMEM((BOTH, D), f32), pltpu.VMEM((BOTH, D), f32),
                        pltpu.SemaphoreType.DMA((L * len(CHUNKS),))],
        compiler_params=large(),
        name="right_factors",
    )(packed, *mats, mat_io, sums)


def norm_kernel(packed, left_packed, left_col, left_row, left_io, time_own, time_got,
                right_col, right_row, right_io, parts, brep_grad, bcol_grad):
    for layer in range(L):
        for piece in range(4):
            wide = min(D, COL_S - piece * D)
            at = layer * COL_ROWS + piece * RANK
            right_col[layer, :, piece * D : piece * D + wide] = packed[at : at + RANK, :wide]
        at = ROW_AT + layer * RANK
        right_row[layer] = packed[at : at + RANK, :]
        at = IO_AT + layer * RANK
        right_io[layer] = packed[at : at + RANK, :PV]

    def small(at):
        row = at - PAY_PROJ
        return left_packed[row // 6, 10 + row % 6 : 11 + row % 6, :]

    time_bias = time_own[FREQ + D :, :] + time_got[FREQ + D :, :]
    lines = [small(PAY_PROJ + row) for row in range(4)] + [small(PAY_COND + row) for row in range(14)]
    lines += [time_bias[0:1], time_bias[1:2], small(PAY_BPATCH), small(PAY_BHEAD)[:, :PV]]
    whole = jnp.zeros((1, 1), f32)
    for row, line in enumerate(lines):
        brep_grad[:, row * D : row * D + line.shape[1]] = line
        whole = whole + total_squares(line)
    split = jnp.zeros((1, 1), f32)
    for layer in range(L):
        line = jnp.concatenate([small(PAY_BCOL + 4 * layer + row) for row in range(4)], 1)[:, :COL_S]
        bcol_grad[layer : layer + 1, :] = line
        split = split + total_squares(line)
    whole = whole + total_squares(time_own[: FREQ + D, :] + time_got[: FREQ + D, :])

    def gram(left, right):
        return jnp.sum(dot_full(left, left, NT) * dot_full(right, right, NT), keepdims=True)

    for layer in range(L):
        split = split + gram(left_col[layer], right_col[layer]) + gram(left_row[layer], right_row[layer])
        whole = whole + gram(left_io[layer], right_io[layer])
    sums = packed[EXTRA_AT : EXTRA_AT + 1, :]
    split = split + sums[:, 0:1]
    whole = whole + sums[:, 1:2]
    loss = small(PAY_BHEAD)[:, PV : PV + 1]
    parts[...] = jnp.concatenate([split, whole, loss, jnp.zeros((1, 125), f32)], 1)


def run_norm(packed, left_packed, lefts, time_own, time_got):
    shapes = [(L, RANK, COL_S), (L, RANK, D), (2, RANK, PV), (1, 128), (1, NBR), (L, COL_S)]
    return pl.pallas_call(
        norm_kernel,
        out_shape=[jax.ShapeDtypeStruct(shape, f32) for shape in shapes],
        compiler_params=pltpu.CompilerParams(vmem_limit_bytes=62 * 2**20),
        name="gradient_norm",
    )(packed, left_packed, *lefts, time_own, time_got)


def error_kernel(mat0, mat1, mat_io, left_col, left_row, left_io, right_col, right_row, right_io,
                 err_col, err_row, err_io, v0, v1, sems, out_sems):
    loads = mat_loads((mat0, mat1), (v0, v1), sems)
    for copies in loads:
        for copy in copies:
            copy.start()
    stores = []
    for layer, place in enumerate((v0, v1)):
        for k, ((at, size), (target, rows)) in enumerate(zip(CHUNKS, layer_chunks(layer, err_col, err_row))):
            if at < COL_S:
                approx = outer(right_col[layer][:, at : at + size], left_col[layer])
            else:
                approx = outer(left_row[layer][:, at - COL_S : at - COL_S + size], right_row[layer])
            loads[layer][k].wait()
            place[at : at + size, :] = place[at : at + size, :] - approx
            store = pltpu.make_async_copy(place.at[rows, :], target, out_sems.at[layer * len(CHUNKS) + k])
            store.start()
            stores.append(store)
        err_io[layer] = mat_io[layer] - outer(right_io[layer], left_io[layer])
    for store in stores:
        store.wait()


def run_error(mats, mat_io, lefts, rights):
    return pl.pallas_call(
        error_kernel,
        in_specs=[ANY, ANY] + [VMEM] * 7,
        out_specs=[ANY, ANY, VMEM],
        out_shape=shapes_of([(L, COL_S, D), (L, ROW_S, D), (2, PV, D)]),
        scratch_shapes=[pltpu.VMEM((BOTH, D), f32), pltpu.VMEM((BOTH, D), f32),
                        pltpu.SemaphoreType.DMA((L * len(CHUNKS),)), pltpu.SemaphoreType.DMA((L * len(CHUNKS),))],
        compiler_params=large(),
        name="next_errors",
    )(*mats, mat_io, *lefts, *rights)


def own_columns(values, first, count):
    across = lax.broadcasted_iota(jnp.int32, (count, D), 1)
    down = lax.broadcasted_iota(jnp.int32, (count, D), 0)
    pick = (across == down + first).astype(f32).astype(bf16)
    high, mid, low = split3(values)
    return dot(high, pick, NT) + (dot(mid, pick, NT) + dot(low, pick, NT))


def update_kernel(core, parts, parts_got, left_col, right_col, right_row, left_row, right_io, left_io,
                  cond_own, cond_got, time_grad, table_grad, bcol_grad, brep_grad,
                  w_col, w_row, w_cond, w_time, w_io, w_table, b_col, b_rep,
                  m_col, m_row, m_cond, m_time, m_io, m_table, m_bcol, m_brep,
                  scalars, n_col, n_row, n_cond, n_time, n_io, n_table, n_bcol, n_brep,
                  v_col, v_row, v_cond, v_time, v_io, v_table, v_bcol, v_brep):
    clip_norm = jnp.sqrt(parts[:, 0:1] + parts_got[:, 0:1] + parts[:, 1:2])
    scaling = jnp.minimum(1.0, clip_limit / clip_norm)
    scalars[...] = jnp.concatenate([parts[:, 2:3], clip_norm, jnp.zeros((1, 126), f32)], 1)

    def advance(weight, momentum, gradient):
        moved = momentum_decay * momentum + scaling * gradient
        return weight - learn_rate * moved, moved

    n_dp = cond_own.shape[0]
    rows = w_cond.shape[0]
    at = core[1] * rows
    for layer in range(L):
        n_col[layer], v_col[layer] = advance(
            w_col[layer], m_col[layer], outer(own_columns(left_col[layer], at, rows), right_col[layer]))
        n_row[layer], v_row[layer] = advance(
            w_row[layer], m_row[layer],
            outer(own_columns(right_row[layer], at, rows), left_row[layer][:, :ROW_S]))
        n_io[layer], v_io[layer] = advance(
            w_io[layer], m_io[layer], outer(right_io[layer], own_columns(left_io[layer], at, rows)))
    half = N_MODS // n_dp // 2
    top = cond_top(rows)
    is_first = core[0] == 0
    pieces = []
    for j in range(n_dp):
        mine, theirs = cond_own[j], cond_got[j]
        for pair in ((mine, theirs), (theirs, mine)):
            block = jnp.where(is_first, pair[0], pair[1])
            if rows > top:
                block = jnp.concatenate([block[:top, :half], block[: rows - top, half : 2 * half]], 0)
            else:
                block = block[:rows, :half]
            pieces.append(block)
    n_cond[...], v_cond[...] = advance(w_cond[...], m_cond[...], jnp.concatenate(pieces, 1))
    n_time[...], v_time[...] = advance(w_time[...], m_time[...], time_grad[...])
    n_table[...], v_table[...] = advance(w_table[...], m_table[...], table_grad[...])
    n_bcol[...], v_bcol[...] = advance(b_col[...], m_bcol[...], bcol_grad[...])
    n_brep[...], v_brep[...] = advance(b_rep[...], m_brep[...], brep_grad[...])


def run_update(core, grads, weights, momenta):
    vmem = pl.BlockSpec(memory_space=pltpu.VMEM)
    shapes = [(1, 128)] + [v.shape for v in weights] * 2
    return pl.pallas_call(
        update_kernel,
        in_specs=[pl.BlockSpec(memory_space=pltpu.SMEM)] + [vmem] * (len(grads) + 2 * len(weights)),
        out_shape=[jax.ShapeDtypeStruct(shape, f32) for shape in shapes],
        compiler_params=pltpu.CompilerParams(vmem_limit_bytes=62 * 2**20),
        name="weight_update",
    )(core, *grads, *weights, *momenta)


def swap(values):
    return lax.ppermute(values, "tensor", [(0, 1), (1, 0)])


def trade(chunks):
    return lax.all_to_all(chunks, "dp", 0, 0, tiled=True)


def spread(values):
    return trade(jnp.broadcast_to(values[None], (lax.axis_size("dp"),) + values.shape))


def exact_parts(values):
    high = lax.reduce_precision(values, 8, 7)
    mid = lax.reduce_precision(values - high, 8, 7)
    return [part.astype(bf16) for part in (high, mid, (values - high) - mid)]


def on_device(
    latents, gauss_noise, time_steps, labels, targets,
    w_col, w_row, w_cond, w_time, w_io, class_table, b_col, b_rep,
    mom_col, mom_row, mom_cond, mom_time, mom_io, mom_table, mom_bcol, mom_brep,
    err_col, err_row, err_io, fac_col, fac_row, fac_io,
):
    n_dp = lax.axis_size("dp")
    index_dp = lax.axis_index("dp")
    index_t = lax.axis_index("tensor")
    core = jnp.stack([index_t, index_dp]).astype(jnp.int32)
    first_core = index_t == 0
    n_all = labels.shape[0]
    per_dp = latents.shape[0]
    count = per_dp // 2
    rows = w_col.shape[1]

    def flip(values):
        return values.transpose(0, 2, 1)

    def halves(mine, theirs, axis):
        pair = jnp.stack([mine, theirs], axis)
        return jnp.where(first_core, pair, jnp.flip(pair, axis))

    row_sh = flip(w_row)
    shard = jnp.concatenate(
        [piece[layer] for layer in range(L)
         for piece in (w_col[:, :, QKV_S:], row_sh[:, :, HALF:], w_col[:, :, :QKV_S], row_sh[:, :, :HALF])], 1
    ).astype(bf16)
    full = lax.all_gather(shard, ("dp", "tensor"))

    block = N_MODS // n_dp
    half_block = block // 2
    classes = jnp.arange(CLASSES, dtype=jnp.int32)
    onehot_t = classes[:, None] == labels[None, :]
    looked = dot(class_table.astype(bf16), onehot_t.astype(bf16), TN).astype(bf16)
    time_rows = w_time.shape[0]
    sizes = [rows * n_all, time_rows * D, 2 * PV * rows, 3 * per_dp]
    wide = -(-sum(sizes) // 256) * 128
    common = jnp.concatenate(
        [part.reshape(-1) for part in
         (looked, w_time.astype(bf16), flip(w_io).astype(bf16), *exact_parts(time_steps))]
    )
    common = jnp.pad(common, (0, 2 * wide - common.shape[0]))
    common = lax.dynamic_slice_in_dim(common.reshape(2, wide), index_t, 1, 0)
    cond_bf = w_cond.astype(bf16).reshape(rows, n_dp, 2, half_block)
    cond_mine = lax.dynamic_slice_in_dim(cond_bf, index_t, 1, 2)[:, :, 0].transpose(1, 0, 2)
    sent = jnp.concatenate(
        [jnp.broadcast_to(common, (n_dp, wide)), cond_mine.reshape(n_dp, rows * half_block)], 1
    )
    got = trade(sent)
    cond_cols = got[:, wide:].reshape(D, half_block)
    mine = got[:, :wide]
    common = halves(mine, swap(mine), 1).reshape(n_dp, 2 * wide)
    ends = np.cumsum([0] + sizes)
    looked = common[:, : ends[1]].reshape(D, n_all).T
    full_time = common[:, ends[1] : ends[2]].reshape(FREQ + D, D)
    full_io = flip(common[:, ends[2] : ends[3]].reshape(n_dp, 2 * PV, rows).transpose(1, 0, 2).reshape(2, PV, D).transpose(0, 2, 1))
    steps_all = jnp.sum(common[:, ends[3] : ends[4]].reshape(n_dp, 3, per_dp).astype(f32), 1).reshape(n_all)

    features = frequency_features(steps_all).astype(bf16)
    first = dot(features, full_time[:FREQ]) + b_rep[START_FIRST:START_SECOND]
    first_act = jax.nn.silu(first).astype(bf16)
    second = dot(first_act, full_time[FREQ:]) + b_rep[START_SECOND:START_PATCH]
    cond = second + looked.astype(f32)
    cond_act = jax.nn.silu(cond).astype(bf16)
    mods = dot(cond_act, cond_cols).reshape(n_dp * 2, count, half_block)
    mods = lax.all_to_all(mods, ("dp", "tensor"), 0, 0, tiled=True)
    mods = mods.transpose(1, 0, 2).reshape(count, N_MODS)
    mods = (mods + b_rep[START_COND:START_FIRST]).reshape(count, 14, D)
    full, mods = lax.optimization_barrier((full, mods))
    full = full.reshape(n_dp, 2, rows, L * GATH)

    def half_of(values):
        split = values.reshape((n_dp, 2, count) + values.shape[1:])
        return lax.dynamic_slice_in_dim(split, index_t, 1, 1).reshape((n_dp * count,) + values.shape[1:])

    halves_of = [half_of(v) for v in (cond_act, features, first, first_act)]
    labels_half = half_of(labels)[:, None]

    def mine_of(values):
        return lax.dynamic_slice_in_dim(values, index_t * count, count, 0)

    steps_own = mine_of(time_steps)[:, None, None]
    xt = (
        (1.0 - steps_own) * flip(mine_of(latents)) + steps_own * flip(mine_of(gauss_noise))
    ).astype(bf16)
    b_line = b_rep[None]
    own = lax.dynamic_slice_in_dim(full, index_t, 1, 1).reshape(D, L * GATH)
    other = lax.dynamic_slice_in_dim(full, 1 - index_t, 1, 1).reshape(D, L * GATH)
    weights = (own, other, b_col, swap(b_col), b_line)
    pos = jnp.asarray(position_table())
    *saved, x2 = run_forward(xt, mods, full_io, pos, weights)
    x2, late_cond = lax.optimization_barrier((x2, w_cond))
    full_cond = lax.all_gather(late_cond.astype(bf16), "dp", axis=0, tiled=True)
    err_col_t, err_io_t = flip(err_col), flip(err_io)
    dx, dmods1, own1, oth1, *smalls = run_middle(
        x2, mods, weights, full_io, flip(mine_of(targets)), err_col_t, err_row
    )
    got1 = swap(oth1)
    dmods, own0, oth0, pay_own, pay_oth = run_last(
        dx, mods, weights, xt, full_io, pos, smalls, dmods1, err_col_t, err_row, saved
    )
    got0, pay_got = swap(oth0), swap(pay_oth)

    place = (index_dp * 2 + index_t).astype(jnp.int32).reshape(1)
    rows_got = trade(run_exchange(n_dp, place, dmods, full_cond, cond))
    fac_col_t, fac_row_t, fac_io_t = flip(fac_col), flip(fac_row), flip(fac_io)
    mat1, left_col1, left_row1 = run_project_second(own1, got1, fac_col_t, fac_row_t)
    mat0, mat_io, sent = run_project_first(
        n_dp, own0, got0, fac_col_t, fac_row_t, left_col1, left_row1,
        pay_own, pay_got, err_io_t, fac_io_t
    )
    mats = (mat0, mat1)
    rows_got, sent = lax.optimization_barrier((rows_got, sent))
    share = jnp.sum(trade(sent), 0)

    cond_mine, cond_their, time_own, table_part = run_modulation(core, rows_got, *halves_of, full_time, labels_half)
    share, cond_mine, cond_their, time_own, table_part = lax.optimization_barrier(
        (share, cond_mine, cond_their, time_own, table_part)
    )
    left_packed = spread(share).reshape(RANK, 16, D)
    cond_got, time_got = swap(cond_their), swap(time_own)
    table_own = lax.dynamic_slice_in_dim(table_part, index_dp * rows, rows, 0)
    cond_sent, table_share, sums = run_rows(n_dp, cond_mine, cond_got, table_own, swap(table_own))
    cond_rows = trade(cond_sent)

    sent, left_col, left_row, left_io = run_right(n_dp, left_packed, mats, mat_io, sums)
    cond_rows, sent = lax.optimization_barrier((cond_rows, sent))
    packed = spread(jnp.sum(trade(sent), 0)).reshape(PACK, D)
    cond_rows_got = swap(cond_rows)
    lefts = (left_col, left_row, left_io)
    right_col, right_row, right_io, parts, brep_grad, bcol_grad = run_norm(
        packed, left_packed, lefts, time_own, time_got
    )
    parts_got = swap(parts)
    next_err_col, next_err_row, next_err_io = run_error(mats, mat_io, lefts, (right_col, right_row, right_io))

    time_at = index_dp * time_rows
    time_grad = (
        lax.dynamic_slice_in_dim(time_own, time_at, time_rows, 0)
        + lax.dynamic_slice_in_dim(time_got, time_at, time_rows, 0)
    )
    olds = (w_col, flip(w_row), w_cond, w_time, flip(w_io), class_table.T, b_col, b_line)
    momenta = (mom_col, flip(mom_row), mom_cond, mom_time, flip(mom_io), mom_table.T, mom_bcol, mom_brep[None])
    scalars, *new = run_update(
        core,
        (parts, parts_got, left_col, right_col, right_row, left_row, right_io, left_io,
         cond_rows, cond_rows_got, time_grad, table_share, bcol_grad, brep_grad),
        olds, momenta,
    )

    def outward(col, row, cond, time, io, table, bcol, brep):
        return (col, flip(row), cond, time, flip(io), table.T, bcol, brep[0])

    return (
        scalars[0, 0], scalars[0, 1], *outward(*new[:8]), *outward(*new[8:]),
        flip(next_err_col), next_err_row, flip(next_err_io), flip(right_col), flip(right_row), flip(right_io),
    )


def solution(mesh):
    weights = (
        P(None, "dp", "tensor"), P(None, "tensor", "dp"), P("dp", None), P("dp", None),
        P(None, "dp", None), P(None, "dp"), P(None, "tensor"), P(),
    )
    errors = (P("dp", None, "tensor"), P("dp", "tensor", None), P("dp", None, None))
    factors = (P(None, "tensor", None), P(None, "tensor", None), P())
    rows = P("dp", None, None)
    return jax.shard_map(
        on_device,
        mesh=mesh,
        in_specs=(rows, rows, P("dp"), P(), rows) + weights + weights + errors + factors,
        out_specs=(P(), P()) + weights + weights + errors + factors,
        check_vma=False,
    )
```

```python
import jax
import jax.numpy as jnp
import numpy as np
from jax import lax
from jax.experimental import pallas as pl
from jax.experimental.pallas import tpu as pltpu
from jax.sharding import PartitionSpec as P

D = 384
HEADS = 6
HD = 64
MLP = 1536
NBR = 8080
CLASSES = 1000
FREQ = 256
PV = 16
GRID = 16
L = 2
TOK = 256
RANK = 8
GROUP = 2
AHEAD, MLP_AHEAD, BACK_AHEAD = 2, 2, 3
LAG = 1

norm_eps = 1e-06
ortho_eps = 1e-06
clip_limit = 1.0
momentum_decay = 0.9
learn_rate = 4.0

HALF = D // 2
HMLP = MLP // 2
QKV_S = 3 * HALF
COL_S = QKV_S + HMLP
ROW_S = HALF + HMLP
OFF_W2 = HMLP
OFF_Q = 2 * HMLP
GATH = 2 * HMLP + 4 * HALF

f32 = jnp.float32
bf16 = jnp.bfloat16
highest = lax.Precision.HIGHEST
NN = (((1,), (0,)), ((), ()))
NT = (((1,), (1,)), ((), ()))
TN = (((0,), (0,)), ((), ()))


def dot(left, right, dims=NN):
    return lax.dot_general(left, right, dims, preferred_element_type=f32)


def dot_full(left, right, dims=NN):
    return lax.dot_general(left, right, dims, precision=highest, preferred_element_type=f32)


def position_table():
    quarter = D // 4
    omega = 1.0 / 10000.0 ** (np.arange(quarter, dtype=np.float32) / quarter)
    index = np.arange(TOK)
    across = (index % GRID).astype(np.float32)[:, None] * omega[None, :].astype(np.float32)
    down = (index // GRID).astype(np.float32)[:, None] * omega[None, :].astype(np.float32)
    table = np.concatenate([np.sin(across), np.cos(across), np.sin(down), np.cos(down)], 1)
    return table.astype(np.float32)


def frequency_features(steps):
    half = FREQ // 2
    rates = jnp.exp(-jnp.log(10000.0) * jnp.arange(half, dtype=f32) / half)
    angles = steps[:, None] * rates[None, :]
    return jnp.concatenate([jnp.cos(angles), jnp.sin(angles)], 1)


def normalize(values):
    centered = values - jnp.mean(values, -1, keepdims=True)
    inv_std = lax.rsqrt(jnp.mean(centered * centered, -1, keepdims=True) + norm_eps)
    return centered * inv_std, inv_std


def norm_back(grad, normed, inv_std):
    mean_grad = jnp.mean(grad, -1, keepdims=True)
    mean_mixed = jnp.mean(grad * normed, -1, keepdims=True)
    return inv_std * (grad - mean_grad - normed * mean_mixed)


def token_sum(values):
    return jnp.sum(values, 0, keepdims=True)


START_FC2 = L * D
START_COND = 2 * L * D
N_MODS = (6 * L + 2) * D
START_FIRST = START_COND + N_MODS
START_SECOND = START_FIRST + D
START_PATCH = START_FIRST + 2 * D
START_HEAD = START_FIRST + 3 * D


def assemble(layer, own, other, bcol_own, bcol_other, wqkv, wo, bqkv, bfc1):
    for side, (weights, bias) in enumerate(((own, bcol_own), (other, bcol_other))):
        for head in range(HEADS // 2):
            for part in range(3):
                at = (3 * head + part) * HD
                to = part * D + side * HALF + head * HD
                wqkv[:, to : to + HD] = weights[:, OFF_Q + at : OFF_Q + at + HD]
                bqkv[:, to : to + HD] = bias[layer : layer + 1, at : at + HD]
        wo[:, side * HALF : (side + 1) * HALF] = weights[:, OFF_Q + QKV_S :]
        bfc1[:, side * HMLP : (side + 1) * HMLP] = bias[layer : layer + 1, QKV_S:]


def vector(b_rep, at):
    return b_rep[:, at : at + D]


def head_mask(which):
    lane = lax.broadcasted_iota(jnp.int32, (1, 2 * HD), 1)
    return (lane < HD) if which == 0 else (lane >= HD)


def keep(values, mask):
    return jnp.where(mask, values, jnp.zeros_like(values))


def gelu_parts(pre):
    squared = pre * pre
    coef = np.float32(np.sqrt(2.0 / np.pi))
    tanh = jnp.tanh(pre * (coef + np.float32(coef * 0.044715) * squared))
    half = 0.5 * (1.0 + tanh)
    slope = half + (0.5 * pre) * (1.0 - tanh * tanh) * (
        coef + np.float32(3.0 * 0.044715 * coef) * squared
    )
    return (pre * half).astype(bf16), slope


def ahead_of(products, depth):
    waiting = [next(products) for _ in range(depth)]
    while waiting:
        ready = waiting.pop(0)
        following = next(products, None)
        if following is not None:
            waiting.append(following)
        yield ready


def run_steps(chains, lag):
    waits = [lag * i for i in range(len(chains))]
    live = dict(enumerate(chains))
    while live:
        for i in list(live):
            if waits[i] > 0:
                waits[i] -= 1
            elif next(live[i], 1) is not None:
                del live[i]


def pair_span(pair):
    return slice(pair * 2 * HD, (pair + 1) * 2 * HD)


def layer_forward(x, mod, own, other, wqkv, wo, bqkv, bfc1, bproj, bfc2, put, result):
    normed, _ = normalize(x)
    input_a = (normed * (1.0 + mod(1)) + mod(0)).astype(bf16)
    put("input_a", input_a)
    yield
    thirds = []
    for part in range(3):
        span = slice(part * D, (part + 1) * D)
        value = (dot(input_a, wqkv[:, span]) + bqkv[:, span]).astype(bf16)
        if part == 0:
            value = value * jnp.asarray(HD**-0.5, bf16)
        put(("query", "keyed", "valued")[part], value)
        thirds.append(value)
        yield
    query, keyed, valued = thirds
    scored = ahead_of(
        (dot(keep(query[:, pair_span(pair)], head_mask(which)), keyed[:, pair_span(pair)], NT)
         for pair in range(HEADS // 2) for which in range(2)), AHEAD
    )
    pieces = []
    for pair in range(HEADS // 2):
        total = None
        for which in range(2):
            scores = next(scored)
            yield
            expo = jnp.exp(scores - jnp.max(scores, -1, keepdims=True))
            probs = expo * (1.0 / jnp.sum(expo, -1, keepdims=True))
            put("probs", probs, 2 * pair + which)
            yield
            mixed = dot(probs.astype(bf16), keep(valued[:, pair_span(pair)], head_mask(which)))
            total = mixed if total is None else total + mixed
        pieces.append(total.astype(bf16))
    mixed = jnp.concatenate(pieces, 1)
    put("mixed", mixed)
    yield
    branch_a = dot(mixed, wo[...], NT) + bproj
    put("branch_a", branch_a)
    middle = x + mod(2) * branch_a
    put("middle", middle)
    yield
    normed_m, _ = normalize(middle)
    input_m = (normed_m * (1.0 + mod(4)) + mod(3)).astype(bf16)
    put("input_m", input_m)
    yield
    branch_m = bfc2
    for side, weights in enumerate((own, other)):
        pre = dot(input_m, weights[:, :HMLP]) + bfc1[:, side * HMLP : (side + 1) * HMLP]
        yield
        acted, slope = gelu_parts(pre)
        put("acted", acted, side)
        put("slope", slope, side)
        yield
        branch_m = branch_m + dot(acted, weights[:, OFF_W2 : OFF_W2 + HMLP], NT)
        yield
    put("branch_m", branch_m)
    result.append(middle + mod(5) * branch_m)


def layer_backward(grad, x, mod, own, other, wqkv, wo, take, rows, stash, mods_out, bias, result, inputs=None):
    branch_m = take("branch_m")
    mods_out(5, token_sum(grad * branch_m))
    grad_branch_m = (grad * mod(5)).astype(bf16)
    bias("fc2", 0, grad_branch_m)
    stash["dym"][rows, :] = grad_branch_m
    yield
    grad_input = None
    acting = ahead_of(
        (dot(grad_branch_m, weights[:, OFF_W2 : OFF_W2 + HMLP]) for weights in (own, other)), MLP_AHEAD
    )
    for side, weights in enumerate((own, other)):
        span = slice(side * HMLP, (side + 1) * HMLP)
        grad_acted = next(acting)
        yield
        grad_pre = (grad_acted * take("slope", side)).astype(bf16)
        stash["dg"][rows, span] = grad_pre
        bias("fc1", side * HMLP, grad_pre)
        yield
        part = dot(grad_pre, weights[:, :HMLP], NT)
        grad_input = part if grad_input is None else grad_input + part
        yield
    middle = take("middle")
    normed_m, inv_m = normalize(middle)
    if inputs is not None:
        inputs[1][rows, :] = (normed_m * (1.0 + mod(4)) + mod(3)).astype(bf16)
    mods_out(3, token_sum(grad_input))
    mods_out(4, token_sum(grad_input * normed_m))
    grad_middle = grad + norm_back(grad_input * (1.0 + mod(4)), normed_m, inv_m)
    yield
    branch_a = take("branch_a")
    mods_out(2, token_sum(grad_middle * branch_a))
    grad_branch_a = (grad_middle * mod(2)).astype(bf16)
    bias("proj", 0, grad_branch_a)
    stash["dya"][rows, :] = grad_branch_a
    yield
    grad_mixed = dot(grad_branch_a, wo[...]).astype(bf16)
    yield
    query, keyed, valued = take("query"), take("keyed"), take("valued")
    scored = ahead_of(
        (dot(keep(grad_mixed[:, pair_span(pair)], head_mask(which)), valued[:, pair_span(pair)], NT)
         for pair in range(HEADS // 2) for which in range(2)), BACK_AHEAD
    )
    grads_q, grads_k, grads_v = [], [], []
    for pair in range(HEADS // 2):
        q_pair, k_pair = query[:, pair_span(pair)], keyed[:, pair_span(pair)]
        grad_q = grad_k = grad_v = None
        for which in range(2):
            mask = head_mask(which)
            grad_probs = next(scored)
            yield
            probs = take("probs", 2 * pair + which)
            row_dot = jnp.sum(grad_probs * probs, -1, keepdims=True)
            grad_scores = (probs * (grad_probs - row_dot)).astype(bf16)
            yield
            part_q = dot(grad_scores, keep(k_pair, mask))
            part_k = dot(grad_scores, keep(q_pair, mask), TN)
            part_v = dot(probs.astype(bf16), keep(grad_mixed[:, pair_span(pair)], mask), TN)
            grad_q = part_q if grad_q is None else grad_q + part_q
            grad_k = part_k if grad_k is None else grad_k + part_k
            grad_v = part_v if grad_v is None else grad_v + part_v
        grads_q.append((grad_q * HD**-0.5).astype(bf16))
        grads_k.append(grad_k.astype(bf16))
        grads_v.append(grad_v.astype(bf16))
    yield
    grad_qkv = jnp.concatenate(grads_q + grads_k + grads_v, 1)
    stash["dqkv"][rows, :] = grad_qkv
    bias("qkv", 0, grad_qkv)
    yield
    grad_input_a = dot(grad_qkv, wqkv[...], NT)
    yield
    normed, inv_a = normalize(x)
    if inputs is not None:
        inputs[0][rows, :] = (normed * (1.0 + mod(1)) + mod(0)).astype(bf16)
    mods_out(0, token_sum(grad_input_a))
    mods_out(1, token_sum(grad_input_a * normed))
    result.append(grad_middle + norm_back(grad_input_a * (1.0 + mod(1)), normed, inv_a))


def weight_grads(input_a, input_m, mixed, acted, stash, places, outs, sems, fills):
    def add(side, start, value):
        rows = slice(start, start + value.shape[0])
        places[side][rows, :] = value if side else places[side][rows, :] + value

    for copy in fills:
        copy.wait()
    copies = []

    def send(side, start, stop):
        rows = pl.ds(start, stop - start)
        copy = pltpu.make_async_copy(places[side].at[rows, :], outs[side].at[rows, :], sems.at[len(copies)])
        copy.start()
        copies.append(copy)

    for part in range(3):
        piece = dot(stash["dqkv"][:, part * D : (part + 1) * D], input_a[...], TN)
        for side in range(2):
            for head in range(HEADS // 2):
                start = side * HALF + head * HD
                place = (3 * head + part) * HD
                add(side, place, piece[start : start + HD, :])
    for side in (1, 0):
        send(side, 0, QKV_S)
    for side in (1, 0):
        add(side, QKV_S, dot(stash["dg"][:, side * HMLP : (side + 1) * HMLP], input_m[...], TN))
        send(side, QKV_S, COL_S)
    for side in (1, 0):
        add(side, COL_S + HALF, dot(acted[:, side * HMLP : (side + 1) * HMLP], stash["dym"][...], TN))
        send(side, COL_S + HALF, BOTH)
    piece = dot(mixed[...], stash["dya"][...], TN)
    for side in (1, 0):
        add(side, COL_S, piece[side * HALF : (side + 1) * HALF, :])
        send(side, COL_S, COL_S + HALF)
    for copy in copies:
        copy.wait()


def error_fills(layer, err_col, err_row, place, sems):
    return [pltpu.make_async_copy(err_col.at[layer], place.at[pl.ds(0, COL_S), :], sems.at[0]),
            pltpu.make_async_copy(err_row.at[layer], place.at[pl.ds(COL_S, ROW_S), :], sems.at[1])]


BIAS = {"qkv": 0, "fc1": 3 * D, "proj": 3 * D + MLP, "fc2": 4 * D + MLP}
BIAS_WIDTH = 5 * D + MLP

PAY_PATCH, PAY_HEAD, PAY_PROJ, PAY_FC2, PAY_BPATCH, PAY_BHEAD, PAY_COND, PAY_BCOL = 0, 16, 32, 34, 36, 37, 38, 52
PAY_ROWS = 64
SMALL_ROWS = PAY_BCOL + 8 - PAY_PROJ


def forward_kernel(core, full, xt, mods, wpatch, pos, own, other, bcol_own, bcol_other, b_rep,
                   query, keyed, valued, probs, branch_a, middle, slope, branch_m, mixed, acted,
                   x2, next_own, next_other, wqkv, wo, bqkv, bfc1, hold_own, hold_other, sems):
    picks = [pltpu.make_async_copy(full.at[:, side, :, pl.ds(GATH, GATH)], hold, sems.at[i])
             for i, (side, hold) in enumerate(((core[0], hold_own), (1 - core[0], hold_other)))]
    leaves = [pltpu.make_async_copy(hold, out, sems.at[2 + i])
              for i, (hold, out) in enumerate(((hold_own, next_own), (hold_other, next_other)))]

    @pl.when(pl.program_id(0) == 0)
    def _():
        for copy in picks:
            copy.start()
        assemble(0, own, other, bcol_own, bcol_other, wqkv, wo, bqkv, bfc1)

    named = dict(query=query, keyed=keyed, valued=valued, mixed=mixed, branch_a=branch_a,
                 middle=middle, branch_m=branch_m)

    def chain(i):
        def put(name, value, index=None):
            if name in ("input_a", "input_m"):
                return
            if name == "probs":
                probs[i, index] = value
            elif name == "acted":
                acted[i, :, index * HMLP : (index + 1) * HMLP] = value
            elif name == "slope":
                slope[i, :, index * HMLP : (index + 1) * HMLP] = value
            else:
                named[name][i] = value

        x = dot(xt[i], wpatch[0], TN) + vector(b_rep, START_PATCH) + pos[...]
        result = []
        yield from layer_forward(x, lambda j: mods[i, j : j + 1, :], own, other, wqkv, wo, bqkv[...],
                                 bfc1[...], vector(b_rep, 0), vector(b_rep, START_FC2), put, result)
        x2[i] = result[0]

    run_steps([chain(i) for i in range(xt.shape[0])], LAG)

    @pl.when(pl.program_id(0) == 0)
    def _():
        for copy, leave in zip(picks, leaves):
            copy.wait()
            leave.start()

    @pl.when(pl.program_id(0) == pl.num_programs(0) - 1)
    def _():
        for leave in leaves:
            leave.wait()


def diagonal(count):
    down = lax.broadcasted_iota(jnp.int32, (count, count), 0)
    across = lax.broadcasted_iota(jnp.int32, (count, count), 1)
    return down == across


def write_bcol(dbias, side, out, layer):
    pieces = []
    for head in range(HEADS // 2):
        for part in range(3):
            start = part * D + side * HALF + head * HD
            pieces.append(dbias[:, start : start + HD])
    start = 3 * D + side * HMLP
    pieces.append(dbias[:, start : start + HMLP])
    pieces.append(jnp.zeros((1, 4 * D - COL_S), f32))
    line = jnp.concatenate(pieces, 1)
    for row in range(4):
        at = PAY_BCOL + 4 * layer + row
        out[at : at + 1, :] = line[:, row * D : (row + 1) * D]


def middle_kernel(x2, mods, own, other, bcol_own, bcol_other, b_rep, whead, targets, err_col, err_row,
                  dx, dmods, grad_own, grad_other, dbias, dhead, dbhead, loss,
                  wqkv, wo, bqkv, bfc1, query, keyed, valued, probs, mixed, branch_a, middle, acted,
                  slope, branch_m, input_a, input_m, s_dqkv, s_dg, s_dya, s_dym, place_own, place_other,
                  out_sems, fill_sems):
    step = pl.program_id(0)
    fills = error_fills(1, err_col, err_row, place_own, fill_sems)

    @pl.when(step == 0)
    def _():
        for copy in fills:
            copy.start()
        assemble(1, own, other, bcol_own, bcol_other, wqkv, wo, bqkv, bfc1)
        dbias[...] = jnp.zeros_like(dbias)
        dhead[...] = jnp.zeros_like(dhead)
        dbhead[...] = jnp.zeros_like(dbhead)
        loss[...] = jnp.zeros_like(loss)

    stacked = dict(mixed=mixed, input_a=input_a, input_m=input_m)
    single = dict(query=query, keyed=keyed, valued=valued, branch_a=branch_a, middle=middle,
                  branch_m=branch_m)
    stash = dict(dqkv=s_dqkv, dg=s_dg, dya=s_dya, dym=s_dym)
    group = x2.shape[0]

    def chain(i):
        rows = pl.ds(pl.multiple_of((step * group + i) * TOK, TOK), TOK)

        def put(name, value, index=None):
            if name == "probs":
                probs[i, index] = value
            elif name == "acted":
                acted[rows, index * HMLP : (index + 1) * HMLP] = value
            elif name == "slope":
                slope[i, :, index * HMLP : (index + 1) * HMLP] = value
            elif name in stacked:
                stacked[name][rows, :] = value
            else:
                single[name][i] = value

        def take(name, index=None):
            if name == "probs":
                return probs[i, index]
            if name == "slope":
                return slope[i, :, index * HMLP : (index + 1) * HMLP]
            return single[name][i]

        def mod(j):
            return mods[i, 6 + j : 7 + j, :]

        def mods_out(j, value):
            dmods[i, j : j + 1, :] = value

        def bias(name, start, value):
            at = BIAS[name] + start
            dbias[:, at : at + value.shape[1]] += token_sum(value.astype(f32))

        result = []
        yield from layer_forward(x2[i], mod, own, other, wqkv, wo, bqkv[...], bfc1[...], vector(b_rep, D),
                                 vector(b_rep, START_FC2 + D), put, result)
        yield
        normed, inv_std = normalize(result[0])
        input_f = (normed * (1.0 + mod(7)) + mod(6)).astype(bf16)
        bhead = jnp.sum(
            jnp.where(diagonal(PV), b_rep[:, START_HEAD : START_HEAD + PV], 0.0), 1, keepdims=True
        )
        yield
        miss = dot(whead[0], input_f, NT) + bhead - targets[i]
        loss[...] += jnp.sum(miss * miss, 0, keepdims=True)
        grad_pred = (2.0 * miss).astype(bf16)
        yield
        dhead[...] += dot(grad_pred, input_f)
        dbhead[...] += jnp.sum(grad_pred.astype(f32), 1, keepdims=True)
        grad_input = dot(grad_pred, whead[0], TN)
        yield
        mods_out(6, token_sum(grad_input))
        mods_out(7, token_sum(grad_input * normed))
        grad = norm_back(grad_input * (1.0 + mod(7)), normed, inv_std)
        result = []
        yield from layer_backward(grad, x2[i], mod, own, other, wqkv, wo, take, rows, stash, mods_out, bias,
                                  result)
        dx[i] = result[0]

    run_steps([chain(i) for i in range(group)], LAG)

    @pl.when(step == pl.num_programs(0) - 1)
    def _():
        weight_grads(input_a, input_m, mixed, acted, stash, (place_own, place_other),
                     (grad_own, grad_other), out_sems, fills)


def last_kernel(dx, mods, own, other, bcol_own, bcol_other, b_rep, xt, wpatch, pos,
                dbias1, dhead, dbhead, loss, dmods1, err_col, err_row,
                query, keyed, valued, probs, branch_a, middle, slope, branch_m, mixed, acted,
                dmods, grad_own, grad_other, pay_own, pay_other,
                wqkv, wo, bqkv, bfc1, a_input_a, a_input_m, a_mixed, a_acted, s_dqkv, s_dg, s_dya, s_dym,
                dbias, sems, place_own, place_other, out_sems, fill_sems):
    step = pl.program_id(0)
    pairs = ((mixed, a_mixed), (acted, a_acted))
    copies = [pltpu.make_async_copy(src, dst, sems.at[i]) for i, (src, dst) in enumerate(pairs)]
    fills = error_fills(0, err_col, err_row, place_own, fill_sems)

    @pl.when(step == 0)
    def _():
        assemble(0, own, other, bcol_own, bcol_other, wqkv, wo, bqkv, bfc1)
        dbias[...] = jnp.zeros_like(dbias)
        pay_own[...] = jnp.zeros_like(pay_own)
        for copy in copies + fills:
            copy.start()

    rows = pl.ds(pl.multiple_of(step * TOK, TOK), TOK)
    single = dict(query=query, keyed=keyed, valued=valued, branch_a=branch_a, middle=middle,
                  branch_m=branch_m)

    def take(name, index=None):
        if name == "probs":
            return probs[0, index]
        if name == "slope":
            return slope[0, :, index * HMLP : (index + 1) * HMLP]
        return single[name][0]

    def mods_out(j, value):
        dmods[0, j : j + 1, :] = value

    def bias(name, start, value):
        at = BIAS[name] + start
        dbias[:, at : at + value.shape[1]] += token_sum(value.astype(f32))

    stash = dict(dqkv=s_dqkv, dg=s_dg, dya=s_dya, dym=s_dym)
    result = []
    x = dot(xt[0], wpatch[0], TN) + vector(b_rep, START_PATCH) + pos[...]
    run_steps([layer_backward(dx[0], x, lambda j: mods[0, j : j + 1, :], own, other, wqkv, wo,
                              take, rows, stash, mods_out, bias, result, (a_input_a, a_input_m))], 0)
    (grad,) = result
    grad = grad.astype(bf16)
    pay_own[PAY_PATCH : PAY_PATCH + PV, :] += dot(xt[0], grad)
    pay_own[PAY_BPATCH : PAY_BPATCH + 1, :] += token_sum(grad.astype(f32))
    dmods[0, 6 : 6 + 8, :] = dmods1[0]
    rounded = dmods[0].astype(bf16).astype(f32)
    dmods[0] = rounded
    pay_own[PAY_COND : PAY_COND + 14, :] += rounded

    @pl.when(step == pl.num_programs(0) - 1)
    def _():
        for copy in copies:
            copy.wait()
        weight_grads(a_input_a, a_input_m, a_mixed, a_acted, stash, (place_own, place_other),
                     (grad_own, grad_other), out_sems, fills)
        pay_own[PAY_HEAD : PAY_HEAD + PV, :] = dhead[...]
        for layer, values in enumerate((dbias, dbias1)):
            pay_own[PAY_PROJ + layer : PAY_PROJ + layer + 1, :] = values[:, BIAS["proj"] : BIAS["proj"] + D]
            pay_own[PAY_FC2 + layer : PAY_FC2 + layer + 1, :] = values[:, BIAS["fc2"] : BIAS["fc2"] + D]
        head_line = jnp.sum(jnp.where(diagonal(PV), dbhead[...], 0.0), 0, keepdims=True)
        pay_own[PAY_BHEAD : PAY_BHEAD + 1, :] = jnp.concatenate(
            [head_line, jnp.sum(loss[...], 1, keepdims=True), jnp.zeros((1, D - PV - 1), f32)], 1
        )
        pay_other[...] = pay_own[...]
        for side, out in enumerate((pay_own, pay_other)):
            for layer, values in enumerate((dbias, dbias1)):
                write_bcol(values, side, out, layer)
        for out in (pay_own, pay_other):
            out[PAY_BCOL + 8 :, :] = jnp.zeros((PAY_ROWS - PAY_BCOL - 8, D), f32)


def per_latent(*shape, group=1):
    zeros = (0,) * len(shape)
    return pl.BlockSpec((group,) + shape, lambda n: (n,) + zeros)


def fixed(*shape):
    zeros = (0,) * len(shape)
    return pl.BlockSpec(shape, lambda n: zeros, pipeline_mode=pl.Buffered(1))


def params():
    return pltpu.CompilerParams(dimension_semantics=("arbitrary",), vmem_limit_bytes=62 * 2**20)


SAVED = [
    ("query", (TOK, D), bf16), ("keyed", (TOK, D), bf16), ("valued", (TOK, D), bf16),
    ("probs", (HEADS, TOK, TOK), f32), ("branch_a", (TOK, D), f32), ("middle", (TOK, D), f32),
    ("slope", (TOK, MLP), f32), ("branch_m", (TOK, D), f32), ("mixed", (TOK, D), bf16),
    ("acted", (TOK, MLP), bf16),
]
BOTH = COL_S + ROW_S
GRAD_SHAPES = [(BOTH, D), (BOTH, D)]
WEIGHT_SCRATCH = [pltpu.VMEM((D, 3 * D), bf16), pltpu.VMEM((D, D), bf16),
                  pltpu.VMEM((1, 3 * D), f32), pltpu.VMEM((1, MLP), f32)]


def weight_specs():
    return [fixed(D, GATH), fixed(D, GATH), fixed(L, COL_S), fixed(L, COL_S), fixed(1, NBR)]


def stash_scratch(count):
    rows = count * TOK
    return [pltpu.VMEM((rows, 3 * D), bf16), pltpu.VMEM((rows, MLP), bf16),
            pltpu.VMEM((rows, D), bf16), pltpu.VMEM((rows, D), bf16)]


def place_scratch():
    return [pltpu.VMEM(shape, f32) for shape in GRAD_SHAPES] + [pltpu.SemaphoreType.DMA((8,)), pltpu.SemaphoreType.DMA((2,))]


def cost(flops, nbytes, count):
    return pl.CostEstimate(flops=int(flops * count), bytes_accessed=int(nbytes * count),
                           transcendentals=int(2e6 * count))


def run_forward(core, full, xt, mods, full_io, pos, weights):
    count = xt.shape[0]
    outs = SAVED + [("x2", (TOK, D), f32)]
    return pl.pallas_call(
        forward_kernel,
        grid=(count // GROUP,),
        in_specs=[pl.BlockSpec(memory_space=pltpu.SMEM), pl.BlockSpec(memory_space=pl.ANY), per_latent(PV, TOK, group=GROUP), per_latent(14, D, group=GROUP),
                  pl.BlockSpec((1, PV, D), lambda n: (0, 0, 0)), fixed(TOK, D)] + weight_specs(),
        out_specs=[per_latent(*shape, group=GROUP) for _, shape, _ in outs]
        + [pl.BlockSpec(memory_space=pl.ANY)] * 2,
        out_shape=[jax.ShapeDtypeStruct((count,) + shape, kind) for _, shape, kind in outs]
        + [jax.ShapeDtypeStruct((full.shape[0], full.shape[2], GATH), bf16)] * 2,
        scratch_shapes=WEIGHT_SCRATCH + [pltpu.VMEM((full.shape[0], full.shape[2], GATH), bf16)] * 2
        + [pltpu.SemaphoreType.DMA((4,))],
        compiler_params=params(),
        cost_estimate=cost(1.0e9, 6e6, count),
        name="forward_first",
    )(core, full, xt, mods, full_io, pos, *weights)


def run_middle(x2, mods, weights, full_io, targets, err_col, err_row):
    count = x2.shape[0]
    rows = count * TOK
    outs = [((count, TOK, D), per_latent(TOK, D, group=GROUP)), ((count, 8, D), per_latent(8, D, group=GROUP))]
    outs += [(shape, pl.BlockSpec(memory_space=pl.ANY)) for shape in GRAD_SHAPES]
    outs += [(shape, fixed(*shape)) for shape in ((1, BIAS_WIDTH), (PV, D), (PV, 1), (1, TOK))]
    return pl.pallas_call(
        middle_kernel,
        grid=(count // GROUP,),
        in_specs=[per_latent(TOK, D, group=GROUP), per_latent(14, D, group=GROUP)] + weight_specs()
        + [pl.BlockSpec((1, PV, D), lambda n: (1, 0, 0)), per_latent(PV, TOK, group=GROUP)]
        + [pl.BlockSpec(memory_space=pl.ANY)] * 2,
        out_specs=[spec for _, spec in outs],
        out_shape=[jax.ShapeDtypeStruct(shape, f32) for shape, _ in outs],
        scratch_shapes=WEIGHT_SCRATCH
        + [pltpu.VMEM((GROUP, TOK, D), bf16)] * 3
        + [pltpu.VMEM((GROUP, HEADS, TOK, TOK), f32), pltpu.VMEM((rows, D), bf16),
           pltpu.VMEM((GROUP, TOK, D), f32), pltpu.VMEM((GROUP, TOK, D), f32), pltpu.VMEM((rows, MLP), bf16),
           pltpu.VMEM((GROUP, TOK, MLP), f32), pltpu.VMEM((GROUP, TOK, D), f32),
           pltpu.VMEM((rows, D), bf16), pltpu.VMEM((rows, D), bf16)]
        + stash_scratch(count) + place_scratch(),
        compiler_params=params(),
        cost_estimate=cost(3.2e9, 3e6, count),
        name="layer_second",
    )(x2, mods, *weights, full_io, targets, err_col, err_row)


def run_last(dx, mods, weights, xt, full_io, pos, smalls, dmods1, err_col, err_row, saved):
    count = dx.shape[0]
    rows = count * TOK
    outs = [((count, 14, D), per_latent(14, D))]
    outs += [(shape, pl.BlockSpec(memory_space=pl.ANY)) for shape in GRAD_SHAPES]
    outs += [(shape, fixed(*shape)) for shape in ((PAY_ROWS, D), (PAY_ROWS, D))]
    return pl.pallas_call(
        last_kernel,
        grid=(count,),
        in_specs=[per_latent(TOK, D), per_latent(14, D)] + weight_specs()
        + [per_latent(PV, TOK), pl.BlockSpec((1, PV, D), lambda n: (0, 0, 0)), fixed(TOK, D)]
        + [fixed(*shape) for shape in ((1, BIAS_WIDTH), (PV, D), (PV, 1), (1, TOK))] + [per_latent(8, D)]
        + [pl.BlockSpec(memory_space=pl.ANY)] * 2
        + [per_latent(*shape) for _, shape, _ in SAVED[:-2]] + [pl.BlockSpec(memory_space=pl.ANY)] * 2,
        out_specs=[spec for _, spec in outs],
        out_shape=[jax.ShapeDtypeStruct(shape, f32) for shape, _ in outs],
        scratch_shapes=WEIGHT_SCRATCH
        + [pltpu.VMEM((rows, D), bf16)] * 3 + [pltpu.VMEM((rows, MLP), bf16)]
        + stash_scratch(count) + [pltpu.VMEM((1, BIAS_WIDTH), f32), pltpu.SemaphoreType.DMA((2,))]
        + place_scratch(),
        compiler_params=params(),
        cost_estimate=cost(2.2e9, 8e6, count),
        name="backward_first",
    )(dx, mods, *weights, xt, full_io, pos, *smalls, dmods1, err_col, err_row,
      *saved[:-2], *[v.reshape(rows, -1) for v in saved[-2:]])


PACK = 128
WIDE = 3 * D


def split3(values):
    high = values.astype(bf16)
    rest = values - high.astype(f32)
    mid = rest.astype(bf16)
    low = (rest - mid.astype(f32)).astype(bf16)
    return high, mid, low


def narrow_dot(small, big, dims):
    parts = split3(small)
    high, mid, low = split3(big)
    first = dot(jnp.concatenate(parts, 0), high, dims)
    second = dot(jnp.concatenate(parts[:2], 0), mid, dims)
    third = dot(parts[0], low, dims)
    r = small.shape[0]
    return first[:r] + ((first[r : 2 * r] + second[:r]) + (first[2 * r :] + second[r:] + third))


def outer(left, right):
    l1, l2, l3 = split3(left)
    r1, r2, r3 = split3(right)
    return dot(
        jnp.concatenate([l1, l1, l2, l2, l1, l3], 0), jnp.concatenate([r1, r2, r1, r2, r3, r1], 0), TN
    )


CHUNKS = [(448 * k, 448) for k in range(3)] + [(COL_S + 480 * k, 480) for k in range(2)]


def layer_chunks(layer, err_col, err_row):
    for at, size in CHUNKS:
        ref, start = (err_col, at) if at < COL_S else (err_row, at - COL_S)
        yield ref.at[layer, pl.ds(start, size), :], pl.ds(at, size)


def project(layer, own, got, fac_col, fac_row, mat, left_col, left_row, v_own, v_got, sems, out_sems):
    loads, stores = [], []
    for k, (at, size) in enumerate(CHUNKS):
        rows = pl.ds(at, size)
        loads.append([pltpu.make_async_copy(src.at[rows, :], dst.at[rows, :], sems.at[2 * k + i])
                      for i, (src, dst) in enumerate(((own, v_own), (got, v_got)))])
        stores.append(pltpu.make_async_copy(v_own.at[rows, :], mat.at[rows, :], out_sems.at[k]))
        for copy in loads[-1]:
            copy.start()
    left_row[...] = jnp.zeros_like(left_row)
    total = None
    for (at, size), copies, store in zip(CHUNKS, loads, stores):
        for copy in copies:
            copy.wait()
        matrix = v_own[at : at + size, :] + v_got[at : at + size, :]
        v_own[at : at + size, :] = matrix
        store.start()
        if at < COL_S:
            part = narrow_dot(fac_col[layer][:, at : at + size], matrix, NN)
            total = part if total is None else total + part
        else:
            left_row[:, at - COL_S : at - COL_S + size] = narrow_dot(fac_row[layer], matrix, NT)
    left_col[...] = total
    for store in stores:
        store.wait()


ANY = pl.BlockSpec(memory_space=pl.ANY)
VMEM = pl.BlockSpec(memory_space=pltpu.VMEM)
SMEM = pl.BlockSpec(memory_space=pltpu.SMEM)
PROJECT_SCRATCH = [pltpu.VMEM((BOTH, D), f32)] * 2 + [
    pltpu.SemaphoreType.DMA((2 * len(CHUNKS),)), pltpu.SemaphoreType.DMA((len(CHUNKS),))]


def large():
    return pltpu.CompilerParams(vmem_limit_bytes=62 * 2**20)


def shapes_of(shapes):
    return [jax.ShapeDtypeStruct(shape, f32) for shape in shapes]


def run_project_second(own, got, fac_col, fac_row):
    return pl.pallas_call(
        lambda *refs: project(1, *refs),
        in_specs=[ANY] * 2 + [VMEM] * 2,
        out_specs=[ANY, VMEM, VMEM],
        out_shape=shapes_of([(BOTH, D), (RANK, D), (RANK, WIDE)]),
        scratch_shapes=PROJECT_SCRATCH,
        compiler_params=large(),
        cost_estimate=pl.CostEstimate(flops=int(1e9), bytes_accessed=int(1.5e7), transcendentals=0),
        name="left_second",
    )(own, got, fac_col, fac_row)


def exchange_kernel(block, place, dmods, full_cond, cond, sent):
    n_dp = sent.shape[0]
    count = dmods.shape[0]
    line = jnp.concatenate([dmods[:, j, :] for j in range(14)], 1)
    grad_act = dot(line.astype(bf16), full_cond[...], NT)
    cond_own = cond[pl.ds(pl.multiple_of(place[0] * count, count), count), :]
    gate = 1.0 / (1.0 + jnp.exp(-cond_own))
    grad_cond = grad_act * (gate * (1.0 + cond_own * (1.0 - gate)))
    sent[:, :count, :] = jnp.broadcast_to(grad_cond[None], (n_dp, count, D))
    for j in range(n_dp):
        sent[j, count:, :] = jnp.concatenate(
            [line[:, j * block : (j + 1) * block], jnp.zeros((count, D - block), f32)], 1
        )


def run_exchange(n_dp, place, dmods, full_cond, cond):
    return pl.pallas_call(
        lambda *refs: exchange_kernel(N_MODS // n_dp, *refs),
        in_specs=[SMEM, VMEM, VMEM, VMEM],
        out_shape=jax.ShapeDtypeStruct((n_dp, 2 * dmods.shape[0], D), f32),
        compiler_params=large(),
        name="modulation_rows",
    )(place, dmods, full_cond, cond)


def project_first_kernel(own, got, fac_col, fac_row,
                         left_col1, left_row1, pay_own, pay_got, err_io, fac_io,
                         mat, mat_io, sent, left_col, left_row, *scratch):
    project(0, own, got, fac_col, fac_row, mat, left_col, left_row, *scratch)
    share = sent.shape[1]
    pay = pay_own[...] + pay_got[...]
    left_io = []
    for index in range(2):
        matrix = pay[index * PV : (index + 1) * PV] + err_io[index]
        mat_io[index] = matrix
        left_io.append(dot_full(fac_io[index], matrix))
    sent[...] = jnp.zeros_like(sent)
    tall = (left_row, left_row1)
    for column in range(RANK):
        pick = slice(column, column + 1)
        lines = [tall[i % 2][pick, (i // 2) * D : (i // 2 + 1) * D] for i in (0, 1)]
        lines += [left_col[pick, :], left_col1[pick, :], left_io[0][pick], left_io[1][pick]]
        lines += [tall[i % 2][pick, (i // 2) * D : (i // 2 + 1) * D] for i in (2, 3, 4, 5)]
        for extra in range(6):
            at = column * 6 + extra
            if at < SMALL_ROWS:
                lines.append(pay[PAY_PROJ + at : PAY_PROJ + at + 1])
        for slot, line in enumerate(lines):
            at = column * 16 + slot
            sent[at // share, at % share : at % share + 1, :] = line


def run_project_first(n_dp, own, got, fac_col, fac_row, left_col1, left_row1,
                      pay_own, pay_got, err_io, fac_io):
    return pl.pallas_call(
        project_first_kernel,
        in_specs=[ANY] * 2 + [VMEM] * 8,
        out_specs=[ANY, VMEM, VMEM],
        out_shape=shapes_of([(BOTH, D), (2, PV, D), (n_dp, PACK // n_dp, D)]),
        scratch_shapes=[pltpu.VMEM((RANK, D), f32), pltpu.VMEM((RANK, WIDE), f32)] + PROJECT_SCRATCH,
        compiler_params=large(),
        cost_estimate=pl.CostEstimate(flops=int(1e9), bytes_accessed=int(1.5e7), transcendentals=0),
        name="left_first",
    )(own, got, fac_col, fac_row, left_col1, left_row1, pay_own, pay_got, err_io, fac_io)


TIME_ROWS = FREQ + D + 8


def modulation_kernel(block, core, got, act_half, features, first, first_act, full_time, labels,
                      cond_mine, cond_their, time_part, table_part):
    n_dp = got.shape[0]
    count = got.shape[1] // 2
    half = block // 2
    grad_cond = got[:, :count, :].reshape(n_dp * count, D)
    cols = got[:, count : 2 * count, :].reshape(n_dp * count, D)
    left, right = cols[:, :half].astype(bf16), cols[:, half:block].astype(bf16)
    is_first = core[0] == 0
    grad_left = dot(act_half[...], left, TN)
    grad_right = dot(act_half[...], right, TN)
    cond_mine[...] = jnp.where(is_first, grad_left, grad_right)
    cond_their[...] = jnp.where(is_first, grad_right, grad_left)
    grad_second = grad_cond.astype(bf16)
    gate = 1.0 / (1.0 + jnp.exp(-first[...]))
    slope = gate * (1.0 + first[...] * (1.0 - gate))
    grad_first = (dot(grad_second, full_time[FREQ:, :], NT) * slope).astype(bf16)
    time_part[:FREQ, :] = dot(features[...], grad_first, TN)
    time_part[FREQ : FREQ + D, :] = dot(first_act[...], grad_second, TN)
    time_part[FREQ + D :, :] = jnp.concatenate(
        [token_sum(grad_first.astype(f32)), token_sum(grad_second.astype(f32)), jnp.zeros((6, D), f32)], 0
    )
    onehot = (labels[...] == lax.broadcasted_iota(jnp.int32, (n_dp * count, CLASSES), 1)).astype(f32).astype(bf16)
    high, mid, low = split3(grad_cond)
    table_part[...] = dot(high, onehot, TN) + (dot(mid, onehot, TN) + dot(low, onehot, TN))


def run_modulation(core, got, act_half, features, first, first_act, full_time, labels):
    half = N_MODS // got.shape[0] // 2
    shapes = [(D, half), (D, half), (TIME_ROWS, D), (D, CLASSES)]
    vmem = pl.BlockSpec(memory_space=pltpu.VMEM)
    return pl.pallas_call(
        lambda *refs: modulation_kernel(2 * half, *refs),
        in_specs=[pl.BlockSpec(memory_space=pltpu.SMEM)] + [vmem] * 7,
        out_shape=[jax.ShapeDtypeStruct(shape, f32) for shape in shapes],
        compiler_params=pltpu.CompilerParams(vmem_limit_bytes=62 * 2**20),
        name="modulation_gradients",
    )(core, got, act_half, features, first, first_act, full_time, labels)


COL_ROWS = 4 * RANK
ROW_AT = L * COL_ROWS
IO_AT = ROW_AT + L * RANK
EXTRA_AT = IO_AT + 2 * RANK


def cond_top(rows):
    return -(-((rows + 1) // 2) // 8) * 8


def ortho(packed, left_col, left_row, left_io):
    columns = []
    blank = jnp.zeros((4, D), f32)
    for index in range(RANK):
        block = packed[index]
        column = jnp.concatenate(
            [block[0:6], jnp.concatenate([block[6:8], blank], 0), jnp.concatenate([block[8:10], blank], 0)], 1
        )
        for earlier in columns:
            column = column - jnp.sum(earlier * column, -1, keepdims=True) * earlier
        column = column * lax.rsqrt(jnp.sum(column * column, -1, keepdims=True) + ortho_eps)
        for layer in range(L):
            left_row[layer, index : index + 1, :] = column[layer : layer + 1]
            left_col[layer, index : index + 1, :] = column[2 + layer : 3 + layer, :D]
            left_io[layer, index : index + 1, :] = column[4 + layer : 5 + layer, :D]
        columns.append(column)


def total_squares(values):
    return jnp.sum(values * values, keepdims=True)


def rows_kernel(cond_own, cond_got, table_own, table_got, sent, table_share, sums):
    cond_grad = cond_own[...] + cond_got[...]
    table = table_own[...] + table_got[...]
    table_share[...] = table
    sums[...] = jnp.concatenate([total_squares(cond_grad), total_squares(table), jnp.zeros((1, D - 2), f32)], 1)
    n_dp = sent.shape[0]
    rows, half = D // n_dp, cond_grad.shape[1]
    top = cond_top(rows)
    for j in range(n_dp):
        piece = cond_grad[j * rows : (j + 1) * rows]
        sent[j, : min(top, rows), :half] = piece[:top]
        if rows > top:
            sent[j, : rows - top, half : 2 * half] = piece[top:]


def run_rows(n_dp, cond_own, cond_got, table_own, table_got):
    return pl.pallas_call(
        rows_kernel,
        out_shape=shapes_of([(n_dp, cond_top(D // n_dp), D), table_own.shape, (1, D)]),
        compiler_params=large(),
        name="modulation_sums",
    )(cond_own, cond_got, table_own, table_got)


def mat_loads(mats, places, sems):
    return [[pltpu.make_async_copy(mat.at[pl.ds(at, size), :], place.at[pl.ds(at, size), :],
                                   sems.at[layer * len(CHUNKS) + k]) for k, (at, size) in enumerate(CHUNKS)]
            for layer, (mat, place) in enumerate(zip(mats, places))]


def right_kernel(packed, mat0, mat1, mat_io, sums, sent, left_col, left_row, left_io, flat, v0, v1, sems):
    loads = mat_loads((mat0, mat1), (v0, v1), sems)
    for copies in loads:
        for copy in copies:
            copy.start()
    ortho(packed, left_col, left_row, left_io)
    for copies in loads:
        for copy in copies:
            copy.wait()
    for layer, mat in enumerate((v0, v1)):
        right = narrow_dot(left_col[layer], mat[:COL_S, :], NT)
        for piece in range(4):
            wide = min(D, COL_S - piece * D)
            at = layer * COL_ROWS + piece * RANK
            if wide < D:
                flat[at : at + RANK, :] = jnp.zeros((RANK, D), f32)
            flat[at : at + RANK, :wide] = right[:, piece * D : piece * D + wide]
        at = ROW_AT + layer * RANK
        flat[at : at + RANK, :] = narrow_dot(left_row[layer][:, :ROW_S], mat[COL_S:, :], NN)
        at = IO_AT + layer * RANK
        flat[at : at + RANK, :] = jnp.zeros((RANK, D), f32)
        flat[at : at + RANK, :PV] = dot_full(left_io[layer], mat_io[layer], NT)
    flat[EXTRA_AT:, :] = jnp.zeros((PACK - EXTRA_AT, D), f32)
    flat[EXTRA_AT : EXTRA_AT + 1, :] = sums[...]
    sent[...] = flat[...].reshape(sent.shape)


def run_right(n_dp, packed, mats, mat_io, sums):
    return pl.pallas_call(
        right_kernel,
        in_specs=[VMEM, ANY, ANY, VMEM, VMEM],
        out_shape=shapes_of([(n_dp, PACK // n_dp, D), (L, RANK, D), (L, RANK, WIDE), (2, RANK, D)]),
        scratch_shapes=[pltpu.VMEM((PACK, D), f32), pltpu.VMEM((BOTH, D), f32), pltpu.VMEM((BOTH, D), f32),
                        pltpu.SemaphoreType.DMA((L * len(CHUNKS),))],
        compiler_params=large(),
        name="right_factors",
    )(packed, *mats, mat_io, sums)


def norm_kernel(packed, left_packed, left_col, left_row, left_io, time_own, time_got,
                right_col, right_row, right_io, parts, brep_grad, bcol_grad):
    for layer in range(L):
        for piece in range(4):
            wide = min(D, COL_S - piece * D)
            at = layer * COL_ROWS + piece * RANK
            right_col[layer, :, piece * D : piece * D + wide] = packed[at : at + RANK, :wide]
        at = ROW_AT + layer * RANK
        right_row[layer] = packed[at : at + RANK, :]
        at = IO_AT + layer * RANK
        right_io[layer] = packed[at : at + RANK, :PV]

    def small(at):
        row = at - PAY_PROJ
        return left_packed[row // 6, 10 + row % 6 : 11 + row % 6, :]

    time_bias = time_own[FREQ + D :, :] + time_got[FREQ + D :, :]
    lines = [small(PAY_PROJ + row) for row in range(4)] + [small(PAY_COND + row) for row in range(14)]
    lines += [time_bias[0:1], time_bias[1:2], small(PAY_BPATCH), small(PAY_BHEAD)[:, :PV]]
    whole = jnp.zeros((1, 1), f32)
    for row, line in enumerate(lines):
        brep_grad[:, row * D : row * D + line.shape[1]] = line
        whole = whole + total_squares(line)
    split = jnp.zeros((1, 1), f32)
    for layer in range(L):
        line = jnp.concatenate([small(PAY_BCOL + 4 * layer + row) for row in range(4)], 1)[:, :COL_S]
        bcol_grad[layer : layer + 1, :] = line
        split = split + total_squares(line)
    whole = whole + total_squares(time_own[: FREQ + D, :] + time_got[: FREQ + D, :])

    def gram(left, right):
        return jnp.sum(dot_full(left, left, NT) * dot_full(right, right, NT), keepdims=True)

    for layer in range(L):
        split = split + gram(left_col[layer], right_col[layer]) + gram(left_row[layer], right_row[layer])
        whole = whole + gram(left_io[layer], right_io[layer])
    sums = packed[EXTRA_AT : EXTRA_AT + 1, :]
    split = split + sums[:, 0:1]
    whole = whole + sums[:, 1:2]
    loss = small(PAY_BHEAD)[:, PV : PV + 1]
    parts[...] = jnp.concatenate([split, whole, loss, jnp.zeros((1, 125), f32)], 1)


def run_norm(packed, left_packed, lefts, time_own, time_got):
    shapes = [(L, RANK, COL_S), (L, RANK, D), (2, RANK, PV), (1, 128), (1, NBR), (L, COL_S)]
    return pl.pallas_call(
        norm_kernel,
        out_shape=[jax.ShapeDtypeStruct(shape, f32) for shape in shapes],
        compiler_params=pltpu.CompilerParams(vmem_limit_bytes=62 * 2**20),
        name="gradient_norm",
    )(packed, left_packed, *lefts, time_own, time_got)


def error_kernel(mat0, mat1, mat_io, left_col, left_row, left_io, right_col, right_row, right_io,
                 err_col, err_row, err_io, v0, v1, sems, out_sems):
    loads = mat_loads((mat0, mat1), (v0, v1), sems)
    for copies in loads:
        for copy in copies:
            copy.start()
    stores = []
    for layer, place in enumerate((v0, v1)):
        for k, ((at, size), (target, rows)) in enumerate(zip(CHUNKS, layer_chunks(layer, err_col, err_row))):
            if at < COL_S:
                approx = outer(right_col[layer][:, at : at + size], left_col[layer])
            else:
                approx = outer(left_row[layer][:, at - COL_S : at - COL_S + size], right_row[layer])
            loads[layer][k].wait()
            place[at : at + size, :] = place[at : at + size, :] - approx
            store = pltpu.make_async_copy(place.at[rows, :], target, out_sems.at[layer * len(CHUNKS) + k])
            store.start()
            stores.append(store)
        err_io[layer] = mat_io[layer] - outer(right_io[layer], left_io[layer])
    for store in stores:
        store.wait()


def run_error(mats, mat_io, lefts, rights):
    return pl.pallas_call(
        error_kernel,
        in_specs=[ANY, ANY] + [VMEM] * 7,
        out_specs=[ANY, ANY, VMEM],
        out_shape=shapes_of([(L, COL_S, D), (L, ROW_S, D), (2, PV, D)]),
        scratch_shapes=[pltpu.VMEM((BOTH, D), f32), pltpu.VMEM((BOTH, D), f32),
                        pltpu.SemaphoreType.DMA((L * len(CHUNKS),)), pltpu.SemaphoreType.DMA((L * len(CHUNKS),))],
        compiler_params=large(),
        name="next_errors",
    )(*mats, mat_io, *lefts, *rights)


def own_columns(values, first, count):
    across = lax.broadcasted_iota(jnp.int32, (count, D), 1)
    down = lax.broadcasted_iota(jnp.int32, (count, D), 0)
    pick = (across == down + first).astype(f32).astype(bf16)
    high, mid, low = split3(values)
    return dot(high, pick, NT) + (dot(mid, pick, NT) + dot(low, pick, NT))


def update_kernel(core, parts, parts_got, left_col, right_col, right_row, left_row, right_io, left_io,
                  cond_own, cond_got, time_grad, table_grad, bcol_grad, brep_grad,
                  w_col, w_row, w_cond, w_time, w_io, w_table, b_col, b_rep,
                  m_col, m_row, m_cond, m_time, m_io, m_table, m_bcol, m_brep,
                  loss, clip, n_col, n_row, n_cond, n_time, n_io, n_table, n_bcol, n_brep,
                  v_col, v_row, v_cond, v_time, v_io, v_table, v_bcol, v_brep):
    clip_norm = jnp.sqrt(parts[:, 0:1] + parts_got[:, 0:1] + parts[:, 1:2])
    scaling = jnp.minimum(1.0, clip_limit / clip_norm)
    loss[...] = parts[:, 2:3]
    clip[...] = clip_norm

    def advance(weight, momentum, gradient):
        moved = momentum_decay * momentum + scaling * gradient
        return weight - learn_rate * moved, moved

    n_dp = cond_own.shape[0]
    rows = w_cond.shape[0]
    at = core[1] * rows
    for layer in range(L):
        n_col[layer], v_col[layer] = advance(
            w_col[layer], m_col[layer], outer(own_columns(left_col[layer], at, rows), right_col[layer]))
        n_row[layer], v_row[layer] = advance(
            w_row[layer], m_row[layer],
            outer(own_columns(right_row[layer], at, rows), left_row[layer][:, :ROW_S]))
        n_io[layer], v_io[layer] = advance(
            w_io[layer], m_io[layer], outer(right_io[layer], own_columns(left_io[layer], at, rows)))
    half = N_MODS // n_dp // 2
    top = cond_top(rows)
    is_first = core[0] == 0
    pieces = []
    for j in range(n_dp):
        mine, theirs = cond_own[j], cond_got[j]
        for pair in ((mine, theirs), (theirs, mine)):
            block = jnp.where(is_first, pair[0], pair[1])
            if rows > top:
                block = jnp.concatenate([block[:top, :half], block[: rows - top, half : 2 * half]], 0)
            else:
                block = block[:rows, :half]
            pieces.append(block)
    n_cond[...], v_cond[...] = advance(w_cond[...], m_cond[...], jnp.concatenate(pieces, 1))
    n_time[...], v_time[...] = advance(w_time[...], m_time[...], time_grad[...])
    n_table[...], v_table[...] = advance(w_table[...], m_table[...], table_grad[...])
    n_bcol[...], v_bcol[...] = advance(b_col[...], m_bcol[...], bcol_grad[...])
    n_brep[...], v_brep[...] = advance(b_rep[...], m_brep[...], brep_grad[...])


def run_update(core, grads, weights, momenta):
    vmem = pl.BlockSpec(memory_space=pltpu.VMEM)
    shapes = [(1, 1), (1, 1)] + [v.shape for v in weights] * 2
    return pl.pallas_call(
        update_kernel,
        in_specs=[pl.BlockSpec(memory_space=pltpu.SMEM)] + [vmem] * (len(grads) + 2 * len(weights)),
        out_shape=[jax.ShapeDtypeStruct(shape, f32) for shape in shapes],
        compiler_params=pltpu.CompilerParams(vmem_limit_bytes=62 * 2**20),
        name="weight_update",
    )(core, *grads, *weights, *momenta)


def swap(values):
    return lax.ppermute(values, "tensor", [(0, 1), (1, 0)])


def trade(chunks):
    return lax.all_to_all(chunks, "dp", 0, 0, tiled=True)


def spread(values):
    return trade(jnp.broadcast_to(values[None], (lax.axis_size("dp"),) + values.shape))


def exact_parts(values):
    high = lax.reduce_precision(values, 8, 7)
    mid = lax.reduce_precision(values - high, 8, 7)
    return [part.astype(bf16) for part in (high, mid, (values - high) - mid)]


def on_device(
    latents, gauss_noise, time_steps, labels, targets,
    w_col, w_row, w_cond, w_time, w_io, class_table, b_col, b_rep,
    mom_col, mom_row, mom_cond, mom_time, mom_io, mom_table, mom_bcol, mom_brep,
    err_col, err_row, err_io, fac_col, fac_row, fac_io,
):
    n_dp = lax.axis_size("dp")
    index_dp = lax.axis_index("dp")
    index_t = lax.axis_index("tensor")
    core = jnp.stack([index_t, index_dp]).astype(jnp.int32)
    first_core = index_t == 0
    n_all = labels.shape[0]
    per_dp = latents.shape[0]
    count = per_dp // 2
    rows = w_col.shape[1]

    def flip(values):
        return values.transpose(0, 2, 1)

    def halves(mine, theirs, axis):
        pair = jnp.stack([mine, theirs], axis)
        return jnp.where(first_core, pair, jnp.flip(pair, axis))

    row_sh = flip(w_row)
    shard = jnp.concatenate(
        [piece[layer] for layer in range(L)
         for piece in (w_col[:, :, QKV_S:], row_sh[:, :, HALF:], w_col[:, :, :QKV_S], row_sh[:, :, :HALF])], 1
    ).astype(bf16)
    full = lax.all_gather(shard, ("dp", "tensor"))

    block = N_MODS // n_dp
    half_block = block // 2
    classes = jnp.arange(CLASSES, dtype=jnp.int32)
    onehot_t = classes[:, None] == labels[None, :]
    looked = dot(class_table.astype(bf16), onehot_t.astype(bf16), TN).astype(bf16)
    time_rows = w_time.shape[0]
    sizes = [rows * n_all, time_rows * D, 2 * PV * rows, 3 * per_dp]
    wide = -(-sum(sizes) // 256) * 128
    common = jnp.concatenate(
        [part.reshape(-1) for part in
         (looked, w_time.astype(bf16), flip(w_io).astype(bf16), *exact_parts(time_steps))]
    )
    common = jnp.pad(common, (0, 2 * wide - common.shape[0]))
    common = lax.dynamic_slice_in_dim(common.reshape(2, wide), index_t, 1, 0)
    cond_bf = w_cond.astype(bf16).reshape(rows, n_dp, 2, half_block)
    cond_mine = lax.dynamic_slice_in_dim(cond_bf, index_t, 1, 2)[:, :, 0].transpose(1, 0, 2)
    sent = jnp.concatenate(
        [jnp.broadcast_to(common, (n_dp, wide)), cond_mine.reshape(n_dp, rows * half_block)], 1
    )
    got = trade(sent)
    cond_cols = got[:, wide:].reshape(D, half_block)
    mine = got[:, :wide]
    common = halves(mine, swap(mine), 1).reshape(n_dp, 2 * wide)
    ends = np.cumsum([0] + sizes)
    looked = common[:, : ends[1]].reshape(D, n_all).T
    full_time = common[:, ends[1] : ends[2]].reshape(FREQ + D, D)
    full_io = flip(common[:, ends[2] : ends[3]].reshape(n_dp, 2 * PV, rows).transpose(1, 0, 2).reshape(2, PV, D).transpose(0, 2, 1))
    steps_all = jnp.sum(common[:, ends[3] : ends[4]].reshape(n_dp, 3, per_dp).astype(f32), 1).reshape(n_all)

    features = frequency_features(steps_all).astype(bf16)
    first = dot(features, full_time[:FREQ]) + b_rep[START_FIRST:START_SECOND]
    first_act = jax.nn.silu(first).astype(bf16)
    second = dot(first_act, full_time[FREQ:]) + b_rep[START_SECOND:START_PATCH]
    cond = second + looked.astype(f32)
    cond_act = jax.nn.silu(cond).astype(bf16)
    mods = dot(cond_act, cond_cols).reshape(n_dp * 2, count, half_block)
    mods = lax.all_to_all(mods, ("dp", "tensor"), 0, 0, tiled=True)
    mods = mods.transpose(1, 0, 2).reshape(count, N_MODS)
    mods = (mods + b_rep[START_COND:START_FIRST]).reshape(count, 14, D)
    def half_of(values):
        split = values.reshape((n_dp, 2, count) + values.shape[1:])
        return lax.dynamic_slice_in_dim(split, index_t, 1, 1).reshape((n_dp * count,) + values.shape[1:])

    halves_of = [half_of(v) for v in (cond_act, features, first, first_act)]
    labels_half = half_of(labels)[:, None]
    place = (index_dp * 2 + index_t).astype(jnp.int32).reshape(1)
    full, mods, halves_of, labels_half, core, place = lax.optimization_barrier(
        (full, mods, halves_of, labels_half, core, place)
    )
    full = full.reshape(n_dp, 2, rows, L * GATH)

    def mine_of(values):
        return lax.dynamic_slice_in_dim(values, index_t * count, count, 0)

    steps_own = mine_of(time_steps)[:, None, None]
    xt = (
        (1.0 - steps_own) * flip(mine_of(latents)) + steps_own * flip(mine_of(gauss_noise))
    ).astype(bf16)
    b_line = b_rep[None]
    first_layer = full[:, :, :, :GATH]
    own = lax.dynamic_slice_in_dim(first_layer, index_t, 1, 1).reshape(D, GATH)
    other = lax.dynamic_slice_in_dim(first_layer, 1 - index_t, 1, 1).reshape(D, GATH)
    biases = (b_col, swap(b_col), b_line)
    weights = (own, other, *biases)
    pos = jnp.asarray(position_table())
    *saved, x2, own1, other1 = run_forward(core, full, xt, mods, full_io, pos, weights)
    weights1 = (own1.reshape(D, GATH), other1.reshape(D, GATH), *biases)
    x2, late_cond = lax.optimization_barrier((x2, w_cond))
    full_cond = lax.all_gather(late_cond.astype(bf16), "dp", axis=0, tiled=True)
    err_col_t, err_io_t = flip(err_col), flip(err_io)
    dx, dmods1, own1, oth1, *smalls = run_middle(
        x2, mods, weights1, full_io, flip(mine_of(targets)), err_col_t, err_row
    )
    got1 = swap(oth1)
    dmods, own0, oth0, pay_own, pay_oth = run_last(
        dx, mods, weights, xt, full_io, pos, smalls, dmods1, err_col_t, err_row, saved
    )
    got0, pay_got = swap(oth0), swap(pay_oth)

    rows_got = trade(run_exchange(n_dp, place, dmods, full_cond, cond))
    fac_col_t, fac_row_t, fac_io_t = flip(fac_col), flip(fac_row), flip(fac_io)
    mat1, left_col1, left_row1 = run_project_second(own1, got1, fac_col_t, fac_row_t)
    mat0, mat_io, sent = run_project_first(
        n_dp, own0, got0, fac_col_t, fac_row_t, left_col1, left_row1,
        pay_own, pay_got, err_io_t, fac_io_t
    )
    mats = (mat0, mat1)
    rows_got, sent = lax.optimization_barrier((rows_got, sent))
    share = jnp.sum(trade(sent), 0)

    cond_mine, cond_their, time_own, table_part = run_modulation(core, rows_got, *halves_of, full_time, labels_half)
    share, cond_mine, cond_their, time_own, table_part = lax.optimization_barrier(
        (share, cond_mine, cond_their, time_own, table_part)
    )
    left_packed = spread(share).reshape(RANK, 16, D)
    cond_got, time_got = swap(cond_their), swap(time_own)
    table_own = lax.dynamic_slice_in_dim(table_part, index_dp * rows, rows, 0)
    cond_sent, table_share, sums = run_rows(n_dp, cond_mine, cond_got, table_own, swap(table_own))
    cond_rows = trade(cond_sent)

    sent, left_col, left_row, left_io = run_right(n_dp, left_packed, mats, mat_io, sums)
    time_at = index_dp * time_rows
    time_grad = (
        lax.dynamic_slice_in_dim(time_own, time_at, time_rows, 0)
        + lax.dynamic_slice_in_dim(time_got, time_at, time_rows, 0)
    )
    cond_rows, sent, time_grad = lax.optimization_barrier((cond_rows, sent, time_grad))
    packed = spread(jnp.sum(trade(sent), 0)).reshape(PACK, D)
    cond_rows_got = swap(cond_rows)
    lefts = (left_col, left_row, left_io)
    right_col, right_row, right_io, parts, brep_grad, bcol_grad = run_norm(
        packed, left_packed, lefts, time_own, time_got
    )
    parts_got = swap(parts)
    next_err_col, next_err_row, next_err_io = run_error(mats, mat_io, lefts, (right_col, right_row, right_io))

    olds = (w_col, flip(w_row), w_cond, w_time, flip(w_io), class_table.T, b_col, b_line)
    momenta = (mom_col, flip(mom_row), mom_cond, mom_time, flip(mom_io), mom_table.T, mom_bcol, mom_brep[None])
    loss, clip_norm, *new = run_update(
        core,
        (parts, parts_got, left_col, right_col, right_row, left_row, right_io, left_io,
         cond_rows, cond_rows_got, time_grad, table_share, bcol_grad, brep_grad),
        olds, momenta,
    )

    def outward(col, row, cond, time, io, table, bcol, brep):
        return (col, flip(row), cond, time, flip(io), table.T, bcol, brep[0])

    return (
        loss.reshape(()), clip_norm.reshape(()), *outward(*new[:8]), *outward(*new[8:]),
        flip(next_err_col), next_err_row, flip(next_err_io), flip(right_col), flip(right_row), flip(right_io),
    )


def solution(mesh):
    weights = (
        P(None, "dp", "tensor"), P(None, "tensor", "dp"), P("dp", None), P("dp", None),
        P(None, "dp", None), P(None, "dp"), P(None, "tensor"), P(),
    )
    errors = (P("dp", None, "tensor"), P("dp", "tensor", None), P("dp", None, None))
    factors = (P(None, "tensor", None), P(None, "tensor", None), P())
    rows = P("dp", None, None)
    return jax.shard_map(
        on_device,
        mesh=mesh,
        in_specs=(rows, rows, P("dp"), P(), rows) + weights + weights + errors + factors,
        out_specs=(P(), P()) + weights + weights + errors + factors,
        check_vma=False,
    )
```

```python
import jax
import jax.numpy as jnp
import numpy as np
from jax import lax
from jax.experimental import pallas as pl
from jax.experimental.pallas import tpu as pltpu
from jax.sharding import PartitionSpec as P

D = 384
HEADS = 6
HD = 64
MLP = 1536
NBR = 8080
CLASSES = 1000
FREQ = 256
PV = 16
GRID = 16
L = 2
TOK = 256
RANK = 8
GROUP = 2
AHEAD, MLP_AHEAD, BACK_AHEAD = 2, 2, 3
LAG = 1

norm_eps = 1e-06
ortho_eps = 1e-06
clip_limit = 1.0
momentum_decay = 0.9
learn_rate = 4.0

HALF = D // 2
HMLP = MLP // 2
QKV_S = 3 * HALF
COL_S = QKV_S + HMLP
ROW_S = HALF + HMLP
OFF_W2 = HMLP
OFF_Q = 2 * HMLP
GATH = 2 * HMLP + 4 * HALF

f32 = jnp.float32
bf16 = jnp.bfloat16
highest = lax.Precision.HIGHEST
NN = (((1,), (0,)), ((), ()))
NT = (((1,), (1,)), ((), ()))
TN = (((0,), (0,)), ((), ()))


def dot(left, right, dims=NN):
    return lax.dot_general(left, right, dims, preferred_element_type=f32)


def dot_full(left, right, dims=NN):
    return lax.dot_general(left, right, dims, precision=highest, preferred_element_type=f32)


def position_table():
    quarter = D // 4
    omega = 1.0 / 10000.0 ** (np.arange(quarter, dtype=np.float32) / quarter)
    index = np.arange(TOK)
    across = (index % GRID).astype(np.float32)[:, None] * omega[None, :].astype(np.float32)
    down = (index // GRID).astype(np.float32)[:, None] * omega[None, :].astype(np.float32)
    table = np.concatenate([np.sin(across), np.cos(across), np.sin(down), np.cos(down)], 1)
    return table.astype(np.float32)


def frequency_features(steps):
    half = FREQ // 2
    rates = jnp.exp(-jnp.log(10000.0) * jnp.arange(half, dtype=f32) / half)
    angles = steps[:, None] * rates[None, :]
    return jnp.concatenate([jnp.cos(angles), jnp.sin(angles)], 1)


def normalize(values):
    centered = values - jnp.mean(values, -1, keepdims=True)
    inv_std = lax.rsqrt(jnp.mean(centered * centered, -1, keepdims=True) + norm_eps)
    return centered * inv_std, inv_std


def norm_back(grad, normed, inv_std):
    mean_grad = jnp.mean(grad, -1, keepdims=True)
    mean_mixed = jnp.mean(grad * normed, -1, keepdims=True)
    return inv_std * (grad - mean_grad - normed * mean_mixed)


def token_sum(values):
    return jnp.sum(values, 0, keepdims=True)


START_FC2 = L * D
START_COND = 2 * L * D
N_MODS = (6 * L + 2) * D
START_FIRST = START_COND + N_MODS
START_SECOND = START_FIRST + D
START_PATCH = START_FIRST + 2 * D
START_HEAD = START_FIRST + 3 * D


def assemble(layer, own, other, bcol_own, bcol_other, wqkv, wo, bqkv, bfc1):
    for side, (weights, bias) in enumerate(((own, bcol_own), (other, bcol_other))):
        for head in range(HEADS // 2):
            for part in range(3):
                at = (3 * head + part) * HD
                to = part * D + side * HALF + head * HD
                wqkv[:, to : to + HD] = weights[:, OFF_Q + at : OFF_Q + at + HD]
                bqkv[:, to : to + HD] = bias[layer : layer + 1, at : at + HD]
        wo[:, side * HALF : (side + 1) * HALF] = weights[:, OFF_Q + QKV_S :]
        bfc1[:, side * HMLP : (side + 1) * HMLP] = bias[layer : layer + 1, QKV_S:]


def vector(b_rep, at):
    return b_rep[:, at : at + D]


def head_mask(which):
    lane = lax.broadcasted_iota(jnp.int32, (1, 2 * HD), 1)
    return (lane < HD) if which == 0 else (lane >= HD)


def keep(values, mask):
    return jnp.where(mask, values, jnp.zeros_like(values))


def gelu_parts(pre):
    squared = pre * pre
    coef = np.float32(np.sqrt(2.0 / np.pi))
    tanh = jnp.tanh(pre * (coef + np.float32(coef * 0.044715) * squared))
    half = 0.5 * (1.0 + tanh)
    slope = half + (0.5 * pre) * (1.0 - tanh * tanh) * (
        coef + np.float32(3.0 * 0.044715 * coef) * squared
    )
    return (pre * half).astype(bf16), slope


def ahead_of(products, depth):
    waiting = [next(products) for _ in range(depth)]
    while waiting:
        ready = waiting.pop(0)
        following = next(products, None)
        if following is not None:
            waiting.append(following)
        yield ready


def run_steps(chains, lag):
    waits = [lag * i for i in range(len(chains))]
    live = dict(enumerate(chains))
    while live:
        for i in list(live):
            if waits[i] > 0:
                waits[i] -= 1
            elif next(live[i], 1) is not None:
                del live[i]


def pair_span(pair):
    return slice(pair * 2 * HD, (pair + 1) * 2 * HD)


def layer_forward(x, mod, own, other, wqkv, wo, bqkv, bfc1, bproj, bfc2, put, result):
    normed, _ = normalize(x)
    input_a = (normed * (1.0 + mod(1)) + mod(0)).astype(bf16)
    put("input_a", input_a)
    yield
    thirds = []
    for part in range(3):
        span = slice(part * D, (part + 1) * D)
        value = (dot(input_a, wqkv[:, span]) + bqkv[:, span]).astype(bf16)
        if part == 0:
            value = value * jnp.asarray(HD**-0.5, bf16)
        put(("query", "keyed", "valued")[part], value)
        thirds.append(value)
        yield
    query, keyed, valued = thirds
    scored = ahead_of(
        (dot(keep(query[:, pair_span(pair)], head_mask(which)), keyed[:, pair_span(pair)], NT)
         for pair in range(HEADS // 2) for which in range(2)), AHEAD
    )
    pieces = []
    for pair in range(HEADS // 2):
        total = None
        for which in range(2):
            scores = next(scored)
            yield
            expo = jnp.exp(scores - jnp.max(scores, -1, keepdims=True))
            probs = expo * (1.0 / jnp.sum(expo, -1, keepdims=True))
            put("probs", probs, 2 * pair + which)
            yield
            mixed = dot(probs.astype(bf16), keep(valued[:, pair_span(pair)], head_mask(which)))
            total = mixed if total is None else total + mixed
        pieces.append(total.astype(bf16))
    mixed = jnp.concatenate(pieces, 1)
    put("mixed", mixed)
    yield
    branch_a = dot(mixed, wo[...], NT) + bproj
    put("branch_a", branch_a)
    middle = x + mod(2) * branch_a
    put("middle", middle)
    yield
    normed_m, _ = normalize(middle)
    input_m = (normed_m * (1.0 + mod(4)) + mod(3)).astype(bf16)
    put("input_m", input_m)
    yield
    branch_m = bfc2
    for side, weights in enumerate((own, other)):
        pre = dot(input_m, weights[:, :HMLP]) + bfc1[:, side * HMLP : (side + 1) * HMLP]
        yield
        acted, slope = gelu_parts(pre)
        put("acted", acted, side)
        put("slope", slope, side)
        yield
        branch_m = branch_m + dot(acted, weights[:, OFF_W2 : OFF_W2 + HMLP], NT)
        yield
    put("branch_m", branch_m)
    result.append(middle + mod(5) * branch_m)


def layer_backward(grad, x, mod, own, other, wqkv, wo, take, rows, stash, mods_out, bias, result, inputs=None):
    branch_m = take("branch_m")
    mods_out(5, token_sum(grad * branch_m))
    grad_branch_m = (grad * mod(5)).astype(bf16)
    bias("fc2", 0, grad_branch_m)
    stash["dym"][rows, :] = grad_branch_m
    yield
    grad_input = None
    acting = ahead_of(
        (dot(grad_branch_m, weights[:, OFF_W2 : OFF_W2 + HMLP]) for weights in (own, other)), MLP_AHEAD
    )
    for side, weights in enumerate((own, other)):
        span = slice(side * HMLP, (side + 1) * HMLP)
        grad_acted = next(acting)
        yield
        grad_pre = (grad_acted * take("slope", side)).astype(bf16)
        stash["dg"][rows, span] = grad_pre
        bias("fc1", side * HMLP, grad_pre)
        yield
        part = dot(grad_pre, weights[:, :HMLP], NT)
        grad_input = part if grad_input is None else grad_input + part
        yield
    middle = take("middle")
    normed_m, inv_m = normalize(middle)
    if inputs is not None:
        inputs[1][rows, :] = (normed_m * (1.0 + mod(4)) + mod(3)).astype(bf16)
    mods_out(3, token_sum(grad_input))
    mods_out(4, token_sum(grad_input * normed_m))
    grad_middle = grad + norm_back(grad_input * (1.0 + mod(4)), normed_m, inv_m)
    yield
    branch_a = take("branch_a")
    mods_out(2, token_sum(grad_middle * branch_a))
    grad_branch_a = (grad_middle * mod(2)).astype(bf16)
    bias("proj", 0, grad_branch_a)
    stash["dya"][rows, :] = grad_branch_a
    yield
    grad_mixed = dot(grad_branch_a, wo[...]).astype(bf16)
    yield
    query, keyed, valued = take("query"), take("keyed"), take("valued")
    scored = ahead_of(
        (dot(keep(grad_mixed[:, pair_span(pair)], head_mask(which)), valued[:, pair_span(pair)], NT)
         for pair in range(HEADS // 2) for which in range(2)), BACK_AHEAD
    )
    grads_q, grads_k, grads_v = [], [], []
    for pair in range(HEADS // 2):
        q_pair, k_pair = query[:, pair_span(pair)], keyed[:, pair_span(pair)]
        grad_q = grad_k = grad_v = None
        for which in range(2):
            mask = head_mask(which)
            grad_probs = next(scored)
            yield
            probs = take("probs", 2 * pair + which)
            row_dot = jnp.sum(grad_probs * probs, -1, keepdims=True)
            grad_scores = (probs * (grad_probs - row_dot)).astype(bf16)
            yield
            part_q = dot(grad_scores, keep(k_pair, mask))
            part_k = dot(grad_scores, keep(q_pair, mask), TN)
            part_v = dot(probs.astype(bf16), keep(grad_mixed[:, pair_span(pair)], mask), TN)
            grad_q = part_q if grad_q is None else grad_q + part_q
            grad_k = part_k if grad_k is None else grad_k + part_k
            grad_v = part_v if grad_v is None else grad_v + part_v
        grads_q.append((grad_q * HD**-0.5).astype(bf16))
        grads_k.append(grad_k.astype(bf16))
        grads_v.append(grad_v.astype(bf16))
    yield
    grad_qkv = jnp.concatenate(grads_q + grads_k + grads_v, 1)
    stash["dqkv"][rows, :] = grad_qkv
    bias("qkv", 0, grad_qkv)
    yield
    grad_input_a = dot(grad_qkv, wqkv[...], NT)
    yield
    normed, inv_a = normalize(x)
    if inputs is not None:
        inputs[0][rows, :] = (normed * (1.0 + mod(1)) + mod(0)).astype(bf16)
    mods_out(0, token_sum(grad_input_a))
    mods_out(1, token_sum(grad_input_a * normed))
    result.append(grad_middle + norm_back(grad_input_a * (1.0 + mod(1)), normed, inv_a))


def weight_grads(input_a, input_m, mixed, acted, stash, places, outs, sems, fills):
    def add(side, start, value):
        rows = slice(start, start + value.shape[0])
        places[side][rows, :] = value if side else places[side][rows, :] + value

    for copy in fills:
        copy.wait()
    copies = []

    def send(side, start, stop):
        rows = pl.ds(start, stop - start)
        copy = pltpu.make_async_copy(places[side].at[rows, :], outs[side].at[rows, :], sems.at[len(copies)])
        copy.start()
        copies.append(copy)

    for part in range(3):
        piece = dot(stash["dqkv"][:, part * D : (part + 1) * D], input_a[...], TN)
        for side in range(2):
            for head in range(HEADS // 2):
                start = side * HALF + head * HD
                place = (3 * head + part) * HD
                add(side, place, piece[start : start + HD, :])
    for side in (1, 0):
        send(side, 0, QKV_S)
    for side in (1, 0):
        add(side, QKV_S, dot(stash["dg"][:, side * HMLP : (side + 1) * HMLP], input_m[...], TN))
        send(side, QKV_S, COL_S)
    for side in (1, 0):
        add(side, COL_S + HALF, dot(acted[:, side * HMLP : (side + 1) * HMLP], stash["dym"][...], TN))
        send(side, COL_S + HALF, BOTH)
    piece = dot(mixed[...], stash["dya"][...], TN)
    for side in (1, 0):
        add(side, COL_S, piece[side * HALF : (side + 1) * HALF, :])
        send(side, COL_S, COL_S + HALF)
    for copy in copies:
        copy.wait()


def error_fills(layer, err_col, err_row, place, sems):
    return [pltpu.make_async_copy(err_col.at[layer], place.at[pl.ds(0, COL_S), :], sems.at[0]),
            pltpu.make_async_copy(err_row.at[layer], place.at[pl.ds(COL_S, ROW_S), :], sems.at[1])]


BIAS = {"qkv": 0, "fc1": 3 * D, "proj": 3 * D + MLP, "fc2": 4 * D + MLP}
BIAS_WIDTH = 5 * D + MLP

PAY_PATCH, PAY_HEAD, PAY_PROJ, PAY_FC2, PAY_BPATCH, PAY_BHEAD, PAY_COND, PAY_BCOL = 0, 16, 32, 34, 36, 37, 38, 52
PAY_ROWS = 64
SMALL_ROWS = PAY_BCOL + 8 - PAY_PROJ


def forward_kernel(core, full, xt, mods, wpatch, pos, own, other, bcol_own, bcol_other, b_rep,
                   query, keyed, valued, probs, branch_a, middle, slope, branch_m, mixed, acted,
                   x2, next_own, next_other, wqkv, wo, bqkv, bfc1, hold_own, hold_other, sems):
    picks = [pltpu.make_async_copy(full.at[:, side, :, pl.ds(GATH, GATH)], hold, sems.at[i])
             for i, (side, hold) in enumerate(((core[0], hold_own), (1 - core[0], hold_other)))]
    leaves = [pltpu.make_async_copy(hold, out, sems.at[2 + i])
              for i, (hold, out) in enumerate(((hold_own, next_own), (hold_other, next_other)))]

    @pl.when(pl.program_id(0) == 0)
    def _():
        for copy in picks:
            copy.start()
        assemble(0, own, other, bcol_own, bcol_other, wqkv, wo, bqkv, bfc1)

    named = dict(query=query, keyed=keyed, valued=valued, mixed=mixed, branch_a=branch_a,
                 middle=middle, branch_m=branch_m)

    def chain(i):
        def put(name, value, index=None):
            if name in ("input_a", "input_m"):
                return
            if name == "probs":
                probs[i, index] = value
            elif name == "acted":
                acted[i, :, index * HMLP : (index + 1) * HMLP] = value
            elif name == "slope":
                slope[i, :, index * HMLP : (index + 1) * HMLP] = value
            else:
                named[name][i] = value

        x = dot(xt[i], wpatch[0], TN) + vector(b_rep, START_PATCH) + pos[...]
        result = []
        yield from layer_forward(x, lambda j: mods[i, j : j + 1, :], own, other, wqkv, wo, bqkv[...],
                                 bfc1[...], vector(b_rep, 0), vector(b_rep, START_FC2), put, result)
        x2[i] = result[0]

    run_steps([chain(i) for i in range(xt.shape[0])], LAG)

    @pl.when(pl.program_id(0) == 0)
    def _():
        for copy, leave in zip(picks, leaves):
            copy.wait()
            leave.start()

    @pl.when(pl.program_id(0) == pl.num_programs(0) - 1)
    def _():
        for leave in leaves:
            leave.wait()


def diagonal(count):
    down = lax.broadcasted_iota(jnp.int32, (count, count), 0)
    across = lax.broadcasted_iota(jnp.int32, (count, count), 1)
    return down == across


def write_bcol(dbias, side, out, layer):
    pieces = []
    for head in range(HEADS // 2):
        for part in range(3):
            start = part * D + side * HALF + head * HD
            pieces.append(dbias[:, start : start + HD])
    start = 3 * D + side * HMLP
    pieces.append(dbias[:, start : start + HMLP])
    pieces.append(jnp.zeros((1, 4 * D - COL_S), f32))
    line = jnp.concatenate(pieces, 1)
    for row in range(4):
        at = PAY_BCOL + 4 * layer + row
        out[at : at + 1, :] = line[:, row * D : (row + 1) * D]


def middle_kernel(x2, mods, own, other, bcol_own, bcol_other, b_rep, whead, targets, err_col, err_row,
                  dx, dmods, grad_own, grad_other, dbias, dhead, dbhead, loss,
                  wqkv, wo, bqkv, bfc1, query, keyed, valued, probs, mixed, branch_a, middle, acted,
                  slope, branch_m, input_a, input_m, s_dqkv, s_dg, s_dya, s_dym, place_own, place_other,
                  out_sems, fill_sems):
    step = pl.program_id(0)
    fills = error_fills(1, err_col, err_row, place_own, fill_sems)

    @pl.when(step == 0)
    def _():
        for copy in fills:
            copy.start()
        assemble(1, own, other, bcol_own, bcol_other, wqkv, wo, bqkv, bfc1)
        dbias[...] = jnp.zeros_like(dbias)
        dhead[...] = jnp.zeros_like(dhead)
        dbhead[...] = jnp.zeros_like(dbhead)
        loss[...] = jnp.zeros_like(loss)

    stacked = dict(mixed=mixed, input_a=input_a, input_m=input_m)
    single = dict(query=query, keyed=keyed, valued=valued, branch_a=branch_a, middle=middle,
                  branch_m=branch_m)
    stash = dict(dqkv=s_dqkv, dg=s_dg, dya=s_dya, dym=s_dym)
    group = x2.shape[0]

    def chain(i):
        rows = pl.ds(pl.multiple_of((step * group + i) * TOK, TOK), TOK)

        def put(name, value, index=None):
            if name == "probs":
                probs[i, index] = value
            elif name == "acted":
                acted[rows, index * HMLP : (index + 1) * HMLP] = value
            elif name == "slope":
                slope[i, :, index * HMLP : (index + 1) * HMLP] = value
            elif name in stacked:
                stacked[name][rows, :] = value
            else:
                single[name][i] = value

        def take(name, index=None):
            if name == "probs":
                return probs[i, index]
            if name == "slope":
                return slope[i, :, index * HMLP : (index + 1) * HMLP]
            return single[name][i]

        def mod(j):
            return mods[i, 6 + j : 7 + j, :]

        def mods_out(j, value):
            dmods[i, j : j + 1, :] = value

        def bias(name, start, value):
            at = BIAS[name] + start
            dbias[:, at : at + value.shape[1]] += token_sum(value.astype(f32))

        result = []
        yield from layer_forward(x2[i], mod, own, other, wqkv, wo, bqkv[...], bfc1[...], vector(b_rep, D),
                                 vector(b_rep, START_FC2 + D), put, result)
        yield
        normed, inv_std = normalize(result[0])
        input_f = (normed * (1.0 + mod(7)) + mod(6)).astype(bf16)
        bhead = jnp.sum(
            jnp.where(diagonal(PV), b_rep[:, START_HEAD : START_HEAD + PV], 0.0), 1, keepdims=True
        )
        yield
        miss = dot(whead[0], input_f, NT) + bhead - targets[i]
        loss[...] += jnp.sum(miss * miss, 0, keepdims=True)
        grad_pred = (2.0 * miss).astype(bf16)
        yield
        dhead[...] += dot(grad_pred, input_f)
        dbhead[...] += jnp.sum(grad_pred.astype(f32), 1, keepdims=True)
        grad_input = dot(grad_pred, whead[0], TN)
        yield
        mods_out(6, token_sum(grad_input))
        mods_out(7, token_sum(grad_input * normed))
        grad = norm_back(grad_input * (1.0 + mod(7)), normed, inv_std)
        result = []
        yield from layer_backward(grad, x2[i], mod, own, other, wqkv, wo, take, rows, stash, mods_out, bias,
                                  result)
        dx[i] = result[0]

    run_steps([chain(i) for i in range(group)], LAG)

    @pl.when(step == pl.num_programs(0) - 1)
    def _():
        weight_grads(input_a, input_m, mixed, acted, stash, (place_own, place_other),
                     (grad_own, grad_other), out_sems, fills)


def last_kernel(dx, mods, own, other, bcol_own, bcol_other, b_rep, xt, wpatch, pos,
                dbias1, dhead, dbhead, loss, dmods1, err_col, err_row,
                query, keyed, valued, probs, branch_a, middle, slope, branch_m, mixed, acted,
                dmods, grad_own, grad_other, pay_own, pay_other,
                wqkv, wo, bqkv, bfc1, a_input_a, a_input_m, a_mixed, a_acted, s_dqkv, s_dg, s_dya, s_dym,
                dbias, sems, place_own, place_other, out_sems, fill_sems):
    step = pl.program_id(0)
    pairs = ((mixed, a_mixed), (acted, a_acted))
    copies = [pltpu.make_async_copy(src, dst, sems.at[i]) for i, (src, dst) in enumerate(pairs)]
    fills = error_fills(0, err_col, err_row, place_own, fill_sems)

    @pl.when(step == 0)
    def _():
        assemble(0, own, other, bcol_own, bcol_other, wqkv, wo, bqkv, bfc1)
        dbias[...] = jnp.zeros_like(dbias)
        pay_own[...] = jnp.zeros_like(pay_own)
        for copy in copies + fills:
            copy.start()

    rows = pl.ds(pl.multiple_of(step * TOK, TOK), TOK)
    single = dict(query=query, keyed=keyed, valued=valued, branch_a=branch_a, middle=middle,
                  branch_m=branch_m)

    def take(name, index=None):
        if name == "probs":
            return probs[0, index]
        if name == "slope":
            return slope[0, :, index * HMLP : (index + 1) * HMLP]
        return single[name][0]

    def mods_out(j, value):
        dmods[0, j : j + 1, :] = value

    def bias(name, start, value):
        at = BIAS[name] + start
        dbias[:, at : at + value.shape[1]] += token_sum(value.astype(f32))

    stash = dict(dqkv=s_dqkv, dg=s_dg, dya=s_dya, dym=s_dym)
    result = []
    x = dot(xt[0], wpatch[0], TN) + vector(b_rep, START_PATCH) + pos[...]
    run_steps([layer_backward(dx[0], x, lambda j: mods[0, j : j + 1, :], own, other, wqkv, wo,
                              take, rows, stash, mods_out, bias, result, (a_input_a, a_input_m))], 0)
    (grad,) = result
    grad = grad.astype(bf16)
    pay_own[PAY_PATCH : PAY_PATCH + PV, :] += dot(xt[0], grad)
    pay_own[PAY_BPATCH : PAY_BPATCH + 1, :] += token_sum(grad.astype(f32))
    dmods[0, 6 : 6 + 8, :] = dmods1[0]
    rounded = dmods[0].astype(bf16).astype(f32)
    dmods[0] = rounded
    pay_own[PAY_COND : PAY_COND + 14, :] += rounded

    @pl.when(step == pl.num_programs(0) - 1)
    def _():
        for copy in copies:
            copy.wait()
        weight_grads(a_input_a, a_input_m, a_mixed, a_acted, stash, (place_own, place_other),
                     (grad_own, grad_other), out_sems, fills)
        pay_own[PAY_HEAD : PAY_HEAD + PV, :] = dhead[...]
        for layer, values in enumerate((dbias, dbias1)):
            pay_own[PAY_PROJ + layer : PAY_PROJ + layer + 1, :] = values[:, BIAS["proj"] : BIAS["proj"] + D]
            pay_own[PAY_FC2 + layer : PAY_FC2 + layer + 1, :] = values[:, BIAS["fc2"] : BIAS["fc2"] + D]
        head_line = jnp.sum(jnp.where(diagonal(PV), dbhead[...], 0.0), 0, keepdims=True)
        pay_own[PAY_BHEAD : PAY_BHEAD + 1, :] = jnp.concatenate(
            [head_line, jnp.sum(loss[...], 1, keepdims=True), jnp.zeros((1, D - PV - 1), f32)], 1
        )
        pay_other[...] = pay_own[...]
        for side, out in enumerate((pay_own, pay_other)):
            for layer, values in enumerate((dbias, dbias1)):
                write_bcol(values, side, out, layer)
        for out in (pay_own, pay_other):
            out[PAY_BCOL + 8 :, :] = jnp.zeros((PAY_ROWS - PAY_BCOL - 8, D), f32)


def per_latent(*shape, group=1):
    zeros = (0,) * len(shape)
    return pl.BlockSpec((group,) + shape, lambda n: (n,) + zeros)


def fixed(*shape):
    zeros = (0,) * len(shape)
    return pl.BlockSpec(shape, lambda n: zeros, pipeline_mode=pl.Buffered(1))


def params():
    return pltpu.CompilerParams(dimension_semantics=("arbitrary",), vmem_limit_bytes=62 * 2**20)


SAVED = [
    ("query", (TOK, D), bf16), ("keyed", (TOK, D), bf16), ("valued", (TOK, D), bf16),
    ("probs", (HEADS, TOK, TOK), f32), ("branch_a", (TOK, D), f32), ("middle", (TOK, D), f32),
    ("slope", (TOK, MLP), f32), ("branch_m", (TOK, D), f32), ("mixed", (TOK, D), bf16),
    ("acted", (TOK, MLP), bf16),
]
BOTH = COL_S + ROW_S
GRAD_SHAPES = [(BOTH, D), (BOTH, D)]
WEIGHT_SCRATCH = [pltpu.VMEM((D, 3 * D), bf16), pltpu.VMEM((D, D), bf16),
                  pltpu.VMEM((1, 3 * D), f32), pltpu.VMEM((1, MLP), f32)]


def weight_specs():
    return [fixed(D, GATH), fixed(D, GATH), fixed(L, COL_S), fixed(L, COL_S), fixed(1, NBR)]


def stash_scratch(count):
    rows = count * TOK
    return [pltpu.VMEM((rows, 3 * D), bf16), pltpu.VMEM((rows, MLP), bf16),
            pltpu.VMEM((rows, D), bf16), pltpu.VMEM((rows, D), bf16)]


def place_scratch():
    return [pltpu.VMEM(shape, f32) for shape in GRAD_SHAPES] + [pltpu.SemaphoreType.DMA((8,)), pltpu.SemaphoreType.DMA((2,))]


def cost(flops, nbytes, count):
    return pl.CostEstimate(flops=int(flops * count), bytes_accessed=int(nbytes * count),
                           transcendentals=int(2e6 * count))


def run_forward(core, full, xt, mods, full_io, pos, weights):
    count = xt.shape[0]
    outs = SAVED + [("x2", (TOK, D), f32)]
    return pl.pallas_call(
        forward_kernel,
        grid=(count // GROUP,),
        in_specs=[pl.BlockSpec(memory_space=pltpu.SMEM), pl.BlockSpec(memory_space=pl.ANY), per_latent(PV, TOK, group=GROUP), per_latent(14, D, group=GROUP),
                  pl.BlockSpec((1, PV, D), lambda n: (0, 0, 0)), fixed(TOK, D)] + weight_specs(),
        out_specs=[per_latent(*shape, group=GROUP) for _, shape, _ in outs]
        + [pl.BlockSpec(memory_space=pl.ANY)] * 2,
        out_shape=[jax.ShapeDtypeStruct((count,) + shape, kind) for _, shape, kind in outs]
        + [jax.ShapeDtypeStruct((full.shape[0], full.shape[2], GATH), bf16)] * 2,
        scratch_shapes=WEIGHT_SCRATCH + [pltpu.VMEM((full.shape[0], full.shape[2], GATH), bf16)] * 2
        + [pltpu.SemaphoreType.DMA((4,))],
        compiler_params=params(),
        cost_estimate=cost(1.0e9, 6e6, count),
        name="forward_first",
    )(core, full, xt, mods, full_io, pos, *weights)


def run_middle(x2, mods, weights, full_io, targets, err_col, err_row):
    count = x2.shape[0]
    rows = count * TOK
    outs = [((count, TOK, D), per_latent(TOK, D, group=GROUP)), ((count, 8, D), per_latent(8, D, group=GROUP))]
    outs += [(shape, pl.BlockSpec(memory_space=pl.ANY)) for shape in GRAD_SHAPES]
    outs += [(shape, fixed(*shape)) for shape in ((1, BIAS_WIDTH), (PV, D), (PV, 1), (1, TOK))]
    return pl.pallas_call(
        middle_kernel,
        grid=(count // GROUP,),
        in_specs=[per_latent(TOK, D, group=GROUP), per_latent(14, D, group=GROUP)] + weight_specs()
        + [pl.BlockSpec((1, PV, D), lambda n: (1, 0, 0)), per_latent(PV, TOK, group=GROUP)]
        + [pl.BlockSpec(memory_space=pl.ANY)] * 2,
        out_specs=[spec for _, spec in outs],
        out_shape=[jax.ShapeDtypeStruct(shape, f32) for shape, _ in outs],
        scratch_shapes=WEIGHT_SCRATCH
        + [pltpu.VMEM((GROUP, TOK, D), bf16)] * 3
        + [pltpu.VMEM((GROUP, HEADS, TOK, TOK), f32), pltpu.VMEM((rows, D), bf16),
           pltpu.VMEM((GROUP, TOK, D), f32), pltpu.VMEM((GROUP, TOK, D), f32), pltpu.VMEM((rows, MLP), bf16),
           pltpu.VMEM((GROUP, TOK, MLP), f32), pltpu.VMEM((GROUP, TOK, D), f32),
           pltpu.VMEM((rows, D), bf16), pltpu.VMEM((rows, D), bf16)]
        + stash_scratch(count) + place_scratch(),
        compiler_params=params(),
        cost_estimate=cost(3.2e9, 3e6, count),
        name="layer_second",
    )(x2, mods, *weights, full_io, targets, err_col, err_row)


def run_last(dx, mods, weights, xt, full_io, pos, smalls, dmods1, err_col, err_row, saved):
    count = dx.shape[0]
    rows = count * TOK
    outs = [((count, 14, D), per_latent(14, D))]
    outs += [(shape, pl.BlockSpec(memory_space=pl.ANY)) for shape in GRAD_SHAPES]
    outs += [(shape, fixed(*shape)) for shape in ((PAY_ROWS, D), (PAY_ROWS, D))]
    return pl.pallas_call(
        last_kernel,
        grid=(count,),
        in_specs=[per_latent(TOK, D), per_latent(14, D)] + weight_specs()
        + [per_latent(PV, TOK), pl.BlockSpec((1, PV, D), lambda n: (0, 0, 0)), fixed(TOK, D)]
        + [fixed(*shape) for shape in ((1, BIAS_WIDTH), (PV, D), (PV, 1), (1, TOK))] + [per_latent(8, D)]
        + [pl.BlockSpec(memory_space=pl.ANY)] * 2
        + [per_latent(*shape) for _, shape, _ in SAVED[:-2]] + [pl.BlockSpec(memory_space=pl.ANY)] * 2,
        out_specs=[spec for _, spec in outs],
        out_shape=[jax.ShapeDtypeStruct(shape, f32) for shape, _ in outs],
        scratch_shapes=WEIGHT_SCRATCH
        + [pltpu.VMEM((rows, D), bf16)] * 3 + [pltpu.VMEM((rows, MLP), bf16)]
        + stash_scratch(count) + [pltpu.VMEM((1, BIAS_WIDTH), f32), pltpu.SemaphoreType.DMA((2,))]
        + place_scratch(),
        compiler_params=params(),
        cost_estimate=cost(2.2e9, 8e6, count),
        name="backward_first",
    )(dx, mods, *weights, xt, full_io, pos, *smalls, dmods1, err_col, err_row,
      *saved[:-2], *[v.reshape(rows, -1) for v in saved[-2:]])


PACK = 128
WIDE = 3 * D


def split3(values):
    high = values.astype(bf16)
    rest = values - high.astype(f32)
    mid = rest.astype(bf16)
    low = (rest - mid.astype(f32)).astype(bf16)
    return high, mid, low


def narrow_dot(small, big, dims):
    parts = split3(small)
    high, mid, low = split3(big)
    first = dot(jnp.concatenate(parts, 0), high, dims)
    second = dot(jnp.concatenate(parts[:2], 0), mid, dims)
    third = dot(parts[0], low, dims)
    r = small.shape[0]
    return first[:r] + ((first[r : 2 * r] + second[:r]) + (first[2 * r :] + second[r:] + third))


def outer(left, right):
    l1, l2, l3 = split3(left)
    r1, r2, r3 = split3(right)
    return dot(
        jnp.concatenate([l1, l1, l2, l2, l1, l3], 0), jnp.concatenate([r1, r2, r1, r2, r3, r1], 0), TN
    )


CHUNKS = [(448 * k, 448) for k in range(3)] + [(COL_S + 480 * k, 480) for k in range(2)]


def layer_chunks(layer, err_col, err_row):
    for at, size in CHUNKS:
        ref, start = (err_col, at) if at < COL_S else (err_row, at - COL_S)
        yield ref.at[layer, pl.ds(start, size), :], pl.ds(at, size)


def begin_project(own, got, mat, v_own, v_got, sems, out_sems):
    loads, stores = [], []
    for k, (at, size) in enumerate(CHUNKS):
        rows = pl.ds(at, size)
        loads.append([pltpu.make_async_copy(src.at[rows, :], dst.at[rows, :], sems.at[2 * k + i])
                      for i, (src, dst) in enumerate(((own, v_own), (got, v_got)))])
        stores.append(pltpu.make_async_copy(v_own.at[rows, :], mat.at[rows, :], out_sems.at[k]))
        for copy in loads[-1]:
            copy.start()
    return loads, stores


def project(layer, loads, stores, fac_col, fac_row, left_col, left_row, v_own, v_got):
    left_row[...] = jnp.zeros_like(left_row)
    total = None
    for (at, size), copies, store in zip(CHUNKS, loads, stores):
        for copy in copies:
            copy.wait()
        matrix = v_own[at : at + size, :] + v_got[at : at + size, :]
        v_own[at : at + size, :] = matrix
        store.start()
        if at < COL_S:
            part = narrow_dot(fac_col[layer][:, at : at + size], matrix, NN)
            total = part if total is None else total + part
        else:
            left_row[:, at - COL_S : at - COL_S + size] = narrow_dot(fac_row[layer], matrix, NT)
    left_col[...] = total


ANY = pl.BlockSpec(memory_space=pl.ANY)
VMEM = pl.BlockSpec(memory_space=pltpu.VMEM)
SMEM = pl.BlockSpec(memory_space=pltpu.SMEM)
PROJECT_SCRATCH = [pltpu.VMEM((BOTH, D), f32)] * 2 + [
    pltpu.SemaphoreType.DMA((2 * len(CHUNKS),)), pltpu.SemaphoreType.DMA((len(CHUNKS),))]


def large():
    return pltpu.CompilerParams(vmem_limit_bytes=62 * 2**20)


def shapes_of(shapes):
    return [jax.ShapeDtypeStruct(shape, f32) for shape in shapes]


def exchange_kernel(block, place, dmods, full_cond, cond, sent):
    n_dp = sent.shape[0]
    count = dmods.shape[0]
    line = jnp.concatenate([dmods[:, j, :] for j in range(14)], 1)
    grad_act = dot(line.astype(bf16), full_cond[...], NT)
    cond_own = cond[pl.ds(pl.multiple_of(place[0] * count, count), count), :]
    gate = 1.0 / (1.0 + jnp.exp(-cond_own))
    grad_cond = grad_act * (gate * (1.0 + cond_own * (1.0 - gate)))
    sent[:, :count, :] = jnp.broadcast_to(grad_cond[None], (n_dp, count, D))
    for j in range(n_dp):
        sent[j, count:, :] = jnp.concatenate(
            [line[:, j * block : (j + 1) * block], jnp.zeros((count, D - block), f32)], 1
        )


def run_exchange(n_dp, place, dmods, full_cond, cond):
    return pl.pallas_call(
        lambda *refs: exchange_kernel(N_MODS // n_dp, *refs),
        in_specs=[SMEM, VMEM, VMEM, VMEM],
        out_shape=jax.ShapeDtypeStruct((n_dp, 2 * dmods.shape[0], D), f32),
        compiler_params=large(),
        name="modulation_rows",
    )(place, dmods, full_cond, cond)


def project_kernel(own1, got1, own0, got0, fac_col, fac_row, pay_own, pay_got, err_io, fac_io,
                   mat1, mat0, mat_io, sent, left_col1, left_row1, left_col, left_row,
                   v_own1, v_got1, sems1, out_sems1, v_own0, v_got0, sems0, out_sems0):
    loads1, stores1 = begin_project(own1, got1, mat1, v_own1, v_got1, sems1, out_sems1)
    loads0, stores0 = begin_project(own0, got0, mat0, v_own0, v_got0, sems0, out_sems0)
    project(1, loads1, stores1, fac_col, fac_row, left_col1, left_row1, v_own1, v_got1)
    project(0, loads0, stores0, fac_col, fac_row, left_col, left_row, v_own0, v_got0)
    share = sent.shape[1]
    pay = pay_own[...] + pay_got[...]
    left_io = []
    for index in range(2):
        matrix = pay[index * PV : (index + 1) * PV] + err_io[index]
        mat_io[index] = matrix
        left_io.append(dot_full(fac_io[index], matrix))
    sent[...] = jnp.zeros_like(sent)
    tall = (left_row, left_row1)
    for column in range(RANK):
        pick = slice(column, column + 1)
        lines = [tall[i % 2][pick, (i // 2) * D : (i // 2 + 1) * D] for i in (0, 1)]
        lines += [left_col[pick, :], left_col1[pick, :], left_io[0][pick], left_io[1][pick]]
        lines += [tall[i % 2][pick, (i // 2) * D : (i // 2 + 1) * D] for i in (2, 3, 4, 5)]
        for extra in range(6):
            at = column * 6 + extra
            if at < SMALL_ROWS:
                lines.append(pay[PAY_PROJ + at : PAY_PROJ + at + 1])
        for slot, line in enumerate(lines):
            at = column * 16 + slot
            sent[at // share, at % share : at % share + 1, :] = line
    for store in stores1 + stores0:
        store.wait()


def run_project(n_dp, own1, got1, own0, got0, fac_col, fac_row, pay_own, pay_got, err_io, fac_io):
    return pl.pallas_call(
        project_kernel,
        in_specs=[ANY] * 4 + [VMEM] * 6,
        out_specs=[ANY, ANY, VMEM, VMEM],
        out_shape=shapes_of([(BOTH, D), (BOTH, D), (2, PV, D), (n_dp, PACK // n_dp, D)]),
        scratch_shapes=[pltpu.VMEM((RANK, D), f32), pltpu.VMEM((RANK, WIDE), f32)] * 2 + PROJECT_SCRATCH * 2,
        compiler_params=large(),
        cost_estimate=pl.CostEstimate(flops=int(1e9), bytes_accessed=int(1.5e7), transcendentals=0),
        name="left_factors",
    )(own1, got1, own0, got0, fac_col, fac_row, pay_own, pay_got, err_io, fac_io)


TIME_ROWS = FREQ + D + 8


def modulation_kernel(block, core, got, act_half, features, first, first_act, full_time, labels,
                      cond_mine, cond_their, time_part, table_part):
    n_dp = got.shape[0]
    count = got.shape[1] // 2
    half = block // 2
    grad_cond = got[:, :count, :].reshape(n_dp * count, D)
    cols = got[:, count : 2 * count, :].reshape(n_dp * count, D)
    left, right = cols[:, :half].astype(bf16), cols[:, half:block].astype(bf16)
    is_first = core[0] == 0
    grad_left = dot(act_half[...], left, TN)
    grad_right = dot(act_half[...], right, TN)
    cond_mine[...] = jnp.where(is_first, grad_left, grad_right)
    cond_their[...] = jnp.where(is_first, grad_right, grad_left)
    grad_second = grad_cond.astype(bf16)
    gate = 1.0 / (1.0 + jnp.exp(-first[...]))
    slope = gate * (1.0 + first[...] * (1.0 - gate))
    grad_first = (dot(grad_second, full_time[FREQ:, :], NT) * slope).astype(bf16)
    time_part[:FREQ, :] = dot(features[...], grad_first, TN)
    time_part[FREQ : FREQ + D, :] = dot(first_act[...], grad_second, TN)
    time_part[FREQ + D :, :] = jnp.concatenate(
        [token_sum(grad_first.astype(f32)), token_sum(grad_second.astype(f32)), jnp.zeros((6, D), f32)], 0
    )
    onehot = (labels[...] == lax.broadcasted_iota(jnp.int32, (n_dp * count, CLASSES), 1)).astype(f32).astype(bf16)
    high, mid, low = split3(grad_cond)
    table_part[...] = dot(high, onehot, TN) + (dot(mid, onehot, TN) + dot(low, onehot, TN))


def run_modulation(core, got, act_half, features, first, first_act, full_time, labels):
    half = N_MODS // got.shape[0] // 2
    shapes = [(D, half), (D, half), (TIME_ROWS, D), (D, CLASSES)]
    vmem = pl.BlockSpec(memory_space=pltpu.VMEM)
    return pl.pallas_call(
        lambda *refs: modulation_kernel(2 * half, *refs),
        in_specs=[pl.BlockSpec(memory_space=pltpu.SMEM)] + [vmem] * 7,
        out_shape=[jax.ShapeDtypeStruct(shape, f32) for shape in shapes],
        compiler_params=pltpu.CompilerParams(vmem_limit_bytes=62 * 2**20),
        name="modulation_gradients",
    )(core, got, act_half, features, first, first_act, full_time, labels)


COL_ROWS = 4 * RANK
ROW_AT = L * COL_ROWS
IO_AT = ROW_AT + L * RANK
EXTRA_AT = IO_AT + 2 * RANK


def cond_top(rows):
    return -(-((rows + 1) // 2) // 8) * 8


def ortho(packed, left_col, left_row, left_io):
    columns = []
    blank = jnp.zeros((4, D), f32)
    for index in range(RANK):
        block = packed[index]
        column = jnp.concatenate(
            [block[0:6], jnp.concatenate([block[6:8], blank], 0), jnp.concatenate([block[8:10], blank], 0)], 1
        )
        for earlier in columns:
            column = column - jnp.sum(earlier * column, -1, keepdims=True) * earlier
        column = column * lax.rsqrt(jnp.sum(column * column, -1, keepdims=True) + ortho_eps)
        for layer in range(L):
            left_row[layer, index : index + 1, :] = column[layer : layer + 1]
            left_col[layer, index : index + 1, :] = column[2 + layer : 3 + layer, :D]
            left_io[layer, index : index + 1, :] = column[4 + layer : 5 + layer, :D]
        columns.append(column)


def total_squares(values):
    return jnp.sum(values * values, keepdims=True)


def rows_kernel(cond_own, cond_got, table_own, table_got, sent, table_share, sums):
    cond_grad = cond_own[...] + cond_got[...]
    table = table_own[...] + table_got[...]
    table_share[...] = table
    sums[...] = jnp.concatenate([total_squares(cond_grad), total_squares(table), jnp.zeros((1, D - 2), f32)], 1)
    n_dp = sent.shape[0]
    rows, half = D // n_dp, cond_grad.shape[1]
    top = cond_top(rows)
    for j in range(n_dp):
        piece = cond_grad[j * rows : (j + 1) * rows]
        sent[j, : min(top, rows), :half] = piece[:top]
        if rows > top:
            sent[j, : rows - top, half : 2 * half] = piece[top:]


def run_rows(n_dp, cond_own, cond_got, table_own, table_got):
    return pl.pallas_call(
        rows_kernel,
        out_shape=shapes_of([(n_dp, cond_top(D // n_dp), D), table_own.shape, (1, D)]),
        compiler_params=large(),
        name="modulation_sums",
    )(cond_own, cond_got, table_own, table_got)


def mat_loads(mats, places, sems):
    return [[pltpu.make_async_copy(mat.at[pl.ds(at, size), :], place.at[pl.ds(at, size), :],
                                   sems.at[layer * len(CHUNKS) + k]) for k, (at, size) in enumerate(CHUNKS)]
            for layer, (mat, place) in enumerate(zip(mats, places))]


def right_kernel(packed, mat0, mat1, mat_io, sums, sent, left_col, left_row, left_io, flat, v0, v1, sems):
    loads = mat_loads((mat0, mat1), (v0, v1), sems)
    for copies in loads:
        for copy in copies:
            copy.start()
    ortho(packed, left_col, left_row, left_io)
    for copies in loads:
        for copy in copies:
            copy.wait()
    for layer, mat in enumerate((v0, v1)):
        right = narrow_dot(left_col[layer], mat[:COL_S, :], NT)
        for piece in range(4):
            wide = min(D, COL_S - piece * D)
            at = layer * COL_ROWS + piece * RANK
            if wide < D:
                flat[at : at + RANK, :] = jnp.zeros((RANK, D), f32)
            flat[at : at + RANK, :wide] = right[:, piece * D : piece * D + wide]
        at = ROW_AT + layer * RANK
        flat[at : at + RANK, :] = narrow_dot(left_row[layer][:, :ROW_S], mat[COL_S:, :], NN)
        at = IO_AT + layer * RANK
        flat[at : at + RANK, :] = jnp.zeros((RANK, D), f32)
        flat[at : at + RANK, :PV] = dot_full(left_io[layer], mat_io[layer], NT)
    flat[EXTRA_AT:, :] = jnp.zeros((PACK - EXTRA_AT, D), f32)
    flat[EXTRA_AT : EXTRA_AT + 1, :] = sums[...]
    sent[...] = flat[...].reshape(sent.shape)


def run_right(n_dp, packed, mats, mat_io, sums):
    return pl.pallas_call(
        right_kernel,
        in_specs=[VMEM, ANY, ANY, VMEM, VMEM],
        out_shape=shapes_of([(n_dp, PACK // n_dp, D), (L, RANK, D), (L, RANK, WIDE), (2, RANK, D)]),
        scratch_shapes=[pltpu.VMEM((PACK, D), f32), pltpu.VMEM((BOTH, D), f32), pltpu.VMEM((BOTH, D), f32),
                        pltpu.SemaphoreType.DMA((L * len(CHUNKS),))],
        compiler_params=large(),
        name="right_factors",
    )(packed, *mats, mat_io, sums)


def norm_kernel(packed, left_packed, left_col, left_row, left_io, time_own, time_got,
                right_col, right_row, right_io, parts, brep_grad, bcol_grad):
    for layer in range(L):
        for piece in range(4):
            wide = min(D, COL_S - piece * D)
            at = layer * COL_ROWS + piece * RANK
            right_col[layer, :, piece * D : piece * D + wide] = packed[at : at + RANK, :wide]
        at = ROW_AT + layer * RANK
        right_row[layer] = packed[at : at + RANK, :]
        at = IO_AT + layer * RANK
        right_io[layer] = packed[at : at + RANK, :PV]

    def small(at):
        row = at - PAY_PROJ
        return left_packed[row // 6, 10 + row % 6 : 11 + row % 6, :]

    time_bias = time_own[FREQ + D :, :] + time_got[FREQ + D :, :]
    lines = [small(PAY_PROJ + row) for row in range(4)] + [small(PAY_COND + row) for row in range(14)]
    lines += [time_bias[0:1], time_bias[1:2], small(PAY_BPATCH), small(PAY_BHEAD)[:, :PV]]
    whole = jnp.zeros((1, 1), f32)
    for row, line in enumerate(lines):
        brep_grad[:, row * D : row * D + line.shape[1]] = line
        whole = whole + total_squares(line)
    split = jnp.zeros((1, 1), f32)
    for layer in range(L):
        line = jnp.concatenate([small(PAY_BCOL + 4 * layer + row) for row in range(4)], 1)[:, :COL_S]
        bcol_grad[layer : layer + 1, :] = line
        split = split + total_squares(line)
    whole = whole + total_squares(time_own[: FREQ + D, :] + time_got[: FREQ + D, :])

    def gram(left, right):
        return jnp.sum(dot_full(left, left, NT) * dot_full(right, right, NT), keepdims=True)

    for layer in range(L):
        split = split + gram(left_col[layer], right_col[layer]) + gram(left_row[layer], right_row[layer])
        whole = whole + gram(left_io[layer], right_io[layer])
    sums = packed[EXTRA_AT : EXTRA_AT + 1, :]
    split = split + sums[:, 0:1]
    whole = whole + sums[:, 1:2]
    loss = small(PAY_BHEAD)[:, PV : PV + 1]
    parts[...] = jnp.concatenate([split, whole, loss, jnp.zeros((1, 125), f32)], 1)


def run_norm(packed, left_packed, lefts, time_own, time_got):
    shapes = [(L, RANK, COL_S), (L, RANK, D), (2, RANK, PV), (1, 128), (1, NBR), (L, COL_S)]
    return pl.pallas_call(
        norm_kernel,
        out_shape=[jax.ShapeDtypeStruct(shape, f32) for shape in shapes],
        compiler_params=pltpu.CompilerParams(vmem_limit_bytes=62 * 2**20),
        name="gradient_norm",
    )(packed, left_packed, *lefts, time_own, time_got)


def next_errors(loads, mat_io, left_col, left_row, left_io, right_col, right_row, right_io,
                err_col, err_row, err_io, v0, v1, out_sems):
    stores = []
    for layer, place in enumerate((v0, v1)):
        for k, ((at, size), (target, rows)) in enumerate(zip(CHUNKS, layer_chunks(layer, err_col, err_row))):
            if at < COL_S:
                approx = outer(right_col[layer][:, at : at + size], left_col[layer])
            else:
                approx = outer(left_row[layer][:, at - COL_S : at - COL_S + size], right_row[layer])
            loads[layer][k].wait()
            place[at : at + size, :] = place[at : at + size, :] - approx
            store = pltpu.make_async_copy(place.at[rows, :], target, out_sems.at[layer * len(CHUNKS) + k])
            store.start()
            stores.append(store)
        err_io[layer] = mat_io[layer] - outer(right_io[layer], left_io[layer])
    return stores


def own_columns(values, first, count):
    across = lax.broadcasted_iota(jnp.int32, (count, D), 1)
    down = lax.broadcasted_iota(jnp.int32, (count, D), 0)
    pick = (across == down + first).astype(f32).astype(bf16)
    high, mid, low = split3(values)
    return dot(high, pick, NT) + (dot(mid, pick, NT) + dot(low, pick, NT))


def update_kernel(core, parts, parts_got, left_col, right_col, right_row, left_row, right_io, left_io,
                  cond_own, cond_got, time_grad, table_grad, bcol_grad, brep_grad,
                  w_col, w_row, w_cond, w_time, w_io, w_table, b_col, b_rep,
                  m_col, m_row, m_cond, m_time, m_io, m_table, m_bcol, m_brep,
                  loss, clip, n_col, n_row, n_cond, n_time, n_io, n_table, n_bcol, n_brep,
                  v_col, v_row, v_cond, v_time, v_io, v_table, v_bcol, v_brep):
    clip_norm = jnp.sqrt(parts[:, 0:1] + parts_got[:, 0:1] + parts[:, 1:2])
    scaling = jnp.minimum(1.0, clip_limit / clip_norm)
    loss[...] = parts[:, 2:3]
    clip[...] = clip_norm

    def advance(weight, momentum, gradient):
        moved = momentum_decay * momentum + scaling * gradient
        return weight - learn_rate * moved, moved

    n_dp = cond_own.shape[0]
    rows = w_cond.shape[0]
    at = core[1] * rows
    for layer in range(L):
        n_col[layer], v_col[layer] = advance(
            w_col[layer], m_col[layer], outer(own_columns(left_col[layer], at, rows), right_col[layer]))
        n_row[layer], v_row[layer] = advance(
            w_row[layer], m_row[layer],
            outer(own_columns(right_row[layer], at, rows), left_row[layer][:, :ROW_S]))
        n_io[layer], v_io[layer] = advance(
            w_io[layer], m_io[layer], outer(right_io[layer], own_columns(left_io[layer], at, rows)))
    half = N_MODS // n_dp // 2
    top = cond_top(rows)
    is_first = core[0] == 0
    pieces = []
    for j in range(n_dp):
        mine, theirs = cond_own[j], cond_got[j]
        for pair in ((mine, theirs), (theirs, mine)):
            block = jnp.where(is_first, pair[0], pair[1])
            if rows > top:
                block = jnp.concatenate([block[:top, :half], block[: rows - top, half : 2 * half]], 0)
            else:
                block = block[:rows, :half]
            pieces.append(block)
    n_cond[...], v_cond[...] = advance(w_cond[...], m_cond[...], jnp.concatenate(pieces, 1))
    n_time[...], v_time[...] = advance(w_time[...], m_time[...], time_grad[...])
    n_table[...], v_table[...] = advance(w_table[...], m_table[...], table_grad[...])
    n_bcol[...], v_bcol[...] = advance(b_col[...], m_bcol[...], bcol_grad[...])
    n_brep[...], v_brep[...] = advance(b_rep[...], m_brep[...], brep_grad[...])


def final_kernel(*refs):
    head, (mat0, mat1, mat_io) = refs[:31], refs[31:34]
    news, (err_col, err_row, err_io, v0, v1, sems, out_sems) = refs[34:52], refs[52:]
    loads = mat_loads((mat0, mat1), (v0, v1), sems)
    for copies in loads:
        for copy in copies:
            copy.start()
    left_col, right_col, right_row, left_row, right_io, left_io = head[3:9]
    stores = next_errors(loads, mat_io, left_col, left_row, left_io, right_col, right_row, right_io,
                         err_col, err_row, err_io, v0, v1, out_sems)
    update_kernel(*head, *news)
    for store in stores:
        store.wait()


def run_final(core, grads, weights, momenta, mats, mat_io):
    shapes = [(1, 1), (1, 1)] + [v.shape for v in weights] * 2
    return pl.pallas_call(
        final_kernel,
        in_specs=[SMEM] + [VMEM] * (len(grads) + 2 * len(weights)) + [ANY, ANY, VMEM],
        out_specs=[VMEM] * len(shapes) + [ANY, ANY, VMEM],
        out_shape=shapes_of(shapes + [(L, COL_S, D), (L, ROW_S, D), (2, PV, D)]),
        scratch_shapes=[pltpu.VMEM((BOTH, D), f32), pltpu.VMEM((BOTH, D), f32),
                        pltpu.SemaphoreType.DMA((L * len(CHUNKS),)), pltpu.SemaphoreType.DMA((L * len(CHUNKS),))],
        compiler_params=pltpu.CompilerParams(vmem_limit_bytes=62 * 2**20),
        name="errors_and_update",
    )(core, *grads, *weights, *momenta, *mats, mat_io)


def swap(values):
    return lax.ppermute(values, "tensor", [(0, 1), (1, 0)])


def trade(chunks):
    return lax.all_to_all(chunks, "dp", 0, 0, tiled=True)


def spread(values):
    return trade(jnp.broadcast_to(values[None], (lax.axis_size("dp"),) + values.shape))


def exact_parts(values):
    high = lax.reduce_precision(values, 8, 7)
    mid = lax.reduce_precision(values - high, 8, 7)
    return [part.astype(bf16) for part in (high, mid, (values - high) - mid)]


def on_device(
    latents, gauss_noise, time_steps, labels, targets,
    w_col, w_row, w_cond, w_time, w_io, class_table, b_col, b_rep,
    mom_col, mom_row, mom_cond, mom_time, mom_io, mom_table, mom_bcol, mom_brep,
    err_col, err_row, err_io, fac_col, fac_row, fac_io,
):
    n_dp = lax.axis_size("dp")
    index_dp = lax.axis_index("dp")
    index_t = lax.axis_index("tensor")
    core = jnp.stack([index_t, index_dp]).astype(jnp.int32)
    first_core = index_t == 0
    n_all = labels.shape[0]
    per_dp = latents.shape[0]
    count = per_dp // 2
    rows = w_col.shape[1]

    def flip(values):
        return values.transpose(0, 2, 1)

    def halves(mine, theirs, axis):
        pair = jnp.stack([mine, theirs], axis)
        return jnp.where(first_core, pair, jnp.flip(pair, axis))

    row_sh = flip(w_row)
    shard = jnp.concatenate(
        [piece[layer] for layer in range(L)
         for piece in (w_col[:, :, QKV_S:], row_sh[:, :, HALF:], w_col[:, :, :QKV_S], row_sh[:, :, :HALF])], 1
    ).astype(bf16)
    full = lax.all_gather(shard, ("dp", "tensor"))

    block = N_MODS // n_dp
    half_block = block // 2
    classes = jnp.arange(CLASSES, dtype=jnp.int32)
    onehot_t = classes[:, None] == labels[None, :]
    looked = dot(class_table.astype(bf16), onehot_t.astype(bf16), TN).astype(bf16)
    time_rows = w_time.shape[0]
    sizes = [rows * n_all, time_rows * D, 2 * PV * rows, 3 * per_dp]
    wide = -(-sum(sizes) // 256) * 128
    common = jnp.concatenate(
        [part.reshape(-1) for part in
         (looked, w_time.astype(bf16), flip(w_io).astype(bf16), *exact_parts(time_steps))]
    )
    common = jnp.pad(common, (0, 2 * wide - common.shape[0]))
    common = lax.dynamic_slice_in_dim(common.reshape(2, wide), index_t, 1, 0)
    cond_bf = w_cond.astype(bf16).reshape(rows, n_dp, 2, half_block)
    cond_mine = lax.dynamic_slice_in_dim(cond_bf, index_t, 1, 2)[:, :, 0].transpose(1, 0, 2)
    sent = jnp.concatenate(
        [jnp.broadcast_to(common, (n_dp, wide)), cond_mine.reshape(n_dp, rows * half_block)], 1
    )
    got = trade(sent)
    cond_cols = got[:, wide:].reshape(D, half_block)
    mine = got[:, :wide]
    common = halves(mine, swap(mine), 1).reshape(n_dp, 2 * wide)
    ends = np.cumsum([0] + sizes)
    looked = common[:, : ends[1]].reshape(D, n_all).T
    full_time = common[:, ends[1] : ends[2]].reshape(FREQ + D, D)
    full_io = flip(common[:, ends[2] : ends[3]].reshape(n_dp, 2 * PV, rows).transpose(1, 0, 2).reshape(2, PV, D).transpose(0, 2, 1))
    steps_all = jnp.sum(common[:, ends[3] : ends[4]].reshape(n_dp, 3, per_dp).astype(f32), 1).reshape(n_all)

    features = frequency_features(steps_all).astype(bf16)
    first = dot(features, full_time[:FREQ]) + b_rep[START_FIRST:START_SECOND]
    first_act = jax.nn.silu(first).astype(bf16)
    second = dot(first_act, full_time[FREQ:]) + b_rep[START_SECOND:START_PATCH]
    cond = second + looked.astype(f32)
    cond_act = jax.nn.silu(cond).astype(bf16)
    mods = dot(cond_act, cond_cols).reshape(n_dp * 2, count, half_block)
    mods = lax.all_to_all(mods, ("dp", "tensor"), 0, 0, tiled=True)
    mods = mods.transpose(1, 0, 2).reshape(count, N_MODS)
    mods = (mods + b_rep[START_COND:START_FIRST]).reshape(count, 14, D)
    def half_of(values):
        split = values.reshape((n_dp, 2, count) + values.shape[1:])
        return lax.dynamic_slice_in_dim(split, index_t, 1, 1).reshape((n_dp * count,) + values.shape[1:])

    halves_of = [half_of(v) for v in (cond_act, features, first, first_act)]
    labels_half = half_of(labels)[:, None]
    place = (index_dp * 2 + index_t).astype(jnp.int32).reshape(1)
    full, mods, halves_of, labels_half, core, place = lax.optimization_barrier(
        (full, mods, halves_of, labels_half, core, place)
    )
    full = full.reshape(n_dp, 2, rows, L * GATH)

    def mine_of(values):
        return lax.dynamic_slice_in_dim(values, index_t * count, count, 0)

    steps_own = mine_of(time_steps)[:, None, None]
    xt = (
        (1.0 - steps_own) * flip(mine_of(latents)) + steps_own * flip(mine_of(gauss_noise))
    ).astype(bf16)
    b_line = b_rep[None]
    first_layer = full[:, :, :, :GATH]
    own = lax.dynamic_slice_in_dim(first_layer, index_t, 1, 1).reshape(D, GATH)
    other = lax.dynamic_slice_in_dim(first_layer, 1 - index_t, 1, 1).reshape(D, GATH)
    biases = (b_col, swap(b_col), b_line)
    weights = (own, other, *biases)
    pos = jnp.asarray(position_table())
    *saved, x2, own1, other1 = run_forward(core, full, xt, mods, full_io, pos, weights)
    weights1 = (own1.reshape(D, GATH), other1.reshape(D, GATH), *biases)
    x2, late_cond = lax.optimization_barrier((x2, w_cond))
    full_cond = lax.all_gather(late_cond.astype(bf16), "dp", axis=0, tiled=True)
    err_col_t, err_io_t = flip(err_col), flip(err_io)
    dx, dmods1, own1, oth1, *smalls = run_middle(
        x2, mods, weights1, full_io, flip(mine_of(targets)), err_col_t, err_row
    )
    got1 = swap(oth1)
    dmods, own0, oth0, pay_own, pay_oth = run_last(
        dx, mods, weights, xt, full_io, pos, smalls, dmods1, err_col_t, err_row, saved
    )
    got0, pay_got = swap(oth0), swap(pay_oth)

    rows_got = trade(run_exchange(n_dp, place, dmods, full_cond, cond))
    fac_col_t, fac_row_t, fac_io_t = flip(fac_col), flip(fac_row), flip(fac_io)
    mat1, mat0, mat_io, sent = run_project(
        n_dp, own1, got1, own0, got0, fac_col_t, fac_row_t, pay_own, pay_got, err_io_t, fac_io_t
    )
    mats = (mat0, mat1)
    rows_got, sent = lax.optimization_barrier((rows_got, sent))
    share = jnp.sum(trade(sent), 0)

    cond_mine, cond_their, time_own, table_part = run_modulation(core, rows_got, *halves_of, full_time, labels_half)
    share, cond_mine, cond_their, time_own, table_part = lax.optimization_barrier(
        (share, cond_mine, cond_their, time_own, table_part)
    )
    left_packed = spread(share).reshape(RANK, 16, D)
    cond_got, time_got = swap(cond_their), swap(time_own)
    table_own = lax.dynamic_slice_in_dim(table_part, index_dp * rows, rows, 0)
    cond_sent, table_share, sums = run_rows(n_dp, cond_mine, cond_got, table_own, swap(table_own))
    cond_rows = trade(cond_sent)

    sent, left_col, left_row, left_io = run_right(n_dp, left_packed, mats, mat_io, sums)
    time_at = index_dp * time_rows
    time_grad = (
        lax.dynamic_slice_in_dim(time_own, time_at, time_rows, 0)
        + lax.dynamic_slice_in_dim(time_got, time_at, time_rows, 0)
    )
    cond_rows, sent, time_grad = lax.optimization_barrier((cond_rows, sent, time_grad))
    packed = spread(jnp.sum(trade(sent), 0)).reshape(PACK, D)
    cond_rows_got = swap(cond_rows)
    lefts = (left_col, left_row, left_io)
    right_col, right_row, right_io, parts, brep_grad, bcol_grad = run_norm(
        packed, left_packed, lefts, time_own, time_got
    )
    parts_got = swap(parts)

    olds = (w_col, flip(w_row), w_cond, w_time, flip(w_io), class_table.T, b_col, b_line)
    momenta = (mom_col, flip(mom_row), mom_cond, mom_time, flip(mom_io), mom_table.T, mom_bcol, mom_brep[None])
    loss, clip_norm, *new, next_err_col, next_err_row, next_err_io = run_final(
        core,
        (parts, parts_got, left_col, right_col, right_row, left_row, right_io, left_io,
         cond_rows, cond_rows_got, time_grad, table_share, bcol_grad, brep_grad),
        olds, momenta, mats, mat_io,
    )

    def outward(col, row, cond, time, io, table, bcol, brep):
        return (col, flip(row), cond, time, flip(io), table.T, bcol, brep[0])

    return (
        loss.reshape(()), clip_norm.reshape(()), *outward(*new[:8]), *outward(*new[8:]),
        flip(next_err_col), next_err_row, flip(next_err_io), flip(right_col), flip(right_row), flip(right_io),
    )


def solution(mesh):
    weights = (
        P(None, "dp", "tensor"), P(None, "tensor", "dp"), P("dp", None), P("dp", None),
        P(None, "dp", None), P(None, "dp"), P(None, "tensor"), P(),
    )
    errors = (P("dp", None, "tensor"), P("dp", "tensor", None), P("dp", None, None))
    factors = (P(None, "tensor", None), P(None, "tensor", None), P())
    rows = P("dp", None, None)
    return jax.shard_map(
        on_device,
        mesh=mesh,
        in_specs=(rows, rows, P("dp"), P(), rows) + weights + weights + errors + factors,
        out_specs=(P(), P()) + weights + weights + errors + factors,
        check_vma=False,
    )
```

```python
import jax
import jax.numpy as jnp
import numpy as np
from jax import lax
from jax.experimental import pallas as pl
from jax.experimental.pallas import tpu as pltpu
from jax.sharding import PartitionSpec as P

D = 384
HEADS = 6
HD = 64
MLP = 1536
NBR = 8080
CLASSES = 1000
FREQ = 256
PV = 16
GRID = 16
L = 2
TOK = 256
RANK = 8
GROUP = 2
AHEAD, MLP_AHEAD, BACK_AHEAD = 2, 2, 6
LAG = 1

norm_eps = 1e-06
ortho_eps = 1e-06
clip_limit = 1.0
momentum_decay = 0.9
learn_rate = 4.0

HALF = D // 2
HMLP = MLP // 2
QKV_S = 3 * HALF
COL_S = QKV_S + HMLP
ROW_S = HALF + HMLP
OFF_W2 = HMLP
OFF_Q = 2 * HMLP
GATH = 2 * HMLP + 4 * HALF

f32 = jnp.float32
bf16 = jnp.bfloat16
highest = lax.Precision.HIGHEST
NN = (((1,), (0,)), ((), ()))
NT = (((1,), (1,)), ((), ()))
TN = (((0,), (0,)), ((), ()))


def dot(left, right, dims=NN):
    return lax.dot_general(left, right, dims, preferred_element_type=f32)


def dot_full(left, right, dims=NN):
    return lax.dot_general(left, right, dims, precision=highest, preferred_element_type=f32)


def position_table():
    quarter = D // 4
    omega = 1.0 / 10000.0 ** (np.arange(quarter, dtype=np.float32) / quarter)
    index = np.arange(TOK)
    across = (index % GRID).astype(np.float32)[:, None] * omega[None, :].astype(np.float32)
    down = (index // GRID).astype(np.float32)[:, None] * omega[None, :].astype(np.float32)
    table = np.concatenate([np.sin(across), np.cos(across), np.sin(down), np.cos(down)], 1)
    return table.astype(np.float32)


def frequency_features(steps):
    half = FREQ // 2
    rates = jnp.exp(-jnp.log(10000.0) * jnp.arange(half, dtype=f32) / half)
    angles = steps[:, None] * rates[None, :]
    return jnp.concatenate([jnp.cos(angles), jnp.sin(angles)], 1)


def normalize(values):
    centered = values - jnp.mean(values, -1, keepdims=True)
    inv_std = lax.rsqrt(jnp.mean(centered * centered, -1, keepdims=True) + norm_eps)
    return centered * inv_std, inv_std


def norm_back(grad, normed, inv_std):
    mean_grad = jnp.mean(grad, -1, keepdims=True)
    mean_mixed = jnp.mean(grad * normed, -1, keepdims=True)
    return inv_std * (grad - mean_grad - normed * mean_mixed)


def token_sum(values):
    return jnp.sum(values, 0, keepdims=True)


START_FC2 = L * D
START_COND = 2 * L * D
N_MODS = (6 * L + 2) * D
START_FIRST = START_COND + N_MODS
START_SECOND = START_FIRST + D
START_PATCH = START_FIRST + 2 * D
START_HEAD = START_FIRST + 3 * D


def assemble(layer, own, other, bcol_own, bcol_other, wqkv, wo, bqkv, bfc1):
    for side, (weights, bias) in enumerate(((own, bcol_own), (other, bcol_other))):
        for head in range(HEADS // 2):
            for part in range(3):
                at = (3 * head + part) * HD
                to = part * D + side * HALF + head * HD
                wqkv[:, to : to + HD] = weights[:, OFF_Q + at : OFF_Q + at + HD]
                bqkv[:, to : to + HD] = bias[layer : layer + 1, at : at + HD]
        wo[:, side * HALF : (side + 1) * HALF] = weights[:, OFF_Q + QKV_S :]
        bfc1[:, side * HMLP : (side + 1) * HMLP] = bias[layer : layer + 1, QKV_S:]


def vector(b_rep, at):
    return b_rep[:, at : at + D]


def head_mask(which):
    lane = lax.broadcasted_iota(jnp.int32, (1, 2 * HD), 1)
    return (lane < HD) if which == 0 else (lane >= HD)


def keep(values, mask):
    return jnp.where(mask, values, jnp.zeros_like(values))


def gelu_parts(pre):
    squared = pre * pre
    coef = np.float32(np.sqrt(2.0 / np.pi))
    tanh = jnp.tanh(pre * (coef + np.float32(coef * 0.044715) * squared))
    half = 0.5 * (1.0 + tanh)
    slope = half + (0.5 * pre) * (1.0 - tanh * tanh) * (
        coef + np.float32(3.0 * 0.044715 * coef) * squared
    )
    return (pre * half).astype(bf16), slope


def ahead_of(products, depth):
    waiting = [next(products) for _ in range(depth)]
    while waiting:
        ready = waiting.pop(0)
        following = next(products, None)
        if following is not None:
            waiting.append(following)
        yield ready


def run_steps(chains, lag):
    waits = [lag * i for i in range(len(chains))]
    live = dict(enumerate(chains))
    while live:
        for i in list(live):
            if waits[i] > 0:
                waits[i] -= 1
            elif next(live[i], 1) is not None:
                del live[i]


def pair_span(pair):
    return slice(pair * 2 * HD, (pair + 1) * 2 * HD)


def layer_forward(x, mod, own, other, wqkv, wo, bqkv, bfc1, bproj, bfc2, put, result):
    normed, _ = normalize(x)
    input_a = (normed * (1.0 + mod(1)) + mod(0)).astype(bf16)
    put("input_a", input_a)
    yield
    thirds = []
    for part in range(3):
        span = slice(part * D, (part + 1) * D)
        value = (dot(input_a, wqkv[:, span]) + bqkv[:, span]).astype(bf16)
        if part == 0:
            value = value * jnp.asarray(HD**-0.5, bf16)
        put(("query", "keyed", "valued")[part], value)
        thirds.append(value)
        yield
    query, keyed, valued = thirds
    scored = ahead_of(
        (dot(keep(query[:, pair_span(pair)], head_mask(which)), keyed[:, pair_span(pair)], NT)
         for pair in range(HEADS // 2) for which in range(2)), AHEAD
    )
    pieces = []
    for pair in range(HEADS // 2):
        total = None
        for which in range(2):
            scores = next(scored)
            yield
            expo = jnp.exp(scores - jnp.max(scores, -1, keepdims=True))
            probs = expo * (1.0 / jnp.sum(expo, -1, keepdims=True))
            put("probs", probs, 2 * pair + which)
            yield
            mixed = dot(probs.astype(bf16), keep(valued[:, pair_span(pair)], head_mask(which)))
            total = mixed if total is None else total + mixed
        pieces.append(total.astype(bf16))
    mixed = jnp.concatenate(pieces, 1)
    put("mixed", mixed)
    yield
    branch_a = dot(mixed, wo[...], NT) + bproj
    put("branch_a", branch_a)
    middle = x + mod(2) * branch_a
    put("middle", middle)
    yield
    normed_m, _ = normalize(middle)
    input_m = (normed_m * (1.0 + mod(4)) + mod(3)).astype(bf16)
    put("input_m", input_m)
    yield
    branch_m = bfc2
    for side, weights in enumerate((own, other)):
        pre = dot(input_m, weights[:, :HMLP]) + bfc1[:, side * HMLP : (side + 1) * HMLP]
        yield
        acted, slope = gelu_parts(pre)
        put("acted", acted, side)
        put("slope", slope, side)
        yield
        branch_m = branch_m + dot(acted, weights[:, OFF_W2 : OFF_W2 + HMLP], NT)
        yield
    put("branch_m", branch_m)
    result.append(middle + mod(5) * branch_m)


def layer_backward(grad, x, mod, own, other, wqkv, wo, take, rows, stash, mods_out, bias, result, inputs=None):
    branch_m = take("branch_m")
    mods_out(5, token_sum(grad * branch_m))
    grad_branch_m = (grad * mod(5)).astype(bf16)
    bias("fc2", 0, grad_branch_m)
    stash["dym"][rows, :] = grad_branch_m
    yield
    grad_input = None
    acting = ahead_of(
        (dot(grad_branch_m, weights[:, OFF_W2 : OFF_W2 + HMLP]) for weights in (own, other)), MLP_AHEAD
    )
    for side, weights in enumerate((own, other)):
        span = slice(side * HMLP, (side + 1) * HMLP)
        grad_acted = next(acting)
        yield
        grad_pre = (grad_acted * take("slope", side)).astype(bf16)
        stash["dg"][rows, span] = grad_pre
        bias("fc1", side * HMLP, grad_pre)
        yield
        part = dot(grad_pre, weights[:, :HMLP], NT)
        grad_input = part if grad_input is None else grad_input + part
        yield
    middle = take("middle")
    normed_m, inv_m = normalize(middle)
    if inputs is not None:
        inputs[1][rows, :] = (normed_m * (1.0 + mod(4)) + mod(3)).astype(bf16)
    mods_out(3, token_sum(grad_input))
    mods_out(4, token_sum(grad_input * normed_m))
    grad_middle = grad + norm_back(grad_input * (1.0 + mod(4)), normed_m, inv_m)
    yield
    branch_a = take("branch_a")
    mods_out(2, token_sum(grad_middle * branch_a))
    grad_branch_a = (grad_middle * mod(2)).astype(bf16)
    bias("proj", 0, grad_branch_a)
    stash["dya"][rows, :] = grad_branch_a
    yield
    grad_mixed = dot(grad_branch_a, wo[...]).astype(bf16)
    yield
    query, keyed, valued = take("query"), take("keyed"), take("valued")
    scored = ahead_of(
        (dot(keep(grad_mixed[:, pair_span(pair)], head_mask(which)), valued[:, pair_span(pair)], NT)
         for pair in range(HEADS // 2) for which in range(2)), BACK_AHEAD
    )
    grads_q, grads_k, grads_v = [], [], []
    for pair in range(HEADS // 2):
        q_pair, k_pair = query[:, pair_span(pair)], keyed[:, pair_span(pair)]
        grad_q = grad_k = grad_v = None
        for which in range(2):
            mask = head_mask(which)
            grad_probs = next(scored)
            yield
            probs = take("probs", 2 * pair + which)
            row_dot = jnp.sum(grad_probs * probs, -1, keepdims=True)
            grad_scores = (probs * (grad_probs - row_dot)).astype(bf16)
            yield
            part_q = dot(grad_scores, keep(k_pair, mask))
            part_k = dot(grad_scores, keep(q_pair, mask), TN)
            part_v = dot(probs.astype(bf16), keep(grad_mixed[:, pair_span(pair)], mask), TN)
            grad_q = part_q if grad_q is None else grad_q + part_q
            grad_k = part_k if grad_k is None else grad_k + part_k
            grad_v = part_v if grad_v is None else grad_v + part_v
        grads_q.append((grad_q * HD**-0.5).astype(bf16))
        grads_k.append(grad_k.astype(bf16))
        grads_v.append(grad_v.astype(bf16))
    yield
    grad_qkv = jnp.concatenate(grads_q + grads_k + grads_v, 1)
    stash["dqkv"][rows, :] = grad_qkv
    bias("qkv", 0, grad_qkv)
    yield
    grad_input_a = dot(grad_qkv, wqkv[...], NT)
    yield
    normed, inv_a = normalize(x)
    if inputs is not None:
        inputs[0][rows, :] = (normed * (1.0 + mod(1)) + mod(0)).astype(bf16)
    mods_out(0, token_sum(grad_input_a))
    mods_out(1, token_sum(grad_input_a * normed))
    result.append(grad_middle + norm_back(grad_input_a * (1.0 + mod(1)), normed, inv_a))


def weight_grads(input_a, input_m, mixed, acted, stash, places, outs, sems, fills):
    def add(side, start, value):
        rows = slice(start, start + value.shape[0])
        places[side][rows, :] = value if side else places[side][rows, :] + value

    for copy in fills:
        copy.wait()
    copies = []

    def send(side, start, stop):
        rows = pl.ds(start, stop - start)
        copy = pltpu.make_async_copy(places[side].at[rows, :], outs[side].at[rows, :], sems.at[len(copies)])
        copy.start()
        copies.append(copy)

    for part in range(3):
        piece = dot(stash["dqkv"][:, part * D : (part + 1) * D], input_a[...], TN)
        for side in range(2):
            for head in range(HEADS // 2):
                start = side * HALF + head * HD
                place = (3 * head + part) * HD
                add(side, place, piece[start : start + HD, :])
    for side in (1, 0):
        send(side, 0, QKV_S)
    for side in (1, 0):
        add(side, QKV_S, dot(stash["dg"][:, side * HMLP : (side + 1) * HMLP], input_m[...], TN))
        send(side, QKV_S, COL_S)
    for side in (1, 0):
        add(side, COL_S + HALF, dot(acted[:, side * HMLP : (side + 1) * HMLP], stash["dym"][...], TN))
        send(side, COL_S + HALF, BOTH)
    piece = dot(mixed[...], stash["dya"][...], TN)
    for side in (1, 0):
        add(side, COL_S, piece[side * HALF : (side + 1) * HALF, :])
        send(side, COL_S, COL_S + HALF)
    for copy in copies:
        copy.wait()


def error_fills(layer, err_col, err_row, place, sems):
    return [pltpu.make_async_copy(err_col.at[layer], place.at[pl.ds(0, COL_S), :], sems.at[0]),
            pltpu.make_async_copy(err_row.at[layer], place.at[pl.ds(COL_S, ROW_S), :], sems.at[1])]


BIAS = {"qkv": 0, "fc1": 3 * D, "proj": 3 * D + MLP, "fc2": 4 * D + MLP}
BIAS_WIDTH = 5 * D + MLP

PAY_PATCH, PAY_HEAD, PAY_PROJ, PAY_FC2, PAY_BPATCH, PAY_BHEAD, PAY_COND, PAY_BCOL = 0, 16, 32, 34, 36, 37, 38, 52
PAY_ROWS = 64
SMALL_ROWS = PAY_BCOL + 8 - PAY_PROJ


def forward_kernel(core, full, xt, mods, wpatch, pos, own, other, bcol_own, bcol_other, b_rep,
                   query, keyed, valued, probs, branch_a, middle, slope, branch_m, mixed, acted,
                   x2, next_own, next_other, wqkv, wo, bqkv, bfc1, hold_own, hold_other, sems):
    picks = [pltpu.make_async_copy(full.at[:, side, :, pl.ds(GATH, GATH)], hold, sems.at[i])
             for i, (side, hold) in enumerate(((core[0], hold_own), (1 - core[0], hold_other)))]
    leaves = [pltpu.make_async_copy(hold, out, sems.at[2 + i])
              for i, (hold, out) in enumerate(((hold_own, next_own), (hold_other, next_other)))]

    @pl.when(pl.program_id(0) == 0)
    def _():
        for copy in picks:
            copy.start()
        assemble(0, own, other, bcol_own, bcol_other, wqkv, wo, bqkv, bfc1)

    named = dict(query=query, keyed=keyed, valued=valued, mixed=mixed, branch_a=branch_a,
                 middle=middle, branch_m=branch_m)

    def chain(i):
        def put(name, value, index=None):
            if name in ("input_a", "input_m"):
                return
            if name == "probs":
                probs[i, index] = value
            elif name == "acted":
                acted[i, :, index * HMLP : (index + 1) * HMLP] = value
            elif name == "slope":
                slope[i, :, index * HMLP : (index + 1) * HMLP] = value
            else:
                named[name][i] = value

        x = dot(xt[i], wpatch[0], TN) + vector(b_rep, START_PATCH) + pos[...]
        result = []
        yield from layer_forward(x, lambda j: mods[i, j : j + 1, :], own, other, wqkv, wo, bqkv[...],
                                 bfc1[...], vector(b_rep, 0), vector(b_rep, START_FC2), put, result)
        x2[i] = result[0]

    run_steps([chain(i) for i in range(xt.shape[0])], LAG)

    @pl.when(pl.program_id(0) == 0)
    def _():
        for copy, leave in zip(picks, leaves):
            copy.wait()
            leave.start()

    @pl.when(pl.program_id(0) == pl.num_programs(0) - 1)
    def _():
        for leave in leaves:
            leave.wait()


def diagonal(count):
    down = lax.broadcasted_iota(jnp.int32, (count, count), 0)
    across = lax.broadcasted_iota(jnp.int32, (count, count), 1)
    return down == across


def write_bcol(dbias, side, out, layer):
    pieces = []
    for head in range(HEADS // 2):
        for part in range(3):
            start = part * D + side * HALF + head * HD
            pieces.append(dbias[:, start : start + HD])
    start = 3 * D + side * HMLP
    pieces.append(dbias[:, start : start + HMLP])
    pieces.append(jnp.zeros((1, 4 * D - COL_S), f32))
    line = jnp.concatenate(pieces, 1)
    for row in range(4):
        at = PAY_BCOL + 4 * layer + row
        out[at : at + 1, :] = line[:, row * D : (row + 1) * D]


def middle_kernel(x2, mods, own, other, bcol_own, bcol_other, b_rep, whead, targets, err_col, err_row,
                  dx, dmods, grad_own, grad_other, dbias, dhead, dbhead, loss,
                  wqkv, wo, bqkv, bfc1, query, keyed, valued, probs, mixed, branch_a, middle, acted,
                  slope, branch_m, input_a, input_m, s_dqkv, s_dg, s_dya, s_dym, place_own, place_other,
                  out_sems, fill_sems):
    step = pl.program_id(0)
    fills = error_fills(1, err_col, err_row, place_own, fill_sems)

    @pl.when(step == 0)
    def _():
        for copy in fills:
            copy.start()
        assemble(1, own, other, bcol_own, bcol_other, wqkv, wo, bqkv, bfc1)
        dbias[...] = jnp.zeros_like(dbias)
        dhead[...] = jnp.zeros_like(dhead)
        dbhead[...] = jnp.zeros_like(dbhead)
        loss[...] = jnp.zeros_like(loss)

    stacked = dict(mixed=mixed, input_a=input_a, input_m=input_m)
    single = dict(query=query, keyed=keyed, valued=valued, branch_a=branch_a, middle=middle,
                  branch_m=branch_m)
    stash = dict(dqkv=s_dqkv, dg=s_dg, dya=s_dya, dym=s_dym)
    group = x2.shape[0]

    def chain(i):
        rows = pl.ds(pl.multiple_of((step * group + i) * TOK, TOK), TOK)

        def put(name, value, index=None):
            if name == "probs":
                probs[i, index] = value
            elif name == "acted":
                acted[rows, index * HMLP : (index + 1) * HMLP] = value
            elif name == "slope":
                slope[i, :, index * HMLP : (index + 1) * HMLP] = value
            elif name in stacked:
                stacked[name][rows, :] = value
            else:
                single[name][i] = value

        def take(name, index=None):
            if name == "probs":
                return probs[i, index]
            if name == "slope":
                return slope[i, :, index * HMLP : (index + 1) * HMLP]
            return single[name][i]

        def mod(j):
            return mods[i, 6 + j : 7 + j, :]

        def mods_out(j, value):
            dmods[i, j : j + 1, :] = value

        def bias(name, start, value):
            at = BIAS[name] + start
            dbias[:, at : at + value.shape[1]] += token_sum(value.astype(f32))

        result = []
        yield from layer_forward(x2[i], mod, own, other, wqkv, wo, bqkv[...], bfc1[...], vector(b_rep, D),
                                 vector(b_rep, START_FC2 + D), put, result)
        yield
        normed, inv_std = normalize(result[0])
        input_f = (normed * (1.0 + mod(7)) + mod(6)).astype(bf16)
        bhead = jnp.sum(
            jnp.where(diagonal(PV), b_rep[:, START_HEAD : START_HEAD + PV], 0.0), 1, keepdims=True
        )
        yield
        miss = dot(whead[0], input_f, NT) + bhead - targets[i]
        loss[...] += jnp.sum(miss * miss, 0, keepdims=True)
        grad_pred = (2.0 * miss).astype(bf16)
        yield
        dhead[...] += dot(grad_pred, input_f)
        dbhead[...] += jnp.sum(grad_pred.astype(f32), 1, keepdims=True)
        grad_input = dot(grad_pred, whead[0], TN)
        yield
        mods_out(6, token_sum(grad_input))
        mods_out(7, token_sum(grad_input * normed))
        grad = norm_back(grad_input * (1.0 + mod(7)), normed, inv_std)
        result = []
        yield from layer_backward(grad, x2[i], mod, own, other, wqkv, wo, take, rows, stash, mods_out, bias,
                                  result)
        dx[i] = result[0]

    run_steps([chain(i) for i in range(group)], LAG)

    @pl.when(step == pl.num_programs(0) - 1)
    def _():
        weight_grads(input_a, input_m, mixed, acted, stash, (place_own, place_other),
                     (grad_own, grad_other), out_sems, fills)


def last_kernel(dx, mods, own, other, bcol_own, bcol_other, b_rep, xt, wpatch, pos,
                dbias1, dhead, dbhead, loss, dmods1, err_col, err_row,
                query, keyed, valued, probs, branch_a, middle, slope, branch_m, mixed, acted,
                dmods, grad_own, grad_other, pay_own, pay_other,
                wqkv, wo, bqkv, bfc1, a_input_a, a_input_m, a_mixed, a_acted, s_dqkv, s_dg, s_dya, s_dym,
                dbias, sems, place_own, place_other, out_sems, fill_sems):
    step = pl.program_id(0)
    pairs = ((mixed, a_mixed), (acted, a_acted))
    copies = [pltpu.make_async_copy(src, dst, sems.at[i]) for i, (src, dst) in enumerate(pairs)]
    fills = error_fills(0, err_col, err_row, place_own, fill_sems)

    @pl.when(step == 0)
    def _():
        assemble(0, own, other, bcol_own, bcol_other, wqkv, wo, bqkv, bfc1)
        dbias[...] = jnp.zeros_like(dbias)
        pay_own[...] = jnp.zeros_like(pay_own)
        for copy in copies + fills:
            copy.start()

    rows = pl.ds(pl.multiple_of(step * TOK, TOK), TOK)
    single = dict(query=query, keyed=keyed, valued=valued, branch_a=branch_a, middle=middle,
                  branch_m=branch_m)

    def take(name, index=None):
        if name == "probs":
            return probs[0, index]
        if name == "slope":
            return slope[0, :, index * HMLP : (index + 1) * HMLP]
        return single[name][0]

    def mods_out(j, value):
        dmods[0, j : j + 1, :] = value

    def bias(name, start, value):
        at = BIAS[name] + start
        dbias[:, at : at + value.shape[1]] += token_sum(value.astype(f32))

    stash = dict(dqkv=s_dqkv, dg=s_dg, dya=s_dya, dym=s_dym)
    result = []
    x = dot(xt[0], wpatch[0], TN) + vector(b_rep, START_PATCH) + pos[...]
    run_steps([layer_backward(dx[0], x, lambda j: mods[0, j : j + 1, :], own, other, wqkv, wo,
                              take, rows, stash, mods_out, bias, result, (a_input_a, a_input_m))], 0)
    (grad,) = result
    grad = grad.astype(bf16)
    pay_own[PAY_PATCH : PAY_PATCH + PV, :] += dot(xt[0], grad)
    pay_own[PAY_BPATCH : PAY_BPATCH + 1, :] += token_sum(grad.astype(f32))
    dmods[0, 6 : 6 + 8, :] = dmods1[0]
    rounded = dmods[0].astype(bf16).astype(f32)
    dmods[0] = rounded
    pay_own[PAY_COND : PAY_COND + 14, :] += rounded

    @pl.when(step == pl.num_programs(0) - 1)
    def _():
        for copy in copies:
            copy.wait()
        weight_grads(a_input_a, a_input_m, a_mixed, a_acted, stash, (place_own, place_other),
                     (grad_own, grad_other), out_sems, fills)
        pay_own[PAY_HEAD : PAY_HEAD + PV, :] = dhead[...]
        for layer, values in enumerate((dbias, dbias1)):
            pay_own[PAY_PROJ + layer : PAY_PROJ + layer + 1, :] = values[:, BIAS["proj"] : BIAS["proj"] + D]
            pay_own[PAY_FC2 + layer : PAY_FC2 + layer + 1, :] = values[:, BIAS["fc2"] : BIAS["fc2"] + D]
        head_line = jnp.sum(jnp.where(diagonal(PV), dbhead[...], 0.0), 0, keepdims=True)
        pay_own[PAY_BHEAD : PAY_BHEAD + 1, :] = jnp.concatenate(
            [head_line, jnp.sum(loss[...], 1, keepdims=True), jnp.zeros((1, D - PV - 1), f32)], 1
        )
        pay_other[...] = pay_own[...]
        for side, out in enumerate((pay_own, pay_other)):
            for layer, values in enumerate((dbias, dbias1)):
                write_bcol(values, side, out, layer)
        for out in (pay_own, pay_other):
            out[PAY_BCOL + 8 :, :] = jnp.zeros((PAY_ROWS - PAY_BCOL - 8, D), f32)


def per_latent(*shape, group=1):
    zeros = (0,) * len(shape)
    return pl.BlockSpec((group,) + shape, lambda n: (n,) + zeros)


def fixed(*shape):
    zeros = (0,) * len(shape)
    return pl.BlockSpec(shape, lambda n: zeros, pipeline_mode=pl.Buffered(1))


def params():
    return pltpu.CompilerParams(dimension_semantics=("arbitrary",), vmem_limit_bytes=62 * 2**20)


SAVED = [
    ("query", (TOK, D), bf16), ("keyed", (TOK, D), bf16), ("valued", (TOK, D), bf16),
    ("probs", (HEADS, TOK, TOK), f32), ("branch_a", (TOK, D), f32), ("middle", (TOK, D), f32),
    ("slope", (TOK, MLP), f32), ("branch_m", (TOK, D), f32), ("mixed", (TOK, D), bf16),
    ("acted", (TOK, MLP), bf16),
]
BOTH = COL_S + ROW_S
GRAD_SHAPES = [(BOTH, D), (BOTH, D)]
WEIGHT_SCRATCH = [pltpu.VMEM((D, 3 * D), bf16), pltpu.VMEM((D, D), bf16),
                  pltpu.VMEM((1, 3 * D), f32), pltpu.VMEM((1, MLP), f32)]


def weight_specs():
    return [fixed(D, GATH), fixed(D, GATH), fixed(L, COL_S), fixed(L, COL_S), fixed(1, NBR)]


def stash_scratch(count):
    rows = count * TOK
    return [pltpu.VMEM((rows, 3 * D), bf16), pltpu.VMEM((rows, MLP), bf16),
            pltpu.VMEM((rows, D), bf16), pltpu.VMEM((rows, D), bf16)]


def place_scratch():
    return [pltpu.VMEM(shape, f32) for shape in GRAD_SHAPES] + [pltpu.SemaphoreType.DMA((8,)), pltpu.SemaphoreType.DMA((2,))]


def cost(flops, nbytes, count):
    return pl.CostEstimate(flops=int(flops * count), bytes_accessed=int(nbytes * count),
                           transcendentals=int(2e6 * count))


def run_forward(core, full, xt, mods, full_io, pos, weights):
    count = xt.shape[0]
    outs = SAVED + [("x2", (TOK, D), f32)]
    return pl.pallas_call(
        forward_kernel,
        grid=(count // GROUP,),
        in_specs=[pl.BlockSpec(memory_space=pltpu.SMEM), pl.BlockSpec(memory_space=pl.ANY), per_latent(PV, TOK, group=GROUP), per_latent(14, D, group=GROUP),
                  pl.BlockSpec((1, PV, D), lambda n: (0, 0, 0)), fixed(TOK, D)] + weight_specs(),
        out_specs=[per_latent(*shape, group=GROUP) for _, shape, _ in outs]
        + [pl.BlockSpec(memory_space=pl.ANY)] * 2,
        out_shape=[jax.ShapeDtypeStruct((count,) + shape, kind) for _, shape, kind in outs]
        + [jax.ShapeDtypeStruct((full.shape[0], full.shape[2], GATH), bf16)] * 2,
        scratch_shapes=WEIGHT_SCRATCH + [pltpu.VMEM((full.shape[0], full.shape[2], GATH), bf16)] * 2
        + [pltpu.SemaphoreType.DMA((4,))],
        compiler_params=params(),
        cost_estimate=cost(1.0e9, 6e6, count),
        name="forward_first",
    )(core, full, xt, mods, full_io, pos, *weights)


def run_middle(x2, mods, weights, full_io, targets, err_col, err_row):
    count = x2.shape[0]
    rows = count * TOK
    outs = [((count, TOK, D), per_latent(TOK, D, group=GROUP)), ((count, 8, D), per_latent(8, D, group=GROUP))]
    outs += [(shape, pl.BlockSpec(memory_space=pl.ANY)) for shape in GRAD_SHAPES]
    outs += [(shape, fixed(*shape)) for shape in ((1, BIAS_WIDTH), (PV, D), (PV, 1), (1, TOK))]
    return pl.pallas_call(
        middle_kernel,
        grid=(count // GROUP,),
        in_specs=[per_latent(TOK, D, group=GROUP), per_latent(14, D, group=GROUP)] + weight_specs()
        + [pl.BlockSpec((1, PV, D), lambda n: (1, 0, 0)), per_latent(PV, TOK, group=GROUP)]
        + [pl.BlockSpec(memory_space=pl.ANY)] * 2,
        out_specs=[spec for _, spec in outs],
        out_shape=[jax.ShapeDtypeStruct(shape, f32) for shape, _ in outs],
        scratch_shapes=WEIGHT_SCRATCH
        + [pltpu.VMEM((GROUP, TOK, D), bf16)] * 3
        + [pltpu.VMEM((GROUP, HEADS, TOK, TOK), f32), pltpu.VMEM((rows, D), bf16),
           pltpu.VMEM((GROUP, TOK, D), f32), pltpu.VMEM((GROUP, TOK, D), f32), pltpu.VMEM((rows, MLP), bf16),
           pltpu.VMEM((GROUP, TOK, MLP), f32), pltpu.VMEM((GROUP, TOK, D), f32),
           pltpu.VMEM((rows, D), bf16), pltpu.VMEM((rows, D), bf16)]
        + stash_scratch(count) + place_scratch(),
        compiler_params=params(),
        cost_estimate=cost(3.2e9, 3e6, count),
        name="layer_second",
    )(x2, mods, *weights, full_io, targets, err_col, err_row)


def run_last(dx, mods, weights, xt, full_io, pos, smalls, dmods1, err_col, err_row, saved):
    count = dx.shape[0]
    rows = count * TOK
    outs = [((count, 14, D), per_latent(14, D))]
    outs += [(shape, pl.BlockSpec(memory_space=pl.ANY)) for shape in GRAD_SHAPES]
    outs += [(shape, fixed(*shape)) for shape in ((PAY_ROWS, D), (PAY_ROWS, D))]
    return pl.pallas_call(
        last_kernel,
        grid=(count,),
        in_specs=[per_latent(TOK, D), per_latent(14, D)] + weight_specs()
        + [per_latent(PV, TOK), pl.BlockSpec((1, PV, D), lambda n: (0, 0, 0)), fixed(TOK, D)]
        + [fixed(*shape) for shape in ((1, BIAS_WIDTH), (PV, D), (PV, 1), (1, TOK))] + [per_latent(8, D)]
        + [pl.BlockSpec(memory_space=pl.ANY)] * 2
        + [per_latent(*shape) for _, shape, _ in SAVED[:-2]] + [pl.BlockSpec(memory_space=pl.ANY)] * 2,
        out_specs=[spec for _, spec in outs],
        out_shape=[jax.ShapeDtypeStruct(shape, f32) for shape, _ in outs],
        scratch_shapes=WEIGHT_SCRATCH
        + [pltpu.VMEM((rows, D), bf16)] * 3 + [pltpu.VMEM((rows, MLP), bf16)]
        + stash_scratch(count) + [pltpu.VMEM((1, BIAS_WIDTH), f32), pltpu.SemaphoreType.DMA((2,))]
        + place_scratch(),
        compiler_params=params(),
        cost_estimate=cost(2.2e9, 8e6, count),
        name="backward_first",
    )(dx, mods, *weights, xt, full_io, pos, *smalls, dmods1, err_col, err_row,
      *saved[:-2], *[v.reshape(rows, -1) for v in saved[-2:]])


PACK = 128
WIDE = 3 * D


def split3(values):
    high = values.astype(bf16)
    rest = values - high.astype(f32)
    mid = rest.astype(bf16)
    low = (rest - mid.astype(f32)).astype(bf16)
    return high, mid, low


def narrow_dot(small, big, dims):
    parts = split3(small)
    high, mid, low = split3(big)
    first = dot(jnp.concatenate(parts, 0), high, dims)
    second = dot(jnp.concatenate(parts[:2], 0), mid, dims)
    third = dot(parts[0], low, dims)
    r = small.shape[0]
    return first[:r] + ((first[r : 2 * r] + second[:r]) + (first[2 * r :] + second[r:] + third))


def outer(left, right):
    l1, l2, l3 = split3(left)
    r1, r2, r3 = split3(right)
    return dot(
        jnp.concatenate([l1, l1, l2, l2, l1, l3], 0), jnp.concatenate([r1, r2, r1, r2, r3, r1], 0), TN
    )


CHUNKS = [(448 * k, 448) for k in range(3)] + [(COL_S + 480 * k, 480) for k in range(2)]


def layer_chunks(layer, err_col, err_row):
    for at, size in CHUNKS:
        ref, start = (err_col, at) if at < COL_S else (err_row, at - COL_S)
        yield ref.at[layer, pl.ds(start, size), :], pl.ds(at, size)


def begin_project(own, got, mat, v_own, v_got, sems, out_sems):
    loads, stores = [], []
    for k, (at, size) in enumerate(CHUNKS):
        rows = pl.ds(at, size)
        loads.append([pltpu.make_async_copy(src.at[rows, :], dst.at[rows, :], sems.at[2 * k + i])
                      for i, (src, dst) in enumerate(((own, v_own), (got, v_got)))])
        stores.append(pltpu.make_async_copy(v_own.at[rows, :], mat.at[rows, :], out_sems.at[k]))
        for copy in loads[-1]:
            copy.start()
    return loads, stores


def project(layer, loads, stores, fac_col, fac_row, left_col, left_row, v_own, v_got):
    left_row[...] = jnp.zeros_like(left_row)
    total = None
    for (at, size), copies, store in zip(CHUNKS, loads, stores):
        for copy in copies:
            copy.wait()
        matrix = v_own[at : at + size, :] + v_got[at : at + size, :]
        v_own[at : at + size, :] = matrix
        store.start()
        if at < COL_S:
            part = narrow_dot(fac_col[layer][:, at : at + size], matrix, NN)
            total = part if total is None else total + part
        else:
            left_row[:, at - COL_S : at - COL_S + size] = narrow_dot(fac_row[layer], matrix, NT)
    left_col[...] = total


ANY = pl.BlockSpec(memory_space=pl.ANY)
VMEM = pl.BlockSpec(memory_space=pltpu.VMEM)
SMEM = pl.BlockSpec(memory_space=pltpu.SMEM)
PROJECT_SCRATCH = [pltpu.VMEM((BOTH, D), f32)] * 2 + [
    pltpu.SemaphoreType.DMA((2 * len(CHUNKS),)), pltpu.SemaphoreType.DMA((len(CHUNKS),))]


def large():
    return pltpu.CompilerParams(vmem_limit_bytes=62 * 2**20)


def shapes_of(shapes):
    return [jax.ShapeDtypeStruct(shape, f32) for shape in shapes]


def exchange_kernel(block, place, dmods, full_cond, cond, sent):
    n_dp = sent.shape[0]
    count = dmods.shape[0]
    line = jnp.concatenate([dmods[:, j, :] for j in range(14)], 1)
    grad_act = dot(line.astype(bf16), full_cond[...], NT)
    cond_own = cond[pl.ds(pl.multiple_of(place[0] * count, count), count), :]
    gate = 1.0 / (1.0 + jnp.exp(-cond_own))
    grad_cond = grad_act * (gate * (1.0 + cond_own * (1.0 - gate)))
    sent[:, :count, :] = jnp.broadcast_to(grad_cond[None], (n_dp, count, D))
    for j in range(n_dp):
        sent[j, count:, :] = jnp.concatenate(
            [line[:, j * block : (j + 1) * block], jnp.zeros((count, D - block), f32)], 1
        )


def run_exchange(n_dp, place, dmods, full_cond, cond):
    return pl.pallas_call(
        lambda *refs: exchange_kernel(N_MODS // n_dp, *refs),
        in_specs=[SMEM, VMEM, VMEM, VMEM],
        out_shape=jax.ShapeDtypeStruct((n_dp, 2 * dmods.shape[0], D), f32),
        compiler_params=large(),
        name="modulation_rows",
    )(place, dmods, full_cond, cond)


def project_kernel(own1, got1, own0, got0, fac_col, fac_row, pay_own, pay_got, err_io, fac_io,
                   mat1, mat0, mat_io, sent, left_col1, left_row1, left_col, left_row,
                   v_own1, v_got1, sems1, out_sems1, v_own0, v_got0, sems0, out_sems0):
    loads1, stores1 = begin_project(own1, got1, mat1, v_own1, v_got1, sems1, out_sems1)
    loads0, stores0 = begin_project(own0, got0, mat0, v_own0, v_got0, sems0, out_sems0)
    project(1, loads1, stores1, fac_col, fac_row, left_col1, left_row1, v_own1, v_got1)
    project(0, loads0, stores0, fac_col, fac_row, left_col, left_row, v_own0, v_got0)
    share = sent.shape[1]
    pay = pay_own[...] + pay_got[...]
    left_io = []
    for index in range(2):
        matrix = pay[index * PV : (index + 1) * PV] + err_io[index]
        mat_io[index] = matrix
        left_io.append(dot_full(fac_io[index], matrix))
    sent[...] = jnp.zeros_like(sent)
    tall = (left_row, left_row1)
    for column in range(RANK):
        pick = slice(column, column + 1)
        lines = [tall[i % 2][pick, (i // 2) * D : (i // 2 + 1) * D] for i in (0, 1)]
        lines += [left_col[pick, :], left_col1[pick, :], left_io[0][pick], left_io[1][pick]]
        lines += [tall[i % 2][pick, (i // 2) * D : (i // 2 + 1) * D] for i in (2, 3, 4, 5)]
        for extra in range(6):
            at = column * 6 + extra
            if at < SMALL_ROWS:
                lines.append(pay[PAY_PROJ + at : PAY_PROJ + at + 1])
        for slot, line in enumerate(lines):
            at = column * 16 + slot
            sent[at // share, at % share : at % share + 1, :] = line
    for store in stores1 + stores0:
        store.wait()


def run_project(n_dp, own1, got1, own0, got0, fac_col, fac_row, pay_own, pay_got, err_io, fac_io):
    return pl.pallas_call(
        project_kernel,
        in_specs=[ANY] * 4 + [VMEM] * 6,
        out_specs=[ANY, ANY, VMEM, VMEM],
        out_shape=shapes_of([(BOTH, D), (BOTH, D), (2, PV, D), (n_dp, PACK // n_dp, D)]),
        scratch_shapes=[pltpu.VMEM((RANK, D), f32), pltpu.VMEM((RANK, WIDE), f32)] * 2 + PROJECT_SCRATCH * 2,
        compiler_params=large(),
        cost_estimate=pl.CostEstimate(flops=int(1e9), bytes_accessed=int(1.5e7), transcendentals=0),
        name="left_factors",
    )(own1, got1, own0, got0, fac_col, fac_row, pay_own, pay_got, err_io, fac_io)


TIME_ROWS = FREQ + D + 8


def modulation_kernel(block, core, got, act_half, features, first, first_act, full_time, labels,
                      cond_mine, cond_their, time_part, table_part):
    n_dp = got.shape[0]
    count = got.shape[1] // 2
    half = block // 2
    grad_cond = got[:, :count, :].reshape(n_dp * count, D)
    cols = got[:, count : 2 * count, :].reshape(n_dp * count, D)
    left, right = cols[:, :half].astype(bf16), cols[:, half:block].astype(bf16)
    is_first = core[0] == 0
    grad_left = dot(act_half[...], left, TN)
    grad_right = dot(act_half[...], right, TN)
    cond_mine[...] = jnp.where(is_first, grad_left, grad_right)
    cond_their[...] = jnp.where(is_first, grad_right, grad_left)
    grad_second = grad_cond.astype(bf16)
    gate = 1.0 / (1.0 + jnp.exp(-first[...]))
    slope = gate * (1.0 + first[...] * (1.0 - gate))
    grad_first = (dot(grad_second, full_time[FREQ:, :], NT) * slope).astype(bf16)
    time_part[:FREQ, :] = dot(features[...], grad_first, TN)
    time_part[FREQ : FREQ + D, :] = dot(first_act[...], grad_second, TN)
    time_part[FREQ + D :, :] = jnp.concatenate(
        [token_sum(grad_first.astype(f32)), token_sum(grad_second.astype(f32)), jnp.zeros((6, D), f32)], 0
    )
    onehot = (labels[...] == lax.broadcasted_iota(jnp.int32, (n_dp * count, CLASSES), 1)).astype(f32).astype(bf16)
    high, mid, low = split3(grad_cond)
    table_part[...] = dot(high, onehot, TN) + (dot(mid, onehot, TN) + dot(low, onehot, TN))


def run_modulation(core, got, act_half, features, first, first_act, full_time, labels):
    half = N_MODS // got.shape[0] // 2
    shapes = [(D, half), (D, half), (TIME_ROWS, D), (D, CLASSES)]
    vmem = pl.BlockSpec(memory_space=pltpu.VMEM)
    return pl.pallas_call(
        lambda *refs: modulation_kernel(2 * half, *refs),
        in_specs=[pl.BlockSpec(memory_space=pltpu.SMEM)] + [vmem] * 7,
        out_shape=[jax.ShapeDtypeStruct(shape, f32) for shape in shapes],
        compiler_params=pltpu.CompilerParams(vmem_limit_bytes=62 * 2**20),
        name="modulation_gradients",
    )(core, got, act_half, features, first, first_act, full_time, labels)


COL_ROWS = 4 * RANK
ROW_AT = L * COL_ROWS
IO_AT = ROW_AT + L * RANK
EXTRA_AT = IO_AT + 2 * RANK


def cond_top(rows):
    return -(-((rows + 1) // 2) // 8) * 8


def ortho(packed, left_col, left_row, left_io):
    columns = []
    blank = jnp.zeros((4, D), f32)
    for index in range(RANK):
        block = packed[index]
        column = jnp.concatenate(
            [block[0:6], jnp.concatenate([block[6:8], blank], 0), jnp.concatenate([block[8:10], blank], 0)], 1
        )
        for earlier in columns:
            column = column - jnp.sum(earlier * column, -1, keepdims=True) * earlier
        column = column * lax.rsqrt(jnp.sum(column * column, -1, keepdims=True) + ortho_eps)
        for layer in range(L):
            left_row[layer, index : index + 1, :] = column[layer : layer + 1]
            left_col[layer, index : index + 1, :] = column[2 + layer : 3 + layer, :D]
            left_io[layer, index : index + 1, :] = column[4 + layer : 5 + layer, :D]
        columns.append(column)


def total_squares(values):
    return jnp.sum(values * values, keepdims=True)


def rows_kernel(cond_own, cond_got, table_own, table_got, sent, table_share, sums):
    cond_grad = cond_own[...] + cond_got[...]
    table = table_own[...] + table_got[...]
    table_share[...] = table
    sums[...] = jnp.concatenate([total_squares(cond_grad), total_squares(table), jnp.zeros((1, D - 2), f32)], 1)
    n_dp = sent.shape[0]
    rows, half = D // n_dp, cond_grad.shape[1]
    top = cond_top(rows)
    for j in range(n_dp):
        piece = cond_grad[j * rows : (j + 1) * rows]
        sent[j, : min(top, rows), :half] = piece[:top]
        if rows > top:
            sent[j, : rows - top, half : 2 * half] = piece[top:]


def run_rows(n_dp, cond_own, cond_got, table_own, table_got):
    return pl.pallas_call(
        rows_kernel,
        out_shape=shapes_of([(n_dp, cond_top(D // n_dp), D), table_own.shape, (1, D)]),
        compiler_params=large(),
        name="modulation_sums",
    )(cond_own, cond_got, table_own, table_got)


def mat_loads(mats, places, sems):
    return [[pltpu.make_async_copy(mat.at[pl.ds(at, size), :], place.at[pl.ds(at, size), :],
                                   sems.at[layer * len(CHUNKS) + k]) for k, (at, size) in enumerate(CHUNKS)]
            for layer, (mat, place) in enumerate(zip(mats, places))]


def right_kernel(packed, mat0, mat1, mat_io, sums, sent, left_col, left_row, left_io, flat, v0, v1, sems):
    loads = mat_loads((mat0, mat1), (v0, v1), sems)
    for copies in loads:
        for copy in copies:
            copy.start()
    ortho(packed, left_col, left_row, left_io)
    for copies in loads:
        for copy in copies:
            copy.wait()
    for layer, mat in enumerate((v0, v1)):
        right = narrow_dot(left_col[layer], mat[:COL_S, :], NT)
        for piece in range(4):
            wide = min(D, COL_S - piece * D)
            at = layer * COL_ROWS + piece * RANK
            if wide < D:
                flat[at : at + RANK, :] = jnp.zeros((RANK, D), f32)
            flat[at : at + RANK, :wide] = right[:, piece * D : piece * D + wide]
        at = ROW_AT + layer * RANK
        flat[at : at + RANK, :] = narrow_dot(left_row[layer][:, :ROW_S], mat[COL_S:, :], NN)
        at = IO_AT + layer * RANK
        flat[at : at + RANK, :] = jnp.zeros((RANK, D), f32)
        flat[at : at + RANK, :PV] = dot_full(left_io[layer], mat_io[layer], NT)
    flat[EXTRA_AT:, :] = jnp.zeros((PACK - EXTRA_AT, D), f32)
    flat[EXTRA_AT : EXTRA_AT + 1, :] = sums[...]
    sent[...] = flat[...].reshape(sent.shape)


def run_right(n_dp, packed, mats, mat_io, sums):
    return pl.pallas_call(
        right_kernel,
        in_specs=[VMEM, ANY, ANY, VMEM, VMEM],
        out_shape=shapes_of([(n_dp, PACK // n_dp, D), (L, RANK, D), (L, RANK, WIDE), (2, RANK, D)]),
        scratch_shapes=[pltpu.VMEM((PACK, D), f32), pltpu.VMEM((BOTH, D), f32), pltpu.VMEM((BOTH, D), f32),
                        pltpu.SemaphoreType.DMA((L * len(CHUNKS),))],
        compiler_params=large(),
        name="right_factors",
    )(packed, *mats, mat_io, sums)


def norm_kernel(packed, left_packed, left_col, left_row, left_io, time_own, time_got,
                right_col, right_row, right_io, parts, brep_grad, bcol_grad):
    for layer in range(L):
        for piece in range(4):
            wide = min(D, COL_S - piece * D)
            at = layer * COL_ROWS + piece * RANK
            right_col[layer, :, piece * D : piece * D + wide] = packed[at : at + RANK, :wide]
        at = ROW_AT + layer * RANK
        right_row[layer] = packed[at : at + RANK, :]
        at = IO_AT + layer * RANK
        right_io[layer] = packed[at : at + RANK, :PV]

    def small(at):
        row = at - PAY_PROJ
        return left_packed[row // 6, 10 + row % 6 : 11 + row % 6, :]

    time_bias = time_own[FREQ + D :, :] + time_got[FREQ + D :, :]
    lines = [small(PAY_PROJ + row) for row in range(4)] + [small(PAY_COND + row) for row in range(14)]
    lines += [time_bias[0:1], time_bias[1:2], small(PAY_BPATCH), small(PAY_BHEAD)[:, :PV]]
    whole = jnp.zeros((1, 1), f32)
    for row, line in enumerate(lines):
        brep_grad[:, row * D : row * D + line.shape[1]] = line
        whole = whole + total_squares(line)
    split = jnp.zeros((1, 1), f32)
    for layer in range(L):
        line = jnp.concatenate([small(PAY_BCOL + 4 * layer + row) for row in range(4)], 1)[:, :COL_S]
        bcol_grad[layer : layer + 1, :] = line
        split = split + total_squares(line)
    whole = whole + total_squares(time_own[: FREQ + D, :] + time_got[: FREQ + D, :])

    def gram(left, right):
        return jnp.sum(dot_full(left, left, NT) * dot_full(right, right, NT), keepdims=True)

    for layer in range(L):
        split = split + gram(left_col[layer], right_col[layer]) + gram(left_row[layer], right_row[layer])
        whole = whole + gram(left_io[layer], right_io[layer])
    sums = packed[EXTRA_AT : EXTRA_AT + 1, :]
    split = split + sums[:, 0:1]
    whole = whole + sums[:, 1:2]
    loss = small(PAY_BHEAD)[:, PV : PV + 1]
    parts[...] = jnp.concatenate([split, whole, loss, jnp.zeros((1, 125), f32)], 1)


def run_norm(packed, left_packed, lefts, time_own, time_got):
    shapes = [(L, RANK, COL_S), (L, RANK, D), (2, RANK, PV), (1, 128), (1, NBR), (L, COL_S)]
    return pl.pallas_call(
        norm_kernel,
        out_shape=[jax.ShapeDtypeStruct(shape, f32) for shape in shapes],
        compiler_params=pltpu.CompilerParams(vmem_limit_bytes=62 * 2**20),
        name="gradient_norm",
    )(packed, left_packed, *lefts, time_own, time_got)


def next_errors(loads, mat_io, left_col, left_row, left_io, right_col, right_row, right_io,
                err_col, err_row, err_io, v0, v1, out_sems):
    stores = []
    for layer, place in enumerate((v0, v1)):
        for k, ((at, size), (target, rows)) in enumerate(zip(CHUNKS, layer_chunks(layer, err_col, err_row))):
            if at < COL_S:
                approx = outer(right_col[layer][:, at : at + size], left_col[layer])
            else:
                approx = outer(left_row[layer][:, at - COL_S : at - COL_S + size], right_row[layer])
            loads[layer][k].wait()
            place[at : at + size, :] = place[at : at + size, :] - approx
            store = pltpu.make_async_copy(place.at[rows, :], target, out_sems.at[layer * len(CHUNKS) + k])
            store.start()
            stores.append(store)
        err_io[layer] = mat_io[layer] - outer(right_io[layer], left_io[layer])
    return stores


def own_columns(values, first, count):
    across = lax.broadcasted_iota(jnp.int32, (count, D), 1)
    down = lax.broadcasted_iota(jnp.int32, (count, D), 0)
    pick = (across == down + first).astype(f32).astype(bf16)
    high, mid, low = split3(values)
    return dot(high, pick, NT) + (dot(mid, pick, NT) + dot(low, pick, NT))


def update_kernel(core, parts, parts_got, left_col, right_col, right_row, left_row, right_io, left_io,
                  cond_own, cond_got, time_grad, table_grad, bcol_grad, brep_grad,
                  w_col, w_row, w_cond, w_time, w_io, w_table, b_col, b_rep,
                  m_col, m_row, m_cond, m_time, m_io, m_table, m_bcol, m_brep,
                  loss, clip, n_col, n_row, n_cond, n_time, n_io, n_table, n_bcol, n_brep,
                  v_col, v_row, v_cond, v_time, v_io, v_table, v_bcol, v_brep):
    clip_norm = jnp.sqrt(parts[:, 0:1] + parts_got[:, 0:1] + parts[:, 1:2])
    scaling = jnp.minimum(1.0, clip_limit / clip_norm)
    loss[...] = parts[:, 2:3]
    clip[...] = clip_norm

    def advance(weight, momentum, gradient):
        moved = momentum_decay * momentum + scaling * gradient
        return weight - learn_rate * moved, moved

    n_dp = cond_own.shape[0]
    rows = w_cond.shape[0]
    at = core[1] * rows
    for layer in range(L):
        n_col[layer], v_col[layer] = advance(
            w_col[layer], m_col[layer], outer(own_columns(left_col[layer], at, rows), right_col[layer]))
        n_row[layer], v_row[layer] = advance(
            w_row[layer], m_row[layer],
            outer(own_columns(right_row[layer], at, rows), left_row[layer][:, :ROW_S]))
        n_io[layer], v_io[layer] = advance(
            w_io[layer], m_io[layer], outer(right_io[layer], own_columns(left_io[layer], at, rows)))
    half = N_MODS // n_dp // 2
    top = cond_top(rows)
    is_first = core[0] == 0
    pieces = []
    for j in range(n_dp):
        mine, theirs = cond_own[j], cond_got[j]
        for pair in ((mine, theirs), (theirs, mine)):
            block = jnp.where(is_first, pair[0], pair[1])
            if rows > top:
                block = jnp.concatenate([block[:top, :half], block[: rows - top, half : 2 * half]], 0)
            else:
                block = block[:rows, :half]
            pieces.append(block)
    n_cond[...], v_cond[...] = advance(w_cond[...], m_cond[...], jnp.concatenate(pieces, 1))
    n_time[...], v_time[...] = advance(w_time[...], m_time[...], time_grad[...])
    n_table[...], v_table[...] = advance(w_table[...], m_table[...], table_grad[...])
    n_bcol[...], v_bcol[...] = advance(b_col[...], m_bcol[...], bcol_grad[...])
    n_brep[...], v_brep[...] = advance(b_rep[...], m_brep[...], brep_grad[...])


def final_kernel(*refs):
    head, (mat0, mat1, mat_io) = refs[:31], refs[31:34]
    news, (err_col, err_row, err_io, v0, v1, sems, out_sems) = refs[34:52], refs[52:]
    loads = mat_loads((mat0, mat1), (v0, v1), sems)
    for copies in loads:
        for copy in copies:
            copy.start()
    left_col, right_col, right_row, left_row, right_io, left_io = head[3:9]
    stores = next_errors(loads, mat_io, left_col, left_row, left_io, right_col, right_row, right_io,
                         err_col, err_row, err_io, v0, v1, out_sems)
    update_kernel(*head, *news)
    for store in stores:
        store.wait()


def run_final(core, grads, weights, momenta, mats, mat_io):
    shapes = [(1, 1), (1, 1)] + [v.shape for v in weights] * 2
    return pl.pallas_call(
        final_kernel,
        in_specs=[SMEM] + [VMEM] * (len(grads) + 2 * len(weights)) + [ANY, ANY, VMEM],
        out_specs=[VMEM] * len(shapes) + [ANY, ANY, VMEM],
        out_shape=shapes_of(shapes + [(L, COL_S, D), (L, ROW_S, D), (2, PV, D)]),
        scratch_shapes=[pltpu.VMEM((BOTH, D), f32), pltpu.VMEM((BOTH, D), f32),
                        pltpu.SemaphoreType.DMA((L * len(CHUNKS),)), pltpu.SemaphoreType.DMA((L * len(CHUNKS),))],
        compiler_params=pltpu.CompilerParams(vmem_limit_bytes=62 * 2**20),
        name="errors_and_update",
    )(core, *grads, *weights, *momenta, *mats, mat_io)


def swap(values):
    return lax.ppermute(values, "tensor", [(0, 1), (1, 0)])


def trade(chunks):
    return lax.all_to_all(chunks, "dp", 0, 0, tiled=True)


def spread(values):
    return trade(jnp.broadcast_to(values[None], (lax.axis_size("dp"),) + values.shape))


def exact_parts(values):
    high = lax.reduce_precision(values, 8, 7)
    mid = lax.reduce_precision(values - high, 8, 7)
    return [part.astype(bf16) for part in (high, mid, (values - high) - mid)]


def on_device(
    latents, gauss_noise, time_steps, labels, targets,
    w_col, w_row, w_cond, w_time, w_io, class_table, b_col, b_rep,
    mom_col, mom_row, mom_cond, mom_time, mom_io, mom_table, mom_bcol, mom_brep,
    err_col, err_row, err_io, fac_col, fac_row, fac_io,
):
    n_dp = lax.axis_size("dp")
    index_dp = lax.axis_index("dp")
    index_t = lax.axis_index("tensor")
    core = jnp.stack([index_t, index_dp]).astype(jnp.int32)
    first_core = index_t == 0
    n_all = labels.shape[0]
    per_dp = latents.shape[0]
    count = per_dp // 2
    rows = w_col.shape[1]

    def flip(values):
        return values.transpose(0, 2, 1)

    def halves(mine, theirs, axis):
        pair = jnp.stack([mine, theirs], axis)
        return jnp.where(first_core, pair, jnp.flip(pair, axis))

    row_sh = flip(w_row)
    shard = jnp.concatenate(
        [piece[layer] for layer in range(L)
         for piece in (w_col[:, :, QKV_S:], row_sh[:, :, HALF:], w_col[:, :, :QKV_S], row_sh[:, :, :HALF])], 1
    ).astype(bf16)
    full = lax.all_gather(shard, ("dp", "tensor"))

    block = N_MODS // n_dp
    half_block = block // 2
    classes = jnp.arange(CLASSES, dtype=jnp.int32)
    onehot_t = classes[:, None] == labels[None, :]
    looked = dot(class_table.astype(bf16), onehot_t.astype(bf16), TN).astype(bf16)
    time_rows = w_time.shape[0]
    sizes = [rows * n_all, time_rows * D, 2 * PV * rows, 3 * per_dp]
    wide = -(-sum(sizes) // 256) * 128
    common = jnp.concatenate(
        [part.reshape(-1) for part in
         (looked, w_time.astype(bf16), flip(w_io).astype(bf16), *exact_parts(time_steps))]
    )
    common = jnp.pad(common, (0, 2 * wide - common.shape[0]))
    common = lax.dynamic_slice_in_dim(common.reshape(2, wide), index_t, 1, 0)
    cond_bf = w_cond.astype(bf16).reshape(rows, n_dp, 2, half_block)
    cond_mine = lax.dynamic_slice_in_dim(cond_bf, index_t, 1, 2)[:, :, 0].transpose(1, 0, 2)
    sent = jnp.concatenate(
        [jnp.broadcast_to(common, (n_dp, wide)), cond_mine.reshape(n_dp, rows * half_block)], 1
    )
    got = trade(sent)
    cond_cols = got[:, wide:].reshape(D, half_block)
    mine = got[:, :wide]
    common = halves(mine, swap(mine), 1).reshape(n_dp, 2 * wide)
    ends = np.cumsum([0] + sizes)
    looked = common[:, : ends[1]].reshape(D, n_all).T
    full_time = common[:, ends[1] : ends[2]].reshape(FREQ + D, D)
    full_io = flip(common[:, ends[2] : ends[3]].reshape(n_dp, 2 * PV, rows).transpose(1, 0, 2).reshape(2, PV, D).transpose(0, 2, 1))
    steps_all = jnp.sum(common[:, ends[3] : ends[4]].reshape(n_dp, 3, per_dp).astype(f32), 1).reshape(n_all)

    features = frequency_features(steps_all).astype(bf16)
    first = dot(features, full_time[:FREQ]) + b_rep[START_FIRST:START_SECOND]
    first_act = jax.nn.silu(first).astype(bf16)
    second = dot(first_act, full_time[FREQ:]) + b_rep[START_SECOND:START_PATCH]
    cond = second + looked.astype(f32)
    cond_act = jax.nn.silu(cond).astype(bf16)
    mods = dot(cond_act, cond_cols).reshape(n_dp * 2, count, half_block)
    mods = lax.all_to_all(mods, ("dp", "tensor"), 0, 0, tiled=True)
    mods = mods.transpose(1, 0, 2).reshape(count, N_MODS)
    mods = (mods + b_rep[START_COND:START_FIRST]).reshape(count, 14, D)
    def half_of(values):
        split = values.reshape((n_dp, 2, count) + values.shape[1:])
        return lax.dynamic_slice_in_dim(split, index_t, 1, 1).reshape((n_dp * count,) + values.shape[1:])

    halves_of = [half_of(v) for v in (cond_act, features, first, first_act)]
    labels_half = half_of(labels)[:, None]
    place = (index_dp * 2 + index_t).astype(jnp.int32).reshape(1)
    full, mods, halves_of, labels_half, core, place = lax.optimization_barrier(
        (full, mods, halves_of, labels_half, core, place)
    )
    full = full.reshape(n_dp, 2, rows, L * GATH)

    def mine_of(values):
        return lax.dynamic_slice_in_dim(values, index_t * count, count, 0)

    steps_own = mine_of(time_steps)[:, None, None]
    xt = (
        (1.0 - steps_own) * flip(mine_of(latents)) + steps_own * flip(mine_of(gauss_noise))
    ).astype(bf16)
    b_line = b_rep[None]
    first_layer = full[:, :, :, :GATH]
    own = lax.dynamic_slice_in_dim(first_layer, index_t, 1, 1).reshape(D, GATH)
    other = lax.dynamic_slice_in_dim(first_layer, 1 - index_t, 1, 1).reshape(D, GATH)
    biases = (b_col, swap(b_col), b_line)
    weights = (own, other, *biases)
    pos = jnp.asarray(position_table())
    *saved, x2, own1, other1 = run_forward(core, full, xt, mods, full_io, pos, weights)
    weights1 = (own1.reshape(D, GATH), other1.reshape(D, GATH), *biases)
    x2, late_cond = lax.optimization_barrier((x2, w_cond))
    full_cond = lax.all_gather(late_cond.astype(bf16), "dp", axis=0, tiled=True)
    err_col_t, err_io_t = flip(err_col), flip(err_io)
    dx, dmods1, own1, oth1, *smalls = run_middle(
        x2, mods, weights1, full_io, flip(mine_of(targets)), err_col_t, err_row
    )
    got1 = swap(oth1)
    dmods, own0, oth0, pay_own, pay_oth = run_last(
        dx, mods, weights, xt, full_io, pos, smalls, dmods1, err_col_t, err_row, saved
    )
    got0, pay_got = swap(oth0), swap(pay_oth)

    rows_got = trade(run_exchange(n_dp, place, dmods, full_cond, cond))
    fac_col_t, fac_row_t, fac_io_t = flip(fac_col), flip(fac_row), flip(fac_io)
    mat1, mat0, mat_io, sent = run_project(
        n_dp, own1, got1, own0, got0, fac_col_t, fac_row_t, pay_own, pay_got, err_io_t, fac_io_t
    )
    mats = (mat0, mat1)
    rows_got, sent = lax.optimization_barrier((rows_got, sent))
    share = jnp.sum(trade(sent), 0)

    cond_mine, cond_their, time_own, table_part = run_modulation(core, rows_got, *halves_of, full_time, labels_half)
    share, cond_mine, cond_their, time_own, table_part = lax.optimization_barrier(
        (share, cond_mine, cond_their, time_own, table_part)
    )
    left_packed = spread(share).reshape(RANK, 16, D)
    cond_got, time_got = swap(cond_their), swap(time_own)
    table_own = lax.dynamic_slice_in_dim(table_part, index_dp * rows, rows, 0)
    cond_sent, table_share, sums = run_rows(n_dp, cond_mine, cond_got, table_own, swap(table_own))
    cond_rows = trade(cond_sent)

    sent, left_col, left_row, left_io = run_right(n_dp, left_packed, mats, mat_io, sums)
    time_at = index_dp * time_rows
    time_grad = (
        lax.dynamic_slice_in_dim(time_own, time_at, time_rows, 0)
        + lax.dynamic_slice_in_dim(time_got, time_at, time_rows, 0)
    )
    cond_rows, sent, time_grad = lax.optimization_barrier((cond_rows, sent, time_grad))
    packed = spread(jnp.sum(trade(sent), 0)).reshape(PACK, D)
    cond_rows_got = swap(cond_rows)
    lefts = (left_col, left_row, left_io)
    right_col, right_row, right_io, parts, brep_grad, bcol_grad = run_norm(
        packed, left_packed, lefts, time_own, time_got
    )
    parts_got = swap(parts)

    olds = (w_col, flip(w_row), w_cond, w_time, flip(w_io), class_table.T, b_col, b_line)
    momenta = (mom_col, flip(mom_row), mom_cond, mom_time, flip(mom_io), mom_table.T, mom_bcol, mom_brep[None])
    loss, clip_norm, *new, next_err_col, next_err_row, next_err_io = run_final(
        core,
        (parts, parts_got, left_col, right_col, right_row, left_row, right_io, left_io,
         cond_rows, cond_rows_got, time_grad, table_share, bcol_grad, brep_grad),
        olds, momenta, mats, mat_io,
    )

    def outward(col, row, cond, time, io, table, bcol, brep):
        return (col, flip(row), cond, time, flip(io), table.T, bcol, brep[0])

    return (
        loss.reshape(()), clip_norm.reshape(()), *outward(*new[:8]), *outward(*new[8:]),
        flip(next_err_col), next_err_row, flip(next_err_io), flip(right_col), flip(right_row), flip(right_io),
    )


def solution(mesh):
    weights = (
        P(None, "dp", "tensor"), P(None, "tensor", "dp"), P("dp", None), P("dp", None),
        P(None, "dp", None), P(None, "dp"), P(None, "tensor"), P(),
    )
    errors = (P("dp", None, "tensor"), P("dp", "tensor", None), P("dp", None, None))
    factors = (P(None, "tensor", None), P(None, "tensor", None), P())
    rows = P("dp", None, None)
    return jax.shard_map(
        on_device,
        mesh=mesh,
        in_specs=(rows, rows, P("dp"), P(), rows) + weights + weights + errors + factors,
        out_specs=(P(), P()) + weights + weights + errors + factors,
        check_vma=False,
    )
```
